256 devices in a mesh: mem: 4 (over z_lo, core), tile: 64 (over x, y, z_hi).
Axes of the slice: x: 4, y: 4, z: 8 (z_hi: 4, z_lo: 2; z = z_hi * 2 + z_lo), core: 2. Of those that a mesh axis runs over, the one named last changes fastest.
Arguments:
- alpha: bfloat16 [80, 512, 32, 128], P('mem', 'tile'), may hold values from -0.8984375 to 0.8984375
- ensemble: bfloat16 [80, 3, 512, 32, 128], P('mem', None, 'tile'), may hold values from -6 to 6
- loc_vert: bfloat16 [128, 128], replicated, may hold values from -0.25 to 1.5, as said below
- obs_col: int32 [64, 2048], P('tile'), may hold values from 0 to 1023
- obs_lev: int32 [64, 2048], P('tile'), may hold values from 0 to 127
- obs_count: int32 [64], P('tile'), may hold values from 512 to 2048
- innovation: float32 [64, 2048], P('tile'), may hold values from -6 to 6
- obs_weight: float32 [64, 2048], P('tile'), may hold values from 1 to 8
Outputs:
- gradient: float32 [80, 512, 32, 128], P('mem', 'tile')
The draws below stay inside these ranges and needn't reach their ends.
Inputs may be any that keep to these rules, and one draw needn't show every extreme that they name: `loc_vert`: a square root of the vertical localization, applied along levels.
All inputs are finite; a program needn't handle non-finite values.
Results may differ from the reference program's by a relative error of at most 0.0019.
Values sent between devices are 32-bit elements; how exact they have to be, the bound alone decides.
No kernel may reach another device: no remote copies, remote signals or barrier semaphores. Data moves between devices by JAX's collectives and lax.ppermute only.
A program may use at most 64 MiB of HBM per device.

```python
import math
import jax
import jax.numpy as jnp
from jax import lax

V = 3
L = 128
NS = 2
CY = 8
CX = 32
NOBS = 2048
MEMBERS = 80
NYC = 512
TILES = 64


def draw_loc_vert(key, part):
    base = jax.random.fold_in(key, 11)
    first, second = jax.random.split(base)
    diagonal = jax.random.uniform(first, (L,), jnp.float32, 0.5, 1.5)
    others = jax.random.normal(second, (L, L), jnp.float32) * (0.5 / jnp.sqrt(L * 1.0))
    whole = jnp.eye(L, dtype=jnp.float32) * diagonal[None, :] + others
    whole = jnp.clip(whole, -0.25, 1.5)
    return whole.astype(jnp.bfloat16)


def plant(array, key, smallest, high):
    longest = array.shape.index(max(array.shape))
    spots = []
    for shift in (0, 1):
        where = [jax.random.randint(jax.random.fold_in(key, axis), (), 0, length) for axis, length in enumerate(array.shape)]
        where[longest] = (where[longest] + shift) % array.shape[longest]
        spots.append(tuple(where))
    return array.at[spots[0]].set(smallest).at[spots[1]].set(high)


def block_scale(key, extent, pieces, smallest, high):
    def one(position, parts):
        draws = jax.random.uniform(jax.random.fold_in(jax.random.fold_in(key, 6), position), (parts,), jnp.float32, smallest / len(pieces), high / len(pieces))
        return jnp.repeat(jnp.exp(draws), extent[position] // parts).reshape((-1,) + (1,) * (len(extent) - position - 1))

    level = one(*pieces[0])
    for cut in pieces[1:]:
        level = level * one(*cut)
    return level


def normal_values(own_key, shape, width, reach, shards=(), kind=jnp.bfloat16):
    gain = block_scale(own_key, shape, shards, -0.22, 0.18) if shards else 1.0
    drawn = jax.random.normal(own_key, shape, jnp.float32) * width * gain
    return jnp.minimum(jnp.maximum(drawn, -reach), reach).astype(kind)


def setup_inputs(seed: int = 0) -> dict:
    key_of = jax.random.split(jax.random.key(seed), 9)
    alpha = normal_values(key_of[0], (MEMBERS, NYC, CX, L), 0.15, 0.8984375, ((0, 4), (1, 64)))
    ensemble = normal_values(key_of[1], (MEMBERS, V, NYC, CX, L), 1.0, 6.0, ((0, 4), (2, 64)))
    loc_vert = draw_loc_vert(jax.random.fold_in(key_of[8], 71), 0)
    obs_col = plant(jax.random.randint(key_of[3], (TILES, NOBS), 0, 4 * CY * CX), jax.random.fold_in(key_of[3], 1), 0, (4 * CY * CX) - 1).astype(jnp.int32)
    obs_lev = plant(jax.random.randint(key_of[4], (TILES, NOBS), 0, L), jax.random.fold_in(key_of[4], 1), 0, L - 1).astype(jnp.int32)
    obs_count = plant(jax.random.randint(key_of[5], (TILES,), NOBS // 4, NOBS + 1), jax.random.fold_in(key_of[5], 1), NOBS // 4, NOBS).astype(jnp.int32)
    innovation = normal_values(key_of[6], (TILES, NOBS), 1.0, 6.0, ((0, 64),), jnp.float32)
    obs_weight = jnp.clip(jnp.exp(math.log(8.0) - 2.0794415 * jax.random.uniform(key_of[7], (TILES, NOBS), jnp.float32) ** block_scale(key_of[7], (TILES, NOBS), ((0, 64),), -0.2, 0.2)), 1.0, 8.0)
    return dict(alpha=alpha, ensemble=ensemble, loc_vert=loc_vert, obs_col=obs_col, obs_lev=obs_lev, obs_count=obs_count, innovation=innovation, obs_weight=obs_weight)


def widen(field, axis):
    pads = [(1, 1) if dim == axis else (0, 0) for dim in range(field.ndim)]
    return jnp.pad(field, pads)


def spread(padded, axis):
    length = padded.shape[axis] - 2
    before = lax.slice_in_dim(padded, 0, length, axis=axis)
    middle = lax.slice_in_dim(padded, 1, length + 1, axis=axis)
    after = lax.slice_in_dim(padded, 2, length + 2, axis=axis)
    return 0.25 * before + 0.5 * middle + 0.25 * after


def smooth(field, row_axis):
    for sweep in range(NS):
        field = spread(widen(field, row_axis), row_axis)
        field = spread(widen(field, row_axis + 1), row_axis + 1)
    return field


def refine(padded, axis):
    length = padded.shape[axis] - 2
    before = lax.slice_in_dim(padded, 0, length, axis=axis)
    middle = lax.slice_in_dim(padded, 1, length + 1, axis=axis)
    after = lax.slice_in_dim(padded, 2, length + 2, axis=axis)
    evens = 0.75 * middle + 0.25 * before
    odds = 0.75 * middle + 0.25 * after
    stacked = jnp.stack([evens, odds], axis=axis + 1)
    shape = list(middle.shape)
    shape[axis] = 2 * length
    return stacked.reshape(shape)


def coarsen(padded, axis):
    length = padded.shape[axis] - 2
    first = lax.slice_in_dim(padded, 0, length, 2, axis=axis)
    second = lax.slice_in_dim(padded, 1, length + 1, 2, axis=axis)
    third = lax.slice_in_dim(padded, 2, length + 2, 2, axis=axis)
    fourth = lax.slice_in_dim(padded, 3, length + 2, 2, axis=axis)
    return 0.25 * first + 0.75 * second + 0.75 * third + 0.25 * fourth


def reference(alpha, ensemble, loc_vert, obs_col, obs_lev, obs_count, innovation, obs_weight):
    def add_member(running, member_item):
        control, member = member_item
        lifted = smooth(jnp.dot(control, loc_vert.T, preferred_element_type=jnp.float32), 0).astype(jnp.bfloat16)
        return running + member.astype(jnp.float32) * lifted.astype(jnp.float32)[None], 0

    initial = jnp.zeros(ensemble.shape[1:], jnp.float32)
    increment, unused = lax.scan(add_member, initial, (alpha, ensemble))
    fine = refine(widen(refine(widen(increment, 1), 1), 2), 2)
    strips = obs_col.shape[0]
    slots = obs_col.shape[1]
    strip_rows = fine.shape[1] // strips
    fine_width = fine.shape[2]
    variable = jnp.broadcast_to((jnp.arange(slots, dtype=jnp.int32) % V)[None, :], (strips, slots))
    row_index = jnp.arange(strips, dtype=jnp.int32)[:, None] * strip_rows + obs_col // fine_width
    col_index = obs_col % fine_width
    values = fine[variable, row_index, col_index, obs_lev]
    live = jnp.arange(slots, dtype=jnp.int32)[None, :] < obs_count[:, None]
    weighted = jnp.where(live, obs_weight * (values - innovation), jnp.zeros_like(values))
    fine_adjoint = jnp.zeros_like(fine).at[variable, row_index, col_index, obs_lev].add(weighted)
    coarse_adjoint = coarsen(widen(coarsen(widen(fine_adjoint, 2), 2), 1), 1)

    def member_gradient(member_item):
        control, member = member_item
        back = jnp.sum(member.astype(jnp.float32) * coarse_adjoint, axis=0)
        back = smooth(back, 0)
        return control.astype(jnp.float32) + jnp.dot(back, loc_vert.astype(jnp.float32), precision=lax.Precision.HIGHEST)

    return lax.map(member_gradient, (alpha, ensemble))
```

```python
import jax
import jax.numpy as jnp
from jax import lax
from jax.experimental import pallas as pl
from jax.experimental.pallas import tpu as pltpu
from jax.sharding import PartitionSpec as P

V = 3
F32 = jnp.float32
BF16 = jnp.bfloat16
SLOTS = 768
GROUP = 4

TILES = 64
EVEN = [(i, i ^ 1) for i in range(TILES)]
ODD = [(i, ((i - 1) ^ 1) + 1) for i in range(1, TILES - 1)] + [(0, TILES - 1), (TILES - 1, 0)]


def nn(a, b):
    return lax.dot_general(a, b, (((1,), (0,)), ((), ())), preferred_element_type=F32)


def nt(a, b):
    return lax.dot_general(a, b, (((1,), (1,)), ((), ())), preferred_element_type=F32)


def tn(a, b):
    return lax.dot_general(a, b, (((0,), (0,)), ((), ())), preferred_element_type=F32)


def halves(x):
    high = x.astype(BF16)
    low = (x - high.astype(F32)).astype(BF16)
    return high, low


def lift(smoothed, loc):
    high, low = halves(smoothed)
    return nt(high, loc) + nt(low, loc)


def call(kernel, out, grid=None, ins=None, outs=None, scratch=(), aliases=None, cost=1000000):
    vmem = pl.BlockSpec(memory_space=pltpu.VMEM)
    kw = {}
    if grid is not None:
        kw["grid"] = grid
    return pl.pallas_call(
        kernel,
        out_shape=out,
        in_specs=ins,
        out_specs=outs if outs is not None else jax.tree.map(lambda o: vmem, out),
        scratch_shapes=scratch,
        input_output_aliases=aliases or {},
        compiler_params=pltpu.CompilerParams(vmem_limit_bytes=24 * 1024 * 1024),
        cost_estimate=pl.CostEstimate(flops=cost, bytes_accessed=cost, transcendentals=0),
        **kw,
    )


def sds(*shape, dtype=F32):
    return jax.ShapeDtypeStruct(shape, dtype)


def own_kernel(alpha_ref, ens_ref, smat_ref, loc_ref, inner_ref, edge_ref):
    @pl.when(pl.program_id(0) == 0)
    def _():
        inner_ref[...] = jnp.zeros_like(inner_ref)

    smat = smat_ref[...]
    loc = loc_ref[...]
    total = [inner_ref[v] for v in range(V)]
    for k in range(GROUP):
        full = lift(nn(smat, alpha_ref[k]), loc)
        edge_ref[k, :64] = full[:64]
        edge_ref[k, 64:] = full[192:]
        lifted = full[64:192].astype(BF16).astype(F32)
        for v in range(V):
            total[v] = total[v] + ens_ref[k, v, 64:192].astype(F32) * lifted
    for v in range(V):
        inner_ref[v] = total[v]


def own_part(alpha, ensemble, smat, loc):
    members = alpha.shape[0]
    return call(
        own_kernel,
        (sds(V, 128, 128), sds(members, 128, 128)),
        grid=(members // GROUP,),
        ins=[
            pl.BlockSpec((GROUP, 256, 128), lambda i: (i, 0, 0)),
            pl.BlockSpec((GROUP, V, 256, 128), lambda i: (i, 0, 0, 0)),
            pl.BlockSpec((256, 256), lambda i: (0, 0)),
            pl.BlockSpec((128, 128), lambda i: (0, 0)),
        ],
        outs=(
            pl.BlockSpec((V, 128, 128), lambda i: (0, 0, 0)),
            pl.BlockSpec((GROUP, 128, 128), lambda i: (i, 0, 0)),
        ),
        cost=20000000,
    )(alpha, ensemble, smat, loc)


def edge_kernel(where_ref, e_ref, o_ref, own_ref, low_ref, high_ref, hmat_ref, loc_ref, inner_ref, inc_ref, se_ref, so_ref):
    step = pl.program_id(0)

    @pl.when(step == 0)
    def _():
        zeros = jnp.zeros((64, 128), F32)
        for v in range(V):
            inc_ref[v, :64] = zeros
            inc_ref[v, 64:192] = inner_ref[v]
            inc_ref[v, 192:] = zeros

    hmat = hmat_ref[...]
    loc = loc_ref[...]
    low = [inc_ref[v, :64] for v in range(V)]
    high = [inc_ref[v, 192:] for v in range(V)]
    for k in range(GROUP):
        halo = jnp.concatenate([e_ref[k].astype(BF16), o_ref[k].astype(BF16)], axis=0)
        lifted = (own_ref[k] + lift(nn(hmat, halo), loc)).astype(BF16).astype(F32)
        for v in range(V):
            low[v] = low[v] + low_ref[k, v, 0].astype(F32) * lifted[:64]
            high[v] = high[v] + high_ref[k, v, 0].astype(F32) * lifted[64:]
    for v in range(V):
        inc_ref[v, :64] = low[v]
        inc_ref[v, 192:] = high[v]

    @pl.when(step == pl.num_programs(0) - 1)
    def _():
        for v in range(V):
            se_ref[v] = inc_ref[v, pl.ds(pl.multiple_of(where_ref[0], 32), 32)]
            so_ref[v] = inc_ref[v, pl.ds(pl.multiple_of(where_ref[1], 32), 32)]


def edge_part(where, from_even, from_odd, own, quarters, hmat, loc, inner):
    members = own.shape[0]
    return call(
        edge_kernel,
        (sds(V, 256, 128), sds(V, 32, 128), sds(V, 32, 128)),
        grid=(members // GROUP,),
        ins=[
            pl.BlockSpec(memory_space=pltpu.SMEM),
            pl.BlockSpec((GROUP, 64, 128), lambda i: (i, 0, 0)),
            pl.BlockSpec((GROUP, 64, 128), lambda i: (i, 0, 0)),
            pl.BlockSpec((GROUP, 128, 128), lambda i: (i, 0, 0)),
            pl.BlockSpec((GROUP, V, 1, 64, 128), lambda i: (i, 0, 0, 0, 0)),
            pl.BlockSpec((GROUP, V, 1, 64, 128), lambda i: (i, 0, 3, 0, 0)),
            pl.BlockSpec((128, 128), lambda i: (0, 0)),
            pl.BlockSpec((128, 128), lambda i: (0, 0)),
            pl.BlockSpec((V, 128, 128), lambda i: (0, 0, 0)),
        ],
        outs=(
            pl.BlockSpec((V, 256, 128), lambda i: (0, 0, 0)),
            pl.BlockSpec((V, 32, 128), lambda i: (0, 0, 0)),
            pl.BlockSpec((V, 32, 128), lambda i: (0, 0, 0)),
        ),
    )(where, from_even, from_odd, own, quarters, quarters, hmat, loc, inner)


def tent(distance):
    return jnp.maximum(1.0 - jnp.abs(distance), 0.0)


def weights_kernel(where_ref, own_ref, e_ref, o_ref, wown_ref, wnear_ref):
    even_row = where_ref[2].astype(F32)
    odd_row = where_ref[3].astype(F32)
    odd_there = where_ref[4].astype(F32)
    cell = lax.broadcasted_iota(jnp.int32, (32, SLOTS), 0).astype(F32)

    def columns(code):
        row = jnp.floor(code * (1.0 / 64.0))
        column = code - 64.0 * row
        return row, tent(cell - (column * 0.5 - 0.25))

    for v in range(V):
        row, across = columns(own_ref[0, v : v + 1, :])
        middle = row * 0.5 - 0.25
        for r in range(8):
            wown_ref[v, 32 * r : 32 * r + 32] = (tent(r - middle) * across).astype(BF16)
        wown_ref[v, 256:288] = (tent(even_row - middle) * across).astype(BF16)
        wown_ref[v, 288:320] = (tent(odd_row - middle) * odd_there * across).astype(BF16)
        for n, ref in enumerate((e_ref, o_ref)):
            row, across = columns(ref[0, v : v + 1, :])
            wnear_ref[n, v, :32] = (0.25 * across).astype(BF16)
            wnear_ref[n, v, 32:] = (0.75 * across).astype(BF16)


def weights(where, own, even, odd):
    vmem = pl.BlockSpec(memory_space=pltpu.VMEM)
    return call(
        weights_kernel,
        (sds(V, 320, SLOTS, dtype=BF16), sds(2, V, 64, SLOTS, dtype=BF16)),
        ins=[pl.BlockSpec(memory_space=pltpu.SMEM), vmem, vmem, vmem],
        cost=5000000,
    )(where, own, even, odd)


def values_kernel(where_ref, inc_ref, e_ref, o_ref, wown_ref, wnear_ref, lev_ref, out_ref):
    level = lax.broadcasted_iota(jnp.int32, (128, SLOTS), 0).astype(F32)

    def pick(cells, weight, row):
        both = jnp.concatenate(halves(cells), axis=1)
        at_all = tn(both, weight)
        at_all = at_all[:128] + at_all[128:]
        hot = level == lev_ref[row : row + 1, :]
        out_ref[row : row + 1, :] = jnp.sum(jnp.where(hot, at_all, 0.0), axis=0, keepdims=True)

    for v in range(V):
        pick(jnp.concatenate([inc_ref[v], e_ref[v], o_ref[v]], axis=0), wown_ref[v], v)
        for n, ref in enumerate((e_ref, o_ref)):
            mine = inc_ref[v, pl.ds(pl.multiple_of(where_ref[n], 32), 32)]
            pick(jnp.concatenate([mine, ref[v]], axis=0), wnear_ref[n, v], 3 * n + 3 + v)


def values(where, inc, even, odd, wown, wnear, lev):
    vmem = pl.BlockSpec(memory_space=pltpu.VMEM)
    return call(
        values_kernel,
        sds(9, SLOTS),
        ins=[pl.BlockSpec(memory_space=pltpu.SMEM)] + [vmem] * 6,
        outs=vmem,
    )(where, inc, even, odd, wown, wnear, lev)


def adjoint_kernel(where_ref, v0, v1, v2, v3, innov_ref, weight_ref, lev_ref, wown_ref, wnear_ref, ens_ref, c_ref, se_ref, so_ref, near, sems):
    members = se_ref.shape[0]
    copies = [
        pltpu.make_async_copy(ens_ref.at[:, :, pl.ds(3 * n, 1)], near.at[:, :, pl.ds(n, 1)], sems.at[n])
        for n in range(2)
    ]
    for copy in copies:
        copy.start()
    level = lax.broadcasted_iota(jnp.int32, (128, SLOTS), 0).astype(F32)
    value = v0[...] + v1[...] + v2[...] + v3[...]
    weighted = weight_ref[...] * (value - innov_ref[...])

    def place(weight, row):
        hot = level == lev_ref[row : row + 1, :]
        spread = jnp.where(hot, weighted[row : row + 1, :], 0.0)
        both = jnp.concatenate(halves(spread), axis=0)
        out = nt(weight, both)
        return out[:, :128] + out[:, 128:]

    for v in range(V):
        c_ref[v] = place(wown_ref[v, :256], v)
        for n in range(2):
            rows = pl.ds(pl.multiple_of(where_ref[n], 32), 32)
            c_ref[v, rows] = c_ref[v, rows] + place(wnear_ref[n, v, :32], 3 * n + 3 + v)
    for copy in copies:
        copy.wait()
    odd_strip = where_ref[5]
    for n, ref in enumerate((se_ref, so_ref)):
        side = (1 - odd_strip) if n == 0 else odd_strip
        start = pl.multiple_of(192 * side, 64)
        adj = [c_ref[v, pl.ds(start, 64)] for v in range(V)]

        @pl.loop(0, members)
        def _(k):
            total = near[k, 0, side].astype(F32) * adj[0]
            for v in range(1, V):
                total = total + near[k, v, side].astype(F32) * adj[v]
            ref[k] = total


def adjoint(where, vals, innov, weight, lev, wown, wnear, quarters):
    members = quarters.shape[0]
    vmem = pl.BlockSpec(memory_space=pltpu.VMEM)
    return call(
        adjoint_kernel,
        (sds(V, 256, 128), sds(members, 64, 128), sds(members, 64, 128)),
        ins=[pl.BlockSpec(memory_space=pltpu.SMEM)] + [vmem] * 9 + [pl.BlockSpec(memory_space=pl.ANY)],
        scratch=[pltpu.VMEM((members, V, 2, 64, 128), BF16), pltpu.SemaphoreType.DMA((2,))],
    )(where, *vals, innov, weight, lev, wown, wnear, quarters)


def drop(smoothed, loc):
    high, low = halves(smoothed)
    return nn(high, loc) + nn(low, loc)


def smooth(matrix, field):
    both = jnp.concatenate(halves(field), axis=1)
    out = nn(matrix, both)
    return out[:, :128] + out[:, 128:]


def back_kernel(alpha_ref, ens_ref, c_ref, smat_ref, loc_ref, out_ref, edge_ref):
    smat = smat_ref[...]
    loc = loc_ref[...]
    for k in range(GROUP):
        back = ens_ref[k, 0].astype(F32) * c_ref[0]
        for v in range(1, V):
            back = back + ens_ref[k, v].astype(F32) * c_ref[v]
        full = alpha_ref[k].astype(F32) + drop(smooth(smat, back), loc)
        out_ref[k] = full
        edge_ref[k, :64] = full[:64]
        edge_ref[k, 64:] = full[192:]


def back_part(alpha, ensemble, c, smat, loc):
    members = alpha.shape[0]
    return call(
        back_kernel,
        (sds(members, 256, 128), sds(members, 128, 128)),
        grid=(members // GROUP,),
        ins=[
            pl.BlockSpec((GROUP, 256, 128), lambda i: (i, 0, 0)),
            pl.BlockSpec((GROUP, V, 256, 128), lambda i: (i, 0, 0, 0)),
            pl.BlockSpec((V, 256, 128), lambda i: (0, 0, 0)),
            pl.BlockSpec((256, 256), lambda i: (0, 0)),
            pl.BlockSpec((128, 128), lambda i: (0, 0)),
        ],
        outs=(
            pl.BlockSpec((GROUP, 256, 128), lambda i: (i, 0, 0)),
            pl.BlockSpec((GROUP, 128, 128), lambda i: (i, 0, 0)),
        ),
        cost=20000000,
    )(alpha, ensemble, c, smat, loc)


def last_kernel(e_ref, o_ref, edge_ref, hmat_ref, loc_ref, unused_ref, out_ref, held):
    side = pl.program_id(1)

    @pl.when(side == 0)
    def _():
        hmat = hmat_ref[...]
        loc = loc_ref[...]
        for k in range(GROUP):
            halo = jnp.concatenate([e_ref[k], o_ref[k]], axis=0)
            full = edge_ref[k] + drop(smooth(hmat, halo), loc)
            out_ref[k, 0] = full[:64]
            held[k] = full[64:]

    @pl.when(side == 1)
    def _():
        out_ref[:, 0] = held[...]


def last_part(from_even, from_odd, edge, hmat, loc, out):
    members = edge.shape[0]
    return call(
        last_kernel,
        sds(members, 4, 64, 128),
        grid=(members // GROUP, 2),
        ins=[
            pl.BlockSpec((GROUP, 64, 128), lambda i, j: (i, 0, 0)),
            pl.BlockSpec((GROUP, 64, 128), lambda i, j: (i, 0, 0)),
            pl.BlockSpec((GROUP, 128, 128), lambda i, j: (i, 0, 0)),
            pl.BlockSpec((128, 128), lambda i, j: (0, 0)),
            pl.BlockSpec((128, 128), lambda i, j: (0, 0)),
            pl.BlockSpec(memory_space=pl.ANY),
        ],
        outs=pl.BlockSpec((GROUP, 1, 64, 128), lambda i, j: (i, 3 * j, 0, 0)),
        scratch=[pltpu.VMEM((GROUP, 64, 128), F32)],
        aliases={5: 0},
    )(from_even, from_odd, edge, hmat, loc, out)


def stencil(gap):
    gap = jnp.abs(gap)
    return jnp.where(gap == 0, 6.0, jnp.where(gap == 1, 4.0, jnp.where(gap == 2, 1.0, 0.0)))


def matrices(tile, tiles, even):
    def across(i, j):
        gap = stencil(i - j)
        return jnp.where((i == j) & ((i == 0) | (i == 31)), 5.0, gap)

    i = lax.broadcasted_iota(jnp.int32, (256, 256), 0)
    j = lax.broadcasted_iota(jnp.int32, (256, 256), 1)
    ri, rj = i // 32, j // 32
    ends = ((ri == 0) & (tile == 0)) | ((ri == 7) & (tile == tiles - 1))
    down = jnp.where((ri == rj) & ends, 5.0, stencil(ri - rj))
    smat = (down * across(i % 32, j % 32) * (1.0 / 256.0)).astype(BF16)
    i = lax.broadcasted_iota(jnp.int32, (128, 128), 0)
    j = lax.broadcasted_iota(jnp.int32, (128, 128), 1)
    ri = i // 32
    ri = jnp.where(ri < 2, ri, ri + 4)
    is_even = j < 64
    above = is_even == even
    rj = jnp.where(above, 8, -2) + (j // 32) % 2
    there = is_even | ((tile > 0) & (tile < tiles - 1))
    hmat = jnp.where(there, stencil(ri - rj), 0.0) * across(i % 32, j % 32) * (1.0 / 256.0)
    return smat, hmat.astype(BF16)


def swap_even(x):
    return lax.ppermute(x, "tile", EVEN)


def swap_odd(x):
    return lax.ppermute(x, "tile", ODD)


def by_variable(x):
    return jnp.pad(x, (0, V * SLOTS - x.shape[0])).reshape(SLOTS, V).T


def on_device(alpha, ensemble, loc_vert, obs_col, obs_lev, obs_count, innovation, obs_weight):
    members = alpha.shape[0]
    tile = lax.axis_index("tile")
    tiles = lax.axis_size("tile")
    even = tile % 2 == 0
    odd_there = (tile > 0) & (tile < tiles - 1)

    high, low = alpha[:, 6:], alpha[:, :2]
    to_even = jnp.where(even, high, low).astype(F32).reshape(members, 64, 128)
    to_odd = jnp.where(even, low, high).astype(F32).reshape(members, 64, 128)
    from_even = swap_even(to_even)
    from_odd = swap_odd(to_odd)

    live = jnp.arange(obs_col.shape[1], dtype=jnp.int32) < obs_count[0]
    own_obs = jnp.stack(
        [
            by_variable(obs_col[0].astype(F32)),
            by_variable(obs_lev[0].astype(F32)),
            by_variable(innovation[0]),
            by_variable(jnp.where(live, obs_weight[0], 0.0)),
        ]
    )
    even_obs = swap_even(own_obs)
    odd_obs = swap_odd(own_obs)
    even_on = jnp.where(even, even_obs[0] < 64.0, even_obs[0] >= 960.0)
    odd_on = jnp.where(even, odd_obs[0] >= 960.0, odd_obs[0] < 64.0) & odd_there
    lev = jnp.concatenate([own_obs[1], even_obs[1], odd_obs[1]])
    innov = jnp.concatenate([own_obs[2], even_obs[2], odd_obs[2]])
    weight = jnp.concatenate(
        [own_obs[3], jnp.where(even_on, even_obs[3], 0.0), jnp.where(odd_on, odd_obs[3], 0.0)]
    )
    at_even = jnp.where(even, 7 * 32, 0)
    at_odd = jnp.where(even, 0, 7 * 32)
    where = jnp.stack(
        [
            at_even,
            at_odd,
            jnp.where(even, 8, -1),
            jnp.where(even, -1, 8),
            odd_there.astype(jnp.int32),
            tile % 2,
        ]
    ).astype(jnp.int32)
    smat, hmat = matrices(tile, tiles, even)

    flat = alpha.reshape(members, 256, 128)
    flat_ens = ensemble.reshape(members, V, 256, 128)
    quarters = ensemble.reshape(members, V, 4, 64, 128)
    inner, own_edge = own_part(flat, flat_ens, smat, loc_vert)
    wown, wnear = weights(where, own_obs, even_obs, odd_obs)
    inc, inc_even, inc_odd = edge_part(where, from_even, from_odd, own_edge, quarters, hmat, loc_vert, inner)
    near_even = swap_even(inc_even)
    near_odd = swap_odd(inc_odd)
    mine = values(where, inc, near_even, near_odd, wown, wnear, lev)
    size = lax.axis_size("mem")
    vals = [mine] + [
        lax.ppermute(mine, "mem", [(i, (i + shift) % size) for i in range(size)]) for shift in range(1, size)
    ]
    c, back_even, back_odd = adjoint(where, vals, innov, weight, lev, wown, wnear, quarters)
    halo_even = swap_even(back_even)
    halo_odd = swap_odd(back_odd)
    out, out_edge = back_part(flat, flat_ens, c, smat, loc_vert)
    out = last_part(halo_even, halo_odd, out_edge, hmat, loc_vert, out.reshape(members, 4, 64, 128))
    return out.reshape(members, 8, 32, 128)


def solution(mesh):
    in_specs = (
        P("mem", "tile", None, None),
        P("mem", None, "tile", None, None),
        P(),
        P("tile", None),
        P("tile", None),
        P("tile"),
        P("tile", None),
        P("tile", None),
    )
    out_specs = P("mem", "tile", None, None)
    return jax.shard_map(
        on_device, mesh=mesh, in_specs=in_specs, out_specs=out_specs, check_vma=False
    )
```

```python
import functools

import jax
import jax.numpy as jnp
from jax import lax
from jax.experimental import pallas as pl
from jax.experimental.pallas import tpu as pltpu
from jax.sharding import PartitionSpec as P

V = 3
F32 = jnp.float32
BF16 = jnp.bfloat16
SLOTS = 768
GROUP = 4
PAIRS = 10

TILES = 64
EVEN = [(i, i ^ 1) for i in range(TILES)]
ODD = [(i, ((i - 1) ^ 1) + 1) for i in range(1, TILES - 1)] + [(0, TILES - 1), (TILES - 1, 0)]


def nn(a, b):
    return lax.dot_general(a, b, (((1,), (0,)), ((), ())), preferred_element_type=F32)


def nt(a, b):
    return lax.dot_general(a, b, (((1,), (1,)), ((), ())), preferred_element_type=F32)


def tn(a, b):
    return lax.dot_general(a, b, (((0,), (0,)), ((), ())), preferred_element_type=F32)


def halves(x):
    high = x.astype(BF16)
    low = (x - high.astype(F32)).astype(BF16)
    return high, low


def lift(smoothed, loc):
    high, low = halves(smoothed)
    return nt(high, loc) + nt(low, loc)


def call(kernel, out, grid=None, ins=None, outs=None, scratch=(), aliases=None, cost=1000000):
    vmem = pl.BlockSpec(memory_space=pltpu.VMEM)
    kw = {}
    if grid is not None:
        kw["grid"] = grid
    return pl.pallas_call(
        kernel,
        out_shape=out,
        in_specs=ins,
        out_specs=outs if outs is not None else jax.tree.map(lambda o: vmem, out),
        scratch_shapes=scratch,
        input_output_aliases=aliases or {},
        compiler_params=pltpu.CompilerParams(vmem_limit_bytes=24 * 1024 * 1024),
        cost_estimate=pl.CostEstimate(flops=cost, bytes_accessed=cost, transcendentals=0),
        **kw,
    )


def sds(*shape, dtype=F32):
    return jax.ShapeDtypeStruct(shape, dtype)


ANY = pl.BlockSpec(memory_space=pl.ANY)
SMEM = pl.BlockSpec(memory_space=pltpu.SMEM)
VMEM = pl.BlockSpec(memory_space=pltpu.VMEM)


def smooth(matrix, field):
    both = jnp.concatenate(halves(field), axis=1)
    out = nn(matrix, both)
    return out[:, :128] + out[:, 128:]


def twice(loc):
    zeros = jnp.zeros_like(loc)
    return jnp.concatenate(
        [jnp.concatenate([loc, zeros], axis=1), jnp.concatenate([zeros, loc], axis=1)], axis=0
    )


def edge_levels(first, second, both, odd, e_ref, o_ref, p):
    out = nt(jnp.concatenate([first, second], axis=1), both)
    low, high = out[:64], out[64:]
    e_ref[p] = jnp.where(odd, low, high)
    o_ref[p] = jnp.where(odd, high, low)


def send_kernel(where_ref, low_ref, high_ref, loc_ref, e_ref, o_ref, token_ref):
    odd = where_ref[5] == 1
    both = twice(loc_ref[:64])
    for p in range(PAIRS):
        members = [jnp.concatenate([low_ref[m, p, 0], high_ref[m, p, 0]], axis=0) for m in range(2)]
        edge_levels(*members, both, odd, e_ref, o_ref, p)
    token_ref[...] = jnp.zeros_like(token_ref)


def send_part(where, quarters, loc):
    edge = lambda q: pl.BlockSpec((2, PAIRS, 1, 64, 128), lambda i: (0, 0, q, 0, 0))
    flat = pl.BlockSpec((PAIRS, 64, 128), lambda i: (0, 0, 0))
    return call(
        send_kernel,
        (sds(PAIRS, 64, 128), sds(PAIRS, 64, 128), sds(8, 128)),
        grid=(1,),
        ins=[SMEM, edge(0), edge(3), pl.BlockSpec((128, 128), lambda i: (0, 0))],
        outs=(flat, flat, pl.BlockSpec((8, 128), lambda i: (0, 0))),
    )(where, quarters, quarters, loc)


def packed(first, second, h):
    return jnp.concatenate([first[:, 64 * h : 64 * h + 64], second[:, 64 * h : 64 * h + 64]], axis=1)


def own_kernel(where_ref, alpha_ref, ens_ref, loc_ref, after_ref, inner_ref, la_ref, lb_ref, xa_ref, xb_ref, smat_ref, hmat_ref, token_ref, eb_ref, ob_ref):
    @pl.when(pl.program_id(0) == 0)
    def _():
        inner_ref[...] = jnp.zeros_like(inner_ref)
        token_ref[...] = jnp.zeros_like(token_ref)
        smat, hmat = matrices(where_ref[6], TILES, where_ref[5] == 0)
        smat_ref[...] = smat
        hmat_ref[...] = hmat

    smat = smat_ref[...]
    loc = loc_ref[...]
    total = [inner_ref[v] for v in range(V)]
    odd = where_ref[5] == 1
    both = twice(loc[64:])
    for p in range(2):
        members = [jnp.concatenate([alpha_ref[m, p, :64], alpha_ref[m, p, 192:]], axis=0) for m in range(2)]
        edge_levels(*members, both, odd, eb_ref, ob_ref, p)
        edges = []
        for m in range(2):
            full = lift(nn(smat, alpha_ref[m, p]), loc)
            edges.append(jnp.concatenate([full[:64], full[192:]], axis=0))
            lifted = full[64:192].astype(BF16).astype(F32)
            for v in range(V):
                total[v] = total[v] + ens_ref[m, p, v, 64:192].astype(F32) * lifted
        for h, (l_ref, x_ref) in enumerate(((la_ref, xa_ref), (lb_ref, xb_ref))):
            l_ref[p] = packed(edges[0], edges[1], h)
            for v in range(V):
                for side in range(2):
                    rows = slice(192 * side, 192 * side + 64)
                    x_ref[p, v, 64 * side : 64 * side + 64] = packed(ens_ref[0, p, v, rows], ens_ref[1, p, v, rows], h)
    for v in range(V):
        inner_ref[v] = total[v]


def own_part(where, alpha, ensemble, loc, after):
    whole = lambda *shape: pl.BlockSpec(shape, lambda i: (0,) * len(shape))
    fields = pl.BlockSpec((2, 128, 128), lambda i: (i, 0, 0))
    members = pl.BlockSpec((2, V, 128, 128), lambda i: (i, 0, 0, 0))
    return call(
        own_kernel,
        (
            sds(V, 128, 128),
            sds(PAIRS, 128, 128),
            sds(PAIRS, 128, 128),
            sds(PAIRS, V, 128, 128, dtype=BF16),
            sds(PAIRS, V, 128, 128, dtype=BF16),
            sds(256, 256, dtype=BF16),
            sds(128, 128, dtype=BF16),
            sds(8, 128),
            sds(PAIRS, 64, 128),
            sds(PAIRS, 64, 128),
        ),
        grid=(PAIRS // 2,),
        ins=[
            SMEM,
            pl.BlockSpec((2, 2, 256, 128), lambda i: (0, i, 0, 0)),
            pl.BlockSpec((2, 2, V, 256, 128), lambda i: (0, i, 0, 0, 0)),
            whole(128, 128),
            whole(8, 128),
        ],
        outs=(
            whole(V, 128, 128),
            fields,
            fields,
            members,
            members,
            whole(256, 256),
            whole(128, 128),
            whole(8, 128),
            pl.BlockSpec((2, 64, 128), lambda i: (i, 0, 0)),
            pl.BlockSpec((2, 64, 128), lambda i: (i, 0, 0)),
        ),
    )(where, alpha, ensemble, loc, after)


def pass_kernel(obs_ref, after_ref, out_ref):
    out_ref[...] = obs_ref[...]


def pass_on(obs, after):
    return call(pass_kernel, sds(*obs.shape), ins=[VMEM, VMEM], outs=VMEM)(obs, after)


def edge_kernel(h, where_ref, e_ref, o_ref, own_ref, x_ref, hmat_ref, loc_ref, inner_ref, after_ref, inc_ref, se_ref, so_ref):
    hmat = hmat_ref[...]
    total = [jnp.zeros((128, 128), F32) for v in range(V)]
    for p in range(PAIRS):
        halo = jnp.concatenate([e_ref[p], o_ref[p]], axis=0)
        lifted = (own_ref[p] + smooth(hmat, halo)).astype(BF16).astype(F32)
        for v in range(V):
            total[v] = total[v] + x_ref[p, v].astype(F32) * lifted
    for v in range(V):
        edges = total[v][:, :64] + total[v][:, 64:]
        inc_ref[v, :64] = edges[:64]
        inc_ref[v, 64:192] = inner_ref[v][:, 64 * h : 64 * h + 64]
        inc_ref[v, 192:] = edges[64:]
        for n, ref in enumerate((se_ref, so_ref)):
            row = inc_ref[v, pl.ds(pl.multiple_of(where_ref[n], 32), 32)]
            ref[v] = jnp.concatenate([row[:16], row[16:]], axis=1)


def edge_part(h, where, from_even, from_odd, own, x, hmat, loc, inner, after):
    return call(
        functools.partial(edge_kernel, h),
        (sds(V, 256, 64), sds(V, 16, 128), sds(V, 16, 128)),
        ins=[SMEM] + [VMEM] * 8,
        outs=(VMEM,) * 3,
    )(where, from_even, from_odd, own, x, hmat, loc, inner, after)


def tent(distance):
    return jnp.maximum(1.0 - jnp.abs(distance), 0.0)


def weights_kernel(where_ref, own_ref, e_ref, o_ref, wown_ref, wnear_ref):
    even_row = where_ref[2].astype(F32)
    odd_row = where_ref[3].astype(F32)
    odd_there = where_ref[4].astype(F32)
    cell = lax.broadcasted_iota(jnp.int32, (32, SLOTS), 0).astype(F32)

    def columns(code):
        row = jnp.floor(code * (1.0 / 64.0))
        column = code - 64.0 * row
        return row, tent(cell - (column * 0.5 - 0.25))

    for v in range(V):
        row, across = columns(own_ref[0, v : v + 1, :])
        middle = row * 0.5 - 0.25
        for r in range(8):
            wown_ref[v, 32 * r : 32 * r + 32] = (tent(r - middle) * across).astype(BF16)
        wown_ref[v, 256:288] = (tent(even_row - middle) * across).astype(BF16)
        wown_ref[v, 288:320] = (tent(odd_row - middle) * odd_there * across).astype(BF16)
        for n, ref in enumerate((e_ref, o_ref)):
            row, across = columns(ref[0, v : v + 1, :])
            wnear_ref[n, v, :32] = (0.25 * across).astype(BF16)
            wnear_ref[n, v, 32:] = (0.75 * across).astype(BF16)


def weights(where, own, even, odd):
    vmem = pl.BlockSpec(memory_space=pltpu.VMEM)
    return call(
        weights_kernel,
        (sds(V, 320, SLOTS, dtype=BF16), sds(2, V, 64, SLOTS, dtype=BF16)),
        ins=[pl.BlockSpec(memory_space=pltpu.SMEM), vmem, vmem, vmem],
        cost=5000000,
    )(where, own, even, odd)


def values_kernel(h, where_ref, inc_ref, e_ref, o_ref, wown_ref, wnear_ref, lev_ref, after_ref, out_ref):
    level = lax.broadcasted_iota(jnp.int32, (64, SLOTS), 0).astype(F32) + 64.0 * h

    def pick(cells, weight, row):
        both = jnp.concatenate(halves(cells), axis=1)
        at_all = tn(both, weight)
        at_all = at_all[:64] + at_all[64:]
        hot = level == lev_ref[row : row + 1, :]
        out_ref[row : row + 1, :] = jnp.sum(jnp.where(hot, at_all, 0.0), axis=0, keepdims=True)

    for v in range(V):
        near = []
        for ref in (e_ref, o_ref):
            row = ref[v]
            near.append(jnp.concatenate([row[:, :64], row[:, 64:]], axis=0))
        pick(jnp.concatenate([inc_ref[v]] + near, axis=0), wown_ref[v], v)
        for n in range(2):
            mine = inc_ref[v, pl.ds(pl.multiple_of(where_ref[n], 32), 32)]
            pick(jnp.concatenate([mine, near[n]], axis=0), wnear_ref[n, v], 3 * n + 3 + v)


def values(h, where, inc, even, odd, wown, wnear, lev, after):
    return call(
        functools.partial(values_kernel, h),
        sds(9, SLOTS),
        ins=[SMEM] + [VMEM] * 7,
        outs=VMEM,
    )(where, inc, even, odd, wown, wnear, lev, after)


def adjoint_kernel(h, where_ref, v0, v1, v2, v3, innov_ref, weight_ref, lev_ref, wown_ref, wnear_ref, x_ref, after_ref, c_ref, se_ref, so_ref):
    level = lax.broadcasted_iota(jnp.int32, (64, SLOTS), 0).astype(F32) + 64.0 * h
    value = v0[...] + v1[...] + v2[...] + v3[...]
    weighted = weight_ref[...] * (value - innov_ref[...])

    def place(weight, row):
        hot = level == lev_ref[row : row + 1, :]
        spread = jnp.where(hot, weighted[row : row + 1, :], 0.0)
        both = jnp.concatenate(halves(spread), axis=0)
        out = nt(weight, both)
        return out[:, :64] + out[:, 64:]

    adj = []
    for v in range(V):
        c_ref[v] = place(wown_ref[v, :256], v)
        for n in range(2):
            rows = pl.ds(pl.multiple_of(where_ref[n], 32), 32)
            c_ref[v, rows] = c_ref[v, rows] + place(wnear_ref[n, v, :32], 3 * n + 3 + v)
        edges = jnp.concatenate([c_ref[v, :64], c_ref[v, 192:]], axis=0)
        adj.append(jnp.concatenate([edges, edges], axis=1))
    odd = where_ref[5] == 1
    for p in range(PAIRS):
        total = x_ref[p, 0].astype(F32) * adj[0]
        for v in range(1, V):
            total = total + x_ref[p, v].astype(F32) * adj[v]
        low, high = total[:64], total[64:]
        se_ref[p] = jnp.where(odd, low, high)
        so_ref[p] = jnp.where(odd, high, low)


def adjoint(h, where, vals, innov, weight, lev, wown, wnear, x, after):
    return call(
        functools.partial(adjoint_kernel, h),
        (sds(V, 256, 64), sds(PAIRS, 64, 128), sds(PAIRS, 64, 128)),
        ins=[SMEM] + [VMEM] * 11,
        outs=(VMEM,) * 3,
    )(where, *vals, innov, weight, lev, wown, wnear, x, after)


def drop(smoothed, loc):
    high, low = halves(smoothed)
    return nn(high, loc) + nn(low, loc)


def back_kernel(alpha_ref, ens_ref, ca_ref, cb_ref, smat_ref, loc_ref, out_ref, edge_ref, c_ref):
    @pl.when(pl.program_id(0) == 0)
    def _():
        for v in range(V):
            c_ref[v] = jnp.concatenate([ca_ref[v], cb_ref[v]], axis=1)

    smat = smat_ref[...]
    loc = loc_ref[...]
    for k in range(GROUP):
        back = ens_ref[k, 0].astype(F32) * c_ref[0]
        for v in range(1, V):
            back = back + ens_ref[k, v].astype(F32) * c_ref[v]
        full = alpha_ref[k].astype(F32) + drop(smooth(smat, back), loc)
        out_ref[k] = full
        edge_ref[k, :64] = full[:64]
        edge_ref[k, 64:] = full[192:]


def back_part(alpha, ensemble, ca, cb, smat, loc):
    members = alpha.shape[0]
    half = pl.BlockSpec((V, 256, 64), lambda i: (0, 0, 0))
    return call(
        back_kernel,
        (sds(members, 256, 128), sds(members, 128, 128)),
        grid=(members // GROUP,),
        ins=[
            pl.BlockSpec((GROUP, 256, 128), lambda i: (i, 0, 0)),
            pl.BlockSpec((GROUP, V, 256, 128), lambda i: (i, 0, 0, 0)),
            half,
            half,
            pl.BlockSpec((256, 256), lambda i: (0, 0)),
            pl.BlockSpec((128, 128), lambda i: (0, 0)),
        ],
        outs=(
            pl.BlockSpec((GROUP, 256, 128), lambda i: (i, 0, 0)),
            pl.BlockSpec((GROUP, 128, 128), lambda i: (i, 0, 0)),
        ),
        scratch=[pltpu.VMEM((V, 256, 128), F32)],
    )(alpha, ensemble, ca, cb, smat, loc)


def halo_terms(e_ref, o_ref, hmat, loc, p):
    halo = jnp.concatenate([e_ref[p], o_ref[p]], axis=0)
    return drop(smooth(hmat, halo), loc)


def first_kernel(e_ref, o_ref, edge_ref, hmat_ref, loc_ref, out_ref):
    hmat = hmat_ref[...]
    loc = twice(loc_ref[:64])
    for p in range(PAIRS):
        terms = halo_terms(e_ref, o_ref, hmat, loc, p)
        out_ref[p] = edge_ref[p] + terms[:, :128]
        out_ref[p + PAIRS] = edge_ref[p + PAIRS] + terms[:, 128:]


def first_part(from_even, from_odd, edge, hmat, loc):
    return call(first_kernel, sds(*edge.shape), ins=[VMEM] * 5, outs=VMEM)(from_even, from_odd, edge, hmat, loc)


def last_kernel(e_ref, o_ref, edge_ref, hmat_ref, loc_ref, unused_ref, out_ref, held, sems):
    hmat = hmat_ref[...]
    loc = twice(loc_ref[64:])
    copies = []
    for p in range(PAIRS):
        terms = halo_terms(e_ref, o_ref, hmat, loc, p)
        for m in range(2):
            full = edge_ref[p + m * PAIRS] + terms[:, 128 * m : 128 * m + 128]
            held[m, p, 0] = full[:64]
            held[m, p, 1] = full[64:]
        if p % 2:
            group = pl.ds(p - 1, 2)
            for side in range(2):
                copies.append(
                    pltpu.make_async_copy(
                        held.at[:, group, side], out_ref.at[:, group, 3 * side], sems.at[p // 2, side]
                    )
                )
                copies[-1].start()
    for copy in copies:
        copy.wait()


def last_part(from_even, from_odd, edge, hmat, loc, out):
    return call(
        last_kernel,
        sds(*out.shape),
        ins=[VMEM] * 5 + [ANY],
        outs=ANY,
        scratch=[pltpu.VMEM((2, PAIRS, 2, 64, 128), F32), pltpu.SemaphoreType.DMA((PAIRS // 2, 2))],
        aliases={5: 0},
    )(from_even, from_odd, edge, hmat, loc, out)


def stencil(gap):
    gap = jnp.abs(gap)
    return jnp.where(gap == 0, 6.0, jnp.where(gap == 1, 4.0, jnp.where(gap == 2, 1.0, 0.0)))


def matrices(tile, tiles, even):
    def across(i, j):
        gap = stencil(i - j)
        return jnp.where((i == j) & ((i == 0) | (i == 31)), 5.0, gap)

    i = lax.broadcasted_iota(jnp.int32, (256, 256), 0)
    j = lax.broadcasted_iota(jnp.int32, (256, 256), 1)
    ri, rj = i // 32, j // 32
    ends = ((ri == 0) & (tile == 0)) | ((ri == 7) & (tile == tiles - 1))
    down = jnp.where((ri == rj) & ends, 5.0, stencil(ri - rj))
    smat = (down * across(i % 32, j % 32) * (1.0 / 256.0)).astype(BF16)
    i = lax.broadcasted_iota(jnp.int32, (128, 128), 0)
    j = lax.broadcasted_iota(jnp.int32, (128, 128), 1)
    ri = i // 32
    ri = jnp.where(ri < 2, ri, ri + 4)
    is_even = j < 64
    above = is_even == even
    rj = jnp.where(above, 8, -2) + (j // 32) % 2
    there = is_even | ((tile > 0) & (tile < tiles - 1))
    hmat = jnp.where(there, stencil(ri - rj), 0.0) * across(i % 32, j % 32) * (1.0 / 256.0)
    return smat, hmat.astype(BF16)


def swap_even(x):
    return lax.ppermute(x, "tile", EVEN)


def swap_odd(x):
    return lax.ppermute(x, "tile", ODD)


def round_mem(mine):
    size = lax.axis_size("mem")
    return [mine] + [
        lax.ppermute(mine, "mem", [(i, (i + shift) % size) for i in range(size)]) for shift in range(1, size)
    ]


def by_variable(x):
    return jnp.pad(x, (0, V * SLOTS - x.shape[0])).reshape(SLOTS, V).T


def on_device(alpha, ensemble, loc_vert, obs_col, obs_lev, obs_count, innovation, obs_weight):
    members = alpha.shape[0]
    tile = lax.axis_index("tile")
    tiles = lax.axis_size("tile")
    even = tile % 2 == 0
    odd_there = (tile > 0) & (tile < tiles - 1)
    where = jnp.stack(
        [
            jnp.where(even, 7 * 32, 0),
            jnp.where(even, 0, 7 * 32),
            jnp.where(even, 8, -1),
            jnp.where(even, -1, 8),
            odd_there.astype(jnp.int32),
            tile % 2,
            tile,
        ]
    ).astype(jnp.int32)

    send_ea, send_oa, token = send_part(where, alpha.reshape(2, PAIRS, 4, 64, 128), loc_vert)
    ea, oa = swap_even(send_ea), swap_odd(send_oa)
    inner, la, lb, xa, xb, smat, hmat, token, send_eb, send_ob = own_part(
        where,
        alpha.reshape(2, PAIRS, 256, 128),
        ensemble.reshape(2, PAIRS, V, 256, 128),
        loc_vert,
        token,
    )
    eb, ob = swap_even(send_eb), swap_odd(send_ob)

    token, obs_col, obs_lev, obs_count, innovation, obs_weight = lax.optimization_barrier(
        (token, obs_col, obs_lev, obs_count, innovation, obs_weight)
    )
    live = jnp.arange(obs_col.shape[1], dtype=jnp.int32) < obs_count[0]
    own_obs = jnp.stack(
        [
            by_variable(obs_col[0].astype(F32) + token[0, 0]),
            by_variable(obs_lev[0].astype(F32)),
            by_variable(innovation[0]),
            by_variable(jnp.where(live, obs_weight[0], 0.0)),
        ]
    )
    own_obs = pass_on(own_obs, ea)
    even_obs = swap_even(own_obs)
    odd_obs = swap_odd(own_obs)
    even_on = jnp.where(even, even_obs[0] < 64.0, even_obs[0] >= 960.0)
    odd_on = jnp.where(even, odd_obs[0] >= 960.0, odd_obs[0] < 64.0) & odd_there
    lev = jnp.concatenate([own_obs[1], even_obs[1], odd_obs[1]])
    innov = jnp.concatenate([own_obs[2], even_obs[2], odd_obs[2]])
    weight = jnp.concatenate(
        [own_obs[3], jnp.where(even_on, even_obs[3], 0.0), jnp.where(odd_on, odd_obs[3], 0.0)]
    )

    inc_a, se_a, so_a = edge_part(0, where, ea, oa, la, xa, hmat, loc_vert, inner, own_obs)
    near_a = swap_even(se_a), swap_odd(so_a)
    wown, wnear = weights(where, own_obs, even_obs, odd_obs)
    mine_a = values(0, where, inc_a, *near_a, wown, wnear, lev, inc_a)
    vals_a = round_mem(mine_a)

    inc_b, se_b, so_b = edge_part(1, where, eb, ob, lb, xb, hmat, loc_vert, inner, mine_a)
    near_b = swap_even(se_b), swap_odd(so_b)

    c_a, back_ea, back_oa = adjoint(0, where, vals_a, innov, weight, lev, wown, wnear, xa, se_b)
    halo_ea, halo_oa = swap_even(back_ea), swap_odd(back_oa)

    mine_b = values(1, where, inc_b, *near_b, wown, wnear, lev, back_ea)
    vals_b = round_mem(mine_b)
    c_b, back_eb, back_ob = adjoint(1, where, vals_b, innov, weight, lev, wown, wnear, xb, mine_b)
    halo_eb, halo_ob = swap_even(back_eb), swap_odd(back_ob)

    out, edge = back_part(
        alpha.reshape(members, 256, 128), ensemble.reshape(members, V, 256, 128), c_a, c_b, smat, loc_vert
    )
    edge = first_part(halo_ea, halo_oa, edge, hmat, loc_vert)
    out = last_part(halo_eb, halo_ob, edge, hmat, loc_vert, out.reshape(2, PAIRS, 4, 64, 128))
    return out.reshape(members, 8, 32, 128)


def solution(mesh):
    in_specs = (
        P("mem", "tile", None, None),
        P("mem", None, "tile", None, None),
        P(),
        P("tile", None),
        P("tile", None),
        P("tile"),
        P("tile", None),
        P("tile", None),
    )
    out_specs = P("mem", "tile", None, None)
    return jax.shard_map(
        on_device, mesh=mesh, in_specs=in_specs, out_specs=out_specs, check_vma=False
    )
```

```python
import functools

import jax
import jax.numpy as jnp
from jax import lax
from jax.experimental import pallas as pl
from jax.experimental.pallas import tpu as pltpu
from jax.sharding import PartitionSpec as P

V = 3
F32 = jnp.float32
BF16 = jnp.bfloat16
SLOTS = 768
GROUP = 4
PAIRS = 10

TILES = 64
EVEN = [(i, i ^ 1) for i in range(TILES)]
ODD = [(i, ((i - 1) ^ 1) + 1) for i in range(1, TILES - 1)] + [(0, TILES - 1), (TILES - 1, 0)]


def nn(a, b):
    return lax.dot_general(a, b, (((1,), (0,)), ((), ())), preferred_element_type=F32)


def nt(a, b):
    return lax.dot_general(a, b, (((1,), (1,)), ((), ())), preferred_element_type=F32)


def tn(a, b):
    return lax.dot_general(a, b, (((0,), (0,)), ((), ())), preferred_element_type=F32)


def halves(x):
    high = x.astype(BF16)
    low = (x - high.astype(F32)).astype(BF16)
    return high, low


def lift(smoothed, loc):
    high, low = halves(smoothed)
    return nt(high, loc) + nt(low, loc)


def call(kernel, out, grid=None, ins=None, outs=None, scratch=(), aliases=None, cost=1000000):
    vmem = pl.BlockSpec(memory_space=pltpu.VMEM)
    kw = {}
    if grid is not None:
        kw["grid"] = grid
    return pl.pallas_call(
        kernel,
        out_shape=out,
        in_specs=ins,
        out_specs=outs if outs is not None else jax.tree.map(lambda o: vmem, out),
        scratch_shapes=scratch,
        input_output_aliases=aliases or {},
        compiler_params=pltpu.CompilerParams(vmem_limit_bytes=16 * 1024 * 1024),
        cost_estimate=pl.CostEstimate(flops=cost, bytes_accessed=cost, transcendentals=0),
        **kw,
    )


def sds(*shape, dtype=F32):
    return jax.ShapeDtypeStruct(shape, dtype)


ANY = pl.BlockSpec(memory_space=pl.ANY)
SMEM = pl.BlockSpec(memory_space=pltpu.SMEM)
VMEM = pl.BlockSpec(memory_space=pltpu.VMEM)


def smooth(matrix, field):
    both = jnp.concatenate(halves(field), axis=1)
    out = nn(matrix, both)
    return out[:, :128] + out[:, 128:]


def twice(loc):
    zeros = jnp.zeros_like(loc)
    return jnp.concatenate(
        [jnp.concatenate([loc, zeros], axis=1), jnp.concatenate([zeros, loc], axis=1)], axis=0
    )


def edge_levels(first, second, both, odd, e_ref, o_ref, p):
    out = nt(jnp.concatenate([first, second], axis=1), both)
    low, high = out[:64], out[64:]
    e_ref[p] = jnp.where(odd, low, high)
    o_ref[p] = jnp.where(odd, high, low)


def send_kernel(where_ref, low_ref, high_ref, loc_ref, e_ref, o_ref, token_ref):
    odd = where_ref[5] == 1
    both = twice(loc_ref[:64])
    for p in range(PAIRS):
        members = [jnp.concatenate([low_ref[m, p, 0], high_ref[m, p, 0]], axis=0) for m in range(2)]
        edge_levels(*members, both, odd, e_ref, o_ref, p)
    token_ref[...] = jnp.zeros_like(token_ref)


def send_part(where, quarters, loc):
    edge = lambda q: pl.BlockSpec((2, PAIRS, 1, 64, 128), lambda i: (0, 0, q, 0, 0))
    flat = pl.BlockSpec((PAIRS, 64, 128), lambda i: (0, 0, 0))
    return call(
        send_kernel,
        (sds(PAIRS, 64, 128), sds(PAIRS, 64, 128), sds(8, 128)),
        grid=(1,),
        ins=[SMEM, edge(0), edge(3), pl.BlockSpec((128, 128), lambda i: (0, 0))],
        outs=(flat, flat, pl.BlockSpec((8, 128), lambda i: (0, 0))),
    )(where, quarters, quarters, loc)


def packed(first, second, h):
    return jnp.concatenate([first[:, 64 * h : 64 * h + 64], second[:, 64 * h : 64 * h + 64]], axis=1)


def own_kernel(where_ref, alpha_ref, ens_ref, loc_ref, after_ref, inner_ref, la_ref, lb_ref, xa_ref, xb_ref, smat_ref, hmat_ref, token_ref, eb_ref, ob_ref):
    @pl.when(pl.program_id(0) == 0)
    def _():
        inner_ref[...] = jnp.zeros_like(inner_ref)
        token_ref[...] = jnp.zeros_like(token_ref)
        smat, hmat = matrices(where_ref[6], TILES, where_ref[5] == 0)
        smat_ref[...] = smat
        hmat_ref[...] = hmat

    smat = smat_ref[...]
    loc = loc_ref[...]
    total = [inner_ref[v] for v in range(V)]
    odd = where_ref[5] == 1
    both = twice(loc[64:])
    for p in range(2):
        members = [jnp.concatenate([alpha_ref[m, p, :64], alpha_ref[m, p, 192:]], axis=0) for m in range(2)]
        edge_levels(*members, both, odd, eb_ref, ob_ref, p)
        edges = []
        for m in range(2):
            full = lift(nn(smat, alpha_ref[m, p]), loc)
            edges.append(jnp.concatenate([full[:64], full[192:]], axis=0))
            lifted = full[64:192].astype(BF16).astype(F32)
            for v in range(V):
                total[v] = total[v] + ens_ref[m, p, v, 64:192].astype(F32) * lifted
        for h, (l_ref, x_ref) in enumerate(((la_ref, xa_ref), (lb_ref, xb_ref))):
            l_ref[p] = packed(edges[0], edges[1], h)
            for v in range(V):
                for side in range(2):
                    rows = slice(192 * side, 192 * side + 64)
                    x_ref[p, v, 64 * side : 64 * side + 64] = packed(ens_ref[0, p, v, rows], ens_ref[1, p, v, rows], h)
    for v in range(V):
        inner_ref[v] = total[v]


def own_part(where, alpha, ensemble, loc, after):
    whole = lambda *shape: pl.BlockSpec(shape, lambda i: (0,) * len(shape))
    fields = pl.BlockSpec((2, 128, 128), lambda i: (i, 0, 0))
    members = pl.BlockSpec((2, V, 128, 128), lambda i: (i, 0, 0, 0))
    return call(
        own_kernel,
        (
            sds(V, 128, 128),
            sds(PAIRS, 128, 128),
            sds(PAIRS, 128, 128),
            sds(PAIRS, V, 128, 128, dtype=BF16),
            sds(PAIRS, V, 128, 128, dtype=BF16),
            sds(256, 256, dtype=BF16),
            sds(128, 128, dtype=BF16),
            sds(8, 128),
            sds(PAIRS, 64, 128),
            sds(PAIRS, 64, 128),
        ),
        grid=(PAIRS // 2,),
        ins=[
            SMEM,
            pl.BlockSpec((2, 2, 256, 128), lambda i: (0, i, 0, 0)),
            pl.BlockSpec((2, 2, V, 256, 128), lambda i: (0, i, 0, 0, 0)),
            whole(128, 128),
            whole(8, 128),
        ],
        outs=(
            whole(V, 128, 128),
            fields,
            fields,
            members,
            members,
            whole(256, 256),
            whole(128, 128),
            whole(8, 128),
            pl.BlockSpec((2, 64, 128), lambda i: (i, 0, 0)),
            pl.BlockSpec((2, 64, 128), lambda i: (i, 0, 0)),
        ),
    )(where, alpha, ensemble, loc, after)


def obs_kernel(count_ref, col_ref, lev_ref, innov_ref, weight_ref, after_ref, out_ref):
    slots = col_ref.shape[1]
    live = lax.broadcasted_iota(jnp.int32, (1, slots), 1) < count_ref[0]
    rows = []
    for field in (
        col_ref[...].astype(F32),
        lev_ref[...].astype(F32),
        innov_ref[...],
        jnp.where(live, weight_ref[...], 0.0),
    ):
        field = jnp.concatenate([field, jnp.zeros((1, V * SLOTS - slots), F32)], axis=1)
        rows += [field[:, 384 * a : 384 * a + 384] for a in range(6)]
    rest = jnp.concatenate(rows, axis=0)
    i = lax.broadcasted_iota(jnp.int32, (384, 384), 0)
    j = lax.broadcasted_iota(jnp.int32, (384, 384), 1)
    order = (i == 3 * (j % 128) + j // 128).astype(F32).astype(BF16)
    total = jnp.zeros((24, 384), F32)
    for piece in range(3):
        part = rest.astype(BF16)
        rest = rest - part.astype(F32)
        total = total + nn(part, order)
    for f in range(4):
        for a in range(6):
            for v in range(V):
                out_ref[f, v : v + 1, 128 * a : 128 * a + 128] = total[6 * f + a : 6 * f + a + 1, 128 * v : 128 * v + 128]


def observations(count, col, lev, innov, weight, after):
    return call(
        obs_kernel,
        sds(4, V, SLOTS),
        ins=[SMEM] + [VMEM] * 5,
        outs=VMEM,
    )(count, col, lev, innov, weight, after)


def edge_kernel(h, where_ref, e_ref, o_ref, own_ref, x_ref, hmat_ref, loc_ref, inner_ref, after_ref, inc_ref, se_ref, so_ref):
    hmat = hmat_ref[...]
    total = [jnp.zeros((128, 128), F32) for v in range(V)]
    for p in range(PAIRS):
        halo = jnp.concatenate([e_ref[p], o_ref[p]], axis=0)
        lifted = (own_ref[p] + smooth(hmat, halo)).astype(BF16).astype(F32)
        for v in range(V):
            total[v] = total[v] + x_ref[p, v].astype(F32) * lifted
    for v in range(V):
        edges = total[v][:, :64] + total[v][:, 64:]
        inc_ref[v, :64] = edges[:64]
        inc_ref[v, 64:192] = inner_ref[v][:, 64 * h : 64 * h + 64]
        inc_ref[v, 192:] = edges[64:]
        for n, ref in enumerate((se_ref, so_ref)):
            row = inc_ref[v, pl.ds(pl.multiple_of(where_ref[n], 32), 32)]
            ref[v] = jnp.concatenate([row[:16], row[16:]], axis=1)


def edge_part(h, where, from_even, from_odd, own, x, hmat, loc, inner, after):
    return call(
        functools.partial(edge_kernel, h),
        (sds(V, 256, 64), sds(V, 16, 128), sds(V, 16, 128)),
        ins=[SMEM] + [VMEM] * 8,
        outs=(VMEM,) * 3,
    )(where, from_even, from_odd, own, x, hmat, loc, inner, after)


def tent(distance):
    return jnp.maximum(1.0 - jnp.abs(distance), 0.0)


def weights_kernel(where_ref, own_ref, e_ref, o_ref, wown_ref, wnear_ref, lev_ref, innov_ref, weight_ref):
    even_row = where_ref[2].astype(F32)
    odd_row = where_ref[3].astype(F32)
    odd_there = where_ref[4].astype(F32)
    cell = lax.broadcasted_iota(jnp.int32, (32, SLOTS), 0).astype(F32)

    def columns(code):
        row = jnp.floor(code * (1.0 / 64.0))
        column = code - 64.0 * row
        return row, tent(cell - (column * 0.5 - 0.25))

    for v in range(V):
        row, across = columns(own_ref[0, v : v + 1, :])
        middle = row * 0.5 - 0.25
        for r in range(8):
            wown_ref[v, 32 * r : 32 * r + 32] = (tent(r - middle) * across).astype(BF16)
        wown_ref[v, 256:288] = (tent(even_row - middle) * across).astype(BF16)
        wown_ref[v, 288:320] = (tent(odd_row - middle) * odd_there * across).astype(BF16)
        for n, ref in enumerate((e_ref, o_ref)):
            row, across = columns(ref[0, v : v + 1, :])
            wnear_ref[n, v, :32] = (0.25 * across).astype(BF16)
            wnear_ref[n, v, 32:] = (0.75 * across).astype(BF16)
    is_odd = where_ref[5]
    for n, ref in enumerate((own_ref, e_ref, o_ref)):
        rows = slice(3 * n, 3 * n + 3)
        lev_ref[rows] = ref[1]
        innov_ref[rows] = ref[2]
        if n == 0:
            weight_ref[rows] = ref[3]
        else:
            first = is_odd == (0 if n == 1 else 1)
            at_edge = jnp.where(first, ref[0], 1023.0 - ref[0]) < 64.0
            there = at_edge & ((n == 1) | (where_ref[4] == 1))
            weight_ref[rows] = jnp.where(there, ref[3], 0.0)


def weights(where, own, even, odd):
    vmem = pl.BlockSpec(memory_space=pltpu.VMEM)
    return call(
        weights_kernel,
        (
            sds(V, 320, SLOTS, dtype=BF16),
            sds(2, V, 64, SLOTS, dtype=BF16),
            sds(9, SLOTS),
            sds(9, SLOTS),
            sds(9, SLOTS),
        ),
        ins=[pl.BlockSpec(memory_space=pltpu.SMEM), vmem, vmem, vmem],
        cost=5000000,
    )(where, own, even, odd)


def values_kernel(h, where_ref, inc_ref, e_ref, o_ref, wown_ref, wnear_ref, lev_ref, after_ref, out_ref):
    level = lax.broadcasted_iota(jnp.int32, (64, SLOTS), 0).astype(F32) + 64.0 * h

    def pick(cells, weight, row):
        both = jnp.concatenate(halves(cells), axis=1)
        at_all = tn(both, weight)
        at_all = at_all[:64] + at_all[64:]
        hot = level == lev_ref[row : row + 1, :]
        out_ref[row : row + 1, :] = jnp.sum(jnp.where(hot, at_all, 0.0), axis=0, keepdims=True)

    for v in range(V):
        near = []
        for ref in (e_ref, o_ref):
            row = ref[v]
            near.append(jnp.concatenate([row[:, :64], row[:, 64:]], axis=0))
        pick(jnp.concatenate([inc_ref[v]] + near, axis=0), wown_ref[v], v)
        for n in range(2):
            mine = inc_ref[v, pl.ds(pl.multiple_of(where_ref[n], 32), 32)]
            pick(jnp.concatenate([mine, near[n]], axis=0), wnear_ref[n, v], 3 * n + 3 + v)


def values(h, where, inc, even, odd, wown, wnear, lev, after):
    return call(
        functools.partial(values_kernel, h),
        sds(9, SLOTS),
        ins=[SMEM] + [VMEM] * 7,
        outs=VMEM,
    )(where, inc, even, odd, wown, wnear, lev, after)


def adjoint_kernel(h, where_ref, v0, v1, v2, v3, innov_ref, weight_ref, lev_ref, wown_ref, wnear_ref, x_ref, after_ref, c_ref, se_ref, so_ref):
    level = lax.broadcasted_iota(jnp.int32, (64, SLOTS), 0).astype(F32) + 64.0 * h
    value = v0[...] + v1[...] + v2[...] + v3[...]
    weighted = weight_ref[...] * (value - innov_ref[...])

    def place(weight, row):
        hot = level == lev_ref[row : row + 1, :]
        spread = jnp.where(hot, weighted[row : row + 1, :], 0.0)
        both = jnp.concatenate(halves(spread), axis=0)
        out = nt(weight, both)
        return out[:, :64] + out[:, 64:]

    adj = []
    for v in range(V):
        c_ref[v] = place(wown_ref[v, :256], v)
        for n in range(2):
            rows = pl.ds(pl.multiple_of(where_ref[n], 32), 32)
            c_ref[v, rows] = c_ref[v, rows] + place(wnear_ref[n, v, :32], 3 * n + 3 + v)
        edges = jnp.concatenate([c_ref[v, :64], c_ref[v, 192:]], axis=0)
        adj.append(jnp.concatenate([edges, edges], axis=1))
    odd = where_ref[5] == 1
    for p in range(PAIRS):
        total = x_ref[p, 0].astype(F32) * adj[0]
        for v in range(1, V):
            total = total + x_ref[p, v].astype(F32) * adj[v]
        low, high = total[:64], total[64:]
        se_ref[p] = jnp.where(odd, low, high)
        so_ref[p] = jnp.where(odd, high, low)


def adjoint(h, where, vals, innov, weight, lev, wown, wnear, x, after):
    return call(
        functools.partial(adjoint_kernel, h),
        (sds(V, 256, 64), sds(PAIRS, 64, 128), sds(PAIRS, 64, 128)),
        ins=[SMEM] + [VMEM] * 11,
        outs=(VMEM,) * 3,
    )(where, *vals, innov, weight, lev, wown, wnear, x, after)


def drop(smoothed, loc):
    high, low = halves(smoothed)
    return nn(high, loc) + nn(low, loc)


def back_kernel(alpha_ref, ens_ref, ca_ref, cb_ref, smat_ref, loc_ref, out_ref, edge_ref, c_ref):
    @pl.when(pl.program_id(0) == 0)
    def _():
        for v in range(V):
            c_ref[v] = jnp.concatenate([ca_ref[v], cb_ref[v]], axis=1)

    smat = smat_ref[...]
    loc = loc_ref[...]
    for k in range(GROUP):
        back = ens_ref[k, 0].astype(F32) * c_ref[0]
        for v in range(1, V):
            back = back + ens_ref[k, v].astype(F32) * c_ref[v]
        full = alpha_ref[k].astype(F32) + drop(smooth(smat, back), loc)
        out_ref[k] = full
        edge_ref[k, :64] = full[:64]
        edge_ref[k, 64:] = full[192:]


def back_part(alpha, ensemble, ca, cb, smat, loc):
    members = alpha.shape[0]
    half = pl.BlockSpec((V, 256, 64), lambda i: (0, 0, 0))
    return call(
        back_kernel,
        (sds(members, 256, 128), sds(members, 128, 128)),
        grid=(members // GROUP,),
        ins=[
            pl.BlockSpec((GROUP, 256, 128), lambda i: (i, 0, 0)),
            pl.BlockSpec((GROUP, V, 256, 128), lambda i: (i, 0, 0, 0)),
            half,
            half,
            pl.BlockSpec((256, 256), lambda i: (0, 0)),
            pl.BlockSpec((128, 128), lambda i: (0, 0)),
        ],
        outs=(
            pl.BlockSpec((GROUP, 256, 128), lambda i: (i, 0, 0)),
            pl.BlockSpec((GROUP, 128, 128), lambda i: (i, 0, 0)),
        ),
        scratch=[pltpu.VMEM((V, 256, 128), F32)],
    )(alpha, ensemble, ca, cb, smat, loc)


def halo_terms(e_ref, o_ref, hmat, loc, p):
    halo = jnp.concatenate([e_ref[p], o_ref[p]], axis=0)
    return drop(smooth(hmat, halo), loc)


def first_kernel(e_ref, o_ref, edge_ref, hmat_ref, loc_ref, out_ref):
    hmat = hmat_ref[...]
    loc = twice(loc_ref[:64])
    for p in range(PAIRS):
        terms = halo_terms(e_ref, o_ref, hmat, loc, p)
        out_ref[p] = edge_ref[p] + terms[:, :128]
        out_ref[p + PAIRS] = edge_ref[p + PAIRS] + terms[:, 128:]


def first_part(from_even, from_odd, edge, hmat, loc):
    return call(first_kernel, sds(*edge.shape), ins=[VMEM] * 5, outs=VMEM)(from_even, from_odd, edge, hmat, loc)


def last_kernel(e_ref, o_ref, edge_ref, hmat_ref, loc_ref, unused_ref, out_ref, held, sems):
    hmat = hmat_ref[...]
    loc = twice(loc_ref[64:])
    copies = []
    for p in range(PAIRS):
        terms = halo_terms(e_ref, o_ref, hmat, loc, p)
        for m in range(2):
            full = edge_ref[p + m * PAIRS] + terms[:, 128 * m : 128 * m + 128]
            held[m, p, 0] = full[:64]
            held[m, p, 1] = full[64:]
        if p % 2:
            group = pl.ds(p - 1, 2)
            for side in range(2):
                copies.append(
                    pltpu.make_async_copy(
                        held.at[:, group, side], out_ref.at[:, group, 3 * side], sems.at[p // 2, side]
                    )
                )
                copies[-1].start()
    for copy in copies:
        copy.wait()


def last_part(from_even, from_odd, edge, hmat, loc, out):
    return call(
        last_kernel,
        sds(*out.shape),
        ins=[VMEM] * 5 + [ANY],
        outs=ANY,
        scratch=[pltpu.VMEM((2, PAIRS, 2, 64, 128), F32), pltpu.SemaphoreType.DMA((PAIRS // 2, 2))],
        aliases={5: 0},
    )(from_even, from_odd, edge, hmat, loc, out)


def stencil(gap):
    gap = jnp.abs(gap)
    return jnp.where(gap == 0, 6.0, jnp.where(gap == 1, 4.0, jnp.where(gap == 2, 1.0, 0.0)))


def matrices(tile, tiles, even):
    def across(i, j):
        gap = stencil(i - j)
        return jnp.where((i == j) & ((i == 0) | (i == 31)), 5.0, gap)

    i = lax.broadcasted_iota(jnp.int32, (256, 256), 0)
    j = lax.broadcasted_iota(jnp.int32, (256, 256), 1)
    ri, rj = i // 32, j // 32
    ends = ((ri == 0) & (tile == 0)) | ((ri == 7) & (tile == tiles - 1))
    down = jnp.where((ri == rj) & ends, 5.0, stencil(ri - rj))
    smat = (down * across(i % 32, j % 32) * (1.0 / 256.0)).astype(BF16)
    i = lax.broadcasted_iota(jnp.int32, (128, 128), 0)
    j = lax.broadcasted_iota(jnp.int32, (128, 128), 1)
    ri = i // 32
    ri = jnp.where(ri < 2, ri, ri + 4)
    is_even = j < 64
    above = is_even == even
    rj = jnp.where(above, 8, -2) + (j // 32) % 2
    there = is_even | ((tile > 0) & (tile < tiles - 1))
    hmat = jnp.where(there, stencil(ri - rj), 0.0) * across(i % 32, j % 32) * (1.0 / 256.0)
    return smat, hmat.astype(BF16)


def swap_even(x):
    return lax.ppermute(x, "tile", EVEN)


def swap_odd(x):
    return lax.ppermute(x, "tile", ODD)


def round_mem(mine):
    size = lax.axis_size("mem")
    return [mine] + [
        lax.ppermute(mine, "mem", [(i, (i + shift) % size) for i in range(size)]) for shift in range(1, size)
    ]


def on_device(alpha, ensemble, loc_vert, obs_col, obs_lev, obs_count, innovation, obs_weight):
    members = alpha.shape[0]
    tile = lax.axis_index("tile")
    tiles = lax.axis_size("tile")
    even = tile % 2 == 0
    odd_there = (tile > 0) & (tile < tiles - 1)
    where = jnp.stack(
        [
            jnp.where(even, 7 * 32, 0),
            jnp.where(even, 0, 7 * 32),
            jnp.where(even, 8, -1),
            jnp.where(even, -1, 8),
            odd_there.astype(jnp.int32),
            tile % 2,
            tile,
        ]
    ).astype(jnp.int32)

    send_ea, send_oa, token = send_part(where, alpha.reshape(2, PAIRS, 4, 64, 128), loc_vert)
    ea, oa = swap_even(send_ea), swap_odd(send_oa)
    inner, la, lb, xa, xb, smat, hmat, token, send_eb, send_ob = own_part(
        where,
        alpha.reshape(2, PAIRS, 256, 128),
        ensemble.reshape(2, PAIRS, V, 256, 128),
        loc_vert,
        token,
    )
    eb, ob = swap_even(send_eb), swap_odd(send_ob)

    own_obs = observations(obs_count, obs_col, obs_lev, innovation, obs_weight, token)
    even_obs = swap_even(own_obs)
    odd_obs = swap_odd(own_obs)

    inc_a, se_a, so_a = edge_part(0, where, ea, oa, la, xa, hmat, loc_vert, inner, own_obs)
    near_a = swap_even(se_a), swap_odd(so_a)
    wown, wnear, lev, innov, weight = weights(where, own_obs, even_obs, odd_obs)
    mine_a = values(0, where, inc_a, *near_a, wown, wnear, lev, inc_a)
    vals_a = round_mem(mine_a)

    inc_b, se_b, so_b = edge_part(1, where, eb, ob, lb, xb, hmat, loc_vert, inner, mine_a)
    near_b = swap_even(se_b), swap_odd(so_b)

    c_a, back_ea, back_oa = adjoint(0, where, vals_a, innov, weight, lev, wown, wnear, xa, se_b)
    halo_ea, halo_oa = swap_even(back_ea), swap_odd(back_oa)

    mine_b = values(1, where, inc_b, *near_b, wown, wnear, lev, back_ea)
    vals_b = round_mem(mine_b)
    c_b, back_eb, back_ob = adjoint(1, where, vals_b, innov, weight, lev, wown, wnear, xb, mine_b)
    halo_eb, halo_ob = swap_even(back_eb), swap_odd(back_ob)

    out, edge = back_part(
        alpha.reshape(members, 256, 128), ensemble.reshape(members, V, 256, 128), c_a, c_b, smat, loc_vert
    )
    edge = first_part(halo_ea, halo_oa, edge, hmat, loc_vert)
    out = last_part(halo_eb, halo_ob, edge, hmat, loc_vert, out.reshape(2, PAIRS, 4, 64, 128))
    return out.reshape(members, 8, 32, 128)


def solution(mesh):
    in_specs = (
        P("mem", "tile", None, None),
        P("mem", None, "tile", None, None),
        P(),
        P("tile", None),
        P("tile", None),
        P("tile"),
        P("tile", None),
        P("tile", None),
    )
    out_specs = P("mem", "tile", None, None)
    return jax.shard_map(
        on_device, mesh=mesh, in_specs=in_specs, out_specs=out_specs, check_vma=False
    )
```

```python
import jax
import jax.numpy as jnp
from jax import lax
from jax.experimental import pallas as pl
from jax.experimental.pallas import tpu as pltpu
from jax.sharding import PartitionSpec as P

V = 3
F32 = jnp.float32
BF16 = jnp.bfloat16
SLOTS = 768
GROUP = 4

TILES = 64
EVEN = [(i, i ^ 1) for i in range(TILES)]
ODD = [(i, ((i - 1) ^ 1) + 1) for i in range(1, TILES - 1)] + [(0, TILES - 1), (TILES - 1, 0)]

MEMS = 4
FIRST = [(TILES * m + a, TILES * m + b) for m in range(MEMS) for a, b in (EVEN if m < MEMS // 2 else ODD)]
SECOND = [(TILES * m + a, TILES * m + b) for m in range(MEMS) for a, b in (ODD if m < MEMS // 2 else EVEN)]


def nn(a, b):
    return lax.dot_general(a, b, (((1,), (0,)), ((), ())), preferred_element_type=F32)


def nt(a, b):
    return lax.dot_general(a, b, (((1,), (1,)), ((), ())), preferred_element_type=F32)


def tn(a, b):
    return lax.dot_general(a, b, (((0,), (0,)), ((), ())), preferred_element_type=F32)


def halves(x):
    high = x.astype(BF16)
    low = (x - high.astype(F32)).astype(BF16)
    return high, low


def lift(smoothed, loc):
    high, low = halves(smoothed)
    return nt(high, loc) + nt(low, loc)


def call(kernel, out, grid=None, ins=None, outs=None, scratch=(), aliases=None, cost=1000000):
    vmem = pl.BlockSpec(memory_space=pltpu.VMEM)
    kw = {}
    if grid is not None:
        kw["grid"] = grid
    return pl.pallas_call(
        kernel,
        out_shape=out,
        in_specs=ins,
        out_specs=outs if outs is not None else jax.tree.map(lambda o: vmem, out),
        scratch_shapes=scratch,
        input_output_aliases=aliases or {},
        compiler_params=pltpu.CompilerParams(vmem_limit_bytes=16 * 1024 * 1024),
        cost_estimate=pl.CostEstimate(flops=cost, bytes_accessed=cost, transcendentals=0),
        **kw,
    )


def sds(*shape, dtype=F32):
    return jax.ShapeDtypeStruct(shape, dtype)


ANY = pl.BlockSpec(memory_space=pl.ANY)
SMEM = pl.BlockSpec(memory_space=pltpu.SMEM)
VMEM = pl.BlockSpec(memory_space=pltpu.VMEM)


def smooth(matrix, field):
    both = jnp.concatenate(halves(field), axis=1)
    out = nn(matrix, both)
    return out[:, :128] + out[:, 128:]


def send_kernel(where_ref, quarters_ref, first_ref, second_ref, token_ref, edges, sems):
    copies = [pltpu.make_async_copy(quarters_ref.at[:, 3 * n], edges.at[n], sems.at[n]) for n in range(2)]
    for copy in copies:
        copy.start()
    token_ref[...] = jnp.zeros_like(token_ref)
    for copy in copies:
        copy.wait()
    low = where_ref[7]
    first_ref[...] = edges[1 - low].astype(F32)
    second_ref[...] = edges[low].astype(F32)


def send_part(where, quarters):
    members = quarters.shape[0]
    return call(
        send_kernel,
        (sds(members, 64, 128), sds(members, 64, 128), sds(8, 128)),
        ins=[SMEM, ANY],
        outs=(VMEM,) * 3,
        scratch=[pltpu.VMEM((2, members, 64, 128), BF16), pltpu.SemaphoreType.DMA((2,))],
    )(where, quarters)


def own_kernel(where_ref, alpha_ref, ens_ref, loc_ref, after_ref, inner_ref, edge_ref, x_ref, smat_ref, hmat_ref, token_ref):
    @pl.when(pl.program_id(0) == 0)
    def _():
        inner_ref[...] = jnp.zeros_like(inner_ref)
        token_ref[...] = jnp.zeros_like(token_ref)
        smat, hmat = matrices(where_ref[6], TILES, where_ref[7] == 0)
        smat_ref[...] = smat
        hmat_ref[...] = hmat

    smat = smat_ref[...]
    loc = loc_ref[...]
    total = [inner_ref[v] for v in range(V)]
    for k in range(GROUP):
        full = lift(nn(smat, alpha_ref[k]), loc)
        edge_ref[k, :64] = full[:64]
        edge_ref[k, 64:] = full[192:]
        lifted = full[64:192].astype(BF16).astype(F32)
        for v in range(V):
            total[v] = total[v] + ens_ref[k, v, 64:192].astype(F32) * lifted
            x_ref[k, v, :64] = ens_ref[k, v, :64]
            x_ref[k, v, 64:] = ens_ref[k, v, 192:]
    for v in range(V):
        inner_ref[v] = total[v]


def own_part(where, alpha, ensemble, loc, after):
    members = alpha.shape[0]
    whole = lambda *shape: pl.BlockSpec(shape, lambda i: (0,) * len(shape))
    return call(
        own_kernel,
        (
            sds(V, 128, 128),
            sds(members, 128, 128),
            sds(members, V, 128, 128, dtype=BF16),
            sds(256, 256, dtype=BF16),
            sds(128, 128, dtype=BF16),
            sds(8, 128),
        ),
        grid=(members // GROUP,),
        ins=[
            SMEM,
            pl.BlockSpec((GROUP, 256, 128), lambda i: (i, 0, 0)),
            pl.BlockSpec((GROUP, V, 256, 128), lambda i: (i, 0, 0, 0)),
            whole(128, 128),
            whole(8, 128),
        ],
        outs=(
            whole(V, 128, 128),
            pl.BlockSpec((GROUP, 128, 128), lambda i: (i, 0, 0)),
            pl.BlockSpec((GROUP, V, 128, 128), lambda i: (i, 0, 0, 0)),
            whole(256, 256),
            whole(128, 128),
            whole(8, 128),
        ),
    )(where, alpha, ensemble, loc, after)


def obs_kernel(count_ref, col_ref, lev_ref, innov_ref, weight_ref, after_ref, out_ref):
    slots = col_ref.shape[1]
    live = lax.broadcasted_iota(jnp.int32, (1, slots), 1) < count_ref[0]
    rows = []
    for field in (
        col_ref[...].astype(F32),
        lev_ref[...].astype(F32),
        innov_ref[...],
        jnp.where(live, weight_ref[...], 0.0),
    ):
        field = jnp.concatenate([field, jnp.zeros((1, V * SLOTS - slots), F32)], axis=1)
        rows += [field[:, 384 * a : 384 * a + 384] for a in range(6)]
    rest = jnp.concatenate(rows, axis=0)
    i = lax.broadcasted_iota(jnp.int32, (384, 384), 0)
    j = lax.broadcasted_iota(jnp.int32, (384, 384), 1)
    order = (i == 3 * (j % 128) + j // 128).astype(F32).astype(BF16)
    total = jnp.zeros((24, 384), F32)
    for piece in range(3):
        part = rest.astype(BF16)
        rest = rest - part.astype(F32)
        total = total + nn(part, order)
    for f in range(4):
        for a in range(6):
            for v in range(V):
                row = 6 * (V * f + v) + a
                out_ref[row : row + 1] = total[6 * f + a : 6 * f + a + 1, 128 * v : 128 * v + 128]


def observations(count, col, lev, innov, weight, after):
    return call(
        obs_kernel,
        sds(4 * V * SLOTS // 128, 128),
        ins=[SMEM] + [VMEM] * 5,
        outs=VMEM,
    )(count, col, lev, innov, weight, after)


def edge_kernel(where_ref, first_ref, second_ref, own_ref, x_ref, hmat_ref, loc_ref, inner_ref, after_even, after_odd, inc_ref, se_ref, so_ref):
    hmat = hmat_ref[...]
    loc = loc_ref[...]
    total = [jnp.zeros((128, 128), F32) for v in range(V)]
    for k in range(own_ref.shape[0]):
        halo = jnp.concatenate([first_ref[k].astype(BF16), second_ref[k].astype(BF16)], axis=0)
        lifted = (own_ref[k] + lift(nn(hmat, halo), loc)).astype(BF16).astype(F32)
        for v in range(V):
            total[v] = total[v] + x_ref[k, v].astype(F32) * lifted
    for v in range(V):
        inc_ref[v, :64] = total[v][:64]
        inc_ref[v, 64:192] = inner_ref[v]
        inc_ref[v, 192:] = total[v][64:]
        for n, ref in enumerate((se_ref, so_ref)):
            ref[v] = inc_ref[v, pl.ds(pl.multiple_of(where_ref[n], 32), 32)]


def edge_part(where, first, second, own, x, hmat, loc, inner, *after):
    return call(
        edge_kernel,
        (sds(V, 256, 128), sds(V, 32, 128), sds(V, 32, 128)),
        ins=[SMEM] + [VMEM] * 9,
        outs=(VMEM,) * 3,
    )(where, first, second, own, x, hmat, loc, inner, *after)


def tent(distance):
    return jnp.maximum(1.0 - jnp.abs(distance), 0.0)


def weights_kernel(where_ref, own_ref, e_ref, o_ref, wown_ref, wnear_ref, lev_ref, innov_ref, weight_ref):
    even_row = where_ref[2].astype(F32)
    odd_row = where_ref[3].astype(F32)
    odd_there = where_ref[4].astype(F32)
    cell = lax.broadcasted_iota(jnp.int32, (32, SLOTS), 0).astype(F32)

    def line(ref, field, v):
        at = 6 * (V * field + v)
        return jnp.concatenate([ref[at + a : at + a + 1] for a in range(6)], axis=1)

    def columns(code):
        row = jnp.floor(code * (1.0 / 64.0))
        column = code - 64.0 * row
        return row, tent(cell - (column * 0.5 - 0.25))

    for v in range(V):
        row, across = columns(line(own_ref, 0, v))
        middle = row * 0.5 - 0.25
        for r in range(8):
            wown_ref[v, 32 * r : 32 * r + 32] = (tent(r - middle) * across).astype(BF16)
        wown_ref[v, 256:288] = (tent(even_row - middle) * across).astype(BF16)
        wown_ref[v, 288:320] = (tent(odd_row - middle) * odd_there * across).astype(BF16)
        for n, ref in enumerate((e_ref, o_ref)):
            row, across = columns(line(ref, 0, v))
            wnear_ref[n, v, :32] = (0.25 * across).astype(BF16)
            wnear_ref[n, v, 32:] = (0.75 * across).astype(BF16)
    is_odd = where_ref[5]
    for n, ref in enumerate((own_ref, e_ref, o_ref)):
        for v in range(V):
            row = slice(3 * n + v, 3 * n + v + 1)
            lev_ref[row] = line(ref, 1, v)
            innov_ref[row] = line(ref, 2, v)
            weight = line(ref, 3, v)
            if n > 0:
                code = line(ref, 0, v)
                first = is_odd == (0 if n == 1 else 1)
                at_edge = jnp.where(first, code, 1023.0 - code) < 64.0
                there = at_edge & ((n == 1) | (where_ref[4] == 1))
                weight = jnp.where(there, weight, 0.0)
            weight_ref[row] = weight


def weights(where, own, even, odd):
    vmem = pl.BlockSpec(memory_space=pltpu.VMEM)
    return call(
        weights_kernel,
        (
            sds(V, 320, SLOTS, dtype=BF16),
            sds(2, V, 64, SLOTS, dtype=BF16),
            sds(9, SLOTS),
            sds(9, SLOTS),
            sds(9, SLOTS),
        ),
        ins=[pl.BlockSpec(memory_space=pltpu.SMEM), vmem, vmem, vmem],
        cost=5000000,
    )(where, own, even, odd)


def picker(lev_ref):
    level = lax.broadcasted_iota(jnp.int32, (128, SLOTS), 0).astype(F32)

    def pick(cells, weight, row):
        both = jnp.concatenate(halves(cells), axis=1)
        at_all = tn(both, weight)
        at_all = at_all[:128] + at_all[128:]
        hot = level == lev_ref[row : row + 1, :]
        return jnp.sum(jnp.where(hot, at_all, 0.0), axis=0, keepdims=True)

    return pick


def mine_kernel(where_ref, inc_ref, wown_ref, wnear_ref, lev_ref, out_ref):
    pick = picker(lev_ref)
    for v in range(V):
        out_ref[v : v + 1] = pick(inc_ref[v], wown_ref[v, :256], v)
        for n in range(2):
            cells = inc_ref[v, pl.ds(pl.multiple_of(where_ref[n], 32), 32)]
            row = 3 * n + 3 + v
            out_ref[row : row + 1] = pick(cells, wnear_ref[n, v, :32], row)


def mine_part(where, inc, wown, wnear, lev):
    return call(
        mine_kernel,
        sds(9, SLOTS),
        ins=[SMEM] + [VMEM] * 4,
        outs=VMEM,
    )(where, inc, wown, wnear, lev)


def values_kernel(mine_ref, e_ref, o_ref, wown_ref, wnear_ref, lev_ref, out_ref):
    pick = picker(lev_ref)

    def put(row, more):
        line = mine_ref[row : row + 1] + more
        for a in range(6):
            out_ref[6 * row + a : 6 * row + a + 1] = line[:, 128 * a : 128 * a + 128]

    for v in range(V):
        put(v, pick(jnp.concatenate([e_ref[v], o_ref[v]], axis=0), wown_ref[v, 256:], v))
        for n, ref in enumerate((e_ref, o_ref)):
            row = 3 * n + 3 + v
            put(row, pick(ref[v], wnear_ref[n, v, 32:], row))


def values(mine, even, odd, wown, wnear, lev):
    return call(
        values_kernel,
        sds(9 * SLOTS // 128, 128),
        ins=[VMEM] * 6,
        outs=VMEM,
    )(mine, even, odd, wown, wnear, lev)


def adjoint_kernel(where_ref, v0, v1, v2, v3, innov_ref, weight_ref, lev_ref, wown_ref, wnear_ref, x_ref, c_ref, first_ref, second_ref):
    level = lax.broadcasted_iota(jnp.int32, (128, SLOTS), 0).astype(F32)
    value = v0[...] + v1[...] + v2[...] + v3[...]

    def place(weight, row):
        line = jnp.concatenate([value[6 * row + a : 6 * row + a + 1] for a in range(6)], axis=1)
        weighted = weight_ref[row : row + 1] * (line - innov_ref[row : row + 1])
        hot = level == lev_ref[row : row + 1, :]
        spread = jnp.where(hot, weighted, 0.0)
        both = jnp.concatenate(halves(spread), axis=0)
        out = nt(weight, both)
        return out[:, :128] + out[:, 128:]

    adj = []
    for v in range(V):
        c_ref[v] = place(wown_ref[v, :256], v)
        for n in range(2):
            rows = pl.ds(pl.multiple_of(where_ref[n], 32), 32)
            c_ref[v, rows] = c_ref[v, rows] + place(wnear_ref[n, v, :32], 3 * n + 3 + v)
        adj.append(jnp.concatenate([c_ref[v, :64], c_ref[v, 192:]], axis=0))
    first_low = where_ref[7] == 1
    for k in range(first_ref.shape[0]):
        total = x_ref[k, 0].astype(F32) * adj[0]
        for v in range(1, V):
            total = total + x_ref[k, v].astype(F32) * adj[v]
        low, high = total[:64], total[64:]
        first_ref[k] = jnp.where(first_low, low, high)
        second_ref[k] = jnp.where(first_low, high, low)


def adjoint(where, vals, innov, weight, lev, wown, wnear, x):
    members = x.shape[0]
    return call(
        adjoint_kernel,
        (sds(V, 256, 128), sds(members, 64, 128), sds(members, 64, 128)),
        ins=[SMEM] + [VMEM] * 10,
        outs=(VMEM,) * 3,
    )(where, *vals, innov, weight, lev, wown, wnear, x)


def drop(smoothed, loc):
    high, low = halves(smoothed)
    return nn(high, loc) + nn(low, loc)


def back_kernel(alpha_ref, ens_ref, c_ref, smat_ref, loc_ref, out_ref, edge_ref):
    smat = smat_ref[...]
    loc = loc_ref[...]
    for k in range(GROUP):
        back = ens_ref[k, 0].astype(F32) * c_ref[0]
        for v in range(1, V):
            back = back + ens_ref[k, v].astype(F32) * c_ref[v]
        full = alpha_ref[k].astype(F32) + drop(smooth(smat, back), loc)
        out_ref[k] = full
        edge_ref[k, :64] = full[:64]
        edge_ref[k, 64:] = full[192:]


def back_part(alpha, ensemble, c, smat, loc):
    members = alpha.shape[0]
    return call(
        back_kernel,
        (sds(members, 256, 128), sds(members, 128, 128)),
        grid=(members // GROUP,),
        ins=[
            pl.BlockSpec((GROUP, 256, 128), lambda i: (i, 0, 0)),
            pl.BlockSpec((GROUP, V, 256, 128), lambda i: (i, 0, 0, 0)),
            pl.BlockSpec((V, 256, 128), lambda i: (0, 0, 0)),
            pl.BlockSpec((256, 256), lambda i: (0, 0)),
            pl.BlockSpec((128, 128), lambda i: (0, 0)),
        ],
        outs=(
            pl.BlockSpec((GROUP, 256, 128), lambda i: (i, 0, 0)),
            pl.BlockSpec((GROUP, 128, 128), lambda i: (i, 0, 0)),
        ),
    )(alpha, ensemble, c, smat, loc)


def last_kernel(first_ref, second_ref, edge_ref, hmat_ref, loc_ref, unused_ref, out_ref, held, sems):
    members = edge_ref.shape[0]
    hmat = hmat_ref[...]
    loc = loc_ref[...]
    copies = []
    for g in range(members // GROUP):
        for k in range(g * GROUP, (g + 1) * GROUP):
            halo = jnp.concatenate([first_ref[k], second_ref[k]], axis=0)
            full = edge_ref[k] + drop(smooth(hmat, halo), loc)
            held[k, 0] = full[:64]
            held[k, 1] = full[64:]
        group = pl.ds(g * GROUP, GROUP)
        for side in range(2):
            copies.append(
                pltpu.make_async_copy(held.at[group, side], out_ref.at[group, 3 * side], sems.at[g, side])
            )
            copies[-1].start()
    for copy in copies:
        copy.wait()


def last_part(first, second, edge, hmat, loc, out):
    members = edge.shape[0]
    return call(
        last_kernel,
        sds(members, 4, 64, 128),
        ins=[VMEM] * 5 + [ANY],
        outs=ANY,
        scratch=[pltpu.VMEM((members, 2, 64, 128), F32), pltpu.SemaphoreType.DMA((members // GROUP, 2))],
        aliases={5: 0},
    )(first, second, edge, hmat, loc, out)


def stencil(gap):
    gap = jnp.abs(gap)
    return jnp.where(gap == 0, 6.0, jnp.where(gap == 1, 4.0, jnp.where(gap == 2, 1.0, 0.0)))


def matrices(tile, tiles, first_high):
    def across(i, j):
        gap = stencil(i - j)
        return jnp.where((i == j) & ((i == 0) | (i == 31)), 5.0, gap)

    i = lax.broadcasted_iota(jnp.int32, (256, 256), 0)
    j = lax.broadcasted_iota(jnp.int32, (256, 256), 1)
    ri, rj = i // 32, j // 32
    ends = ((ri == 0) & (tile == 0)) | ((ri == 7) & (tile == tiles - 1))
    down = jnp.where((ri == rj) & ends, 5.0, stencil(ri - rj))
    smat = (down * across(i % 32, j % 32) * (1.0 / 256.0)).astype(BF16)
    i = lax.broadcasted_iota(jnp.int32, (128, 128), 0)
    j = lax.broadcasted_iota(jnp.int32, (128, 128), 1)
    ri = i // 32
    ri = jnp.where(ri < 2, ri, ri + 4)
    above = (j < 64) == first_high
    rj = jnp.where(above, 8, -2) + (j // 32) % 2
    there = (above & (tile < tiles - 1)) | (jnp.logical_not(above) & (tile > 0))
    hmat = jnp.where(there, stencil(ri - rj), 0.0) * across(i % 32, j % 32) * (1.0 / 256.0)
    return smat, hmat.astype(BF16)


def swap_even(x):
    return lax.ppermute(x, "tile", EVEN)


def swap_odd(x):
    return lax.ppermute(x, "tile", ODD)


def swap_first(x):
    return lax.ppermute(x, ("mem", "tile"), FIRST)


def swap_second(x):
    return lax.ppermute(x, ("mem", "tile"), SECOND)


def round_mem(mine):
    size = lax.axis_size("mem")
    return [mine] + [
        lax.ppermute(mine, "mem", [(i, (i + shift) % size) for i in range(size)]) for shift in range(1, size)
    ]


def on_device(alpha, ensemble, loc_vert, obs_col, obs_lev, obs_count, innovation, obs_weight):
    members = alpha.shape[0]
    tile = lax.axis_index("tile")
    tiles = lax.axis_size("tile")
    even = tile % 2 == 0
    first_low = (tile + lax.axis_index("mem") // (MEMS // 2)) % 2
    where = jnp.stack(
        [
            jnp.where(even, 7 * 32, 0),
            jnp.where(even, 0, 7 * 32),
            jnp.where(even, 8, -1),
            jnp.where(even, -1, 8),
            ((tile > 0) & (tile < tiles - 1)).astype(jnp.int32),
            tile % 2,
            tile,
            first_low,
        ]
    ).astype(jnp.int32)
    flat = alpha.reshape(members, 256, 128)
    flat_ens = ensemble.reshape(members, V, 256, 128)

    send_first, send_second, token = send_part(where, alpha.reshape(members, 4, 64, 128))
    first, second = swap_first(send_first), swap_second(send_second)
    inner, own_edge, x, smat, hmat, token = own_part(where, flat, flat_ens, loc_vert, token)
    own_obs = observations(obs_count, obs_col, obs_lev, innovation, obs_weight, token)
    even_obs = swap_even(own_obs)
    odd_obs = swap_odd(own_obs)

    inc, se, so = edge_part(where, first, second, own_edge, x, hmat, loc_vert, inner, even_obs, odd_obs)
    near_even, near_odd = swap_even(se), swap_odd(so)
    wown, wnear, lev, innov, weight = weights(where, own_obs, even_obs, odd_obs)
    mine = mine_part(where, inc, wown, wnear, lev)
    vals = round_mem(values(mine, near_even, near_odd, wown, wnear, lev))
    c, back_first, back_second = adjoint(where, vals, innov, weight, lev, wown, wnear, x)
    halo_first, halo_second = swap_first(back_first), swap_second(back_second)
    out, edge = back_part(flat, flat_ens, c, smat, loc_vert)
    out = last_part(halo_first, halo_second, edge, hmat, loc_vert, out.reshape(members, 4, 64, 128))
    return out.reshape(members, 8, 32, 128)


def solution(mesh):
    in_specs = (
        P("mem", "tile", None, None),
        P("mem", None, "tile", None, None),
        P(),
        P("tile", None),
        P("tile", None),
        P("tile"),
        P("tile", None),
        P("tile", None),
    )
    out_specs = P("mem", "tile", None, None)
    return jax.shard_map(
        on_device, mesh=mesh, in_specs=in_specs, out_specs=out_specs, check_vma=False
    )
```

```python
import functools

import jax
import jax.numpy as jnp
from jax import lax
from jax.experimental import pallas as pl
from jax.experimental.pallas import tpu as pltpu
from jax.sharding import PartitionSpec as P

V = 3
F32 = jnp.float32
BF16 = jnp.bfloat16
SLOTS = 768
GROUP = 4
HEAD = 12

TILES = 64
EVEN = [(i, i ^ 1) for i in range(TILES)]
ODD = [(i, ((i - 1) ^ 1) + 1) for i in range(1, TILES - 1)] + [(0, TILES - 1), (TILES - 1, 0)]

MEMS = 4
FIRST = [(TILES * m + a, TILES * m + b) for m in range(MEMS) for a, b in (ODD if m % 2 else EVEN)]
SECOND = [(TILES * m + a, TILES * m + b) for m in range(MEMS) for a, b in (EVEN if m % 2 else ODD)]


def nn(a, b):
    return lax.dot_general(a, b, (((1,), (0,)), ((), ())), preferred_element_type=F32)


def nt(a, b):
    return lax.dot_general(a, b, (((1,), (1,)), ((), ())), preferred_element_type=F32)


def tn(a, b):
    return lax.dot_general(a, b, (((0,), (0,)), ((), ())), preferred_element_type=F32)


def halves(x):
    high = x.astype(BF16)
    low = (x - high.astype(F32)).astype(BF16)
    return high, low


def lift(smoothed, loc):
    high, low = halves(smoothed)
    return nt(high, loc) + nt(low, loc)


def call(kernel, out, grid=None, ins=None, outs=None, scratch=(), aliases=None, cost=1000000):
    vmem = pl.BlockSpec(memory_space=pltpu.VMEM)
    kw = {}
    if grid is not None:
        kw["grid"] = grid
    return pl.pallas_call(
        kernel,
        out_shape=out,
        in_specs=ins,
        out_specs=outs if outs is not None else jax.tree.map(lambda o: vmem, out),
        scratch_shapes=scratch,
        input_output_aliases=aliases or {},
        compiler_params=pltpu.CompilerParams(vmem_limit_bytes=16 * 1024 * 1024),
        cost_estimate=pl.CostEstimate(flops=cost, bytes_accessed=cost, transcendentals=0),
        **kw,
    )


def sds(*shape, dtype=F32):
    return jax.ShapeDtypeStruct(shape, dtype)


ANY = pl.BlockSpec(memory_space=pl.ANY)
SMEM = pl.BlockSpec(memory_space=pltpu.SMEM)
VMEM = pl.BlockSpec(memory_space=pltpu.VMEM)


def smooth(matrix, field):
    both = jnp.concatenate(halves(field), axis=1)
    out = nn(matrix, both)
    return out[:, :128] + out[:, 128:]


def send_kernel(where_ref, quarters_ref, first_ref, second_ref, token_ref, edges, sems):
    head = pl.ds(0, HEAD)
    copies = [pltpu.make_async_copy(quarters_ref.at[head, 3 * n], edges.at[n], sems.at[n]) for n in range(2)]
    for copy in copies:
        copy.start()
    token_ref[...] = jnp.zeros_like(token_ref)
    for copy in copies:
        copy.wait()
    low = where_ref[7]
    first_ref[...] = edges[1 - low].astype(F32)
    second_ref[...] = edges[low].astype(F32)


def send_part(where, quarters):
    members = HEAD
    return call(
        send_kernel,
        (sds(members, 64, 128), sds(members, 64, 128), sds(8, 128)),
        ins=[SMEM, ANY],
        outs=(VMEM,) * 3,
        scratch=[pltpu.VMEM((2, members, 64, 128), BF16), pltpu.SemaphoreType.DMA((2,))],
    )(where, quarters)


def own_kernel(where_ref, alpha_ref, ens_ref, loc_ref, after_ref, inner_ref, edge_ref, x_ref, smat_ref, hmat_ref, token_ref, first_ref, second_ref):
    @pl.when(pl.program_id(0) == 0)
    def _():
        inner_ref[...] = jnp.zeros_like(inner_ref)
        token_ref[...] = jnp.zeros_like(token_ref)
        smat, hmat = matrices(where_ref[6], TILES, where_ref[7] == 0)
        smat_ref[...] = smat
        hmat_ref[...] = hmat

    smat = smat_ref[...]
    loc = loc_ref[...]
    total = [inner_ref[v] for v in range(V)]
    for k in range(GROUP):
        full = lift(nn(smat, alpha_ref[k]), loc)
        edge_ref[k, :64] = full[:64]
        edge_ref[k, 64:] = full[192:]
        lifted = full[64:192].astype(BF16).astype(F32)
        for v in range(V):
            total[v] = total[v] + ens_ref[k, v, 64:192].astype(F32) * lifted
            x_ref[k, v, :64] = ens_ref[k, v, :64]
            x_ref[k, v, 64:] = ens_ref[k, v, 192:]
    for v in range(V):
        inner_ref[v] = total[v]

    @pl.when(pl.program_id(0) >= HEAD // GROUP)
    def _():
        low = where_ref[7] == 1
        for k in range(GROUP):
            rows = [alpha_ref[k, :64].astype(F32), alpha_ref[k, 192:].astype(F32)]
            first_ref[k] = jnp.where(low, rows[0], rows[1])
            second_ref[k] = jnp.where(low, rows[1], rows[0])


def own_part(where, alpha, ensemble, loc, after):
    members = alpha.shape[0]
    whole = lambda *shape: pl.BlockSpec(shape, lambda i: (0,) * len(shape))
    rest = pl.BlockSpec((GROUP, 64, 128), lambda i: (jnp.maximum(i - HEAD // GROUP, 0), 0, 0))
    return call(
        own_kernel,
        (
            sds(V, 128, 128),
            sds(members, 128, 128),
            sds(members, V, 128, 128, dtype=BF16),
            sds(256, 256, dtype=BF16),
            sds(128, 128, dtype=BF16),
            sds(8, 128),
            sds(members - HEAD, 64, 128),
            sds(members - HEAD, 64, 128),
        ),
        grid=(members // GROUP,),
        ins=[
            SMEM,
            pl.BlockSpec((GROUP, 256, 128), lambda i: (i, 0, 0)),
            pl.BlockSpec((GROUP, V, 256, 128), lambda i: (i, 0, 0, 0)),
            whole(128, 128),
            whole(8, 128),
        ],
        outs=(
            whole(V, 128, 128),
            pl.BlockSpec((GROUP, 128, 128), lambda i: (i, 0, 0)),
            pl.BlockSpec((GROUP, V, 128, 128), lambda i: (i, 0, 0, 0)),
            whole(256, 256),
            whole(128, 128),
            whole(8, 128),
            rest,
            rest,
        ),
    )(where, alpha, ensemble, loc, after)


def obs_kernel(count_ref, col_ref, lev_ref, innov_ref, weight_ref, after_ref, out_ref):
    slots = col_ref.shape[1]
    live = lax.broadcasted_iota(jnp.int32, (1, slots), 1) < count_ref[0]
    rows = []
    for field in (
        col_ref[...].astype(F32),
        lev_ref[...].astype(F32),
        innov_ref[...],
        jnp.where(live, weight_ref[...], 0.0),
    ):
        field = jnp.concatenate([field, jnp.zeros((1, V * SLOTS - slots), F32)], axis=1)
        rows += [field[:, 384 * a : 384 * a + 384] for a in range(6)]
    rest = jnp.concatenate(rows, axis=0)
    i = lax.broadcasted_iota(jnp.int32, (384, 384), 0)
    j = lax.broadcasted_iota(jnp.int32, (384, 384), 1)
    order = (i == 3 * (j % 128) + j // 128).astype(F32).astype(BF16)
    total = jnp.zeros((24, 384), F32)
    for piece in range(3):
        part = rest.astype(BF16)
        rest = rest - part.astype(F32)
        total = total + nn(part, order)
    for f in range(4):
        for a in range(6):
            for v in range(V):
                row = 6 * (V * f + v) + a
                out_ref[row : row + 1] = total[6 * f + a : 6 * f + a + 1, 128 * v : 128 * v + 128]


def observations(count, col, lev, innov, weight, after):
    return call(
        obs_kernel,
        sds(4 * V * SLOTS // 128, 128),
        ins=[SMEM] + [VMEM] * 5,
        outs=VMEM,
    )(count, col, lev, innov, weight, after)


def edge_terms(first_ref, second_ref, own_ref, x_ref, hmat_ref, loc_ref, start, total):
    hmat = hmat_ref[...]
    loc = loc_ref[...]
    for k in range(first_ref.shape[0]):
        halo = jnp.concatenate([first_ref[k].astype(BF16), second_ref[k].astype(BF16)], axis=0)
        lifted = (own_ref[start + k] + lift(nn(hmat, halo), loc)).astype(BF16).astype(F32)
        for v in range(V):
            total[v] = total[v] + x_ref[start + k, v].astype(F32) * lifted
    return total


def head_kernel(first_ref, second_ref, own_ref, x_ref, hmat_ref, loc_ref, total_ref):
    zeros = [jnp.zeros((128, 128), F32) for v in range(V)]
    total = edge_terms(first_ref, second_ref, own_ref, x_ref, hmat_ref, loc_ref, 0, zeros)
    for v in range(V):
        total_ref[v] = total[v]


def head_part(first, second, own, x, hmat, loc):
    return call(head_kernel, sds(V, 128, 128), ins=[VMEM] * 6, outs=VMEM)(first, second, own, x, hmat, loc)


def edge_kernel(where_ref, first_ref, second_ref, own_ref, x_ref, hmat_ref, loc_ref, inner_ref, head_ref, after_obs, inc_ref, keep_ref, give_ref):
    total = [head_ref[v] for v in range(V)]
    total = edge_terms(first_ref, second_ref, own_ref, x_ref, hmat_ref, loc_ref, HEAD, total)
    for v in range(V):
        inc_ref[v, :64] = total[v][:64]
        inc_ref[v, 64:192] = inner_ref[v]
        inc_ref[v, 192:] = total[v][64:]
        keep_ref[v] = inc_ref[v, pl.ds(pl.multiple_of(where_ref[8], 32), 32)]
        give_ref[v] = inc_ref[v, pl.ds(pl.multiple_of(where_ref[9], 32), 32)]


def edge_part(where, first, second, own, x, hmat, loc, inner, head, after):
    return call(
        edge_kernel,
        (sds(V, 256, 128), sds(V, 32, 128), sds(V, 32, 128)),
        ins=[SMEM] + [VMEM] * 9,
        outs=(VMEM,) * 3,
    )(where, first, second, own, x, hmat, loc, inner, head, after)


def tent(distance):
    return jnp.maximum(1.0 - jnp.abs(distance), 0.0)


def weights_kernel(where_ref, own_ref, here_ref, there_ref, wown_ref, wnear_ref, lev_ref, innov_ref, weight_ref, e_ref, o_ref):
    core_0 = where_ref[10] == 0
    e_ref[...] = jnp.where(core_0, here_ref[...], there_ref[...])
    o_ref[...] = jnp.where(core_0, there_ref[...], here_ref[...])
    even_row = where_ref[2].astype(F32)
    odd_row = where_ref[3].astype(F32)
    odd_there = where_ref[4].astype(F32)
    cell = lax.broadcasted_iota(jnp.int32, (32, SLOTS), 0).astype(F32)

    def line(ref, field, v):
        at = 6 * (V * field + v)
        return jnp.concatenate([ref[at + a : at + a + 1] for a in range(6)], axis=1)

    def columns(code):
        row = jnp.floor(code * (1.0 / 64.0))
        column = code - 64.0 * row
        return row, tent(cell - (column * 0.5 - 0.25))

    for v in range(V):
        row, across = columns(line(own_ref, 0, v))
        middle = row * 0.5 - 0.25
        for r in range(8):
            wown_ref[v, 32 * r : 32 * r + 32] = (tent(r - middle) * across).astype(BF16)
        wown_ref[v, 256:288] = (tent(even_row - middle) * across).astype(BF16)
        wown_ref[v, 288:320] = (tent(odd_row - middle) * odd_there * across).astype(BF16)
        for n, ref in enumerate((e_ref, o_ref)):
            row, across = columns(line(ref, 0, v))
            wnear_ref[n, v, :32] = (0.25 * across).astype(BF16)
            wnear_ref[n, v, 32:] = (0.75 * across).astype(BF16)
    is_odd = where_ref[5]
    for n, ref in enumerate((own_ref, e_ref, o_ref)):
        for v in range(V):
            row = slice(3 * n + v, 3 * n + v + 1)
            lev_ref[row] = line(ref, 1, v)
            innov_ref[row] = line(ref, 2, v)
            weight = line(ref, 3, v)
            if n > 0:
                code = line(ref, 0, v)
                first = is_odd == (0 if n == 1 else 1)
                at_edge = jnp.where(first, code, 1023.0 - code) < 64.0
                there = at_edge & ((n == 1) | (where_ref[4] == 1))
                weight = jnp.where(there, weight, 0.0)
            weight_ref[row] = weight


def weights(where, own, here, there):
    return call(
        weights_kernel,
        (
            sds(V, 320, SLOTS, dtype=BF16),
            sds(2, V, 64, SLOTS, dtype=BF16),
            sds(9, SLOTS),
            sds(9, SLOTS),
            sds(9, SLOTS),
        ),
        ins=[SMEM, VMEM, VMEM, VMEM],
        scratch=[pltpu.VMEM(own.shape, F32), pltpu.VMEM(own.shape, F32)],
    )(where, own, here, there)


def picker(lev_ref):
    level = lax.broadcasted_iota(jnp.int32, (128, SLOTS), 0).astype(F32)

    def pick(cells, weight, row):
        both = jnp.concatenate(halves(cells), axis=1)
        at_all = tn(both, weight)
        at_all = at_all[:128] + at_all[128:]
        hot = level == lev_ref[pl.ds(row, 1), :]
        return jnp.sum(jnp.where(hot, at_all, 0.0), axis=0, keepdims=True)

    return pick


def mine_kernel(where_ref, inc_ref, wown_ref, wnear_ref, lev_ref, out_ref):
    pick = picker(lev_ref)
    for v in range(V):
        out_ref[v : v + 1] = pick(inc_ref[v], wown_ref[v, :256], v)
        for n in range(2):
            cells = inc_ref[v, pl.ds(pl.multiple_of(where_ref[n], 32), 32)]
            row = 3 * n + 3 + v
            out_ref[row : row + 1] = pick(cells, wnear_ref[n, v, :32], row)


def mine_part(where, inc, wown, wnear, lev):
    return call(
        mine_kernel,
        sds(9, SLOTS),
        ins=[SMEM] + [VMEM] * 4,
        outs=VMEM,
    )(where, inc, wown, wnear, lev)


def values_kernel(where_ref, mine_ref, near_ref, wown_ref, wnear_ref, lev_ref, out_ref):
    pick = picker(lev_ref)
    core = where_ref[10]

    def put(row, line):
        for a in range(6):
            out_ref[pl.ds(6 * row + a, 1)] = line[:, 128 * a : 128 * a + 128]

    for v in range(V):
        for n in range(2):
            row = 3 * n + 3 + v
            put(row, mine_ref[row : row + 1])
    for v in range(V):
        halo = pl.ds(pl.multiple_of(256 + 32 * core, 32), 32)
        put(v, mine_ref[v : v + 1] + pick(near_ref[v], wown_ref[v, halo], v))
        row = 3 * core + 3 + v
        put(row, mine_ref[pl.ds(row, 1)] + pick(near_ref[v], wnear_ref[core, v, 32:], row))


def values(where, mine, near, wown, wnear, lev):
    return call(
        values_kernel,
        sds(9 * SLOTS // 128, 128),
        ins=[SMEM] + [VMEM] * 5,
        outs=VMEM,
    )(where, mine, near, wown, wnear, lev)


def adjoint_kernel(where_ref, v0, v1, v2, v3, innov_ref, weight_ref, lev_ref, wown_ref, wnear_ref, x_ref, c_ref, first_ref, second_ref):
    level = lax.broadcasted_iota(jnp.int32, (128, SLOTS), 0).astype(F32)
    value = v0[...] + v1[...] + v2[...] + v3[...]

    def place(weight, row):
        line = jnp.concatenate([value[6 * row + a : 6 * row + a + 1] for a in range(6)], axis=1)
        weighted = weight_ref[row : row + 1] * (line - innov_ref[row : row + 1])
        hot = level == lev_ref[row : row + 1, :]
        spread = jnp.where(hot, weighted, 0.0)
        both = jnp.concatenate(halves(spread), axis=0)
        out = nt(weight, both)
        return out[:, :128] + out[:, 128:]

    adj = []
    for v in range(V):
        c_ref[v] = place(wown_ref[v, :256], v)
        for n in range(2):
            rows = pl.ds(pl.multiple_of(where_ref[n], 32), 32)
            c_ref[v, rows] = c_ref[v, rows] + place(wnear_ref[n, v, :32], 3 * n + 3 + v)
        adj.append(jnp.concatenate([c_ref[v, :64], c_ref[v, 192:]], axis=0))
    first_low = where_ref[7] == 1
    for k in range(first_ref.shape[0]):
        total = x_ref[k, 0].astype(F32) * adj[0]
        for v in range(1, V):
            total = total + x_ref[k, v].astype(F32) * adj[v]
        low, high = total[:64], total[64:]
        first_ref[k] = jnp.where(first_low, low, high)
        second_ref[k] = jnp.where(first_low, high, low)


def adjoint(where, vals, innov, weight, lev, wown, wnear, x):
    members = HEAD
    return call(
        adjoint_kernel,
        (sds(V, 256, 128), sds(members, 64, 128), sds(members, 64, 128)),
        ins=[SMEM] + [VMEM] * 10,
        outs=(VMEM,) * 3,
    )(where, *vals, innov, weight, lev, wown, wnear, x)


def drop(smoothed, loc):
    high, low = halves(smoothed)
    return nn(high, loc) + nn(low, loc)


def back_kernel(where_ref, alpha_ref, ens_ref, c_ref, smat_ref, loc_ref, out_ref, edge_ref, first_ref, second_ref):
    low = where_ref[7] == 1
    smat = smat_ref[...]
    loc = loc_ref[...]
    for k in range(GROUP):
        back = ens_ref[k, 0].astype(F32) * c_ref[0]
        for v in range(1, V):
            back = back + ens_ref[k, v].astype(F32) * c_ref[v]
        first_ref[k] = jnp.where(low, back[:64], back[192:])
        second_ref[k] = jnp.where(low, back[192:], back[:64])
        full = alpha_ref[k].astype(F32) + drop(smooth(smat, back), loc)
        out_ref[k] = full
        edge_ref[k, :64] = full[:64]
        edge_ref[k, 64:] = full[192:]


def back_part(where, alpha, ensemble, c, smat, loc):
    members = alpha.shape[0]
    rest = pl.BlockSpec((GROUP, 64, 128), lambda i: (jnp.maximum(i - HEAD // GROUP, 0), 0, 0))
    return call(
        back_kernel,
        (
            sds(members, 256, 128),
            sds(members, 128, 128),
            sds(members - HEAD, 64, 128),
            sds(members - HEAD, 64, 128),
        ),
        grid=(members // GROUP,),
        ins=[
            SMEM,
            pl.BlockSpec((GROUP, 256, 128), lambda i: (i, 0, 0)),
            pl.BlockSpec((GROUP, V, 256, 128), lambda i: (i, 0, 0, 0)),
            pl.BlockSpec((V, 256, 128), lambda i: (0, 0, 0)),
            pl.BlockSpec((256, 256), lambda i: (0, 0)),
            pl.BlockSpec((128, 128), lambda i: (0, 0)),
        ],
        outs=(
            pl.BlockSpec((GROUP, 256, 128), lambda i: (i, 0, 0)),
            pl.BlockSpec((GROUP, 128, 128), lambda i: (i, 0, 0)),
            rest,
            rest,
        ),
    )(where, alpha, ensemble, c, smat, loc)


def last_kernel(start, first_ref, second_ref, edge_ref, hmat_ref, loc_ref, unused_ref, out_ref, held, sems):
    hmat = hmat_ref[...]
    loc = loc_ref[...]
    copies = []
    for g in range(first_ref.shape[0] // GROUP):
        for k in range(g * GROUP, (g + 1) * GROUP):
            halo = jnp.concatenate([first_ref[k], second_ref[k]], axis=0)
            full = edge_ref[start + k] + drop(smooth(hmat, halo), loc)
            held[k, 0] = full[:64]
            held[k, 1] = full[64:]
        here, there = pl.ds(g * GROUP, GROUP), pl.ds(start + g * GROUP, GROUP)
        for side in range(2):
            copies.append(
                pltpu.make_async_copy(held.at[here, side], out_ref.at[there, 3 * side], sems.at[g, side])
            )
            copies[-1].start()
    for copy in copies:
        copy.wait()


def last_part(start, first, second, edge, hmat, loc, out):
    count = first.shape[0]
    return call(
        functools.partial(last_kernel, start),
        sds(*out.shape),
        ins=[VMEM] * 5 + [ANY],
        outs=ANY,
        scratch=[pltpu.VMEM((count, 2, 64, 128), F32), pltpu.SemaphoreType.DMA((count // GROUP, 2))],
        aliases={5: 0},
    )(first, second, edge, hmat, loc, out)


def stencil(gap):
    gap = jnp.abs(gap)
    return jnp.where(gap == 0, 6.0, jnp.where(gap == 1, 4.0, jnp.where(gap == 2, 1.0, 0.0)))


def matrices(tile, tiles, first_high):
    def across(i, j):
        gap = stencil(i - j)
        return jnp.where((i == j) & ((i == 0) | (i == 31)), 5.0, gap)

    i = lax.broadcasted_iota(jnp.int32, (256, 256), 0)
    j = lax.broadcasted_iota(jnp.int32, (256, 256), 1)
    ri, rj = i // 32, j // 32
    ends = ((ri == 0) & (tile == 0)) | ((ri == 7) & (tile == tiles - 1))
    down = jnp.where((ri == rj) & ends, 5.0, stencil(ri - rj))
    smat = (down * across(i % 32, j % 32) * (1.0 / 256.0)).astype(BF16)
    i = lax.broadcasted_iota(jnp.int32, (128, 128), 0)
    j = lax.broadcasted_iota(jnp.int32, (128, 128), 1)
    ri = i // 32
    ri = jnp.where(ri < 2, ri, ri + 4)
    above = (j < 64) == first_high
    rj = jnp.where(above, 8, -2) + (j // 32) % 2
    there = (above & (tile < tiles - 1)) | (jnp.logical_not(above) & (tile > 0))
    hmat = jnp.where(there, stencil(ri - rj), 0.0) * across(i % 32, j % 32) * (1.0 / 256.0)
    return smat, hmat.astype(BF16)


def swap_first(x):
    return lax.ppermute(x, ("mem", "tile"), FIRST)


def swap_second(x):
    return lax.ppermute(x, ("mem", "tile"), SECOND)


def swap_core(x):
    return lax.ppermute(x, "mem", [(m, m ^ 1) for m in range(MEMS)])


def round_mem(mine):
    size = lax.axis_size("mem")
    return [mine] + [
        lax.ppermute(mine, "mem", [(i, (i + shift) % size) for i in range(size)]) for shift in range(1, size)
    ]


def on_device(alpha, ensemble, loc_vert, obs_col, obs_lev, obs_count, innovation, obs_weight):
    members = alpha.shape[0]
    tile = lax.axis_index("tile")
    tiles = lax.axis_size("tile")
    even = tile % 2 == 0
    core = lax.axis_index("mem") % 2
    first_low = (tile + core) % 2
    where = jnp.stack(
        [
            jnp.where(even, 7 * 32, 0),
            jnp.where(even, 0, 7 * 32),
            jnp.where(even, 8, -1),
            jnp.where(even, -1, 8),
            ((tile > 0) & (tile < tiles - 1)).astype(jnp.int32),
            tile % 2,
            tile,
            first_low,
            7 * 32 * (1 - first_low),
            7 * 32 * first_low,
            core,
        ]
    ).astype(jnp.int32)
    flat = alpha.reshape(members, 256, 128)
    flat_ens = ensemble.reshape(members, V, 256, 128)

    send_first, send_second, token = send_part(where, alpha.reshape(members, 4, 64, 128))
    first, second = swap_first(send_first), swap_second(send_second)
    inner, own_edge, x, smat, hmat, token, send_first, send_second = own_part(where, flat, flat_ens, loc_vert, token)
    first_rest, second_rest = swap_first(send_first), swap_second(send_second)
    own_obs = observations(obs_count, obs_col, obs_lev, innovation, obs_weight, token)
    here_obs = swap_first(own_obs)

    head = head_part(first, second, own_edge, x, hmat, loc_vert)
    inc, keep, give = edge_part(
        where, first_rest, second_rest, own_edge, x, hmat, loc_vert, inner, head, here_obs
    )
    near = swap_first(keep + swap_core(give))
    there_obs = swap_core(here_obs)
    wown, wnear, lev, innov, weight = weights(where, own_obs, here_obs, there_obs)
    mine = mine_part(where, inc, wown, wnear, lev)
    vals = round_mem(values(where, mine, near, wown, wnear, lev))
    c, back_first, back_second = adjoint(where, vals, innov, weight, lev, wown, wnear, x)
    halo_first, halo_second = swap_first(back_first), swap_second(back_second)
    out, edge, back_first, back_second = back_part(where, flat, flat_ens, c, smat, loc_vert)
    rest_first, rest_second = swap_first(back_first), swap_second(back_second)
    out = last_part(0, halo_first, halo_second, edge, hmat, loc_vert, out.reshape(members, 4, 64, 128))
    out = last_part(HEAD, rest_first, rest_second, edge, hmat, loc_vert, out)
    return out.reshape(members, 8, 32, 128)


def solution(mesh):
    in_specs = (
        P("mem", "tile", None, None),
        P("mem", None, "tile", None, None),
        P(),
        P("tile", None),
        P("tile", None),
        P("tile"),
        P("tile", None),
        P("tile", None),
    )
    out_specs = P("mem", "tile", None, None)
    return jax.shard_map(
        on_device, mesh=mesh, in_specs=in_specs, out_specs=out_specs, check_vma=False
    )
```

```python
import functools

import jax
import jax.numpy as jnp
from jax import lax
from jax.experimental import pallas as pl
from jax.experimental.pallas import tpu as pltpu
from jax.sharding import PartitionSpec as P

V = 3
F32 = jnp.float32
BF16 = jnp.bfloat16
SLOTS = 768
GROUP = 4
HEAD = 12
OBS = 72

TILES = 64
EVEN = [(i, i ^ 1) for i in range(TILES)]
ODD = [(i, ((i - 1) ^ 1) + 1) for i in range(1, TILES - 1)] + [(0, 0), (TILES - 1, TILES - 1)]

MEMS = 4
FIRST = [(TILES * m + a, TILES * m + b) for m in range(MEMS) for a, b in (ODD if m % 2 else EVEN)]
SECOND = [(TILES * m + a, TILES * m + b) for m in range(MEMS) for a, b in (EVEN if m % 2 else ODD)]


def nn(a, b):
    return lax.dot_general(a, b, (((1,), (0,)), ((), ())), preferred_element_type=F32)


def nt(a, b):
    return lax.dot_general(a, b, (((1,), (1,)), ((), ())), preferred_element_type=F32)


def tn(a, b):
    return lax.dot_general(a, b, (((0,), (0,)), ((), ())), preferred_element_type=F32)


def halves(x):
    high = x.astype(BF16)
    low = (x - high.astype(F32)).astype(BF16)
    return high, low


def lift(smoothed, loc):
    high, low = halves(smoothed)
    return nt(high, loc) + nt(low, loc)


def call(kernel, out, grid=None, ins=None, outs=None, scratch=(), aliases=None, cost=1000000):
    vmem = pl.BlockSpec(memory_space=pltpu.VMEM)
    kw = {}
    if grid is not None:
        kw["grid"] = grid
    return pl.pallas_call(
        kernel,
        out_shape=out,
        in_specs=ins,
        out_specs=outs if outs is not None else jax.tree.map(lambda o: vmem, out),
        scratch_shapes=scratch,
        input_output_aliases=aliases or {},
        compiler_params=pltpu.CompilerParams(vmem_limit_bytes=16 * 1024 * 1024),
        cost_estimate=pl.CostEstimate(flops=cost, bytes_accessed=cost, transcendentals=0),
        **kw,
    )


def sds(*shape, dtype=F32):
    return jax.ShapeDtypeStruct(shape, dtype)


ANY = pl.BlockSpec(memory_space=pl.ANY)
SMEM = pl.BlockSpec(memory_space=pltpu.SMEM)
VMEM = pl.BlockSpec(memory_space=pltpu.VMEM)


def smooth(matrix, field):
    both = jnp.concatenate(halves(field), axis=1)
    out = nn(matrix, both)
    return out[:, :128] + out[:, 128:]


def sort_observations(count, col_ref, lev_ref, innov_ref, weight_ref, out_ref):
    slots = col_ref.shape[1]
    live = lax.broadcasted_iota(jnp.int32, (1, slots), 1) < count
    rows = []
    for field in (
        col_ref[...].astype(F32),
        lev_ref[...].astype(F32),
        innov_ref[...],
        jnp.where(live, weight_ref[...], 0.0),
    ):
        field = jnp.concatenate([field, jnp.zeros((1, V * SLOTS - slots), F32)], axis=1)
        rows += [field[:, 384 * a : 384 * a + 384] for a in range(6)]
    rest = jnp.concatenate(rows, axis=0)
    i = lax.broadcasted_iota(jnp.int32, (384, 384), 0)
    j = lax.broadcasted_iota(jnp.int32, (384, 384), 1)
    order = (i == 3 * (j % 128) + j // 128).astype(F32).astype(BF16)
    total = jnp.zeros((24, 384), F32)
    for piece in range(3):
        part = rest.astype(BF16)
        rest = rest - part.astype(F32)
        total = total + nn(part, order)
    for f in range(4):
        for a in range(6):
            for v in range(V):
                row = 6 * (V * f + v) + a
                out_ref[row : row + 1] = total[6 * f + a : 6 * f + a + 1, 128 * v : 128 * v + 128]


def send_kernel(where_ref, count_ref, col_ref, lev_ref, innov_ref, weight_ref, quarters_ref, first_ref, second_ref, obs_ref, edges, sems):
    head = pl.ds(0, HEAD)
    copies = [pltpu.make_async_copy(quarters_ref.at[head, 3 * n], edges.at[n], sems.at[n]) for n in range(2)]
    for copy in copies:
        copy.start()
    sort_observations(count_ref[0], col_ref, lev_ref, innov_ref, weight_ref, obs_ref)
    first_ref[64 * HEAD :] = obs_ref[...]
    for copy in copies:
        copy.wait()
    low = where_ref[7]
    for k in range(HEAD):
        first_ref[64 * k : 64 * k + 64] = edges[1 - low, k].astype(F32)
        second_ref[64 * k : 64 * k + 64] = edges[low, k].astype(F32)


def send_part(where, count, col, lev, innov, weight, quarters):
    return call(
        send_kernel,
        (sds(64 * HEAD + OBS, 128), sds(64 * HEAD, 128), sds(OBS, 128)),
        ins=[SMEM, SMEM] + [VMEM] * 4 + [ANY],
        outs=(VMEM,) * 3,
        scratch=[pltpu.VMEM((2, HEAD, 64, 128), BF16), pltpu.SemaphoreType.DMA((2,))],
    )(where, count, col, lev, innov, weight, quarters)


def own_kernel(where_ref, alpha_ref, ens_ref, loc_ref, after_ref, inner_ref, edge_ref, x_ref, smat_ref, hmat_ref, first_ref, second_ref):
    @pl.when(pl.program_id(0) == 0)
    def _():
        inner_ref[...] = jnp.zeros_like(inner_ref)
        smat, hmat = matrices(where_ref[6], TILES, where_ref[7] == 0)
        smat_ref[...] = smat
        hmat_ref[...] = hmat

    smat = smat_ref[...]
    loc = loc_ref[...]
    total = [inner_ref[v] for v in range(V)]
    for k in range(GROUP):
        full = lift(nn(smat, alpha_ref[k]), loc)
        edge_ref[k, :64] = full[:64]
        edge_ref[k, 64:] = full[192:]
        lifted = full[64:192].astype(BF16).astype(F32)
        for v in range(V):
            total[v] = total[v] + ens_ref[k, v, 64:192].astype(F32) * lifted
            x_ref[k, v, :64] = ens_ref[k, v, :64]
            x_ref[k, v, 64:] = ens_ref[k, v, 192:]
    for v in range(V):
        inner_ref[v] = total[v]

    @pl.when(pl.program_id(0) >= HEAD // GROUP)
    def _():
        low = where_ref[7] == 1
        for k in range(GROUP):
            rows = [alpha_ref[k, :64].astype(F32), alpha_ref[k, 192:].astype(F32)]
            first_ref[k] = jnp.where(low, rows[0], rows[1])
            second_ref[k] = jnp.where(low, rows[1], rows[0])


def own_part(where, alpha, ensemble, loc, after):
    members = alpha.shape[0]
    whole = lambda *shape: pl.BlockSpec(shape, lambda i: (0,) * len(shape))
    rest = pl.BlockSpec((GROUP, 64, 128), lambda i: (jnp.maximum(i - HEAD // GROUP, 0), 0, 0))
    return call(
        own_kernel,
        (
            sds(V, 128, 128),
            sds(members, 128, 128),
            sds(members, V, 128, 128, dtype=BF16),
            sds(256, 256, dtype=BF16),
            sds(128, 128, dtype=BF16),
            sds(members - HEAD, 64, 128),
            sds(members - HEAD, 64, 128),
        ),
        grid=(members // GROUP,),
        ins=[
            SMEM,
            pl.BlockSpec((GROUP, 256, 128), lambda i: (i, 0, 0)),
            pl.BlockSpec((GROUP, V, 256, 128), lambda i: (i, 0, 0, 0)),
            whole(128, 128),
            whole(OBS, 128),
        ],
        outs=(
            whole(V, 128, 128),
            pl.BlockSpec((GROUP, 128, 128), lambda i: (i, 0, 0)),
            pl.BlockSpec((GROUP, V, 128, 128), lambda i: (i, 0, 0, 0)),
            whole(256, 256),
            whole(128, 128),
            rest,
            rest,
        ),
    )(where, alpha, ensemble, loc, after)


def edge_terms(first_ref, second_ref, own_ref, x_ref, hmat_ref, loc_ref, start, total):
    hmat = hmat_ref[...]
    loc = loc_ref[...]
    for k in range(second_ref.shape[0] // 64):
        rows = slice(64 * k, 64 * k + 64)
        halo = jnp.concatenate([first_ref[rows].astype(BF16), second_ref[rows].astype(BF16)], axis=0)
        lifted = (own_ref[start + k] + lift(nn(hmat, halo), loc)).astype(BF16).astype(F32)
        for v in range(V):
            total[v] = total[v] + x_ref[start + k, v].astype(F32) * lifted
    return total


def head_kernel(first_ref, second_ref, own_ref, x_ref, hmat_ref, loc_ref, after_ref, total_ref):
    zeros = [jnp.zeros((128, 128), F32) for v in range(V)]
    total = edge_terms(first_ref, second_ref, own_ref, x_ref, hmat_ref, loc_ref, 0, zeros)
    for v in range(V):
        total_ref[v] = total[v]


def head_part(first, second, own, x, hmat, loc, after):
    return call(head_kernel, sds(V, 128, 128), ins=[VMEM] * 7, outs=VMEM)(
        first, second, own, x, hmat, loc, after
    )


def edge_kernel(where_ref, first_ref, second_ref, own_ref, x_ref, hmat_ref, loc_ref, inner_ref, head_ref, inc_ref, keep_ref, give_ref):
    total = [head_ref[v] for v in range(V)]
    total = edge_terms(first_ref, second_ref, own_ref, x_ref, hmat_ref, loc_ref, HEAD, total)
    for v in range(V):
        inc_ref[v, :64] = total[v][:64]
        inc_ref[v, 64:192] = inner_ref[v]
        inc_ref[v, 192:] = total[v][64:]
        keep_ref[v] = inc_ref[v, pl.ds(pl.multiple_of(where_ref[8], 32), 32)]
        give_ref[v] = inc_ref[v, pl.ds(pl.multiple_of(where_ref[9], 32), 32)]


def edge_part(where, first, second, own, x, hmat, loc, inner, head):
    return call(
        edge_kernel,
        (sds(V, 256, 128), sds(V, 32, 128), sds(V, 32, 128)),
        ins=[SMEM] + [VMEM] * 8,
        outs=(VMEM,) * 3,
    )(where, first, second, own, x, hmat, loc, inner, head)


def tent(distance):
    return jnp.maximum(1.0 - jnp.abs(distance), 0.0)


def weights_kernel(where_ref, own_ref, here_ref, there_ref, wown_ref, wnear_ref, lev_ref, innov_ref, weight_ref, e_ref, o_ref):
    core_0 = where_ref[10] == 0
    e_ref[...] = jnp.where(core_0, here_ref[...], there_ref[...])
    o_ref[...] = jnp.where(core_0, there_ref[...], here_ref[...])
    even_row = where_ref[2].astype(F32)
    odd_row = where_ref[3].astype(F32)
    odd_there = where_ref[4].astype(F32)
    cell = lax.broadcasted_iota(jnp.int32, (32, SLOTS), 0).astype(F32)

    def line(ref, field, v):
        at = 6 * (V * field + v)
        return jnp.concatenate([ref[at + a : at + a + 1] for a in range(6)], axis=1)

    def columns(code):
        row = jnp.floor(code * (1.0 / 64.0))
        column = code - 64.0 * row
        return row, tent(cell - (column * 0.5 - 0.25))

    for v in range(V):
        row, across = columns(line(own_ref, 0, v))
        middle = row * 0.5 - 0.25
        for r in range(8):
            wown_ref[v, 32 * r : 32 * r + 32] = (tent(r - middle) * across).astype(BF16)
        wown_ref[v, 256:288] = (tent(even_row - middle) * across).astype(BF16)
        wown_ref[v, 288:320] = (tent(odd_row - middle) * odd_there * across).astype(BF16)
        for n, ref in enumerate((e_ref, o_ref)):
            row, across = columns(line(ref, 0, v))
            wnear_ref[n, v, :32] = (0.25 * across).astype(BF16)
            wnear_ref[n, v, 32:] = (0.75 * across).astype(BF16)
    is_odd = where_ref[5]
    for n, ref in enumerate((own_ref, e_ref, o_ref)):
        for v in range(V):
            row = slice(3 * n + v, 3 * n + v + 1)
            lev_ref[row] = line(ref, 1, v)
            innov_ref[row] = line(ref, 2, v)
            weight = line(ref, 3, v)
            if n > 0:
                code = line(ref, 0, v)
                first = is_odd == (0 if n == 1 else 1)
                at_edge = jnp.where(first, code, 1023.0 - code) < 64.0
                there = at_edge & ((n == 1) | (where_ref[4] == 1))
                weight = jnp.where(there, weight, 0.0)
            weight_ref[row] = weight


def weights(where, own, here, there):
    return call(
        weights_kernel,
        (
            sds(V, 320, SLOTS, dtype=BF16),
            sds(2, V, 64, SLOTS, dtype=BF16),
            sds(9, SLOTS),
            sds(9, SLOTS),
            sds(9, SLOTS),
        ),
        ins=[SMEM, VMEM, VMEM, VMEM],
        scratch=[pltpu.VMEM(own.shape, F32), pltpu.VMEM(own.shape, F32)],
    )(where, own, here, there)


def picker(lev_ref):
    level = lax.broadcasted_iota(jnp.int32, (128, SLOTS), 0).astype(F32)

    def pick(cells, weight, row):
        both = jnp.concatenate(halves(cells), axis=1)
        at_all = tn(both, weight)
        at_all = at_all[:128] + at_all[128:]
        hot = level == lev_ref[pl.ds(row, 1), :]
        return jnp.sum(jnp.where(hot, at_all, 0.0), axis=0, keepdims=True)

    return pick


def mine_kernel(where_ref, inc_ref, wown_ref, wnear_ref, lev_ref, out_ref):
    pick = picker(lev_ref)
    for v in range(V):
        out_ref[v : v + 1] = pick(inc_ref[v], wown_ref[v, :256], v)
        for n in range(2):
            cells = inc_ref[v, pl.ds(pl.multiple_of(where_ref[n], 32), 32)]
            row = 3 * n + 3 + v
            out_ref[row : row + 1] = pick(cells, wnear_ref[n, v, :32], row)


def mine_part(where, inc, wown, wnear, lev):
    return call(
        mine_kernel,
        sds(9, SLOTS),
        ins=[SMEM] + [VMEM] * 4,
        outs=VMEM,
    )(where, inc, wown, wnear, lev)


def values_kernel(where_ref, mine_ref, near_ref, wown_ref, wnear_ref, lev_ref, out_ref):
    pick = picker(lev_ref)
    core = where_ref[10]

    def put(row, line):
        for a in range(6):
            out_ref[pl.ds(6 * row + a, 1)] = line[:, 128 * a : 128 * a + 128]

    for v in range(V):
        for n in range(2):
            row = 3 * n + 3 + v
            put(row, mine_ref[row : row + 1])
    for v in range(V):
        halo = pl.ds(pl.multiple_of(256 + 32 * core, 32), 32)
        put(v, mine_ref[v : v + 1] + pick(near_ref[v], wown_ref[v, halo], v))
        row = 3 * core + 3 + v
        put(row, mine_ref[pl.ds(row, 1)] + pick(near_ref[v], wnear_ref[core, v, 32:], row))


def values(where, mine, near, wown, wnear, lev):
    return call(
        values_kernel,
        sds(9 * SLOTS // 128, 128),
        ins=[SMEM] + [VMEM] * 5,
        outs=VMEM,
    )(where, mine, near, wown, wnear, lev)


def adjoint_kernel(where_ref, v0, v1, v2, v3, innov_ref, weight_ref, lev_ref, wown_ref, wnear_ref, x_ref, c_ref, first_ref, second_ref):
    level = lax.broadcasted_iota(jnp.int32, (128, SLOTS), 0).astype(F32)
    value = v0[...] + v1[...] + v2[...] + v3[...]

    def place(weight, row):
        line = jnp.concatenate([value[6 * row + a : 6 * row + a + 1] for a in range(6)], axis=1)
        weighted = weight_ref[row : row + 1] * (line - innov_ref[row : row + 1])
        hot = level == lev_ref[row : row + 1, :]
        spread = jnp.where(hot, weighted, 0.0)
        both = jnp.concatenate(halves(spread), axis=0)
        out = nt(weight, both)
        return out[:, :128] + out[:, 128:]

    adj = []
    for v in range(V):
        c_ref[v] = place(wown_ref[v, :256], v)
        for n in range(2):
            rows = pl.ds(pl.multiple_of(where_ref[n], 32), 32)
            c_ref[v, rows] = c_ref[v, rows] + place(wnear_ref[n, v, :32], 3 * n + 3 + v)
        adj.append(jnp.concatenate([c_ref[v, :64], c_ref[v, 192:]], axis=0))
    first_low = where_ref[7] == 1
    for k in range(first_ref.shape[0]):
        total = x_ref[k, 0].astype(F32) * adj[0]
        for v in range(1, V):
            total = total + x_ref[k, v].astype(F32) * adj[v]
        low, high = total[:64], total[64:]
        first_ref[k] = jnp.where(first_low, low, high)
        second_ref[k] = jnp.where(first_low, high, low)


def adjoint(where, vals, innov, weight, lev, wown, wnear, x):
    members = HEAD
    return call(
        adjoint_kernel,
        (sds(V, 256, 128), sds(members, 64, 128), sds(members, 64, 128)),
        ins=[SMEM] + [VMEM] * 10,
        outs=(VMEM,) * 3,
    )(where, *vals, innov, weight, lev, wown, wnear, x)


def drop(smoothed, loc):
    high, low = halves(smoothed)
    return nn(high, loc) + nn(low, loc)


def back_kernel(where_ref, alpha_ref, ens_ref, c_ref, smat_ref, loc_ref, out_ref, edge_ref, first_ref, second_ref):
    low = where_ref[7] == 1
    smat = smat_ref[...]
    loc = loc_ref[...]
    for k in range(GROUP):
        back = ens_ref[k, 0].astype(F32) * c_ref[0]
        for v in range(1, V):
            back = back + ens_ref[k, v].astype(F32) * c_ref[v]
        first_ref[k] = jnp.where(low, back[:64], back[192:])
        second_ref[k] = jnp.where(low, back[192:], back[:64])
        full = alpha_ref[k].astype(F32) + drop(smooth(smat, back), loc)
        out_ref[k] = full
        edge_ref[k, :64] = full[:64]
        edge_ref[k, 64:] = full[192:]


def back_part(where, alpha, ensemble, c, smat, loc):
    members = alpha.shape[0]
    rest = pl.BlockSpec((GROUP, 64, 128), lambda i: (jnp.maximum(i - HEAD // GROUP, 0), 0, 0))
    return call(
        back_kernel,
        (
            sds(members, 256, 128),
            sds(members, 128, 128),
            sds(members - HEAD, 64, 128),
            sds(members - HEAD, 64, 128),
        ),
        grid=(members // GROUP,),
        ins=[
            SMEM,
            pl.BlockSpec((GROUP, 256, 128), lambda i: (i, 0, 0)),
            pl.BlockSpec((GROUP, V, 256, 128), lambda i: (i, 0, 0, 0)),
            pl.BlockSpec((V, 256, 128), lambda i: (0, 0, 0)),
            pl.BlockSpec((256, 256), lambda i: (0, 0)),
            pl.BlockSpec((128, 128), lambda i: (0, 0)),
        ],
        outs=(
            pl.BlockSpec((GROUP, 256, 128), lambda i: (i, 0, 0)),
            pl.BlockSpec((GROUP, 128, 128), lambda i: (i, 0, 0)),
            rest,
            rest,
        ),
    )(where, alpha, ensemble, c, smat, loc)


def last_kernel(start, first_ref, second_ref, edge_ref, hmat_ref, loc_ref, unused_ref, out_ref, held, sems):
    hmat = hmat_ref[...]
    loc = loc_ref[...]
    copies = []
    for g in range(first_ref.shape[0] // GROUP):
        for k in range(g * GROUP, (g + 1) * GROUP):
            halo = jnp.concatenate([first_ref[k], second_ref[k]], axis=0)
            full = edge_ref[start + k] + drop(smooth(hmat, halo), loc)
            held[k, 0] = full[:64]
            held[k, 1] = full[64:]
        here, there = pl.ds(g * GROUP, GROUP), pl.ds(start + g * GROUP, GROUP)
        for side in range(2):
            copies.append(
                pltpu.make_async_copy(held.at[here, side], out_ref.at[there, 3 * side], sems.at[g, side])
            )
            copies[-1].start()
    for copy in copies:
        copy.wait()


def last_part(start, first, second, edge, hmat, loc, out):
    count = first.shape[0]
    return call(
        functools.partial(last_kernel, start),
        sds(*out.shape),
        ins=[VMEM] * 5 + [ANY],
        outs=ANY,
        scratch=[pltpu.VMEM((count, 2, 64, 128), F32), pltpu.SemaphoreType.DMA((count // GROUP, 2))],
        aliases={5: 0},
    )(first, second, edge, hmat, loc, out)


def stencil(gap):
    gap = jnp.abs(gap)
    return jnp.where(gap == 0, 6.0, jnp.where(gap == 1, 4.0, jnp.where(gap == 2, 1.0, 0.0)))


def matrices(tile, tiles, first_high):
    def across(i, j):
        gap = stencil(i - j)
        return jnp.where((i == j) & ((i == 0) | (i == 31)), 5.0, gap)

    i = lax.broadcasted_iota(jnp.int32, (256, 256), 0)
    j = lax.broadcasted_iota(jnp.int32, (256, 256), 1)
    ri, rj = i // 32, j // 32
    ends = ((ri == 0) & (tile == 0)) | ((ri == 7) & (tile == tiles - 1))
    down = jnp.where((ri == rj) & ends, 5.0, stencil(ri - rj))
    smat = (down * across(i % 32, j % 32) * (1.0 / 256.0)).astype(BF16)
    i = lax.broadcasted_iota(jnp.int32, (128, 128), 0)
    j = lax.broadcasted_iota(jnp.int32, (128, 128), 1)
    ri = i // 32
    ri = jnp.where(ri < 2, ri, ri + 4)
    above = (j < 64) == first_high
    rj = jnp.where(above, 8, -2) + (j // 32) % 2
    there = (above & (tile < tiles - 1)) | (jnp.logical_not(above) & (tile > 0))
    hmat = jnp.where(there, stencil(ri - rj), 0.0) * across(i % 32, j % 32) * (1.0 / 256.0)
    return smat, hmat.astype(BF16)


def swap_first(x):
    return lax.ppermute(x, ("mem", "tile"), FIRST)


def swap_second(x):
    return lax.ppermute(x, ("mem", "tile"), SECOND)


def swap_core(x):
    return lax.ppermute(x, "mem", [(m, m ^ 1) for m in range(MEMS)])


def round_mem(mine):
    size = lax.axis_size("mem")
    return [mine] + [
        lax.ppermute(mine, "mem", [(i, (i + shift) % size) for i in range(size)]) for shift in range(1, size)
    ]


def on_device(alpha, ensemble, loc_vert, obs_col, obs_lev, obs_count, innovation, obs_weight):
    members = alpha.shape[0]
    tile = lax.axis_index("tile")
    tiles = lax.axis_size("tile")
    even = tile % 2 == 0
    core = lax.axis_index("mem") % 2
    first_low = (tile + core) % 2
    where = jnp.stack(
        [
            jnp.where(even, 7 * 32, 0),
            jnp.where(even, 0, 7 * 32),
            jnp.where(even, 8, -1),
            jnp.where(even, -1, 8),
            ((tile > 0) & (tile < tiles - 1)).astype(jnp.int32),
            tile % 2,
            tile,
            first_low,
            7 * 32 * (1 - first_low),
            7 * 32 * first_low,
            core,
        ]
    ).astype(jnp.int32)
    flat = alpha.reshape(members, 256, 128)
    flat_ens = ensemble.reshape(members, V, 256, 128)

    send_first, send_second, own_obs = send_part(
        where, obs_count, obs_col, obs_lev, innovation, obs_weight, alpha.reshape(members, 4, 64, 128)
    )
    first, second = swap_first(send_first), swap_second(send_second)
    inner, own_edge, x, smat, hmat, send_first, send_second = own_part(where, flat, flat_ens, loc_vert, own_obs)
    rest = send_first.reshape(-1, 128), send_second.reshape(-1, 128)
    first_rest, second_rest = swap_first(rest[0]), swap_second(rest[1])
    here_obs = first[64 * HEAD :]
    there_obs = swap_core(here_obs)
    wown, wnear, lev, innov, weight = weights(where, own_obs, here_obs, there_obs)
    head = head_part(first, second, own_edge, x, hmat, loc_vert, lev)
    inc, keep, give = edge_part(where, first_rest, second_rest, own_edge, x, hmat, loc_vert, inner, head)
    near = swap_first(keep + swap_core(give))
    mine = mine_part(where, inc, wown, wnear, lev)
    vals = round_mem(values(where, mine, near, wown, wnear, lev))
    c, back_first, back_second = adjoint(where, vals, innov, weight, lev, wown, wnear, x)
    halo_first, halo_second = swap_first(back_first), swap_second(back_second)
    out, edge, back_first, back_second = back_part(where, flat, flat_ens, c, smat, loc_vert)
    rest_first, rest_second = swap_first(back_first), swap_second(back_second)
    out = last_part(0, halo_first, halo_second, edge, hmat, loc_vert, out.reshape(members, 4, 64, 128))
    out = last_part(HEAD, rest_first, rest_second, edge, hmat, loc_vert, out)
    return out.reshape(members, 8, 32, 128)


def solution(mesh):
    in_specs = (
        P("mem", "tile", None, None),
        P("mem", None, "tile", None, None),
        P(),
        P("tile", None),
        P("tile", None),
        P("tile"),
        P("tile", None),
        P("tile", None),
    )
    out_specs = P("mem", "tile", None, None)
    return jax.shard_map(
        on_device, mesh=mesh, in_specs=in_specs, out_specs=out_specs, check_vma=False
    )
```

```python
import functools

import jax
import jax.numpy as jnp
from jax import lax
from jax.experimental import pallas as pl
from jax.experimental.pallas import tpu as pltpu
from jax.sharding import PartitionSpec as P

V = 3
F32 = jnp.float32
BF16 = jnp.bfloat16
SLOTS = 768
GROUP = 4
HEAD = 12
OBS = 72

TILES = 64
MEMS = 4


def swap_pairs(odd_core):
    pairs = []
    for m in range(MEMS):
        for t in range(TILES):
            beside = ((t - 1) ^ 1) + 1 if m % 2 == odd_core else t ^ 1
            if 0 <= beside < TILES:
                pairs.append((TILES * m + t, TILES * m + beside))
            else:
                pairs.append((TILES * m + t, TILES * (m ^ 2) + t))
    return pairs


FIRST = swap_pairs(1)
SECOND = swap_pairs(0)


def nn(a, b):
    return lax.dot_general(a, b, (((1,), (0,)), ((), ())), preferred_element_type=F32)


def nt(a, b):
    return lax.dot_general(a, b, (((1,), (1,)), ((), ())), preferred_element_type=F32)


def tn(a, b):
    return lax.dot_general(a, b, (((0,), (0,)), ((), ())), preferred_element_type=F32)


def halves(x):
    high = x.astype(BF16)
    low = (x - high.astype(F32)).astype(BF16)
    return high, low


def lift(smoothed, loc):
    high, low = halves(smoothed)
    return nt(high, loc) + nt(low, loc)


def call(kernel, out, grid=None, ins=None, outs=None, scratch=(), aliases=None, cost=1000, vmem=16):
    kw = {}
    if grid is not None:
        kw["grid"] = grid
    return pl.pallas_call(
        kernel,
        out_shape=out,
        in_specs=ins,
        out_specs=outs if outs is not None else jax.tree.map(lambda o: VMEM, out),
        scratch_shapes=scratch,
        input_output_aliases=aliases or {},
        compiler_params=pltpu.CompilerParams(vmem_limit_bytes=vmem * 1024 * 1024),
        cost_estimate=pl.CostEstimate(flops=cost, bytes_accessed=cost, transcendentals=0),
        **kw,
    )


def sds(*shape, dtype=F32):
    return jax.ShapeDtypeStruct(shape, dtype)


ANY = pl.BlockSpec(memory_space=pl.ANY)
SMEM = pl.BlockSpec(memory_space=pltpu.SMEM)
VMEM = pl.BlockSpec(memory_space=pltpu.VMEM)
HBM = pl.BlockSpec(memory_space=pltpu.HBM)


def smooth(matrix, field):
    both = jnp.concatenate(halves(field), axis=1)
    out = nn(matrix, both)
    return out[:, :128] + out[:, 128:]


def sort_observations(count, col_ref, lev_ref, innov_ref, weight_ref, out_ref):
    slots = col_ref.shape[1]
    live = lax.broadcasted_iota(jnp.int32, (1, slots), 1) < count
    rows = []
    for field in (
        col_ref[...].astype(F32),
        lev_ref[...].astype(F32),
        innov_ref[...],
        jnp.where(live, weight_ref[...], 0.0),
    ):
        field = jnp.concatenate([field, jnp.zeros((1, V * SLOTS - slots), F32)], axis=1)
        rows += [field[:, 384 * a : 384 * a + 384] for a in range(6)]
    rest = jnp.concatenate(rows, axis=0)
    i = lax.broadcasted_iota(jnp.int32, (384, 384), 0)
    j = lax.broadcasted_iota(jnp.int32, (384, 384), 1)
    order = (i == 3 * (j % 128) + j // 128).astype(F32).astype(BF16)
    total = jnp.zeros((24, 384), F32)
    for piece in range(3):
        part = rest.astype(BF16)
        rest = rest - part.astype(F32)
        total = total + nn(part, order)
    for f in range(4):
        for a in range(6):
            for v in range(V):
                row = 6 * (V * f + v) + a
                out_ref[row : row + 1] = total[6 * f + a : 6 * f + a + 1, 128 * v : 128 * v + 128]


def send_kernel(where_ref, count_ref, *refs):
    obs_in, (quarters_ref, first_ref, second_ref, obs_ref), obs_here, (edges, sems) = refs[:4], refs[4:8], refs[8:12], refs[12:]
    head = pl.ds(0, HEAD)
    copies = [pltpu.make_async_copy(quarters_ref.at[head, 3 * n], edges.at[n], sems.at[n]) for n in range(2)]
    fetches = [pltpu.make_async_copy(obs_in[n], obs_here[n], sems.at[2 + n]) for n in range(4)]
    for copy in fetches + copies:
        copy.start()
    for copy in fetches:
        copy.wait()
    sort_observations(count_ref[0], *obs_here, obs_ref)
    first_ref[64 * HEAD :] = obs_ref[...]
    for copy in copies:
        copy.wait()
    low = where_ref[7]
    for k in range(HEAD):
        first_ref[64 * k : 64 * k + 64] = edges[1 - low, k].astype(F32)
        second_ref[64 * k : 64 * k + 64] = edges[low, k].astype(F32)


def send_part(where, count, col, lev, innov, weight, quarters):
    return call(
        send_kernel,
        (sds(64 * HEAD + OBS, 128), sds(64 * HEAD, 128), sds(OBS, 128)),
        ins=[SMEM, SMEM] + [HBM] * 5,
        outs=(VMEM,) * 3,
        scratch=[pltpu.VMEM(a.shape, a.dtype) for a in (col, lev, innov, weight)]
        + [pltpu.VMEM((2, HEAD, 64, 128), BF16), pltpu.SemaphoreType.DMA((6,))],
        vmem=58,
    )(where, count, col, lev, innov, weight, quarters)


def own_kernel(where_ref, alpha_ref, ens_ref, loc_ref, after_ref, inner_ref, edge_ref, x_ref, smat_ref, hmat_ref, first_ref, second_ref):
    @pl.when(pl.program_id(0) == 0)
    def _():
        inner_ref[...] = jnp.zeros_like(inner_ref)
        smat, hmat = matrices(where_ref[6], TILES, where_ref[7] == 0)
        smat_ref[...] = smat
        hmat_ref[...] = hmat

    smat = smat_ref[...]
    loc = loc_ref[...]
    total = [inner_ref[v] for v in range(V)]
    for k in range(GROUP):
        full = lift(nn(smat, alpha_ref[k]), loc)
        edge_ref[k, :64] = full[:64]
        edge_ref[k, 64:] = full[192:]
        lifted = full[64:192].astype(BF16).astype(F32)
        for v in range(V):
            total[v] = total[v] + ens_ref[k, v, 64:192].astype(F32) * lifted
            x_ref[k, v, :64] = ens_ref[k, v, :64]
            x_ref[k, v, 64:] = ens_ref[k, v, 192:]
    for v in range(V):
        inner_ref[v] = total[v]

    @pl.when(pl.program_id(0) >= HEAD // GROUP)
    def _():
        low = where_ref[7] == 1
        for k in range(GROUP):
            rows = [alpha_ref[k, :64].astype(F32), alpha_ref[k, 192:].astype(F32)]
            first_ref[k] = jnp.where(low, rows[0], rows[1])
            second_ref[k] = jnp.where(low, rows[1], rows[0])


def own_part(where, alpha, ensemble, loc, after):
    members = alpha.shape[0]
    whole = lambda *shape: pl.BlockSpec(shape, lambda i: (0,) * len(shape))
    rest = pl.BlockSpec((GROUP, 64, 128), lambda i: (jnp.maximum(i - HEAD // GROUP, 0), 0, 0))
    return call(
        own_kernel,
        (
            sds(V, 128, 128),
            sds(members, 128, 128),
            sds(members, V, 128, 128, dtype=BF16),
            sds(256, 256, dtype=BF16),
            sds(128, 128, dtype=BF16),
            sds(members - HEAD, 64, 128),
            sds(members - HEAD, 64, 128),
        ),
        grid=(members // GROUP,),
        ins=[
            SMEM,
            pl.BlockSpec((GROUP, 256, 128), lambda i: (i, 0, 0)),
            pl.BlockSpec((GROUP, V, 256, 128), lambda i: (i, 0, 0, 0)),
            whole(128, 128),
            whole(OBS, 128),
        ],
        outs=(
            whole(V, 128, 128),
            pl.BlockSpec((GROUP, 128, 128), lambda i: (i, 0, 0)),
            pl.BlockSpec((GROUP, V, 128, 128), lambda i: (i, 0, 0, 0)),
            whole(256, 256),
            whole(128, 128),
            rest,
            rest,
        ),
    )(where, alpha, ensemble, loc, after)


def edge_terms(first_ref, second_ref, own_ref, x_ref, hmat_ref, loc_ref, start, total):
    hmat = hmat_ref[...]
    loc = loc_ref[...]
    for k in range(second_ref.shape[0] // 64):
        rows = slice(64 * k, 64 * k + 64)
        halo = jnp.concatenate([first_ref[rows].astype(BF16), second_ref[rows].astype(BF16)], axis=0)
        lifted = (own_ref[start + k] + lift(nn(hmat, halo), loc)).astype(BF16).astype(F32)
        for v in range(V):
            total[v] = total[v] + x_ref[start + k, v].astype(F32) * lifted
    return total


def head_kernel(first_ref, second_ref, own_ref, x_ref, hmat_ref, loc_ref, after_ref, total_ref):
    zeros = [jnp.zeros((128, 128), F32) for v in range(V)]
    total = edge_terms(first_ref, second_ref, own_ref, x_ref, hmat_ref, loc_ref, 0, zeros)
    for v in range(V):
        total_ref[v] = total[v]


def head_part(first, second, own, x, hmat, loc, after):
    return call(head_kernel, sds(V, 128, 128), ins=[VMEM] * 7, outs=VMEM)(
        first, second, own, x, hmat, loc, after
    )


def edge_kernel(where_ref, first_ref, second_ref, own_ref, x_ref, hmat_ref, loc_ref, inner_ref, head_ref, inc_ref, keep_ref, give_ref):
    total = [head_ref[v] for v in range(V)]
    total = edge_terms(first_ref, second_ref, own_ref, x_ref, hmat_ref, loc_ref, HEAD, total)
    for v in range(V):
        inc_ref[v, :64] = total[v][:64]
        inc_ref[v, 64:192] = inner_ref[v]
        inc_ref[v, 192:] = total[v][64:]
        keep_ref[v] = inc_ref[v, pl.ds(pl.multiple_of(where_ref[8], 32), 32)]
        give_ref[v] = inc_ref[v, pl.ds(pl.multiple_of(where_ref[9], 32), 32)]


def edge_part(where, first, second, own, x, hmat, loc, inner, head):
    return call(
        edge_kernel,
        (sds(V, 256, 128), sds(V, 32, 128), sds(V, 32, 128)),
        ins=[SMEM] + [VMEM] * 8,
        outs=(VMEM,) * 3,
    )(where, first, second, own, x, hmat, loc, inner, head)


def tent(distance):
    return jnp.maximum(1.0 - jnp.abs(distance), 0.0)


def weights_kernel(where_ref, own_ref, here_ref, there_ref, wown_ref, wnear_ref, lev_ref, innov_ref, weight_ref, e_ref, o_ref):
    core_0 = where_ref[10] == 0
    e_ref[...] = jnp.where(core_0, here_ref[...], there_ref[...])
    o_ref[...] = jnp.where(core_0, there_ref[...], here_ref[...])
    even_row = where_ref[2].astype(F32)
    odd_row = where_ref[3].astype(F32)
    odd_there = where_ref[4].astype(F32)
    cell = lax.broadcasted_iota(jnp.int32, (32, SLOTS), 0).astype(F32)

    def line(ref, field, v):
        at = 6 * (V * field + v)
        return jnp.concatenate([ref[at + a : at + a + 1] for a in range(6)], axis=1)

    def columns(code):
        row = jnp.floor(code * (1.0 / 64.0))
        column = code - 64.0 * row
        return row, tent(cell - (column * 0.5 - 0.25))

    for v in range(V):
        row, across = columns(line(own_ref, 0, v))
        middle = row * 0.5 - 0.25
        for r in range(8):
            wown_ref[v, 32 * r : 32 * r + 32] = (tent(r - middle) * across).astype(BF16)
        wown_ref[v, 256:288] = (tent(even_row - middle) * across).astype(BF16)
        wown_ref[v, 288:320] = (tent(odd_row - middle) * odd_there * across).astype(BF16)
        for n, ref in enumerate((e_ref, o_ref)):
            row, across = columns(line(ref, 0, v))
            wnear_ref[n, v, :32] = (0.25 * across).astype(BF16)
            wnear_ref[n, v, 32:] = (0.75 * across).astype(BF16)
    is_odd = where_ref[5]
    for n, ref in enumerate((own_ref, e_ref, o_ref)):
        for v in range(V):
            row = slice(3 * n + v, 3 * n + v + 1)
            lev_ref[row] = line(ref, 1, v)
            innov_ref[row] = line(ref, 2, v)
            weight = line(ref, 3, v)
            if n > 0:
                code = line(ref, 0, v)
                first = is_odd == (0 if n == 1 else 1)
                at_edge = jnp.where(first, code, 1023.0 - code) < 64.0
                there = at_edge & ((n == 1) | (where_ref[4] == 1))
                weight = jnp.where(there, weight, 0.0)
            weight_ref[row] = weight


def weights(where, own, here, there):
    return call(
        weights_kernel,
        (
            sds(V, 320, SLOTS, dtype=BF16),
            sds(2, V, 64, SLOTS, dtype=BF16),
            sds(9, SLOTS),
            sds(9, SLOTS),
            sds(9, SLOTS),
        ),
        ins=[SMEM, VMEM, VMEM, VMEM],
        scratch=[pltpu.VMEM(own.shape, F32), pltpu.VMEM(own.shape, F32)],
    )(where, own, here, there)


def picker(lev_ref):
    level = lax.broadcasted_iota(jnp.int32, (128, SLOTS), 0).astype(F32)

    def pick(cells, weight, row):
        both = jnp.concatenate(halves(cells), axis=1)
        at_all = tn(both, weight)
        at_all = at_all[:128] + at_all[128:]
        hot = level == lev_ref[pl.ds(row, 1), :]
        return jnp.sum(jnp.where(hot, at_all, 0.0), axis=0, keepdims=True)

    return pick


def mine_kernel(where_ref, inc_ref, wown_ref, wnear_ref, lev_ref, out_ref):
    pick = picker(lev_ref)
    for v in range(V):
        out_ref[v : v + 1] = pick(inc_ref[v], wown_ref[v, :256], v)
        for n in range(2):
            cells = inc_ref[v, pl.ds(pl.multiple_of(where_ref[n], 32), 32)]
            row = 3 * n + 3 + v
            out_ref[row : row + 1] = pick(cells, wnear_ref[n, v, :32], row)


def mine_part(where, inc, wown, wnear, lev):
    return call(
        mine_kernel,
        sds(9, SLOTS),
        ins=[SMEM] + [VMEM] * 4,
        outs=VMEM,
    )(where, inc, wown, wnear, lev)


def values_kernel(where_ref, mine_ref, near_ref, wown_ref, wnear_ref, lev_ref, out_ref):
    pick = picker(lev_ref)
    core = where_ref[10]

    def put(row, line):
        for a in range(6):
            out_ref[pl.ds(6 * row + a, 1)] = line[:, 128 * a : 128 * a + 128]

    for v in range(V):
        for n in range(2):
            row = 3 * n + 3 + v
            put(row, mine_ref[row : row + 1])
    for v in range(V):
        halo = pl.ds(pl.multiple_of(256 + 32 * core, 32), 32)
        put(v, mine_ref[v : v + 1] + pick(near_ref[v], wown_ref[v, halo], v))
        row = 3 * core + 3 + v
        put(row, mine_ref[pl.ds(row, 1)] + pick(near_ref[v], wnear_ref[core, v, 32:], row))


def values(where, mine, near, wown, wnear, lev):
    return call(
        values_kernel,
        sds(9 * SLOTS // 128, 128),
        ins=[SMEM] + [VMEM] * 5,
        outs=VMEM,
    )(where, mine, near, wown, wnear, lev)


def adjoint_kernel(where_ref, v0, v1, v2, v3, innov_ref, weight_ref, lev_ref, wown_ref, wnear_ref, x_ref, c_ref, first_ref, second_ref):
    level = lax.broadcasted_iota(jnp.int32, (128, SLOTS), 0).astype(F32)
    value = v0[...] + v1[...] + v2[...] + v3[...]

    def place(weight, row):
        line = jnp.concatenate([value[6 * row + a : 6 * row + a + 1] for a in range(6)], axis=1)
        weighted = weight_ref[row : row + 1] * (line - innov_ref[row : row + 1])
        hot = level == lev_ref[row : row + 1, :]
        spread = jnp.where(hot, weighted, 0.0)
        both = jnp.concatenate(halves(spread), axis=0)
        out = nt(weight, both)
        return out[:, :128] + out[:, 128:]

    adj = []
    for v in range(V):
        c_ref[v] = place(wown_ref[v, :256], v)
        for n in range(2):
            rows = pl.ds(pl.multiple_of(where_ref[n], 32), 32)
            c_ref[v, rows] = c_ref[v, rows] + place(wnear_ref[n, v, :32], 3 * n + 3 + v)
        adj.append(jnp.concatenate([c_ref[v, :64], c_ref[v, 192:]], axis=0))
    first_low = where_ref[7] == 1
    for k in range(first_ref.shape[0]):
        total = x_ref[k, 0].astype(F32) * adj[0]
        for v in range(1, V):
            total = total + x_ref[k, v].astype(F32) * adj[v]
        low, high = total[:64], total[64:]
        first_ref[k] = jnp.where(first_low, low, high)
        second_ref[k] = jnp.where(first_low, high, low)


def adjoint(where, vals, innov, weight, lev, wown, wnear, x):
    members = HEAD
    return call(
        adjoint_kernel,
        (sds(V, 256, 128), sds(members, 64, 128), sds(members, 64, 128)),
        ins=[SMEM] + [VMEM] * 10,
        outs=(VMEM,) * 3,
    )(where, *vals, innov, weight, lev, wown, wnear, x)


def drop(smoothed, loc):
    high, low = halves(smoothed)
    return nn(high, loc) + nn(low, loc)


def back_kernel(where_ref, alpha_ref, ens_ref, c_ref, smat_ref, loc_ref, out_ref, edge_ref, first_ref, second_ref):
    low = where_ref[7] == 1
    smat = smat_ref[...]
    loc = loc_ref[...]
    for k in range(GROUP):
        back = ens_ref[k, 0].astype(F32) * c_ref[0]
        for v in range(1, V):
            back = back + ens_ref[k, v].astype(F32) * c_ref[v]
        first_ref[k] = jnp.where(low, back[:64], back[192:])
        second_ref[k] = jnp.where(low, back[192:], back[:64])
        full = alpha_ref[k].astype(F32) + drop(smooth(smat, back), loc)
        out_ref[k] = full
        edge_ref[k, :64] = full[:64]
        edge_ref[k, 64:] = full[192:]


def back_part(where, alpha, ensemble, c, smat, loc):
    members = alpha.shape[0]
    rest = pl.BlockSpec((GROUP, 64, 128), lambda i: (jnp.maximum(i - HEAD // GROUP, 0), 0, 0))
    return call(
        back_kernel,
        (
            sds(members, 256, 128),
            sds(members, 128, 128),
            sds(members - HEAD, 64, 128),
            sds(members - HEAD, 64, 128),
        ),
        grid=(members // GROUP,),
        ins=[
            SMEM,
            pl.BlockSpec((GROUP, 256, 128), lambda i: (i, 0, 0)),
            pl.BlockSpec((GROUP, V, 256, 128), lambda i: (i, 0, 0, 0)),
            pl.BlockSpec((V, 256, 128), lambda i: (0, 0, 0)),
            pl.BlockSpec((256, 256), lambda i: (0, 0)),
            pl.BlockSpec((128, 128), lambda i: (0, 0)),
        ],
        outs=(
            pl.BlockSpec((GROUP, 256, 128), lambda i: (i, 0, 0)),
            pl.BlockSpec((GROUP, 128, 128), lambda i: (i, 0, 0)),
            rest,
            rest,
        ),
    )(where, alpha, ensemble, c, smat, loc)


def last_kernel(start, first_ref, second_ref, edge_ref, hmat_ref, loc_ref, unused_ref, out_ref, held, sems):
    hmat = hmat_ref[...]
    loc = loc_ref[...]
    copies = []
    for g in range(first_ref.shape[0] // GROUP):
        for k in range(g * GROUP, (g + 1) * GROUP):
            halo = jnp.concatenate([first_ref[k], second_ref[k]], axis=0)
            full = edge_ref[start + k] + drop(smooth(hmat, halo), loc)
            held[k, 0] = full[:64]
            held[k, 1] = full[64:]
        here, there = pl.ds(g * GROUP, GROUP), pl.ds(start + g * GROUP, GROUP)
        for side in range(2):
            copies.append(
                pltpu.make_async_copy(held.at[here, side], out_ref.at[there, 3 * side], sems.at[g, side])
            )
            copies[-1].start()
    for copy in copies:
        copy.wait()


def last_part(start, first, second, edge, hmat, loc, out):
    count = first.shape[0]
    return call(
        functools.partial(last_kernel, start),
        sds(*out.shape),
        ins=[VMEM] * 5 + [ANY],
        outs=ANY,
        scratch=[pltpu.VMEM((count, 2, 64, 128), F32), pltpu.SemaphoreType.DMA((count // GROUP, 2))],
        aliases={5: 0},
    )(first, second, edge, hmat, loc, out)


def stencil(gap):
    gap = jnp.abs(gap)
    return jnp.where(gap == 0, 6.0, jnp.where(gap == 1, 4.0, jnp.where(gap == 2, 1.0, 0.0)))


def matrices(tile, tiles, first_high):
    def across(i, j):
        gap = stencil(i - j)
        return jnp.where((i == j) & ((i == 0) | (i == 31)), 5.0, gap)

    i = lax.broadcasted_iota(jnp.int32, (256, 256), 0)
    j = lax.broadcasted_iota(jnp.int32, (256, 256), 1)
    ri, rj = i // 32, j // 32
    ends = ((ri == 0) & (tile == 0)) | ((ri == 7) & (tile == tiles - 1))
    down = jnp.where((ri == rj) & ends, 5.0, stencil(ri - rj))
    smat = (down * across(i % 32, j % 32) * (1.0 / 256.0)).astype(BF16)
    i = lax.broadcasted_iota(jnp.int32, (128, 128), 0)
    j = lax.broadcasted_iota(jnp.int32, (128, 128), 1)
    ri = i // 32
    ri = jnp.where(ri < 2, ri, ri + 4)
    above = (j < 64) == first_high
    rj = jnp.where(above, 8, -2) + (j // 32) % 2
    there = (above & (tile < tiles - 1)) | (jnp.logical_not(above) & (tile > 0))
    hmat = jnp.where(there, stencil(ri - rj), 0.0) * across(i % 32, j % 32) * (1.0 / 256.0)
    return smat, hmat.astype(BF16)


def swap_first(x):
    return lax.ppermute(x, ("mem", "tile"), FIRST)


def swap_second(x):
    return lax.ppermute(x, ("mem", "tile"), SECOND)


def swap_core(x):
    return lax.ppermute(x, "mem", [(m, m ^ 1) for m in range(MEMS)])


def round_mem(mine):
    size = lax.axis_size("mem")
    return [mine] + [
        lax.ppermute(mine, "mem", [(i, (i + shift) % size) for i in range(size)]) for shift in range(1, size)
    ]


def on_device(alpha, ensemble, loc_vert, obs_col, obs_lev, obs_count, innovation, obs_weight):
    members = alpha.shape[0]
    tile = lax.axis_index("tile")
    tiles = lax.axis_size("tile")
    even = tile % 2 == 0
    core = lax.axis_index("mem") % 2
    first_low = (tile + core) % 2
    where = jnp.stack(
        [
            jnp.where(even, 7 * 32, 0),
            jnp.where(even, 0, 7 * 32),
            jnp.where(even, 8, -1),
            jnp.where(even, -1, 8),
            ((tile > 0) & (tile < tiles - 1)).astype(jnp.int32),
            tile % 2,
            tile,
            first_low,
            7 * 32 * (1 - first_low),
            7 * 32 * first_low,
            core,
        ]
    ).astype(jnp.int32)
    flat = alpha.reshape(members, 256, 128)
    flat_ens = ensemble.reshape(members, V, 256, 128)

    send_first, send_second, own_obs = send_part(
        where, obs_count, obs_col, obs_lev, innovation, obs_weight, alpha.reshape(members, 4, 64, 128)
    )
    first, second = swap_first(send_first), swap_second(send_second)
    inner, own_edge, x, smat, hmat, send_first, send_second = own_part(where, flat, flat_ens, loc_vert, own_obs)
    rest = send_first.reshape(-1, 128), send_second.reshape(-1, 128)
    first_rest, second_rest = swap_first(rest[0]), swap_second(rest[1])
    here_obs = first[64 * HEAD :]
    there_obs = swap_core(here_obs)
    wown, wnear, lev, innov, weight = weights(where, own_obs, here_obs, there_obs)
    head = head_part(first, second, own_edge, x, hmat, loc_vert, lev)
    inc, keep, give = edge_part(where, first_rest, second_rest, own_edge, x, hmat, loc_vert, inner, head)
    near = swap_first(keep + swap_core(give))
    mine = mine_part(where, inc, wown, wnear, lev)
    vals = round_mem(values(where, mine, near, wown, wnear, lev))
    c, back_first, back_second = adjoint(where, vals, innov, weight, lev, wown, wnear, x)
    halo_first, halo_second = swap_first(back_first), swap_second(back_second)
    out, edge, back_first, back_second = back_part(where, flat, flat_ens, c, smat, loc_vert)
    rest_first, rest_second = swap_first(back_first), swap_second(back_second)
    out = last_part(0, halo_first, halo_second, edge, hmat, loc_vert, out.reshape(members, 4, 64, 128))
    out = last_part(HEAD, rest_first, rest_second, edge, hmat, loc_vert, out)
    return out.reshape(members, 8, 32, 128)


def solution(mesh):
    in_specs = (
        P("mem", "tile", None, None),
        P("mem", None, "tile", None, None),
        P(),
        P("tile", None),
        P("tile", None),
        P("tile"),
        P("tile", None),
        P("tile", None),
    )
    out_specs = P("mem", "tile", None, None)
    return jax.shard_map(
        on_device, mesh=mesh, in_specs=in_specs, out_specs=out_specs, check_vma=False
    )
```

```python
import functools

import jax
import jax.numpy as jnp
from jax import lax
from jax.experimental import pallas as pl
from jax.experimental.pallas import tpu as pltpu
from jax.sharding import PartitionSpec as P

V = 3
F32 = jnp.float32
BF16 = jnp.bfloat16
SLOTS = 768
GROUP = 4
HEAD = 12
OBS = 72

TILES = 64
MEMS = 4


def swap_pairs(odd_core):
    pairs = []
    for m in range(MEMS):
        for t in range(TILES):
            beside = ((t - 1) ^ 1) + 1 if m % 2 == odd_core else t ^ 1
            pairs.append((TILES * m + t, TILES * m + beside % TILES))
    return pairs


FIRST = swap_pairs(1)
SECOND = swap_pairs(0)


def nn(a, b):
    return lax.dot_general(a, b, (((1,), (0,)), ((), ())), preferred_element_type=F32)


def nt(a, b):
    return lax.dot_general(a, b, (((1,), (1,)), ((), ())), preferred_element_type=F32)


def tn(a, b):
    return lax.dot_general(a, b, (((0,), (0,)), ((), ())), preferred_element_type=F32)


def halves(x):
    high = x.astype(BF16)
    low = (x - high.astype(F32)).astype(BF16)
    return high, low


def lift(smoothed, loc):
    high, low = halves(smoothed)
    return nt(high, loc) + nt(low, loc)


def call(kernel, out, grid=None, ins=None, outs=None, scratch=(), aliases=None, cost=1000, vmem=16):
    kw = {}
    if grid is not None:
        kw["grid"] = grid
    return pl.pallas_call(
        kernel,
        out_shape=out,
        in_specs=ins,
        out_specs=outs if outs is not None else jax.tree.map(lambda o: VMEM, out),
        scratch_shapes=scratch,
        input_output_aliases=aliases or {},
        compiler_params=pltpu.CompilerParams(vmem_limit_bytes=vmem * 1024 * 1024),
        cost_estimate=pl.CostEstimate(flops=cost, bytes_accessed=cost, transcendentals=0),
        **kw,
    )


def sds(*shape, dtype=F32):
    return jax.ShapeDtypeStruct(shape, dtype)


ANY = pl.BlockSpec(memory_space=pl.ANY)
SMEM = pl.BlockSpec(memory_space=pltpu.SMEM)
VMEM = pl.BlockSpec(memory_space=pltpu.VMEM)
HBM = pl.BlockSpec(memory_space=pltpu.HBM)


def smooth(matrix, field):
    both = jnp.concatenate(halves(field), axis=1)
    out = nn(matrix, both)
    return out[:, :128] + out[:, 128:]


def side_of_first():
    return lax.rem(lax.axis_index("tile") + lax.axis_index("mem"), 2)


def sort_observations(count, col_ref, lev_ref, innov_ref, weight_ref, out_ref):
    slots = col_ref.shape[1]
    live = lax.broadcasted_iota(jnp.int32, (1, slots), 1) < count
    rows = []
    for field in (
        col_ref[...].astype(F32),
        lev_ref[...].astype(F32),
        innov_ref[...],
        jnp.where(live, weight_ref[...], 0.0),
    ):
        field = jnp.concatenate([field, jnp.zeros((1, V * SLOTS - slots), F32)], axis=1)
        rows += [field[:, 384 * a : 384 * a + 384] for a in range(6)]
    rest = jnp.concatenate(rows, axis=0)
    i = lax.broadcasted_iota(jnp.int32, (384, 384), 0)
    j = lax.broadcasted_iota(jnp.int32, (384, 384), 1)
    order = (i == 3 * (j % 128) + j // 128).astype(F32).astype(BF16)
    total = jnp.zeros((24, 384), F32)
    for piece in range(3):
        part = rest.astype(BF16)
        rest = rest - part.astype(F32)
        total = total + nn(part, order)
    for f in range(4):
        for a in range(6):
            for v in range(V):
                row = 6 * (V * f + v) + a
                out_ref[row : row + 1] = total[6 * f + a : 6 * f + a + 1, 128 * v : 128 * v + 128]


def send_kernel(count_ref, *refs):
    obs_in, (quarters_ref, first_ref, second_ref, obs_ref), obs_here, (edges, sems) = refs[:4], refs[4:8], refs[8:12], refs[12:]
    head = pl.ds(0, HEAD)
    copies = [pltpu.make_async_copy(quarters_ref.at[head, 3 * n], edges.at[n], sems.at[n]) for n in range(2)]
    fetches = [pltpu.make_async_copy(obs_in[n], obs_here[n], sems.at[2 + n]) for n in range(4)]
    for copy in fetches + copies:
        copy.start()
    for copy in fetches:
        copy.wait()
    sort_observations(count_ref[0], *obs_here, obs_ref)
    first_ref[64 * HEAD :] = obs_ref[...]
    for copy in copies:
        copy.wait()
    low = side_of_first()
    for k in range(HEAD):
        first_ref[64 * k : 64 * k + 64] = edges[1 - low, k].astype(F32)
        second_ref[64 * k : 64 * k + 64] = edges[low, k].astype(F32)


def send_part(count, col, lev, innov, weight, quarters):
    return call(
        send_kernel,
        (sds(64 * HEAD + OBS, 128), sds(64 * HEAD, 128), sds(OBS, 128)),
        ins=[SMEM] + [HBM] * 5,
        outs=(VMEM,) * 3,
        scratch=[pltpu.VMEM(a.shape, a.dtype) for a in (col, lev, innov, weight)]
        + [pltpu.VMEM((2, HEAD, 64, 128), BF16), pltpu.SemaphoreType.DMA((6,))],
        vmem=56,
    )(count, col, lev, innov, weight, quarters)


def own_kernel(where_ref, alpha_ref, ens_ref, loc_ref, after_ref, inner_ref, edge_ref, x_ref, smat_ref, hmat_ref, first_ref, second_ref):
    @pl.when(pl.program_id(0) == 0)
    def _():
        inner_ref[...] = jnp.zeros_like(inner_ref)
        smat, hmat = matrices(where_ref[6], TILES, where_ref[7] == 0)
        smat_ref[...] = smat
        hmat_ref[...] = hmat

    smat = smat_ref[...]
    loc = loc_ref[...]
    total = [inner_ref[v] for v in range(V)]
    for k in range(GROUP):
        full = lift(nn(smat, alpha_ref[k]), loc)
        edge_ref[k, :64] = full[:64]
        edge_ref[k, 64:] = full[192:]
        lifted = full[64:192].astype(BF16).astype(F32)
        for v in range(V):
            total[v] = total[v] + ens_ref[k, v, 64:192].astype(F32) * lifted
            x_ref[k, v, :64] = ens_ref[k, v, :64]
            x_ref[k, v, 64:] = ens_ref[k, v, 192:]
    for v in range(V):
        inner_ref[v] = total[v]

    @pl.when(pl.program_id(0) >= HEAD // GROUP)
    def _():
        low = where_ref[7] == 1
        for k in range(GROUP):
            rows = [alpha_ref[k, :64].astype(F32), alpha_ref[k, 192:].astype(F32)]
            first_ref[k] = jnp.where(low, rows[0], rows[1])
            second_ref[k] = jnp.where(low, rows[1], rows[0])


def own_part(where, alpha, ensemble, loc, after):
    members = alpha.shape[0]
    whole = lambda *shape: pl.BlockSpec(shape, lambda i: (0,) * len(shape))
    rest = pl.BlockSpec((GROUP, 64, 128), lambda i: (jnp.maximum(i - HEAD // GROUP, 0), 0, 0))
    return call(
        own_kernel,
        (
            sds(V, 128, 128),
            sds(members, 128, 128),
            sds(members, V, 128, 128, dtype=BF16),
            sds(256, 256, dtype=BF16),
            sds(128, 128, dtype=BF16),
            sds(members - HEAD, 64, 128),
            sds(members - HEAD, 64, 128),
        ),
        grid=(members // GROUP,),
        ins=[
            SMEM,
            pl.BlockSpec((GROUP, 256, 128), lambda i: (i, 0, 0)),
            pl.BlockSpec((GROUP, V, 256, 128), lambda i: (i, 0, 0, 0)),
            whole(128, 128),
            whole(OBS, 128),
        ],
        outs=(
            whole(V, 128, 128),
            pl.BlockSpec((GROUP, 128, 128), lambda i: (i, 0, 0)),
            pl.BlockSpec((GROUP, V, 128, 128), lambda i: (i, 0, 0, 0)),
            whole(256, 256),
            whole(128, 128),
            rest,
            rest,
        ),
    )(where, alpha, ensemble, loc, after)


def edge_terms(first_ref, second_ref, own_ref, x_ref, hmat_ref, loc_ref, start, total):
    hmat = hmat_ref[...]
    loc = loc_ref[...]
    for k in range(second_ref.shape[0] // 64):
        rows = slice(64 * k, 64 * k + 64)
        halo = jnp.concatenate([first_ref[rows].astype(BF16), second_ref[rows].astype(BF16)], axis=0)
        lifted = (own_ref[start + k] + lift(nn(hmat, halo), loc)).astype(BF16).astype(F32)
        for v in range(V):
            total[v] = total[v] + x_ref[start + k, v].astype(F32) * lifted
    return total


def head_kernel(first_ref, second_ref, own_ref, x_ref, hmat_ref, loc_ref, after_ref, total_ref):
    zeros = [jnp.zeros((128, 128), F32) for v in range(V)]
    total = edge_terms(first_ref, second_ref, own_ref, x_ref, hmat_ref, loc_ref, 0, zeros)
    for v in range(V):
        total_ref[v] = total[v]


def head_part(first, second, own, x, hmat, loc, after):
    return call(head_kernel, sds(V, 128, 128), ins=[VMEM] * 7, outs=VMEM)(
        first, second, own, x, hmat, loc, after
    )


def edge_kernel(where_ref, first_ref, second_ref, own_ref, x_ref, hmat_ref, loc_ref, inner_ref, head_ref, inc_ref, keep_ref, give_ref):
    total = [head_ref[v] for v in range(V)]
    total = edge_terms(first_ref, second_ref, own_ref, x_ref, hmat_ref, loc_ref, HEAD, total)
    for v in range(V):
        inc_ref[v, :64] = total[v][:64]
        inc_ref[v, 64:192] = inner_ref[v]
        inc_ref[v, 192:] = total[v][64:]
        keep_ref[v] = inc_ref[v, pl.ds(pl.multiple_of(where_ref[8], 32), 32)]
        give_ref[v] = inc_ref[v, pl.ds(pl.multiple_of(where_ref[9], 32), 32)]


def edge_part(where, first, second, own, x, hmat, loc, inner, head):
    return call(
        edge_kernel,
        (sds(V, 256, 128), sds(V, 32, 128), sds(V, 32, 128)),
        ins=[SMEM] + [VMEM] * 8,
        outs=(VMEM,) * 3,
    )(where, first, second, own, x, hmat, loc, inner, head)


def tent(distance):
    return jnp.maximum(1.0 - jnp.abs(distance), 0.0)


def weights_kernel(where_ref, own_ref, here_ref, there_ref, wown_ref, wnear_ref, lev_ref, innov_ref, weight_ref, e_ref, o_ref):
    core_0 = where_ref[10] == 0
    e_ref[...] = jnp.where(core_0, here_ref[...], there_ref[...])
    o_ref[...] = jnp.where(core_0, there_ref[...], here_ref[...])
    even_row = where_ref[2].astype(F32)
    odd_row = where_ref[3].astype(F32)
    odd_there = where_ref[4].astype(F32)
    cell = lax.broadcasted_iota(jnp.int32, (32, SLOTS), 0).astype(F32)

    def line(ref, field, v):
        at = 6 * (V * field + v)
        return jnp.concatenate([ref[at + a : at + a + 1] for a in range(6)], axis=1)

    def columns(code):
        row = jnp.floor(code * (1.0 / 64.0))
        column = code - 64.0 * row
        return row, tent(cell - (column * 0.5 - 0.25))

    for v in range(V):
        row, across = columns(line(own_ref, 0, v))
        middle = row * 0.5 - 0.25
        for r in range(8):
            wown_ref[v, 32 * r : 32 * r + 32] = (tent(r - middle) * across).astype(BF16)
        wown_ref[v, 256:288] = (tent(even_row - middle) * across).astype(BF16)
        wown_ref[v, 288:320] = (tent(odd_row - middle) * odd_there * across).astype(BF16)
        for n, ref in enumerate((e_ref, o_ref)):
            row, across = columns(line(ref, 0, v))
            wnear_ref[n, v, :32] = (0.25 * across).astype(BF16)
            wnear_ref[n, v, 32:] = (0.75 * across).astype(BF16)
    is_odd = where_ref[5]
    for n, ref in enumerate((own_ref, e_ref, o_ref)):
        for v in range(V):
            row = slice(3 * n + v, 3 * n + v + 1)
            lev_ref[row] = line(ref, 1, v)
            innov_ref[row] = line(ref, 2, v)
            weight = line(ref, 3, v)
            if n > 0:
                code = line(ref, 0, v)
                first = is_odd == (0 if n == 1 else 1)
                at_edge = jnp.where(first, code, 1023.0 - code) < 64.0
                there = at_edge & ((n == 1) | (where_ref[4] == 1))
                weight = jnp.where(there, weight, 0.0)
            weight_ref[row] = weight


def weights(where, own, here, there):
    return call(
        weights_kernel,
        (
            sds(V, 320, SLOTS, dtype=BF16),
            sds(2, V, 64, SLOTS, dtype=BF16),
            sds(9, SLOTS),
            sds(9, SLOTS),
            sds(9, SLOTS),
        ),
        ins=[SMEM, VMEM, VMEM, VMEM],
        scratch=[pltpu.VMEM(own.shape, F32), pltpu.VMEM(own.shape, F32)],
    )(where, own, here, there)


def picker(lev_ref):
    level = lax.broadcasted_iota(jnp.int32, (128, SLOTS), 0).astype(F32)

    def pick(cells, weight, row):
        both = jnp.concatenate(halves(cells), axis=1)
        at_all = tn(both, weight)
        at_all = at_all[:128] + at_all[128:]
        hot = level == lev_ref[pl.ds(row, 1), :]
        return jnp.sum(jnp.where(hot, at_all, 0.0), axis=0, keepdims=True)

    return pick


def mine_kernel(where_ref, inc_ref, wown_ref, wnear_ref, lev_ref, out_ref):
    pick = picker(lev_ref)
    for v in range(V):
        out_ref[v : v + 1] = pick(inc_ref[v], wown_ref[v, :256], v)
        for n in range(2):
            cells = inc_ref[v, pl.ds(pl.multiple_of(where_ref[n], 32), 32)]
            row = 3 * n + 3 + v
            out_ref[row : row + 1] = pick(cells, wnear_ref[n, v, :32], row)


def mine_part(where, inc, wown, wnear, lev):
    return call(
        mine_kernel,
        sds(9, SLOTS),
        ins=[SMEM] + [VMEM] * 4,
        outs=VMEM,
    )(where, inc, wown, wnear, lev)


def values_kernel(where_ref, mine_ref, near_ref, wown_ref, wnear_ref, lev_ref, out_ref):
    pick = picker(lev_ref)
    core = where_ref[10]

    def put(row, line):
        for a in range(6):
            out_ref[pl.ds(6 * row + a, 1)] = line[:, 128 * a : 128 * a + 128]

    for v in range(V):
        for n in range(2):
            row = 3 * n + 3 + v
            put(row, mine_ref[row : row + 1])
    for v in range(V):
        halo = pl.ds(pl.multiple_of(256 + 32 * core, 32), 32)
        put(v, mine_ref[v : v + 1] + pick(near_ref[v], wown_ref[v, halo], v))
        row = 3 * core + 3 + v
        put(row, mine_ref[pl.ds(row, 1)] + pick(near_ref[v], wnear_ref[core, v, 32:], row))


def values(where, mine, near, wown, wnear, lev):
    return call(
        values_kernel,
        sds(9 * SLOTS // 128, 128),
        ins=[SMEM] + [VMEM] * 5,
        outs=VMEM,
    )(where, mine, near, wown, wnear, lev)


def adjoint_kernel(where_ref, v0, v1, innov_ref, weight_ref, lev_ref, wown_ref, wnear_ref, x_ref, c_ref, first_ref, second_ref):
    level = lax.broadcasted_iota(jnp.int32, (128, SLOTS), 0).astype(F32)
    value = v0[...] + v1[...]

    def place(weight, row):
        line = jnp.concatenate([value[6 * row + a : 6 * row + a + 1] for a in range(6)], axis=1)
        weighted = weight_ref[row : row + 1] * (line - innov_ref[row : row + 1])
        hot = level == lev_ref[row : row + 1, :]
        spread = jnp.where(hot, weighted, 0.0)
        both = jnp.concatenate(halves(spread), axis=0)
        out = nt(weight, both)
        return out[:, :128] + out[:, 128:]

    adj = []
    for v in range(V):
        c_ref[v] = place(wown_ref[v, :256], v)
        for n in range(2):
            rows = pl.ds(pl.multiple_of(where_ref[n], 32), 32)
            c_ref[v, rows] = c_ref[v, rows] + place(wnear_ref[n, v, :32], 3 * n + 3 + v)
        adj.append(jnp.concatenate([c_ref[v, :64], c_ref[v, 192:]], axis=0))
    first_low = where_ref[7] == 1
    for k in range(first_ref.shape[0]):
        total = x_ref[k, 0].astype(F32) * adj[0]
        for v in range(1, V):
            total = total + x_ref[k, v].astype(F32) * adj[v]
        low, high = total[:64], total[64:]
        first_ref[k] = jnp.where(first_low, low, high)
        second_ref[k] = jnp.where(first_low, high, low)


def adjoint(where, vals, innov, weight, lev, wown, wnear, x):
    members = HEAD
    return call(
        adjoint_kernel,
        (sds(V, 256, 128), sds(members, 64, 128), sds(members, 64, 128)),
        ins=[SMEM] + [VMEM] * 8,
        outs=(VMEM,) * 3,
    )(where, *vals, innov, weight, lev, wown, wnear, x)


def drop(smoothed, loc):
    high, low = halves(smoothed)
    return nn(high, loc) + nn(low, loc)


def back_kernel(where_ref, alpha_ref, ens_ref, c_ref, smat_ref, loc_ref, out_ref, edge_ref, first_ref, second_ref):
    low = where_ref[7] == 1
    smat = smat_ref[...]
    loc = loc_ref[...]
    for k in range(GROUP):
        back = ens_ref[k, 0].astype(F32) * c_ref[0]
        for v in range(1, V):
            back = back + ens_ref[k, v].astype(F32) * c_ref[v]
        first_ref[k] = jnp.where(low, back[:64], back[192:])
        second_ref[k] = jnp.where(low, back[192:], back[:64])
        full = alpha_ref[k].astype(F32) + drop(smooth(smat, back), loc)
        out_ref[k] = full
        edge_ref[k, :64] = full[:64]
        edge_ref[k, 64:] = full[192:]


def back_part(where, alpha, ensemble, c, smat, loc):
    members = alpha.shape[0]
    rest = pl.BlockSpec((GROUP, 64, 128), lambda i: (jnp.maximum(i - HEAD // GROUP, 0), 0, 0))
    return call(
        back_kernel,
        (
            sds(members, 256, 128),
            sds(members, 128, 128),
            sds(members - HEAD, 64, 128),
            sds(members - HEAD, 64, 128),
        ),
        grid=(members // GROUP,),
        ins=[
            SMEM,
            pl.BlockSpec((GROUP, 256, 128), lambda i: (i, 0, 0)),
            pl.BlockSpec((GROUP, V, 256, 128), lambda i: (i, 0, 0, 0)),
            pl.BlockSpec((V, 256, 128), lambda i: (0, 0, 0)),
            pl.BlockSpec((256, 256), lambda i: (0, 0)),
            pl.BlockSpec((128, 128), lambda i: (0, 0)),
        ],
        outs=(
            pl.BlockSpec((GROUP, 256, 128), lambda i: (i, 0, 0)),
            pl.BlockSpec((GROUP, 128, 128), lambda i: (i, 0, 0)),
            rest,
            rest,
        ),
    )(where, alpha, ensemble, c, smat, loc)


def last_kernel(start, first_ref, second_ref, edge_ref, hmat_ref, loc_ref, unused_ref, out_ref, held, sems):
    hmat = hmat_ref[...]
    loc = loc_ref[...]
    copies = []
    for g in range(first_ref.shape[0] // GROUP):
        for k in range(g * GROUP, (g + 1) * GROUP):
            halo = jnp.concatenate([first_ref[k], second_ref[k]], axis=0)
            full = edge_ref[start + k] + drop(smooth(hmat, halo), loc)
            held[k, 0] = full[:64]
            held[k, 1] = full[64:]
        here, there = pl.ds(g * GROUP, GROUP), pl.ds(start + g * GROUP, GROUP)
        for side in range(2):
            copies.append(
                pltpu.make_async_copy(held.at[here, side], out_ref.at[there, 3 * side], sems.at[g, side])
            )
            copies[-1].start()
    for copy in copies:
        copy.wait()


def last_part(start, first, second, edge, hmat, loc, out):
    count = first.shape[0]
    return call(
        functools.partial(last_kernel, start),
        sds(*out.shape),
        ins=[VMEM] * 5 + [ANY],
        outs=ANY,
        scratch=[pltpu.VMEM((count, 2, 64, 128), F32), pltpu.SemaphoreType.DMA((count // GROUP, 2))],
        aliases={5: 0},
    )(first, second, edge, hmat, loc, out)


def stencil(gap):
    gap = jnp.abs(gap)
    return jnp.where(gap == 0, 6.0, jnp.where(gap == 1, 4.0, jnp.where(gap == 2, 1.0, 0.0)))


def matrices(tile, tiles, first_high):
    def across(i, j):
        gap = stencil(i - j)
        return jnp.where((i == j) & ((i == 0) | (i == 31)), 5.0, gap)

    i = lax.broadcasted_iota(jnp.int32, (256, 256), 0)
    j = lax.broadcasted_iota(jnp.int32, (256, 256), 1)
    ri, rj = i // 32, j // 32
    ends = ((ri == 0) & (tile == 0)) | ((ri == 7) & (tile == tiles - 1))
    down = jnp.where((ri == rj) & ends, 5.0, stencil(ri - rj))
    smat = (down * across(i % 32, j % 32) * (1.0 / 256.0)).astype(BF16)
    i = lax.broadcasted_iota(jnp.int32, (128, 128), 0)
    j = lax.broadcasted_iota(jnp.int32, (128, 128), 1)
    ri = i // 32
    ri = jnp.where(ri < 2, ri, ri + 4)
    above = (j < 64) == first_high
    rj = jnp.where(above, 8, -2) + (j // 32) % 2
    there = (above & (tile < tiles - 1)) | (jnp.logical_not(above) & (tile > 0))
    hmat = jnp.where(there, stencil(ri - rj), 0.0) * across(i % 32, j % 32) * (1.0 / 256.0)
    return smat, hmat.astype(BF16)


def swap_first(x):
    return lax.ppermute(x, ("mem", "tile"), FIRST)


def swap_second(x):
    return lax.ppermute(x, ("mem", "tile"), SECOND)


def swap_core(x):
    return lax.ppermute(x, "mem", [(m, m ^ 1) for m in range(MEMS)])


def swap_chip(x):
    return lax.ppermute(x, "mem", [(m, m ^ 2) for m in range(MEMS)])


def on_device(alpha, ensemble, loc_vert, obs_col, obs_lev, obs_count, innovation, obs_weight):
    members = alpha.shape[0]
    tile = lax.axis_index("tile")
    tiles = lax.axis_size("tile")
    even = tile % 2 == 0
    core = lax.axis_index("mem") % 2
    first_low = side_of_first()
    where = jnp.stack(
        [
            jnp.where(even, 7 * 32, 0),
            jnp.where(even, 0, 7 * 32),
            jnp.where(even, 8, -1),
            jnp.where(even, -1, 8),
            ((tile > 0) & (tile < tiles - 1)).astype(jnp.int32),
            tile % 2,
            tile,
            first_low,
            7 * 32 * (1 - first_low),
            7 * 32 * first_low,
            core,
        ]
    ).astype(jnp.int32)
    flat = alpha.reshape(members, 256, 128)
    flat_ens = ensemble.reshape(members, V, 256, 128)

    send_first, send_second, own_obs = send_part(
        obs_count, obs_col, obs_lev, innovation, obs_weight, alpha.reshape(members, 4, 64, 128)
    )
    first, second = swap_first(send_first), swap_second(send_second)
    inner, own_edge, x, smat, hmat, send_first, send_second = own_part(where, flat, flat_ens, loc_vert, own_obs)
    rest = send_first.reshape(-1, 128), send_second.reshape(-1, 128)
    first_rest, second_rest = swap_first(rest[0]), swap_second(rest[1])
    here_obs = first[64 * HEAD :]
    there_obs = swap_core(here_obs)
    wown, wnear, lev, innov, weight = weights(where, own_obs, here_obs, there_obs)
    head = head_part(first, second, own_edge, x, hmat, loc_vert, lev)
    inc, keep, give = edge_part(where, first_rest, second_rest, own_edge, x, hmat, loc_vert, inner, head)
    near = swap_first(keep + swap_core(give))
    mine = mine_part(where, inc, wown, wnear, lev)
    vals = values(where, mine, near, wown, wnear, lev)
    vals = vals + swap_core(vals)
    vals = vals, swap_chip(vals)
    c, back_first, back_second = adjoint(where, vals, innov, weight, lev, wown, wnear, x)
    halo_first, halo_second = swap_first(back_first), swap_second(back_second)
    out, edge, back_first, back_second = back_part(where, flat, flat_ens, c, smat, loc_vert)
    rest_first, rest_second = swap_first(back_first), swap_second(back_second)
    out = last_part(0, halo_first, halo_second, edge, hmat, loc_vert, out.reshape(members, 4, 64, 128))
    out = last_part(HEAD, rest_first, rest_second, edge, hmat, loc_vert, out)
    return out.reshape(members, 8, 32, 128)


def solution(mesh):
    in_specs = (
        P("mem", "tile", None, None),
        P("mem", None, "tile", None, None),
        P(),
        P("tile", None),
        P("tile", None),
        P("tile"),
        P("tile", None),
        P("tile", None),
    )
    out_specs = P("mem", "tile", None, None)
    return jax.shard_map(
        on_device, mesh=mesh, in_specs=in_specs, out_specs=out_specs, check_vma=False
    )
```

```python
import functools

import jax
import jax.numpy as jnp
from jax import lax
from jax.experimental import pallas as pl
from jax.experimental.pallas import tpu as pltpu
from jax.sharding import PartitionSpec as P

V = 3
F32 = jnp.float32
BF16 = jnp.bfloat16
SLOTS = 768
GROUP = 4
HEAD = 12
OBS = 72

TILES = 64
MEMS = 4


def partners(odd, spare):
    pairs = []
    for m in range(MEMS):
        for t in range(TILES):
            beside = ((t - 1) ^ 1) + 1 if odd(m) else t ^ 1
            there = (m, beside) if 0 <= beside < TILES else (m ^ spare, t)
            pairs.append((TILES * m + t, TILES * there[0] + there[1]))
    return pairs


FIRST = partners(lambda m: True, 1)
SECOND = partners(lambda m: False, 1)
NEAR = partners(lambda m: m % 2 == 1, 2)


def nn(a, b):
    return lax.dot_general(a, b, (((1,), (0,)), ((), ())), preferred_element_type=F32)


def nt(a, b):
    return lax.dot_general(a, b, (((1,), (1,)), ((), ())), preferred_element_type=F32)


def tn(a, b):
    return lax.dot_general(a, b, (((0,), (0,)), ((), ())), preferred_element_type=F32)


def halves(x):
    high = x.astype(BF16)
    low = (x - high.astype(F32)).astype(BF16)
    return high, low


def lift(smoothed, loc):
    high, low = halves(smoothed)
    return nt(high, loc) + nt(low, loc)


def call(kernel, out, grid=None, ins=None, outs=None, scratch=(), aliases=None, cost=1000, vmem=16):
    kw = {}
    if grid is not None:
        kw["grid"] = grid
    return pl.pallas_call(
        kernel,
        out_shape=out,
        in_specs=ins,
        out_specs=outs if outs is not None else jax.tree.map(lambda o: VMEM, out),
        scratch_shapes=scratch,
        input_output_aliases=aliases or {},
        compiler_params=pltpu.CompilerParams(vmem_limit_bytes=vmem * 1024 * 1024),
        cost_estimate=pl.CostEstimate(flops=cost, bytes_accessed=cost, transcendentals=0),
        **kw,
    )


def sds(*shape, dtype=F32):
    return jax.ShapeDtypeStruct(shape, dtype)


ANY = pl.BlockSpec(memory_space=pl.ANY)
SMEM = pl.BlockSpec(memory_space=pltpu.SMEM)
VMEM = pl.BlockSpec(memory_space=pltpu.VMEM)
HBM = pl.BlockSpec(memory_space=pltpu.HBM)


def smooth(matrix, field):
    both = jnp.concatenate(halves(field), axis=1)
    out = nn(matrix, both)
    return out[:, :128] + out[:, 128:]


def side_of_first():
    return lax.rem(lax.axis_index("tile") + 1, 2)


def sort_observations(count, col_ref, lev_ref, innov_ref, weight_ref, out_ref):
    slots = col_ref.shape[1]
    live = lax.broadcasted_iota(jnp.int32, (1, slots), 1) < count
    rows = []
    for field in (
        col_ref[...].astype(F32),
        lev_ref[...].astype(F32),
        innov_ref[...],
        jnp.where(live, weight_ref[...], 0.0),
    ):
        field = jnp.concatenate([field, jnp.zeros((1, V * SLOTS - slots), F32)], axis=1)
        rows += [field[:, 384 * a : 384 * a + 384] for a in range(6)]
    rest = jnp.concatenate(rows, axis=0)
    i = lax.broadcasted_iota(jnp.int32, (384, 384), 0)
    j = lax.broadcasted_iota(jnp.int32, (384, 384), 1)
    order = (i == 3 * (j % 128) + j // 128).astype(F32).astype(BF16)
    total = jnp.zeros((24, 384), F32)
    for piece in range(3):
        part = rest.astype(BF16)
        rest = rest - part.astype(F32)
        total = total + nn(part, order)
    for f in range(4):
        for a in range(6):
            for v in range(V):
                row = 6 * (V * f + v) + a
                out_ref[row : row + 1] = total[6 * f + a : 6 * f + a + 1, 128 * v : 128 * v + 128]


def send_kernel(count_ref, *refs):
    obs_in, (quarters_ref, first_ref, second_ref, obs_ref), obs_here, (edges, sems) = refs[:4], refs[4:8], refs[8:12], refs[12:]
    head = pl.ds(0, HEAD)
    copies = [pltpu.make_async_copy(quarters_ref.at[head, 3 * n], edges.at[n], sems.at[n]) for n in range(2)]
    fetches = [pltpu.make_async_copy(obs_in[n], obs_here[n], sems.at[2 + n]) for n in range(4)]
    for copy in fetches + copies:
        copy.start()
    for copy in fetches:
        copy.wait()
    sort_observations(count_ref[0], *obs_here, obs_ref)
    first_ref[64 * HEAD :] = obs_ref[...]
    second_ref[64 * HEAD :] = obs_ref[...]
    for copy in copies:
        copy.wait()
    low = side_of_first()
    for k in range(HEAD):
        first_ref[64 * k : 64 * k + 64] = edges[1 - low, k].astype(F32)
        second_ref[64 * k : 64 * k + 64] = edges[low, k].astype(F32)


def send_part(count, col, lev, innov, weight, quarters):
    return call(
        send_kernel,
        (sds(64 * HEAD + OBS, 128), sds(64 * HEAD + OBS, 128), sds(OBS, 128)),
        ins=[SMEM] + [HBM] * 5,
        outs=(VMEM,) * 3,
        scratch=[pltpu.VMEM(a.shape, a.dtype) for a in (col, lev, innov, weight)]
        + [pltpu.VMEM((2, HEAD, 64, 128), BF16), pltpu.SemaphoreType.DMA((6,))],
        vmem=56,
    )(count, col, lev, innov, weight, quarters)


def own_kernel(where_ref, alpha_ref, ens_ref, loc_ref, after_ref, inner_ref, edge_ref, x_ref, smat_ref, hmat_ref, first_ref, second_ref):
    @pl.when(pl.program_id(0) == 0)
    def _():
        inner_ref[...] = jnp.zeros_like(inner_ref)
        smat, hmat = matrices(where_ref[6], TILES, where_ref[7] == 0)
        smat_ref[...] = smat
        hmat_ref[...] = hmat

    smat = smat_ref[...]
    loc = loc_ref[...]
    total = [inner_ref[v] for v in range(V)]
    for k in range(GROUP):
        full = lift(nn(smat, alpha_ref[k]), loc)
        edge_ref[k, :64] = full[:64]
        edge_ref[k, 64:] = full[192:]
        lifted = full[64:192].astype(BF16).astype(F32)
        for v in range(V):
            total[v] = total[v] + ens_ref[k, v, 64:192].astype(F32) * lifted
            x_ref[k, v, :64] = ens_ref[k, v, :64]
            x_ref[k, v, 64:] = ens_ref[k, v, 192:]
    for v in range(V):
        inner_ref[v] = total[v]

    @pl.when(pl.program_id(0) >= HEAD // GROUP)
    def _():
        low = where_ref[7] == 1
        for k in range(GROUP):
            rows = [alpha_ref[k, :64].astype(F32), alpha_ref[k, 192:].astype(F32)]
            first_ref[k] = jnp.where(low, rows[0], rows[1])
            second_ref[k] = jnp.where(low, rows[1], rows[0])


def own_part(where, alpha, ensemble, loc, after):
    members = alpha.shape[0]
    whole = lambda *shape: pl.BlockSpec(shape, lambda i: (0,) * len(shape))
    rest = pl.BlockSpec((GROUP, 64, 128), lambda i: (jnp.maximum(i - HEAD // GROUP, 0), 0, 0))
    return call(
        own_kernel,
        (
            sds(V, 128, 128),
            sds(members, 128, 128),
            sds(members, V, 128, 128, dtype=BF16),
            sds(256, 256, dtype=BF16),
            sds(128, 128, dtype=BF16),
            sds(members - HEAD, 64, 128),
            sds(members - HEAD, 64, 128),
        ),
        grid=(members // GROUP,),
        ins=[
            SMEM,
            pl.BlockSpec((GROUP, 256, 128), lambda i: (i, 0, 0)),
            pl.BlockSpec((GROUP, V, 256, 128), lambda i: (i, 0, 0, 0)),
            whole(128, 128),
            whole(OBS, 128),
        ],
        outs=(
            whole(V, 128, 128),
            pl.BlockSpec((GROUP, 128, 128), lambda i: (i, 0, 0)),
            pl.BlockSpec((GROUP, V, 128, 128), lambda i: (i, 0, 0, 0)),
            whole(256, 256),
            whole(128, 128),
            rest,
            rest,
        ),
    )(where, alpha, ensemble, loc, after)


def edge_terms(first_ref, second_ref, own_ref, x_ref, hmat_ref, loc_ref, start, count, total):
    hmat = hmat_ref[...]
    loc = loc_ref[...]
    for k in range(count):
        rows = slice(64 * k, 64 * k + 64)
        halo = jnp.concatenate([first_ref[rows].astype(BF16), second_ref[rows].astype(BF16)], axis=0)
        lifted = (own_ref[start + k] + lift(nn(hmat, halo), loc)).astype(BF16).astype(F32)
        for v in range(V):
            total[v] = total[v] + x_ref[start + k, v].astype(F32) * lifted
    return total


def head_kernel(first_ref, second_ref, own_ref, x_ref, hmat_ref, loc_ref, after_ref, total_ref):
    zeros = [jnp.zeros((128, 128), F32) for v in range(V)]
    total = edge_terms(first_ref, second_ref, own_ref, x_ref, hmat_ref, loc_ref, 0, HEAD, zeros)
    for v in range(V):
        total_ref[v] = total[v]


def head_part(first, second, own, x, hmat, loc, after):
    return call(head_kernel, sds(V, 128, 128), ins=[VMEM] * 7, outs=VMEM)(
        first, second, own, x, hmat, loc, after
    )


def edge_kernel(where_ref, first_ref, second_ref, own_ref, x_ref, hmat_ref, loc_ref, inner_ref, head_ref, inc_ref, keep_ref, give_ref):
    total = [head_ref[v] for v in range(V)]
    total = edge_terms(first_ref, second_ref, own_ref, x_ref, hmat_ref, loc_ref, HEAD, own_ref.shape[0] - HEAD, total)
    for v in range(V):
        inc_ref[v, :64] = total[v][:64]
        inc_ref[v, 64:192] = inner_ref[v]
        inc_ref[v, 192:] = total[v][64:]
        keep_ref[v] = inc_ref[v, pl.ds(pl.multiple_of(where_ref[8], 32), 32)]
        give_ref[v] = inc_ref[v, pl.ds(pl.multiple_of(where_ref[9], 32), 32)]


def edge_part(where, first, second, own, x, hmat, loc, inner, head):
    return call(
        edge_kernel,
        (sds(V, 256, 128), sds(V, 32, 128), sds(V, 32, 128)),
        ins=[SMEM] + [VMEM] * 8,
        outs=(VMEM,) * 3,
    )(where, first, second, own, x, hmat, loc, inner, head)


def tent(distance):
    return jnp.maximum(1.0 - jnp.abs(distance), 0.0)


def weights_kernel(where_ref, own_ref, o_ref, e_ref, wown_ref, wnear_ref, lev_ref, innov_ref, weight_ref):
    even_row = where_ref[2].astype(F32)
    odd_row = where_ref[3].astype(F32)
    odd_there = where_ref[4].astype(F32)
    cell = lax.broadcasted_iota(jnp.int32, (32, SLOTS), 0).astype(F32)

    def line(ref, field, v):
        at = ref.shape[0] - OBS + 6 * (V * field + v)
        return jnp.concatenate([ref[at + a : at + a + 1] for a in range(6)], axis=1)

    def columns(code):
        row = jnp.floor(code * (1.0 / 64.0))
        column = code - 64.0 * row
        return row, tent(cell - (column * 0.5 - 0.25))

    for v in range(V):
        row, across = columns(line(own_ref, 0, v))
        middle = row * 0.5 - 0.25
        for r in range(8):
            wown_ref[v, 32 * r : 32 * r + 32] = (tent(r - middle) * across).astype(BF16)
        wown_ref[v, 256:288] = (tent(even_row - middle) * across).astype(BF16)
        wown_ref[v, 288:320] = (tent(odd_row - middle) * odd_there * across).astype(BF16)
        for n, ref in enumerate((e_ref, o_ref)):
            row, across = columns(line(ref, 0, v))
            wnear_ref[n, v, :32] = (0.25 * across).astype(BF16)
            wnear_ref[n, v, 32:] = (0.75 * across).astype(BF16)
    is_odd = where_ref[5]
    for n, ref in enumerate((own_ref, e_ref, o_ref)):
        for v in range(V):
            row = slice(3 * n + v, 3 * n + v + 1)
            lev_ref[row] = line(ref, 1, v)
            innov_ref[row] = line(ref, 2, v)
            weight = line(ref, 3, v)
            if n > 0:
                code = line(ref, 0, v)
                first = is_odd == (0 if n == 1 else 1)
                at_edge = jnp.where(first, code, 1023.0 - code) < 64.0
                there = at_edge & ((n == 1) | (where_ref[4] == 1))
                weight = jnp.where(there, weight, 0.0)
            weight_ref[row] = weight


def weights(where, own, first, second):
    return call(
        weights_kernel,
        (
            sds(V, 320, SLOTS, dtype=BF16),
            sds(2, V, 64, SLOTS, dtype=BF16),
            sds(9, SLOTS),
            sds(9, SLOTS),
            sds(9, SLOTS),
        ),
        ins=[SMEM, VMEM, VMEM, VMEM],
    )(where, own, first, second)


def picker(lev_ref):
    level = lax.broadcasted_iota(jnp.int32, (128, SLOTS), 0).astype(F32)

    def pick(cells, weight, row):
        both = jnp.concatenate(halves(cells), axis=1)
        at_all = tn(both, weight)
        at_all = at_all[:128] + at_all[128:]
        hot = level == lev_ref[pl.ds(row, 1), :]
        return jnp.sum(jnp.where(hot, at_all, 0.0), axis=0, keepdims=True)

    return pick


def mine_kernel(where_ref, inc_ref, wown_ref, wnear_ref, lev_ref, out_ref):
    pick = picker(lev_ref)
    for v in range(V):
        out_ref[v : v + 1] = pick(inc_ref[v], wown_ref[v, :256], v)
        for n in range(2):
            cells = inc_ref[v, pl.ds(pl.multiple_of(where_ref[n], 32), 32)]
            row = 3 * n + 3 + v
            out_ref[row : row + 1] = pick(cells, wnear_ref[n, v, :32], row)


def mine_part(where, inc, wown, wnear, lev):
    return call(
        mine_kernel,
        sds(9, SLOTS),
        ins=[SMEM] + [VMEM] * 4,
        outs=VMEM,
    )(where, inc, wown, wnear, lev)


def values_kernel(where_ref, mine_ref, near_ref, wown_ref, wnear_ref, lev_ref, out_ref):
    pick = picker(lev_ref)
    core = where_ref[10]

    def put(row, line):
        for a in range(6):
            out_ref[pl.ds(6 * row + a, 1)] = line[:, 128 * a : 128 * a + 128]

    for v in range(V):
        for n in range(2):
            row = 3 * n + 3 + v
            put(row, mine_ref[row : row + 1])
    for v in range(V):
        halo = pl.ds(pl.multiple_of(256 + 32 * core, 32), 32)
        put(v, mine_ref[v : v + 1] + pick(near_ref[v], wown_ref[v, halo], v))
        row = 3 * core + 3 + v
        put(row, mine_ref[pl.ds(row, 1)] + pick(near_ref[v], wnear_ref[core, v, 32:], row))


def values(where, mine, near, wown, wnear, lev):
    return call(
        values_kernel,
        sds(9 * SLOTS // 128, 128),
        ins=[SMEM] + [VMEM] * 5,
        outs=VMEM,
    )(where, mine, near, wown, wnear, lev)


def adjoint_kernel(where_ref, v0, v1, innov_ref, weight_ref, lev_ref, wown_ref, wnear_ref, x_ref, c_ref, first_ref, second_ref):
    level = lax.broadcasted_iota(jnp.int32, (128, SLOTS), 0).astype(F32)
    value = v0[...] + v1[...]

    def place(weight, row):
        line = jnp.concatenate([value[6 * row + a : 6 * row + a + 1] for a in range(6)], axis=1)
        weighted = weight_ref[row : row + 1] * (line - innov_ref[row : row + 1])
        hot = level == lev_ref[row : row + 1, :]
        spread = jnp.where(hot, weighted, 0.0)
        both = jnp.concatenate(halves(spread), axis=0)
        out = nt(weight, both)
        return out[:, :128] + out[:, 128:]

    adj = []
    for v in range(V):
        c_ref[v] = place(wown_ref[v, :256], v)
        for n in range(2):
            rows = pl.ds(pl.multiple_of(where_ref[n], 32), 32)
            c_ref[v, rows] = c_ref[v, rows] + place(wnear_ref[n, v, :32], 3 * n + 3 + v)
        adj.append(jnp.concatenate([c_ref[v, :64], c_ref[v, 192:]], axis=0))
    first_low = where_ref[7] == 1
    for k in range(first_ref.shape[0]):
        total = x_ref[k, 0].astype(F32) * adj[0]
        for v in range(1, V):
            total = total + x_ref[k, v].astype(F32) * adj[v]
        low, high = total[:64], total[64:]
        first_ref[k] = jnp.where(first_low, low, high)
        second_ref[k] = jnp.where(first_low, high, low)


def adjoint(where, vals, innov, weight, lev, wown, wnear, x):
    members = HEAD
    return call(
        adjoint_kernel,
        (sds(V, 256, 128), sds(members, 64, 128), sds(members, 64, 128)),
        ins=[SMEM] + [VMEM] * 8,
        outs=(VMEM,) * 3,
    )(where, *vals, innov, weight, lev, wown, wnear, x)


def drop(smoothed, loc):
    high, low = halves(smoothed)
    return nn(high, loc) + nn(low, loc)


def back_kernel(where_ref, alpha_ref, ens_ref, c_ref, smat_ref, loc_ref, out_ref, edge_ref, first_ref, second_ref):
    low = where_ref[7] == 1
    smat = smat_ref[...]
    loc = loc_ref[...]
    for k in range(GROUP):
        back = ens_ref[k, 0].astype(F32) * c_ref[0]
        for v in range(1, V):
            back = back + ens_ref[k, v].astype(F32) * c_ref[v]
        first_ref[k] = jnp.where(low, back[:64], back[192:])
        second_ref[k] = jnp.where(low, back[192:], back[:64])
        full = alpha_ref[k].astype(F32) + drop(smooth(smat, back), loc)
        out_ref[k] = full
        edge_ref[k, :64] = full[:64]
        edge_ref[k, 64:] = full[192:]


def back_part(where, alpha, ensemble, c, smat, loc):
    members = alpha.shape[0]
    rest = pl.BlockSpec((GROUP, 64, 128), lambda i: (jnp.maximum(i - HEAD // GROUP, 0), 0, 0))
    return call(
        back_kernel,
        (
            sds(members, 256, 128),
            sds(members, 128, 128),
            sds(members - HEAD, 64, 128),
            sds(members - HEAD, 64, 128),
        ),
        grid=(members // GROUP,),
        ins=[
            SMEM,
            pl.BlockSpec((GROUP, 256, 128), lambda i: (i, 0, 0)),
            pl.BlockSpec((GROUP, V, 256, 128), lambda i: (i, 0, 0, 0)),
            pl.BlockSpec((V, 256, 128), lambda i: (0, 0, 0)),
            pl.BlockSpec((256, 256), lambda i: (0, 0)),
            pl.BlockSpec((128, 128), lambda i: (0, 0)),
        ],
        outs=(
            pl.BlockSpec((GROUP, 256, 128), lambda i: (i, 0, 0)),
            pl.BlockSpec((GROUP, 128, 128), lambda i: (i, 0, 0)),
            rest,
            rest,
        ),
    )(where, alpha, ensemble, c, smat, loc)


def last_kernel(start, first_ref, second_ref, edge_ref, hmat_ref, loc_ref, unused_ref, out_ref, held, sems):
    hmat = hmat_ref[...]
    loc = loc_ref[...]
    copies = []
    for g in range(first_ref.shape[0] // GROUP):
        for k in range(g * GROUP, (g + 1) * GROUP):
            halo = jnp.concatenate([first_ref[k], second_ref[k]], axis=0)
            full = edge_ref[start + k] + drop(smooth(hmat, halo), loc)
            held[k, 0] = full[:64]
            held[k, 1] = full[64:]
        here, there = pl.ds(g * GROUP, GROUP), pl.ds(start + g * GROUP, GROUP)
        for side in range(2):
            copies.append(
                pltpu.make_async_copy(held.at[here, side], out_ref.at[there, 3 * side], sems.at[g, side])
            )
            copies[-1].start()
    for copy in copies:
        copy.wait()


def last_part(start, first, second, edge, hmat, loc, out):
    count = first.shape[0]
    return call(
        functools.partial(last_kernel, start),
        sds(*out.shape),
        ins=[VMEM] * 5 + [ANY],
        outs=ANY,
        scratch=[pltpu.VMEM((count, 2, 64, 128), F32), pltpu.SemaphoreType.DMA((count // GROUP, 2))],
        aliases={5: 0},
    )(first, second, edge, hmat, loc, out)


def stencil(gap):
    gap = jnp.abs(gap)
    return jnp.where(gap == 0, 6.0, jnp.where(gap == 1, 4.0, jnp.where(gap == 2, 1.0, 0.0)))


def matrices(tile, tiles, first_high):
    def across(i, j):
        gap = stencil(i - j)
        return jnp.where((i == j) & ((i == 0) | (i == 31)), 5.0, gap)

    i = lax.broadcasted_iota(jnp.int32, (256, 256), 0)
    j = lax.broadcasted_iota(jnp.int32, (256, 256), 1)
    ri, rj = i // 32, j // 32
    ends = ((ri == 0) & (tile == 0)) | ((ri == 7) & (tile == tiles - 1))
    down = jnp.where((ri == rj) & ends, 5.0, stencil(ri - rj))
    smat = (down * across(i % 32, j % 32) * (1.0 / 256.0)).astype(BF16)
    i = lax.broadcasted_iota(jnp.int32, (128, 128), 0)
    j = lax.broadcasted_iota(jnp.int32, (128, 128), 1)
    ri = i // 32
    ri = jnp.where(ri < 2, ri, ri + 4)
    above = (j < 64) == first_high
    rj = jnp.where(above, 8, -2) + (j // 32) % 2
    there = (above & (tile < tiles - 1)) | (jnp.logical_not(above) & (tile > 0))
    hmat = jnp.where(there, stencil(ri - rj), 0.0) * across(i % 32, j % 32) * (1.0 / 256.0)
    return smat, hmat.astype(BF16)


def swap_first(x):
    return lax.ppermute(x, ("mem", "tile"), FIRST)


def swap_second(x):
    return lax.ppermute(x, ("mem", "tile"), SECOND)


def swap_near(x):
    return lax.ppermute(x, ("mem", "tile"), NEAR)


def swap_core(x):
    return lax.ppermute(x, "mem", [(m, m ^ 1) for m in range(MEMS)])


def swap_chip(x):
    return lax.ppermute(x, "mem", [(m, m ^ 2) for m in range(MEMS)])


def on_device(alpha, ensemble, loc_vert, obs_col, obs_lev, obs_count, innovation, obs_weight):
    members = alpha.shape[0]
    tile = lax.axis_index("tile")
    tiles = lax.axis_size("tile")
    even = tile % 2 == 0
    core = lax.axis_index("mem") % 2
    first_low = side_of_first()
    where = jnp.stack(
        [
            jnp.where(even, 7 * 32, 0),
            jnp.where(even, 0, 7 * 32),
            jnp.where(even, 8, -1),
            jnp.where(even, -1, 8),
            ((tile > 0) & (tile < tiles - 1)).astype(jnp.int32),
            tile % 2,
            tile,
            first_low,
            7 * 32 * (1 - (tile + core) % 2),
            7 * 32 * ((tile + core) % 2),
            core,
        ]
    ).astype(jnp.int32)
    flat = alpha.reshape(members, 256, 128)
    flat_ens = ensemble.reshape(members, V, 256, 128)

    send_first, send_second, own_obs = send_part(
        obs_count, obs_col, obs_lev, innovation, obs_weight, alpha.reshape(members, 4, 64, 128)
    )
    first, second = swap_first(send_first), swap_second(send_second)
    inner, own_edge, x, smat, hmat, send_first, send_second = own_part(where, flat, flat_ens, loc_vert, own_obs)
    rest = send_first.reshape(-1, 128), send_second.reshape(-1, 128)
    first_rest, second_rest = swap_first(rest[0]), swap_second(rest[1])
    wown, wnear, lev, innov, weight = weights(where, own_obs, first, second)
    head = head_part(first, second, own_edge, x, hmat, loc_vert, lev)
    inc, keep, give = edge_part(where, first_rest, second_rest, own_edge, x, hmat, loc_vert, inner, head)
    near = swap_near(keep + swap_core(give))
    mine = mine_part(where, inc, wown, wnear, lev)
    vals = values(where, mine, near, wown, wnear, lev)
    vals = vals + swap_core(vals)
    vals = vals, swap_chip(vals)
    c, back_first, back_second = adjoint(where, vals, innov, weight, lev, wown, wnear, x)
    halo_first, halo_second = swap_first(back_first), swap_second(back_second)
    out, edge, back_first, back_second = back_part(where, flat, flat_ens, c, smat, loc_vert)
    rest_first, rest_second = swap_first(back_first), swap_second(back_second)
    out = last_part(0, halo_first, halo_second, edge, hmat, loc_vert, out.reshape(members, 4, 64, 128))
    out = last_part(HEAD, rest_first, rest_second, edge, hmat, loc_vert, out)
    return out.reshape(members, 8, 32, 128)


def solution(mesh):
    in_specs = (
        P("mem", "tile", None, None),
        P("mem", None, "tile", None, None),
        P(),
        P("tile", None),
        P("tile", None),
        P("tile"),
        P("tile", None),
        P("tile", None),
    )
    out_specs = P("mem", "tile", None, None)
    return jax.shard_map(
        on_device, mesh=mesh, in_specs=in_specs, out_specs=out_specs, check_vma=False
    )
```

```python
import functools

import jax
import jax.numpy as jnp
from jax import lax
from jax.experimental import pallas as pl
from jax.experimental.pallas import tpu as pltpu
from jax.sharding import PartitionSpec as P

V = 3
F32 = jnp.float32
BF16 = jnp.bfloat16
SLOTS = 768
GROUP = 4
HEAD = 16
HEAD_BACK = 12
OBS = 72

TILES = 64
MEMS = 4


def partners(odd, spare):
    pairs = []
    for m in range(MEMS):
        for t in range(TILES):
            beside = ((t - 1) ^ 1) + 1 if odd(m) else t ^ 1
            there = (m, beside) if 0 <= beside < TILES else (m ^ spare, t)
            pairs.append((TILES * m + t, TILES * there[0] + there[1]))
    return pairs


FIRST = partners(lambda m: True, 1)
SECOND = partners(lambda m: False, 1)
NEAR = partners(lambda m: m % 2 == 1, 2)


def nn(a, b):
    return lax.dot_general(a, b, (((1,), (0,)), ((), ())), preferred_element_type=F32)


def nt(a, b):
    return lax.dot_general(a, b, (((1,), (1,)), ((), ())), preferred_element_type=F32)


def tn(a, b):
    return lax.dot_general(a, b, (((0,), (0,)), ((), ())), preferred_element_type=F32)


def halves(x):
    high = x.astype(BF16)
    low = (x - high.astype(F32)).astype(BF16)
    return high, low


def lift(smoothed, loc):
    high, low = halves(smoothed)
    return nt(high, loc) + nt(low, loc)


def call(kernel, out, grid=None, ins=None, outs=None, scratch=(), aliases=None, cost=1000, vmem=16):
    kw = {}
    if grid is not None:
        kw["grid"] = grid
    return pl.pallas_call(
        kernel,
        out_shape=out,
        in_specs=ins,
        out_specs=outs if outs is not None else jax.tree.map(lambda o: VMEM, out),
        scratch_shapes=scratch,
        input_output_aliases=aliases or {},
        compiler_params=pltpu.CompilerParams(vmem_limit_bytes=vmem * 1024 * 1024),
        cost_estimate=pl.CostEstimate(flops=cost, bytes_accessed=cost, transcendentals=0),
        **kw,
    )


def sds(*shape, dtype=F32):
    return jax.ShapeDtypeStruct(shape, dtype)


ANY = pl.BlockSpec(memory_space=pl.ANY)
SMEM = pl.BlockSpec(memory_space=pltpu.SMEM)
VMEM = pl.BlockSpec(memory_space=pltpu.VMEM)
HBM = pl.BlockSpec(memory_space=pltpu.HBM)


def smooth(matrix, field):
    both = jnp.concatenate(halves(field), axis=1)
    out = nn(matrix, both)
    return out[:, :128] + out[:, 128:]


def side_of_first():
    return lax.rem(lax.axis_index("tile") + 1, 2)


def sort_observations(count, col_ref, lev_ref, innov_ref, weight_ref, out_ref):
    slots = col_ref.shape[1]
    live = lax.broadcasted_iota(jnp.int32, (1, slots), 1) < count
    rows = []
    for field in (
        col_ref[...].astype(F32),
        lev_ref[...].astype(F32),
        innov_ref[...],
        jnp.where(live, weight_ref[...], 0.0),
    ):
        field = jnp.concatenate([field, jnp.zeros((1, V * SLOTS - slots), F32)], axis=1)
        rows += [field[:, 384 * a : 384 * a + 384] for a in range(6)]
    rest = jnp.concatenate(rows, axis=0)
    i = lax.broadcasted_iota(jnp.int32, (384, 384), 0)
    j = lax.broadcasted_iota(jnp.int32, (384, 384), 1)
    order = (i == 3 * (j % 128) + j // 128).astype(F32).astype(BF16)
    total = jnp.zeros((24, 384), F32)
    for piece in range(3):
        part = rest.astype(BF16)
        rest = rest - part.astype(F32)
        total = total + nn(part, order)
    for f in range(4):
        for a in range(6):
            for v in range(V):
                row = 6 * (V * f + v) + a
                out_ref[row : row + 1] = total[6 * f + a : 6 * f + a + 1, 128 * v : 128 * v + 128]


def edge_rows(quarters_ref, start, first_ref, second_ref, edges, sems):
    count = edges.shape[1]
    members = pl.ds(start, count)
    copies = [pltpu.make_async_copy(quarters_ref.at[members, 3 * n], edges.at[n], sems.at[n]) for n in range(2)]
    for copy in copies:
        copy.start()
    for copy in copies:
        copy.wait()
    low = side_of_first()
    for k in range(count):
        first_ref[64 * k : 64 * k + 64] = edges[1 - low, k].astype(F32)
        second_ref[64 * k : 64 * k + 64] = edges[low, k].astype(F32)


def send_kernel(quarters_ref, first_ref, second_ref, token_ref, edges, sems):
    token_ref[...] = jnp.zeros_like(token_ref)
    edge_rows(quarters_ref, 0, first_ref, second_ref, edges, sems)


def send_part(quarters):
    return call(
        send_kernel,
        (sds(64 * HEAD, 128), sds(64 * HEAD, 128), sds(8, 128)),
        ins=[HBM],
        outs=(VMEM,) * 3,
        scratch=[pltpu.VMEM((2, HEAD, 64, 128), BF16), pltpu.SemaphoreType.DMA((2,))],
        vmem=56,
    )(quarters)


def rest_kernel(count_ref, col_ref, lev_ref, innov_ref, weight_ref, quarters_ref, after_ref, first_ref, second_ref, obs_ref, edges, sems):
    edge_rows(quarters_ref, HEAD, first_ref, second_ref, edges, sems)
    sort_observations(count_ref[0], col_ref, lev_ref, innov_ref, weight_ref, obs_ref)
    end = first_ref.shape[0] - OBS
    first_ref[end:] = obs_ref[...]
    second_ref[end:] = obs_ref[...]


def rest_part(count, col, lev, innov, weight, quarters, after):
    members = quarters.shape[0] - HEAD
    return call(
        rest_kernel,
        (sds(64 * members + OBS, 128), sds(64 * members + OBS, 128), sds(OBS, 128)),
        ins=[SMEM] + [VMEM] * 4 + [ANY, VMEM],
        outs=(VMEM,) * 3,
        scratch=[pltpu.VMEM((2, members, 64, 128), BF16), pltpu.SemaphoreType.DMA((2,))],
    )(count, col, lev, innov, weight, quarters, after)


def own_kernel(where_ref, alpha_ref, ens_ref, loc_ref, after_ref, inner_ref, edge_ref, x_ref, smat_ref, hmat_ref):
    @pl.when(pl.program_id(0) == 0)
    def _():
        inner_ref[...] = jnp.zeros_like(inner_ref)
        smat, hmat = matrices(where_ref[6], TILES, where_ref[7] == 0)
        smat_ref[...] = smat
        hmat_ref[...] = hmat

    smat = smat_ref[...]
    loc = loc_ref[...]
    total = [inner_ref[v] for v in range(V)]
    for k in range(GROUP):
        full = lift(nn(smat, alpha_ref[k]), loc)
        edge_ref[k, :64] = full[:64]
        edge_ref[k, 64:] = full[192:]
        lifted = full[64:192].astype(BF16).astype(F32)
        for v in range(V):
            total[v] = total[v] + ens_ref[k, v, 64:192].astype(F32) * lifted
            x_ref[k, v, :64] = ens_ref[k, v, :64]
            x_ref[k, v, 64:] = ens_ref[k, v, 192:]
    for v in range(V):
        inner_ref[v] = total[v]


def own_part(where, alpha, ensemble, loc, after):
    members = alpha.shape[0]
    whole = lambda *shape: pl.BlockSpec(shape, lambda i: (0,) * len(shape))
    return call(
        own_kernel,
        (
            sds(V, 128, 128),
            sds(members, 128, 128),
            sds(members, V, 128, 128, dtype=BF16),
            sds(256, 256, dtype=BF16),
            sds(128, 128, dtype=BF16),
        ),
        grid=(members // GROUP,),
        ins=[
            SMEM,
            pl.BlockSpec((GROUP, 256, 128), lambda i: (i, 0, 0)),
            pl.BlockSpec((GROUP, V, 256, 128), lambda i: (i, 0, 0, 0)),
            whole(128, 128),
            whole(8, 128),
        ],
        outs=(
            whole(V, 128, 128),
            pl.BlockSpec((GROUP, 128, 128), lambda i: (i, 0, 0)),
            pl.BlockSpec((GROUP, V, 128, 128), lambda i: (i, 0, 0, 0)),
            whole(256, 256),
            whole(128, 128),
        ),
    )(where, alpha, ensemble, loc, after)


def edge_terms(first_ref, second_ref, own_ref, x_ref, hmat_ref, loc_ref, start, count, total):
    hmat = hmat_ref[...]
    loc = loc_ref[...]
    for k in range(count):
        rows = slice(64 * k, 64 * k + 64)
        halo = jnp.concatenate([first_ref[rows].astype(BF16), second_ref[rows].astype(BF16)], axis=0)
        lifted = (own_ref[start + k] + lift(nn(hmat, halo), loc)).astype(BF16).astype(F32)
        for v in range(V):
            total[v] = total[v] + x_ref[start + k, v].astype(F32) * lifted
    return total


def head_kernel(first_ref, second_ref, own_ref, x_ref, hmat_ref, loc_ref, total_ref):
    zeros = [jnp.zeros((128, 128), F32) for v in range(V)]
    total = edge_terms(first_ref, second_ref, own_ref, x_ref, hmat_ref, loc_ref, 0, HEAD, zeros)
    for v in range(V):
        total_ref[v] = total[v]


def head_part(first, second, own, x, hmat, loc):
    return call(head_kernel, sds(V, 128, 128), ins=[VMEM] * 6, outs=VMEM)(first, second, own, x, hmat, loc)


def edge_kernel(where_ref, first_ref, second_ref, own_ref, x_ref, hmat_ref, loc_ref, inner_ref, head_ref, inc_ref, keep_ref, give_ref):
    total = [head_ref[v] for v in range(V)]
    total = edge_terms(first_ref, second_ref, own_ref, x_ref, hmat_ref, loc_ref, HEAD, own_ref.shape[0] - HEAD, total)
    for v in range(V):
        inc_ref[v, :64] = total[v][:64]
        inc_ref[v, 64:192] = inner_ref[v]
        inc_ref[v, 192:] = total[v][64:]
        keep_ref[v] = inc_ref[v, pl.ds(pl.multiple_of(where_ref[8], 32), 32)]
        give_ref[v] = inc_ref[v, pl.ds(pl.multiple_of(where_ref[9], 32), 32)]


def edge_part(where, first, second, own, x, hmat, loc, inner, head):
    return call(
        edge_kernel,
        (sds(V, 256, 128), sds(V, 32, 128), sds(V, 32, 128)),
        ins=[SMEM] + [VMEM] * 8,
        outs=(VMEM,) * 3,
    )(where, first, second, own, x, hmat, loc, inner, head)


def tent(distance):
    return jnp.maximum(1.0 - jnp.abs(distance), 0.0)


def weights_kernel(where_ref, own_ref, o_ref, e_ref, after_ref, wown_ref, wnear_ref, lev_ref, innov_ref, weight_ref, hot_ref):
    level = lax.broadcasted_iota(jnp.int32, (128, SLOTS), 0).astype(F32)
    even_row = where_ref[2].astype(F32)
    odd_row = where_ref[3].astype(F32)
    odd_there = where_ref[4].astype(F32)
    cell = lax.broadcasted_iota(jnp.int32, (32, SLOTS), 0).astype(F32)

    def line(ref, field, v):
        at = ref.shape[0] - OBS + 6 * (V * field + v)
        return jnp.concatenate([ref[at + a : at + a + 1] for a in range(6)], axis=1)

    def columns(code):
        row = jnp.floor(code * (1.0 / 64.0))
        column = code - 64.0 * row
        return row, tent(cell - (column * 0.5 - 0.25))

    for v in range(V):
        row, across = columns(line(own_ref, 0, v))
        middle = row * 0.5 - 0.25
        for r in range(8):
            wown_ref[v, 32 * r : 32 * r + 32] = (tent(r - middle) * across).astype(BF16)
        wown_ref[v, 256:288] = (tent(even_row - middle) * across).astype(BF16)
        wown_ref[v, 288:320] = (tent(odd_row - middle) * odd_there * across).astype(BF16)
        for n, ref in enumerate((e_ref, o_ref)):
            row, across = columns(line(ref, 0, v))
            wnear_ref[n, v, :32] = (0.25 * across).astype(BF16)
            wnear_ref[n, v, 32:] = (0.75 * across).astype(BF16)
    is_odd = where_ref[5]
    for n, ref in enumerate((own_ref, e_ref, o_ref)):
        for v in range(V):
            row = slice(3 * n + v, 3 * n + v + 1)
            lev = line(ref, 1, v)
            lev_ref[row] = lev
            hot_ref[3 * n + v] = jnp.where(level == lev, 1.0, 0.0).astype(BF16)
            innov_ref[row] = line(ref, 2, v)
            weight = line(ref, 3, v)
            if n > 0:
                code = line(ref, 0, v)
                first = is_odd == (0 if n == 1 else 1)
                at_edge = jnp.where(first, code, 1023.0 - code) < 64.0
                there = at_edge & ((n == 1) | (where_ref[4] == 1))
                weight = jnp.where(there, weight, 0.0)
            weight_ref[row] = weight


def weights(where, own, first, second, after):
    return call(
        weights_kernel,
        (
            sds(V, 320, SLOTS, dtype=BF16),
            sds(2, V, 64, SLOTS, dtype=BF16),
            sds(9, SLOTS),
            sds(9, SLOTS),
            sds(9, SLOTS),
            sds(9, 128, SLOTS, dtype=BF16),
        ),
        ins=[SMEM] + [VMEM] * 4,
    )(where, own, first, second, after)


def picker(lev_ref):
    level = lax.broadcasted_iota(jnp.int32, (128, SLOTS), 0).astype(F32)

    def pick(cells, weight, row):
        both = jnp.concatenate(halves(cells), axis=1)
        at_all = tn(both, weight)
        at_all = at_all[:128] + at_all[128:]
        hot = level == lev_ref[pl.ds(row, 1), :]
        return jnp.sum(jnp.where(hot, at_all, 0.0), axis=0, keepdims=True)

    return pick


def mine_kernel(where_ref, inc_ref, wown_ref, wnear_ref, lev_ref, out_ref):
    pick = picker(lev_ref)
    for v in range(V):
        out_ref[v : v + 1] = pick(inc_ref[v], wown_ref[v, :256], v)
        for n in range(2):
            cells = inc_ref[v, pl.ds(pl.multiple_of(where_ref[n], 32), 32)]
            row = 3 * n + 3 + v
            out_ref[row : row + 1] = pick(cells, wnear_ref[n, v, :32], row)


def mine_part(where, inc, wown, wnear, lev):
    return call(
        mine_kernel,
        sds(9, SLOTS),
        ins=[SMEM] + [VMEM] * 4,
        outs=VMEM,
    )(where, inc, wown, wnear, lev)


def values_kernel(where_ref, mine_ref, near_ref, wown_ref, wnear_ref, lev_ref, out_ref):
    pick = picker(lev_ref)
    core = where_ref[10]

    def put(row, line):
        for a in range(6):
            out_ref[pl.ds(6 * row + a, 1)] = line[:, 128 * a : 128 * a + 128]

    for v in range(V):
        for n in range(2):
            row = 3 * n + 3 + v
            put(row, mine_ref[row : row + 1])
    for v in range(V):
        halo = pl.ds(pl.multiple_of(256 + 32 * core, 32), 32)
        put(v, mine_ref[v : v + 1] + pick(near_ref[v], wown_ref[v, halo], v))
        row = 3 * core + 3 + v
        put(row, mine_ref[pl.ds(row, 1)] + pick(near_ref[v], wnear_ref[core, v, 32:], row))


def values(where, mine, near, wown, wnear, lev):
    return call(
        values_kernel,
        sds(9 * SLOTS // 128, 128),
        ins=[SMEM] + [VMEM] * 5,
        outs=VMEM,
    )(where, mine, near, wown, wnear, lev)


def adjoint_kernel(where_ref, v0, v1, innov_ref, weight_ref, hot_ref, wown_ref, wnear_ref, x_ref, c_ref, first_ref, second_ref):
    value = v0[...] + v1[...]

    def place(weight, row):
        line = jnp.concatenate([value[6 * row + a : 6 * row + a + 1] for a in range(6)], axis=1)
        weighted = weight_ref[row : row + 1] * (line - innov_ref[row : row + 1])
        hot = hot_ref[row]
        both = jnp.concatenate([hot * half for half in halves(weighted)], axis=0)
        out = nt(weight, both)
        return out[:, :128] + out[:, 128:]

    adj = []
    for v in range(V):
        c_ref[v] = place(wown_ref[v, :256], v)
        for n in range(2):
            rows = pl.ds(pl.multiple_of(where_ref[n], 32), 32)
            c_ref[v, rows] = c_ref[v, rows] + place(wnear_ref[n, v, :32], 3 * n + 3 + v)
        adj.append(jnp.concatenate([c_ref[v, :64], c_ref[v, 192:]], axis=0))
    first_low = where_ref[7] == 1
    for k in range(first_ref.shape[0]):
        total = x_ref[k, 0].astype(F32) * adj[0]
        for v in range(1, V):
            total = total + x_ref[k, v].astype(F32) * adj[v]
        low, high = total[:64], total[64:]
        first_ref[k] = jnp.where(first_low, low, high)
        second_ref[k] = jnp.where(first_low, high, low)


def adjoint(where, vals, innov, weight, hot, wown, wnear, x):
    members = HEAD_BACK
    return call(
        adjoint_kernel,
        (sds(V, 256, 128), sds(members, 64, 128), sds(members, 64, 128)),
        ins=[SMEM] + [VMEM] * 8,
        outs=(VMEM,) * 3,
    )(where, *vals, innov, weight, hot, wown, wnear, x)


def drop(smoothed, loc):
    high, low = halves(smoothed)
    return nn(high, loc) + nn(low, loc)


def back_kernel(where_ref, alpha_ref, ens_ref, c_ref, smat_ref, loc_ref, out_ref, edge_ref, first_ref, second_ref):
    low = where_ref[7] == 1
    smat = smat_ref[...]
    loc = loc_ref[...]
    for k in range(GROUP):
        back = ens_ref[k, 0].astype(F32) * c_ref[0]
        for v in range(1, V):
            back = back + ens_ref[k, v].astype(F32) * c_ref[v]
        first_ref[k] = jnp.where(low, back[:64], back[192:])
        second_ref[k] = jnp.where(low, back[192:], back[:64])
        full = alpha_ref[k].astype(F32) + drop(smooth(smat, back), loc)
        out_ref[k] = full
        edge_ref[k, :64] = full[:64]
        edge_ref[k, 64:] = full[192:]


def back_part(where, alpha, ensemble, c, smat, loc):
    members = alpha.shape[0]
    rest = pl.BlockSpec((GROUP, 64, 128), lambda i: (jnp.maximum(i - HEAD_BACK // GROUP, 0), 0, 0))
    return call(
        back_kernel,
        (
            sds(members, 256, 128),
            sds(members, 128, 128),
            sds(members - HEAD_BACK, 64, 128),
            sds(members - HEAD_BACK, 64, 128),
        ),
        grid=(members // GROUP,),
        ins=[
            SMEM,
            pl.BlockSpec((GROUP, 256, 128), lambda i: (i, 0, 0)),
            pl.BlockSpec((GROUP, V, 256, 128), lambda i: (i, 0, 0, 0)),
            pl.BlockSpec((V, 256, 128), lambda i: (0, 0, 0)),
            pl.BlockSpec((256, 256), lambda i: (0, 0)),
            pl.BlockSpec((128, 128), lambda i: (0, 0)),
        ],
        outs=(
            pl.BlockSpec((GROUP, 256, 128), lambda i: (i, 0, 0)),
            pl.BlockSpec((GROUP, 128, 128), lambda i: (i, 0, 0)),
            rest,
            rest,
        ),
    )(where, alpha, ensemble, c, smat, loc)


def last_kernel(start, first_ref, second_ref, edge_ref, hmat_ref, loc_ref, unused_ref, out_ref, held, sems):
    hmat = hmat_ref[...]
    loc = loc_ref[...]
    copies = []
    for g in range(first_ref.shape[0] // GROUP):
        for k in range(g * GROUP, (g + 1) * GROUP):
            halo = jnp.concatenate([first_ref[k], second_ref[k]], axis=0)
            full = edge_ref[start + k] + drop(smooth(hmat, halo), loc)
            held[k, 0] = full[:64]
            held[k, 1] = full[64:]
        here, there = pl.ds(g * GROUP, GROUP), pl.ds(start + g * GROUP, GROUP)
        for side in range(2):
            copies.append(
                pltpu.make_async_copy(held.at[here, side], out_ref.at[there, 3 * side], sems.at[g, side])
            )
            copies[-1].start()
    for copy in copies:
        copy.wait()


def last_part(start, first, second, edge, hmat, loc, out):
    count = first.shape[0]
    return call(
        functools.partial(last_kernel, start),
        sds(*out.shape),
        ins=[VMEM] * 5 + [ANY],
        outs=ANY,
        scratch=[pltpu.VMEM((count, 2, 64, 128), F32), pltpu.SemaphoreType.DMA((count // GROUP, 2))],
        aliases={5: 0},
    )(first, second, edge, hmat, loc, out)


def stencil(gap):
    gap = jnp.abs(gap)
    return jnp.where(gap == 0, 6.0, jnp.where(gap == 1, 4.0, jnp.where(gap == 2, 1.0, 0.0)))


def matrices(tile, tiles, first_high):
    def across(i, j):
        gap = stencil(i - j)
        return jnp.where((i == j) & ((i == 0) | (i == 31)), 5.0, gap)

    i = lax.broadcasted_iota(jnp.int32, (256, 256), 0)
    j = lax.broadcasted_iota(jnp.int32, (256, 256), 1)
    ri, rj = i // 32, j // 32
    ends = ((ri == 0) & (tile == 0)) | ((ri == 7) & (tile == tiles - 1))
    down = jnp.where((ri == rj) & ends, 5.0, stencil(ri - rj))
    smat = (down * across(i % 32, j % 32) * (1.0 / 256.0)).astype(BF16)
    i = lax.broadcasted_iota(jnp.int32, (128, 128), 0)
    j = lax.broadcasted_iota(jnp.int32, (128, 128), 1)
    ri = i // 32
    ri = jnp.where(ri < 2, ri, ri + 4)
    above = (j < 64) == first_high
    rj = jnp.where(above, 8, -2) + (j // 32) % 2
    there = (above & (tile < tiles - 1)) | (jnp.logical_not(above) & (tile > 0))
    hmat = jnp.where(there, stencil(ri - rj), 0.0) * across(i % 32, j % 32) * (1.0 / 256.0)
    return smat, hmat.astype(BF16)


def swap_first(x):
    return lax.ppermute(x, ("mem", "tile"), FIRST)


def swap_second(x):
    return lax.ppermute(x, ("mem", "tile"), SECOND)


def swap_near(x):
    return lax.ppermute(x, ("mem", "tile"), NEAR)


def swap_core(x):
    return lax.ppermute(x, "mem", [(m, m ^ 1) for m in range(MEMS)])


def swap_chip(x):
    return lax.ppermute(x, "mem", [(m, m ^ 2) for m in range(MEMS)])


def on_device(alpha, ensemble, loc_vert, obs_col, obs_lev, obs_count, innovation, obs_weight):
    members = alpha.shape[0]
    tile = lax.axis_index("tile")
    tiles = lax.axis_size("tile")
    even = tile % 2 == 0
    core = lax.axis_index("mem") % 2
    first_low = side_of_first()
    where = jnp.stack(
        [
            jnp.where(even, 7 * 32, 0),
            jnp.where(even, 0, 7 * 32),
            jnp.where(even, 8, -1),
            jnp.where(even, -1, 8),
            ((tile > 0) & (tile < tiles - 1)).astype(jnp.int32),
            tile % 2,
            tile,
            first_low,
            7 * 32 * (1 - (tile + core) % 2),
            7 * 32 * ((tile + core) % 2),
            core,
        ]
    ).astype(jnp.int32)
    flat = alpha.reshape(members, 256, 128)
    flat_ens = ensemble.reshape(members, V, 256, 128)

    quarters = alpha.reshape(members, 4, 64, 128)
    send_first, send_second, token = send_part(quarters)
    first, second = swap_first(send_first), swap_second(send_second)
    inner, own_edge, x, smat, hmat = own_part(where, flat, flat_ens, loc_vert, token)
    send_first, send_second, own_obs = rest_part(
        obs_count, obs_col, obs_lev, innovation, obs_weight, quarters, hmat
    )
    first_rest, second_rest = swap_first(send_first), swap_second(send_second)
    head = head_part(first, second, own_edge, x, hmat, loc_vert)
    inc, keep, give = edge_part(where, first_rest, second_rest, own_edge, x, hmat, loc_vert, inner, head)
    edges = keep + swap_core(give)
    near = swap_near(edges)
    wown, wnear, lev, innov, weight, hot = weights(where, own_obs, first_rest, second_rest, edges)
    mine = mine_part(where, inc, wown, wnear, lev)
    vals = values(where, mine, near, wown, wnear, lev)
    vals = vals + swap_core(vals)
    vals = vals, swap_chip(vals)
    c, back_first, back_second = adjoint(where, vals, innov, weight, hot, wown, wnear, x)
    halo_first, halo_second = swap_first(back_first), swap_second(back_second)
    out, edge, back_first, back_second = back_part(where, flat, flat_ens, c, smat, loc_vert)
    rest_first, rest_second = swap_first(back_first), swap_second(back_second)
    out = last_part(0, halo_first, halo_second, edge, hmat, loc_vert, out.reshape(members, 4, 64, 128))
    out = last_part(HEAD_BACK, rest_first, rest_second, edge, hmat, loc_vert, out)
    return out.reshape(members, 8, 32, 128)


def solution(mesh):
    in_specs = (
        P("mem", "tile", None, None),
        P("mem", None, "tile", None, None),
        P(),
        P("tile", None),
        P("tile", None),
        P("tile"),
        P("tile", None),
        P("tile", None),
    )
    out_specs = P("mem", "tile", None, None)
    return jax.shard_map(
        on_device, mesh=mesh, in_specs=in_specs, out_specs=out_specs, check_vma=False
    )
```

```python
import functools

import jax
import jax.numpy as jnp
from jax import lax
from jax.experimental import pallas as pl
from jax.experimental.pallas import tpu as pltpu
from jax.sharding import PartitionSpec as P

V = 3
F32 = jnp.float32
BF16 = jnp.bfloat16
SLOTS = 768
GROUP = 4
HEAD = 16
HEAD_BACK = 12
OBS = 80
HALF = OBS // 2

TILES = 64
MEMS = 4


def partners(odd, spare):
    pairs = []
    for m in range(MEMS):
        for t in range(TILES):
            beside = ((t - 1) ^ 1) + 1 if odd(m) else t ^ 1
            there = (m, beside) if 0 <= beside < TILES else (m ^ spare, t)
            pairs.append((TILES * m + t, TILES * there[0] + there[1]))
    return pairs


FIRST = partners(lambda m: True, 1)
SECOND = partners(lambda m: False, 1)
NEAR = partners(lambda m: m % 2 == 1, 2)


def nn(a, b):
    return lax.dot_general(a, b, (((1,), (0,)), ((), ())), preferred_element_type=F32)


def nt(a, b):
    return lax.dot_general(a, b, (((1,), (1,)), ((), ())), preferred_element_type=F32)


def tn(a, b):
    return lax.dot_general(a, b, (((0,), (0,)), ((), ())), preferred_element_type=F32)


def halves(x):
    high = x.astype(BF16)
    low = (x - high.astype(F32)).astype(BF16)
    return high, low


def lift(smoothed, loc):
    high, low = halves(smoothed)
    return nt(high, loc) + nt(low, loc)


def call(kernel, out, grid=None, ins=None, outs=None, scratch=(), aliases=None, cost=1000, vmem=16):
    kw = {}
    if grid is not None:
        kw["grid"] = grid
    return pl.pallas_call(
        kernel,
        out_shape=out,
        in_specs=ins,
        out_specs=outs if outs is not None else jax.tree.map(lambda o: VMEM, out),
        scratch_shapes=scratch,
        input_output_aliases=aliases or {},
        compiler_params=pltpu.CompilerParams(vmem_limit_bytes=vmem * 1024 * 1024),
        cost_estimate=pl.CostEstimate(flops=cost, bytes_accessed=cost, transcendentals=0),
        **kw,
    )


def sds(*shape, dtype=F32):
    return jax.ShapeDtypeStruct(shape, dtype)


ANY = pl.BlockSpec(memory_space=pl.ANY)
SMEM = pl.BlockSpec(memory_space=pltpu.SMEM)
VMEM = pl.BlockSpec(memory_space=pltpu.VMEM)
HBM = pl.BlockSpec(memory_space=pltpu.HBM)


def smooth(matrix, field):
    both = jnp.concatenate(halves(field), axis=1)
    out = nn(matrix, both)
    return out[:, :128] + out[:, 128:]


def side_of_first():
    return lax.rem(lax.axis_index("tile") + 1, 2)


def sort_observations(count, col_ref, lev_ref, innov_ref, weight_ref, out_ref):
    slots = col_ref.shape[1]
    live = lax.broadcasted_iota(jnp.int32, (1, slots), 1) < count
    rows = []
    for field in (
        col_ref[...].astype(F32),
        lev_ref[...].astype(F32),
        innov_ref[...],
        jnp.where(live, weight_ref[...], 0.0),
    ):
        field = jnp.concatenate([field, jnp.zeros((1, V * SLOTS - slots), F32)], axis=1)
        rows += [field[:, 384 * a : 384 * a + 384] for a in range(6)]
    rest = jnp.concatenate(rows, axis=0)
    i = lax.broadcasted_iota(jnp.int32, (384, 384), 0)
    j = lax.broadcasted_iota(jnp.int32, (384, 384), 1)
    order = (i == 3 * (j % 128) + j // 128).astype(F32).astype(BF16)
    total = jnp.zeros((24, 384), F32)
    for piece in range(3):
        part = rest.astype(BF16)
        rest = rest - part.astype(F32)
        total = total + nn(part, order)
    out_ref[72:] = jnp.zeros((OBS - 72, 128), F32)
    for f in range(4):
        for a in range(6):
            for v in range(V):
                row = 6 * (V * f + v) + a
                out_ref[row : row + 1] = total[6 * f + a : 6 * f + a + 1, 128 * v : 128 * v + 128]


def send_kernel(quarters_ref, first_ref, second_ref, token_ref, edges, rows, fetched, sent):
    token_ref[...] = jnp.zeros_like(token_ref)
    groups = HEAD // GROUP
    fetches, sends = [], []
    for g in range(groups):
        members = pl.ds(g * GROUP, GROUP)
        for n in range(2):
            fetches.append(
                pltpu.make_async_copy(quarters_ref.at[members, 3 * n], edges.at[n, members], fetched.at[g, n])
            )
            fetches[-1].start()
    low = side_of_first()
    for g in range(groups):
        for fetch in fetches[2 * g : 2 * g + 2]:
            fetch.wait()
        for k in range(g * GROUP, (g + 1) * GROUP):
            rows[0, 64 * k : 64 * k + 64] = edges[1 - low, k].astype(F32)
            rows[1, 64 * k : 64 * k + 64] = edges[low, k].astype(F32)
        part = pl.ds(64 * GROUP * g, 64 * GROUP)
        for n, ref in enumerate((first_ref, second_ref)):
            sends.append(pltpu.make_async_copy(rows.at[n, part], ref.at[part], sent.at[g, n]))
            sends[-1].start()
    for send in sends:
        send.wait()


def send_part(quarters):
    return call(
        send_kernel,
        (sds(64 * HEAD, 128), sds(64 * HEAD, 128), sds(8, 128)),
        ins=[HBM],
        outs=(HBM, HBM, VMEM),
        scratch=[
            pltpu.VMEM((2, HEAD, 64, 128), BF16),
            pltpu.VMEM((2, 64 * HEAD, 128), F32),
            pltpu.SemaphoreType.DMA((HEAD // GROUP, 2)),
            pltpu.SemaphoreType.DMA((HEAD // GROUP, 2)),
        ],
        vmem=56,
    )(quarters)


def rest_kernel(count_ref, col_ref, lev_ref, innov_ref, weight_ref, quarters_ref, after_ref, first_ref, second_ref, obs_ref, edges, sems):
    count = edges.shape[1]
    members = pl.ds(HEAD, count)
    copies = [pltpu.make_async_copy(quarters_ref.at[members, 3 * n], edges.at[n], sems.at[n]) for n in range(2)]
    for copy in copies:
        copy.start()
    sort_observations(count_ref[0], col_ref, lev_ref, innov_ref, weight_ref, obs_ref)
    core = lax.rem(lax.axis_index("mem"), 2)
    half = obs_ref[pl.ds(pl.multiple_of(HALF * core, 8), HALF)]
    first_ref[64 * count :] = half
    second_ref[64 * count :] = half
    for copy in copies:
        copy.wait()
    low = side_of_first()
    for k in range(count):
        first_ref[64 * k : 64 * k + 64] = edges[1 - low, k].astype(F32)
        second_ref[64 * k : 64 * k + 64] = edges[low, k].astype(F32)


def rest_part(count, col, lev, innov, weight, quarters, after):
    members = quarters.shape[0] - HEAD
    return call(
        rest_kernel,
        (sds(64 * members + HALF, 128), sds(64 * members + HALF, 128), sds(OBS, 128)),
        ins=[SMEM] + [VMEM] * 4 + [ANY, VMEM],
        outs=(VMEM,) * 3,
        scratch=[pltpu.VMEM((2, members, 64, 128), BF16), pltpu.SemaphoreType.DMA((2,))],
    )(count, col, lev, innov, weight, quarters, after)


def own_kernel(where_ref, alpha_ref, ens_ref, loc_ref, after_ref, inner_ref, edge_ref, x_ref, smat_ref, hmat_ref):
    @pl.when(pl.program_id(0) == 0)
    def _():
        inner_ref[...] = jnp.zeros_like(inner_ref)
        smat, hmat = matrices(where_ref[6], TILES, where_ref[7] == 0)
        smat_ref[...] = smat
        hmat_ref[...] = hmat

    smat = smat_ref[...]
    loc = loc_ref[...]
    total = [inner_ref[v] for v in range(V)]
    for k in range(GROUP):
        full = lift(nn(smat, alpha_ref[k]), loc)
        edge_ref[k, :64] = full[:64]
        edge_ref[k, 64:] = full[192:]
        lifted = full[64:192].astype(BF16).astype(F32)
        for v in range(V):
            total[v] = total[v] + ens_ref[k, v, 64:192].astype(F32) * lifted
            x_ref[k, v, :64] = ens_ref[k, v, :64]
            x_ref[k, v, 64:] = ens_ref[k, v, 192:]
    for v in range(V):
        inner_ref[v] = total[v]


def own_part(where, alpha, ensemble, loc, after):
    members = alpha.shape[0]
    whole = lambda *shape: pl.BlockSpec(shape, lambda i: (0,) * len(shape))
    return call(
        own_kernel,
        (
            sds(V, 128, 128),
            sds(members, 128, 128),
            sds(members, V, 128, 128, dtype=BF16),
            sds(256, 256, dtype=BF16),
            sds(128, 128, dtype=BF16),
        ),
        grid=(members // GROUP,),
        ins=[
            SMEM,
            pl.BlockSpec((GROUP, 256, 128), lambda i: (i, 0, 0)),
            pl.BlockSpec((GROUP, V, 256, 128), lambda i: (i, 0, 0, 0)),
            whole(128, 128),
            whole(8, 128),
        ],
        outs=(
            whole(V, 128, 128),
            pl.BlockSpec((GROUP, 128, 128), lambda i: (i, 0, 0)),
            pl.BlockSpec((GROUP, V, 128, 128), lambda i: (i, 0, 0, 0)),
            whole(256, 256),
            whole(128, 128),
        ),
    )(where, alpha, ensemble, loc, after)


def edge_terms(first_ref, second_ref, own_ref, x_ref, hmat_ref, loc_ref, start, count, total):
    hmat = hmat_ref[...]
    loc = loc_ref[...]
    for k in range(count):
        rows = slice(64 * k, 64 * k + 64)
        halo = jnp.concatenate([first_ref[rows].astype(BF16), second_ref[rows].astype(BF16)], axis=0)
        lifted = (own_ref[start + k] + lift(nn(hmat, halo), loc)).astype(BF16).astype(F32)
        for v in range(V):
            total[v] = total[v] + x_ref[start + k, v].astype(F32) * lifted
    return total


def head_kernel(first_ref, second_ref, own_ref, x_ref, hmat_ref, loc_ref, total_ref):
    zeros = [jnp.zeros((128, 128), F32) for v in range(V)]
    total = edge_terms(first_ref, second_ref, own_ref, x_ref, hmat_ref, loc_ref, 0, HEAD, zeros)
    for v in range(V):
        total_ref[v] = total[v]


def head_part(first, second, own, x, hmat, loc):
    return call(head_kernel, sds(V, 128, 128), ins=[VMEM] * 6, outs=VMEM)(first, second, own, x, hmat, loc)


def edge_kernel(where_ref, first_ref, second_ref, own_ref, x_ref, hmat_ref, loc_ref, inner_ref, head_ref, inc_ref, keep_ref, give_ref):
    total = [head_ref[v] for v in range(V)]
    total = edge_terms(first_ref, second_ref, own_ref, x_ref, hmat_ref, loc_ref, HEAD, own_ref.shape[0] - HEAD, total)
    for v in range(V):
        inc_ref[v, :64] = total[v][:64]
        inc_ref[v, 64:192] = inner_ref[v]
        inc_ref[v, 192:] = total[v][64:]
        keep_ref[32 * v : 32 * v + 32] = inc_ref[v, pl.ds(pl.multiple_of(where_ref[8], 32), 32)]
        give_ref[32 * v : 32 * v + 32] = inc_ref[v, pl.ds(pl.multiple_of(where_ref[9], 32), 32)]
    end = first_ref.shape[0] - HALF
    give_ref[32 * V : 32 * V + HALF] = first_ref[end:]
    give_ref[32 * V + HALF :] = second_ref[end:]


def edge_part(where, first, second, own, x, hmat, loc, inner, head):
    return call(
        edge_kernel,
        (sds(V, 256, 128), sds(V * 32, 128), sds(V * 32 + OBS, 128)),
        ins=[SMEM] + [VMEM] * 8,
        outs=(VMEM,) * 3,
    )(where, first, second, own, x, hmat, loc, inner, head)


def tent(distance):
    return jnp.maximum(1.0 - jnp.abs(distance), 0.0)


def weights_kernel(where_ref, own_ref, here_ref, there_ref, after_ref, wown_ref, wnear_ref, lev_ref, innov_ref, weight_ref, hot_ref, o_ref, e_ref):
    core = where_ref[10]
    for half, ref in ((core, here_ref), (1 - core, there_ref)):
        rows = pl.ds(pl.multiple_of(HALF * half, 8), HALF)
        o_ref[rows] = ref[32 * V : 32 * V + HALF]
        e_ref[rows] = ref[32 * V + HALF :]
    level = lax.broadcasted_iota(jnp.int32, (128, SLOTS), 0).astype(F32)
    even_row = where_ref[2].astype(F32)
    odd_row = where_ref[3].astype(F32)
    odd_there = where_ref[4].astype(F32)
    cell = lax.broadcasted_iota(jnp.int32, (32, SLOTS), 0).astype(F32)

    def line(ref, field, v):
        at = 6 * (V * field + v)
        return jnp.concatenate([ref[at + a : at + a + 1] for a in range(6)], axis=1)

    def columns(code):
        row = jnp.floor(code * (1.0 / 64.0))
        column = code - 64.0 * row
        return row, tent(cell - (column * 0.5 - 0.25))

    for v in range(V):
        row, across = columns(line(own_ref, 0, v))
        middle = row * 0.5 - 0.25
        for r in range(8):
            wown_ref[v, 32 * r : 32 * r + 32] = (tent(r - middle) * across).astype(BF16)
        wown_ref[v, 256:288] = (tent(even_row - middle) * across).astype(BF16)
        wown_ref[v, 288:320] = (tent(odd_row - middle) * odd_there * across).astype(BF16)
        for n, ref in enumerate((e_ref, o_ref)):
            row, across = columns(line(ref, 0, v))
            wnear_ref[n, v, :32] = (0.25 * across).astype(BF16)
            wnear_ref[n, v, 32:] = (0.75 * across).astype(BF16)
    is_odd = where_ref[5]
    for n, ref in enumerate((own_ref, e_ref, o_ref)):
        for v in range(V):
            row = slice(3 * n + v, 3 * n + v + 1)
            lev = line(ref, 1, v)
            lev_ref[row] = lev
            hot_ref[3 * n + v] = jnp.where(level == lev, 1.0, 0.0).astype(BF16)
            innov_ref[row] = line(ref, 2, v)
            weight = line(ref, 3, v)
            if n > 0:
                code = line(ref, 0, v)
                first = is_odd == (0 if n == 1 else 1)
                at_edge = jnp.where(first, code, 1023.0 - code) < 64.0
                there = at_edge & ((n == 1) | (where_ref[4] == 1))
                weight = jnp.where(there, weight, 0.0)
            weight_ref[row] = weight


def weights(where, own, here, there, after):
    return call(
        weights_kernel,
        (
            sds(V, 320, SLOTS, dtype=BF16),
            sds(2, V, 64, SLOTS, dtype=BF16),
            sds(9, SLOTS),
            sds(9, SLOTS),
            sds(9, SLOTS),
            sds(9, 128, SLOTS, dtype=BF16),
        ),
        ins=[SMEM] + [VMEM] * 4,
        scratch=[pltpu.VMEM((OBS, 128), F32), pltpu.VMEM((OBS, 128), F32)],
    )(where, own, here, there, after)


def picker(lev_ref):
    level = lax.broadcasted_iota(jnp.int32, (128, SLOTS), 0).astype(F32)

    def pick(cells, weight, row):
        both = jnp.concatenate(halves(cells), axis=1)
        at_all = tn(both, weight)
        at_all = at_all[:128] + at_all[128:]
        hot = level == lev_ref[pl.ds(row, 1), :]
        return jnp.sum(jnp.where(hot, at_all, 0.0), axis=0, keepdims=True)

    return pick


def mine_kernel(where_ref, inc_ref, wown_ref, wnear_ref, lev_ref, out_ref):
    pick = picker(lev_ref)
    for v in range(V):
        out_ref[v : v + 1] = pick(inc_ref[v], wown_ref[v, :256], v)
        for n in range(2):
            cells = inc_ref[v, pl.ds(pl.multiple_of(where_ref[n], 32), 32)]
            row = 3 * n + 3 + v
            out_ref[row : row + 1] = pick(cells, wnear_ref[n, v, :32], row)


def mine_part(where, inc, wown, wnear, lev):
    return call(
        mine_kernel,
        sds(9, SLOTS),
        ins=[SMEM] + [VMEM] * 4,
        outs=VMEM,
    )(where, inc, wown, wnear, lev)


def values_kernel(where_ref, mine_ref, near_ref, wown_ref, wnear_ref, lev_ref, out_ref):
    pick = picker(lev_ref)
    core = where_ref[10]

    def put(row, line):
        for a in range(6):
            out_ref[pl.ds(6 * row + a, 1)] = line[:, 128 * a : 128 * a + 128]

    for v in range(V):
        for n in range(2):
            row = 3 * n + 3 + v
            put(row, mine_ref[row : row + 1])
    for v in range(V):
        halo = pl.ds(pl.multiple_of(256 + 32 * core, 32), 32)
        put(v, mine_ref[v : v + 1] + pick(near_ref[32 * v : 32 * v + 32], wown_ref[v, halo], v))
        row = 3 * core + 3 + v
        put(row, mine_ref[pl.ds(row, 1)] + pick(near_ref[32 * v : 32 * v + 32], wnear_ref[core, v, 32:], row))


def values(where, mine, near, wown, wnear, lev):
    return call(
        values_kernel,
        sds(9 * SLOTS // 128, 128),
        ins=[SMEM] + [VMEM] * 5,
        outs=VMEM,
    )(where, mine, near, wown, wnear, lev)


def adjoint_kernel(where_ref, v0, v1, innov_ref, weight_ref, hot_ref, wown_ref, wnear_ref, x_ref, c_ref, first_ref, second_ref):
    value = v0[...] + v1[...]

    def place(weight, row):
        line = jnp.concatenate([value[6 * row + a : 6 * row + a + 1] for a in range(6)], axis=1)
        weighted = weight_ref[row : row + 1] * (line - innov_ref[row : row + 1])
        hot = hot_ref[row]
        both = jnp.concatenate([hot * half for half in halves(weighted)], axis=0)
        out = nt(weight, both)
        return out[:, :128] + out[:, 128:]

    adj = []
    for v in range(V):
        c_ref[v] = place(wown_ref[v, :256], v)
        for n in range(2):
            rows = pl.ds(pl.multiple_of(where_ref[n], 32), 32)
            c_ref[v, rows] = c_ref[v, rows] + place(wnear_ref[n, v, :32], 3 * n + 3 + v)
        adj.append(jnp.concatenate([c_ref[v, :64], c_ref[v, 192:]], axis=0))
    first_low = where_ref[7] == 1
    for k in range(first_ref.shape[0]):
        total = x_ref[k, 0].astype(F32) * adj[0]
        for v in range(1, V):
            total = total + x_ref[k, v].astype(F32) * adj[v]
        low, high = total[:64], total[64:]
        first_ref[k] = jnp.where(first_low, low, high)
        second_ref[k] = jnp.where(first_low, high, low)


def adjoint(where, vals, innov, weight, hot, wown, wnear, x):
    members = HEAD_BACK
    return call(
        adjoint_kernel,
        (sds(V, 256, 128), sds(members, 64, 128), sds(members, 64, 128)),
        ins=[SMEM] + [VMEM] * 8,
        outs=(VMEM,) * 3,
    )(where, *vals, innov, weight, hot, wown, wnear, x)


def drop(smoothed, loc):
    high, low = halves(smoothed)
    return nn(high, loc) + nn(low, loc)


def back_kernel(where_ref, alpha_ref, ens_ref, c_ref, smat_ref, loc_ref, out_ref, edge_ref, first_ref, second_ref):
    low = where_ref[7] == 1
    smat = smat_ref[...]
    loc = loc_ref[...]
    for k in range(GROUP):
        back = ens_ref[k, 0].astype(F32) * c_ref[0]
        for v in range(1, V):
            back = back + ens_ref[k, v].astype(F32) * c_ref[v]
        first_ref[k] = jnp.where(low, back[:64], back[192:])
        second_ref[k] = jnp.where(low, back[192:], back[:64])
        full = alpha_ref[k].astype(F32) + drop(smooth(smat, back), loc)
        out_ref[k] = full
        edge_ref[k, :64] = full[:64]
        edge_ref[k, 64:] = full[192:]


def back_part(where, alpha, ensemble, c, smat, loc):
    members = alpha.shape[0]
    rest = pl.BlockSpec((GROUP, 64, 128), lambda i: (jnp.maximum(i - HEAD_BACK // GROUP, 0), 0, 0))
    return call(
        back_kernel,
        (
            sds(members, 256, 128),
            sds(members, 128, 128),
            sds(members - HEAD_BACK, 64, 128),
            sds(members - HEAD_BACK, 64, 128),
        ),
        grid=(members // GROUP,),
        ins=[
            SMEM,
            pl.BlockSpec((GROUP, 256, 128), lambda i: (i, 0, 0)),
            pl.BlockSpec((GROUP, V, 256, 128), lambda i: (i, 0, 0, 0)),
            pl.BlockSpec((V, 256, 128), lambda i: (0, 0, 0)),
            pl.BlockSpec((256, 256), lambda i: (0, 0)),
            pl.BlockSpec((128, 128), lambda i: (0, 0)),
        ],
        outs=(
            pl.BlockSpec((GROUP, 256, 128), lambda i: (i, 0, 0)),
            pl.BlockSpec((GROUP, 128, 128), lambda i: (i, 0, 0)),
            rest,
            rest,
        ),
    )(where, alpha, ensemble, c, smat, loc)


def last_kernel(start, first_ref, second_ref, edge_ref, hmat_ref, loc_ref, unused_ref, out_ref, held, sems):
    hmat = hmat_ref[...]
    loc = loc_ref[...]
    copies = []
    for g in range(first_ref.shape[0] // GROUP):
        for k in range(g * GROUP, (g + 1) * GROUP):
            halo = jnp.concatenate([first_ref[k], second_ref[k]], axis=0)
            full = edge_ref[start + k] + drop(smooth(hmat, halo), loc)
            held[k, 0] = full[:64]
            held[k, 1] = full[64:]
        here, there = pl.ds(g * GROUP, GROUP), pl.ds(start + g * GROUP, GROUP)
        for side in range(2):
            copies.append(
                pltpu.make_async_copy(held.at[here, side], out_ref.at[there, 3 * side], sems.at[g, side])
            )
            copies[-1].start()
    for copy in copies:
        copy.wait()


def last_part(start, first, second, edge, hmat, loc, out):
    count = first.shape[0]
    return call(
        functools.partial(last_kernel, start),
        sds(*out.shape),
        ins=[VMEM] * 5 + [ANY],
        outs=ANY,
        scratch=[pltpu.VMEM((count, 2, 64, 128), F32), pltpu.SemaphoreType.DMA((count // GROUP, 2))],
        aliases={5: 0},
    )(first, second, edge, hmat, loc, out)


def stencil(gap):
    gap = jnp.abs(gap)
    return jnp.where(gap == 0, 6.0, jnp.where(gap == 1, 4.0, jnp.where(gap == 2, 1.0, 0.0)))


def matrices(tile, tiles, first_high):
    def across(i, j):
        gap = stencil(i - j)
        return jnp.where((i == j) & ((i == 0) | (i == 31)), 5.0, gap)

    i = lax.broadcasted_iota(jnp.int32, (256, 256), 0)
    j = lax.broadcasted_iota(jnp.int32, (256, 256), 1)
    ri, rj = i // 32, j // 32
    ends = ((ri == 0) & (tile == 0)) | ((ri == 7) & (tile == tiles - 1))
    down = jnp.where((ri == rj) & ends, 5.0, stencil(ri - rj))
    smat = (down * across(i % 32, j % 32) * (1.0 / 256.0)).astype(BF16)
    i = lax.broadcasted_iota(jnp.int32, (128, 128), 0)
    j = lax.broadcasted_iota(jnp.int32, (128, 128), 1)
    ri = i // 32
    ri = jnp.where(ri < 2, ri, ri + 4)
    above = (j < 64) == first_high
    rj = jnp.where(above, 8, -2) + (j // 32) % 2
    there = (above & (tile < tiles - 1)) | (jnp.logical_not(above) & (tile > 0))
    hmat = jnp.where(there, stencil(ri - rj), 0.0) * across(i % 32, j % 32) * (1.0 / 256.0)
    return smat, hmat.astype(BF16)


def swap_first(x):
    return lax.ppermute(x, ("mem", "tile"), FIRST)


def swap_second(x):
    return lax.ppermute(x, ("mem", "tile"), SECOND)


def swap_near(x):
    return lax.ppermute(x, ("mem", "tile"), NEAR)


def swap_core(x):
    return lax.ppermute(x, "mem", [(m, m ^ 1) for m in range(MEMS)])


def swap_chip(x):
    return lax.ppermute(x, "mem", [(m, m ^ 2) for m in range(MEMS)])


def on_device(alpha, ensemble, loc_vert, obs_col, obs_lev, obs_count, innovation, obs_weight):
    members = alpha.shape[0]
    tile = lax.axis_index("tile")
    tiles = lax.axis_size("tile")
    even = tile % 2 == 0
    core = lax.axis_index("mem") % 2
    first_low = side_of_first()
    where = jnp.stack(
        [
            jnp.where(even, 7 * 32, 0),
            jnp.where(even, 0, 7 * 32),
            jnp.where(even, 8, -1),
            jnp.where(even, -1, 8),
            ((tile > 0) & (tile < tiles - 1)).astype(jnp.int32),
            tile % 2,
            tile,
            first_low,
            7 * 32 * (1 - (tile + core) % 2),
            7 * 32 * ((tile + core) % 2),
            core,
        ]
    ).astype(jnp.int32)
    flat = alpha.reshape(members, 256, 128)
    flat_ens = ensemble.reshape(members, V, 256, 128)

    quarters = alpha.reshape(members, 4, 64, 128)
    send_first, send_second, token = send_part(quarters)
    first, second = swap_first(send_first), swap_second(send_second)
    inner, own_edge, x, smat, hmat = own_part(where, flat, flat_ens, loc_vert, token)
    send_first, send_second, own_obs = rest_part(
        obs_count, obs_col, obs_lev, innovation, obs_weight, quarters, hmat
    )
    first_rest, second_rest = swap_first(send_first), swap_second(send_second)
    head = head_part(first, second, own_edge, x, hmat, loc_vert)
    inc, keep, give = edge_part(where, first_rest, second_rest, own_edge, x, hmat, loc_vert, inner, head)
    got = swap_core(give)
    edges = keep + got[: V * 32]
    near = swap_near(edges)
    wown, wnear, lev, innov, weight, hot = weights(where, own_obs, give, got, edges)
    mine = mine_part(where, inc, wown, wnear, lev)
    vals = values(where, mine, near, wown, wnear, lev)
    vals = vals + swap_core(vals)
    vals = vals, swap_chip(vals)
    c, back_first, back_second = adjoint(where, vals, innov, weight, hot, wown, wnear, x)
    halo_first, halo_second = swap_first(back_first), swap_second(back_second)
    out, edge, back_first, back_second = back_part(where, flat, flat_ens, c, smat, loc_vert)
    rest_first, rest_second = swap_first(back_first), swap_second(back_second)
    out = last_part(0, halo_first, halo_second, edge, hmat, loc_vert, out.reshape(members, 4, 64, 128))
    out = last_part(HEAD_BACK, rest_first, rest_second, edge, hmat, loc_vert, out)
    return out.reshape(members, 8, 32, 128)


def solution(mesh):
    in_specs = (
        P("mem", "tile", None, None),
        P("mem", None, "tile", None, None),
        P(),
        P("tile", None),
        P("tile", None),
        P("tile"),
        P("tile", None),
        P("tile", None),
    )
    out_specs = P("mem", "tile", None, None)
    return jax.shard_map(
        on_device, mesh=mesh, in_specs=in_specs, out_specs=out_specs, check_vma=False
    )
```

```python
import functools

import jax
import jax.numpy as jnp
from jax import lax
from jax.experimental import pallas as pl
from jax.experimental.pallas import tpu as pltpu
from jax.sharding import PartitionSpec as P

V = 3
F32 = jnp.float32
BF16 = jnp.bfloat16
SLOTS = 768
GROUP = 4
HEAD = 16
HEAD_BACK = 12
OBS = 80
HALF = OBS // 2

TILES = 64
MEMS = 4


def partners(odd, spare):
    pairs = []
    for m in range(MEMS):
        for t in range(TILES):
            beside = ((t - 1) ^ 1) + 1 if odd(m) else t ^ 1
            there = (m, beside) if 0 <= beside < TILES else (m ^ spare, t)
            pairs.append((TILES * m + t, TILES * there[0] + there[1]))
    return pairs


FIRST = partners(lambda m: True, 1)
SECOND = partners(lambda m: False, 1)
NEAR = partners(lambda m: m % 2 == 1, 2)


def nn(a, b):
    return lax.dot_general(a, b, (((1,), (0,)), ((), ())), preferred_element_type=F32)


def nt(a, b):
    return lax.dot_general(a, b, (((1,), (1,)), ((), ())), preferred_element_type=F32)


def tn(a, b):
    return lax.dot_general(a, b, (((0,), (0,)), ((), ())), preferred_element_type=F32)


def halves(x):
    high = x.astype(BF16)
    low = (x - high.astype(F32)).astype(BF16)
    return high, low


def lift(smoothed, loc):
    high, low = halves(smoothed)
    return nt(high, loc) + nt(low, loc)


def call(kernel, out, grid=None, ins=None, outs=None, scratch=(), aliases=None, cost=1000, vmem=16):
    kw = {}
    if grid is not None:
        kw["grid"] = grid
    return pl.pallas_call(
        kernel,
        out_shape=out,
        in_specs=ins,
        out_specs=outs if outs is not None else jax.tree.map(lambda o: VMEM, out),
        scratch_shapes=scratch,
        input_output_aliases=aliases or {},
        compiler_params=pltpu.CompilerParams(vmem_limit_bytes=vmem * 1024 * 1024),
        cost_estimate=pl.CostEstimate(flops=cost, bytes_accessed=cost, transcendentals=0),
        **kw,
    )


def sds(*shape, dtype=F32):
    return jax.ShapeDtypeStruct(shape, dtype)


ANY = pl.BlockSpec(memory_space=pl.ANY)
SMEM = pl.BlockSpec(memory_space=pltpu.SMEM)
VMEM = pl.BlockSpec(memory_space=pltpu.VMEM)
HBM = pl.BlockSpec(memory_space=pltpu.HBM)


def smooth(matrix, field):
    both = jnp.concatenate(halves(field), axis=1)
    out = nn(matrix, both)
    return out[:, :128] + out[:, 128:]


def side_of_first():
    return lax.rem(lax.axis_index("tile") + 1, 2)


def sort_observations(count, col_ref, lev_ref, innov_ref, weight_ref, out_ref):
    slots = col_ref.shape[1]
    live = lax.broadcasted_iota(jnp.int32, (1, slots), 1) < count
    rows = []
    for field in (
        col_ref[...].astype(F32),
        lev_ref[...].astype(F32),
        innov_ref[...],
        jnp.where(live, weight_ref[...], 0.0),
    ):
        field = jnp.concatenate([field, jnp.zeros((1, V * SLOTS - slots), F32)], axis=1)
        rows += [field[:, 384 * a : 384 * a + 384] for a in range(6)]
    rest = jnp.concatenate(rows, axis=0)
    i = lax.broadcasted_iota(jnp.int32, (384, 384), 0)
    j = lax.broadcasted_iota(jnp.int32, (384, 384), 1)
    order = (i == 3 * (j % 128) + j // 128).astype(F32).astype(BF16)
    total = jnp.zeros((24, 384), F32)
    for piece in range(3):
        part = rest.astype(BF16)
        rest = rest - part.astype(F32)
        total = total + nn(part, order)
    out_ref[72:] = jnp.zeros((OBS - 72, 128), F32)
    for f in range(4):
        for a in range(6):
            for v in range(V):
                row = 6 * (V * f + v) + a
                out_ref[row : row + 1] = total[6 * f + a : 6 * f + a + 1, 128 * v : 128 * v + 128]


def send_kernel(quarters_ref, first_ref, second_ref, token_ref, edges, rows, fetched, sent):
    token_ref[...] = jnp.zeros_like(token_ref)
    low = side_of_first()
    members = pl.ds(0, HEAD)
    fetches = [
        pltpu.make_async_copy(quarters_ref.at[members, quarter], edges.at[n], fetched.at[n])
        for n, quarter in enumerate((3 * (1 - low), 3 * low))
    ]
    sends = [pltpu.make_async_copy(rows.at[n], ref, sent.at[n]) for n, ref in enumerate((first_ref, second_ref))]
    for fetch in fetches:
        fetch.start()
    for n in range(2):
        fetches[n].wait()
        for k in range(HEAD):
            rows[n, 64 * k : 64 * k + 64] = edges[n, k].astype(F32)
        sends[n].start()
    for send in sends:
        send.wait()


def send_part(quarters):
    return call(
        send_kernel,
        (sds(64 * HEAD, 128), sds(64 * HEAD, 128), sds(8, 128)),
        ins=[HBM],
        outs=(HBM, HBM, VMEM),
        scratch=[
            pltpu.VMEM((2, HEAD, 64, 128), BF16),
            pltpu.VMEM((2, 64 * HEAD, 128), F32),
            pltpu.SemaphoreType.DMA((2,)),
            pltpu.SemaphoreType.DMA((2,)),
        ],
        vmem=56,
    )(quarters)


def rest_kernel(count_ref, col_ref, lev_ref, innov_ref, weight_ref, quarters_ref, after_ref, first_ref, second_ref, obs_ref, edges, sems):
    count = edges.shape[1]
    members = pl.ds(HEAD, count)
    copies = [pltpu.make_async_copy(quarters_ref.at[members, 3 * n], edges.at[n], sems.at[n]) for n in range(2)]
    for copy in copies:
        copy.start()
    sort_observations(count_ref[0], col_ref, lev_ref, innov_ref, weight_ref, obs_ref)
    core = lax.rem(lax.axis_index("mem"), 2)
    half = obs_ref[pl.ds(pl.multiple_of(HALF * core, 8), HALF)]
    first_ref[64 * count :] = half
    second_ref[64 * count :] = half
    for copy in copies:
        copy.wait()
    low = side_of_first()
    for k in range(count):
        first_ref[64 * k : 64 * k + 64] = edges[1 - low, k].astype(F32)
        second_ref[64 * k : 64 * k + 64] = edges[low, k].astype(F32)


def rest_part(count, col, lev, innov, weight, quarters, after):
    members = quarters.shape[0] - HEAD
    return call(
        rest_kernel,
        (sds(64 * members + HALF, 128), sds(64 * members + HALF, 128), sds(OBS, 128)),
        ins=[SMEM] + [VMEM] * 4 + [ANY, VMEM],
        outs=(VMEM,) * 3,
        scratch=[pltpu.VMEM((2, members, 64, 128), BF16), pltpu.SemaphoreType.DMA((2,))],
    )(count, col, lev, innov, weight, quarters, after)


def own_kernel(where_ref, alpha_ref, ens_ref, loc_ref, after_ref, inner_ref, edge_ref, x_ref, smat_ref, hmat_ref):
    @pl.when(pl.program_id(0) == 0)
    def _():
        inner_ref[...] = jnp.zeros_like(inner_ref)
        smat, hmat = matrices(where_ref[6], TILES, where_ref[7] == 0)
        smat_ref[...] = smat
        hmat_ref[...] = hmat

    smat = smat_ref[...]
    loc = loc_ref[...]
    total = [inner_ref[v] for v in range(V)]
    for k in range(GROUP):
        full = lift(nn(smat, alpha_ref[k]), loc)
        edge_ref[k, :64] = full[:64]
        edge_ref[k, 64:] = full[192:]
        lifted = full[64:192].astype(BF16).astype(F32)
        for v in range(V):
            total[v] = total[v] + ens_ref[k, v, 64:192].astype(F32) * lifted
            x_ref[k, v, :64] = ens_ref[k, v, :64]
            x_ref[k, v, 64:] = ens_ref[k, v, 192:]
    for v in range(V):
        inner_ref[v] = total[v]


def own_part(where, alpha, ensemble, loc, after):
    members = alpha.shape[0]
    whole = lambda *shape: pl.BlockSpec(shape, lambda i: (0,) * len(shape))
    return call(
        own_kernel,
        (
            sds(V, 128, 128),
            sds(members, 128, 128),
            sds(members, V, 128, 128, dtype=BF16),
            sds(256, 256, dtype=BF16),
            sds(128, 128, dtype=BF16),
        ),
        grid=(members // GROUP,),
        ins=[
            SMEM,
            pl.BlockSpec((GROUP, 256, 128), lambda i: (i, 0, 0)),
            pl.BlockSpec((GROUP, V, 256, 128), lambda i: (i, 0, 0, 0)),
            whole(128, 128),
            whole(8, 128),
        ],
        outs=(
            whole(V, 128, 128),
            pl.BlockSpec((GROUP, 128, 128), lambda i: (i, 0, 0)),
            pl.BlockSpec((GROUP, V, 128, 128), lambda i: (i, 0, 0, 0)),
            whole(256, 256),
            whole(128, 128),
        ),
    )(where, alpha, ensemble, loc, after)


def edge_terms(first_ref, second_ref, own_ref, x_ref, hmat_ref, loc_ref, start, count, total):
    hmat = hmat_ref[...]
    loc = loc_ref[...]
    for k in range(count):
        rows = slice(64 * k, 64 * k + 64)
        halo = jnp.concatenate([first_ref[rows].astype(BF16), second_ref[rows].astype(BF16)], axis=0)
        lifted = (own_ref[start + k] + lift(nn(hmat, halo), loc)).astype(BF16).astype(F32)
        for v in range(V):
            total[v] = total[v] + x_ref[start + k, v].astype(F32) * lifted
    return total


def head_kernel(first_ref, second_ref, own_ref, x_ref, hmat_ref, loc_ref, total_ref):
    zeros = [jnp.zeros((128, 128), F32) for v in range(V)]
    total = edge_terms(first_ref, second_ref, own_ref, x_ref, hmat_ref, loc_ref, 0, HEAD, zeros)
    for v in range(V):
        total_ref[v] = total[v]


def head_part(first, second, own, x, hmat, loc):
    return call(head_kernel, sds(V, 128, 128), ins=[VMEM] * 6, outs=VMEM)(first, second, own, x, hmat, loc)


def edge_kernel(where_ref, first_ref, second_ref, own_ref, x_ref, hmat_ref, loc_ref, inner_ref, head_ref, inc_ref, keep_ref, give_ref):
    total = [head_ref[v] for v in range(V)]
    total = edge_terms(first_ref, second_ref, own_ref, x_ref, hmat_ref, loc_ref, HEAD, own_ref.shape[0] - HEAD, total)
    for v in range(V):
        inc_ref[v, :64] = total[v][:64]
        inc_ref[v, 64:192] = inner_ref[v]
        inc_ref[v, 192:] = total[v][64:]
        keep_ref[32 * v : 32 * v + 32] = inc_ref[v, pl.ds(pl.multiple_of(where_ref[8], 32), 32)]
        give_ref[32 * v : 32 * v + 32] = inc_ref[v, pl.ds(pl.multiple_of(where_ref[9], 32), 32)]
    end = first_ref.shape[0] - HALF
    give_ref[32 * V : 32 * V + HALF] = first_ref[end:]
    give_ref[32 * V + HALF :] = second_ref[end:]


def edge_part(where, first, second, own, x, hmat, loc, inner, head):
    return call(
        edge_kernel,
        (sds(V, 256, 128), sds(V * 32, 128), sds(V * 32 + OBS, 128)),
        ins=[SMEM] + [VMEM] * 8,
        outs=(VMEM,) * 3,
    )(where, first, second, own, x, hmat, loc, inner, head)


def tent(distance):
    return jnp.maximum(1.0 - jnp.abs(distance), 0.0)


def weights_kernel(where_ref, own_ref, here_ref, there_ref, after_ref, wown_ref, wnear_ref, lev_ref, innov_ref, weight_ref, hot_ref, o_ref, e_ref):
    core = where_ref[10]
    for half, ref in ((core, here_ref), (1 - core, there_ref)):
        rows = pl.ds(pl.multiple_of(HALF * half, 8), HALF)
        o_ref[rows] = ref[32 * V : 32 * V + HALF]
        e_ref[rows] = ref[32 * V + HALF :]
    level = lax.broadcasted_iota(jnp.int32, (128, SLOTS), 0).astype(F32)
    even_row = where_ref[2].astype(F32)
    odd_row = where_ref[3].astype(F32)
    odd_there = where_ref[4].astype(F32)
    cell = lax.broadcasted_iota(jnp.int32, (32, SLOTS), 0).astype(F32)

    def line(ref, field, v):
        at = 6 * (V * field + v)
        return jnp.concatenate([ref[at + a : at + a + 1] for a in range(6)], axis=1)

    def columns(code):
        row = jnp.floor(code * (1.0 / 64.0))
        column = code - 64.0 * row
        return row, tent(cell - (column * 0.5 - 0.25))

    for v in range(V):
        row, across = columns(line(own_ref, 0, v))
        middle = row * 0.5 - 0.25
        for r in range(8):
            wown_ref[v, 32 * r : 32 * r + 32] = (tent(r - middle) * across).astype(BF16)
        wown_ref[v, 256:288] = (tent(even_row - middle) * across).astype(BF16)
        wown_ref[v, 288:320] = (tent(odd_row - middle) * odd_there * across).astype(BF16)
        for n, ref in enumerate((e_ref, o_ref)):
            row, across = columns(line(ref, 0, v))
            wnear_ref[n, v, :32] = (0.25 * across).astype(BF16)
            wnear_ref[n, v, 32:] = (0.75 * across).astype(BF16)
    is_odd = where_ref[5]
    for n, ref in enumerate((own_ref, e_ref, o_ref)):
        for v in range(V):
            row = slice(3 * n + v, 3 * n + v + 1)
            lev = line(ref, 1, v)
            lev_ref[row] = lev
            hot_ref[3 * n + v] = jnp.where(level == lev, 1.0, 0.0).astype(BF16)
            innov_ref[row] = line(ref, 2, v)
            weight = line(ref, 3, v)
            if n > 0:
                code = line(ref, 0, v)
                first = is_odd == (0 if n == 1 else 1)
                at_edge = jnp.where(first, code, 1023.0 - code) < 64.0
                there = at_edge & ((n == 1) | (where_ref[4] == 1))
                weight = jnp.where(there, weight, 0.0)
            weight_ref[row] = weight


def weights(where, own, here, there, after):
    return call(
        weights_kernel,
        (
            sds(V, 320, SLOTS, dtype=BF16),
            sds(2, V, 64, SLOTS, dtype=BF16),
            sds(9, SLOTS),
            sds(9, SLOTS),
            sds(9, SLOTS),
            sds(9, 128, SLOTS, dtype=BF16),
        ),
        ins=[SMEM] + [VMEM] * 4,
        scratch=[pltpu.VMEM((OBS, 128), F32), pltpu.VMEM((OBS, 128), F32)],
    )(where, own, here, there, after)


def picker(lev_ref):
    level = lax.broadcasted_iota(jnp.int32, (128, SLOTS), 0).astype(F32)

    def pick(cells, weight, row):
        both = jnp.concatenate(halves(cells), axis=0)
        at_all = tn(both, jnp.concatenate([weight, weight], axis=0))
        hot = level == lev_ref[pl.ds(row, 1), :]
        return jnp.sum(jnp.where(hot, at_all, 0.0), axis=0, keepdims=True)

    return pick


def mine_kernel(where_ref, inc_ref, wown_ref, wnear_ref, lev_ref, out_ref):
    pick = picker(lev_ref)
    for v in range(V):
        out_ref[v : v + 1] = pick(inc_ref[v], wown_ref[v, :256], v)
        for n in range(2):
            cells = inc_ref[v, pl.ds(pl.multiple_of(where_ref[n], 32), 32)]
            row = 3 * n + 3 + v
            out_ref[row : row + 1] = pick(cells, wnear_ref[n, v, :32], row)


def mine_part(where, inc, wown, wnear, lev):
    return call(
        mine_kernel,
        sds(9, SLOTS),
        ins=[SMEM] + [VMEM] * 4,
        outs=VMEM,
    )(where, inc, wown, wnear, lev)


def values_kernel(where_ref, mine_ref, near_ref, wown_ref, wnear_ref, lev_ref, out_ref):
    pick = picker(lev_ref)
    core = where_ref[10]

    def put(row, line):
        for a in range(6):
            out_ref[pl.ds(6 * row + a, 1)] = line[:, 128 * a : 128 * a + 128]

    for v in range(V):
        for n in range(2):
            row = 3 * n + 3 + v
            put(row, mine_ref[row : row + 1])
    for v in range(V):
        halo = pl.ds(pl.multiple_of(256 + 32 * core, 32), 32)
        put(v, mine_ref[v : v + 1] + pick(near_ref[32 * v : 32 * v + 32], wown_ref[v, halo], v))
        row = 3 * core + 3 + v
        put(row, mine_ref[pl.ds(row, 1)] + pick(near_ref[32 * v : 32 * v + 32], wnear_ref[core, v, 32:], row))


def values(where, mine, near, wown, wnear, lev):
    return call(
        values_kernel,
        sds(9 * SLOTS // 128, 128),
        ins=[SMEM] + [VMEM] * 5,
        outs=VMEM,
    )(where, mine, near, wown, wnear, lev)


def adjoint_kernel(where_ref, v0, v1, innov_ref, weight_ref, hot_ref, wown_ref, wnear_ref, x_ref, c_ref, first_ref, second_ref):
    value = v0[...] + v1[...]

    def place(weight, row):
        line = jnp.concatenate([value[6 * row + a : 6 * row + a + 1] for a in range(6)], axis=1)
        weighted = weight_ref[row : row + 1] * (line - innov_ref[row : row + 1])
        hot = hot_ref[row]
        both = jnp.concatenate([hot * half for half in halves(weighted)], axis=0)
        out = nt(weight, both)
        return out[:, :128] + out[:, 128:]

    adj = []
    for v in range(V):
        c_ref[v] = place(wown_ref[v, :256], v)
        for n in range(2):
            rows = pl.ds(pl.multiple_of(where_ref[n], 32), 32)
            c_ref[v, rows] = c_ref[v, rows] + place(wnear_ref[n, v, :32], 3 * n + 3 + v)
        adj.append(jnp.concatenate([c_ref[v, :64], c_ref[v, 192:]], axis=0))
    first_low = where_ref[7] == 1
    for k in range(first_ref.shape[0]):
        total = x_ref[k, 0].astype(F32) * adj[0]
        for v in range(1, V):
            total = total + x_ref[k, v].astype(F32) * adj[v]
        low, high = total[:64], total[64:]
        first_ref[k] = jnp.where(first_low, low, high)
        second_ref[k] = jnp.where(first_low, high, low)


def adjoint(where, vals, innov, weight, hot, wown, wnear, x):
    members = HEAD_BACK
    return call(
        adjoint_kernel,
        (sds(V, 256, 128), sds(members, 64, 128), sds(members, 64, 128)),
        ins=[SMEM] + [VMEM] * 8,
        outs=(VMEM,) * 3,
    )(where, *vals, innov, weight, hot, wown, wnear, x)


def drop(smoothed, loc):
    high, low = halves(smoothed)
    return nn(high, loc) + nn(low, loc)


def back_kernel(where_ref, alpha_ref, ens_ref, c_ref, smat_ref, loc_ref, out_ref, edge_ref, first_ref, second_ref):
    low = where_ref[7] == 1
    smat = smat_ref[...]
    loc = loc_ref[...]
    for k in range(GROUP):
        back = ens_ref[k, 0].astype(F32) * c_ref[0]
        for v in range(1, V):
            back = back + ens_ref[k, v].astype(F32) * c_ref[v]
        first_ref[k] = jnp.where(low, back[:64], back[192:])
        second_ref[k] = jnp.where(low, back[192:], back[:64])
        full = alpha_ref[k].astype(F32) + drop(smooth(smat, back), loc)
        out_ref[k] = full
        edge_ref[k, :64] = full[:64]
        edge_ref[k, 64:] = full[192:]


def back_part(where, alpha, ensemble, c, smat, loc):
    members = alpha.shape[0]
    rest = pl.BlockSpec((GROUP, 64, 128), lambda i: (jnp.maximum(i - HEAD_BACK // GROUP, 0), 0, 0))
    return call(
        back_kernel,
        (
            sds(members, 256, 128),
            sds(members, 128, 128),
            sds(members - HEAD_BACK, 64, 128),
            sds(members - HEAD_BACK, 64, 128),
        ),
        grid=(members // GROUP,),
        ins=[
            SMEM,
            pl.BlockSpec((GROUP, 256, 128), lambda i: (i, 0, 0)),
            pl.BlockSpec((GROUP, V, 256, 128), lambda i: (i, 0, 0, 0)),
            pl.BlockSpec((V, 256, 128), lambda i: (0, 0, 0)),
            pl.BlockSpec((256, 256), lambda i: (0, 0)),
            pl.BlockSpec((128, 128), lambda i: (0, 0)),
        ],
        outs=(
            pl.BlockSpec((GROUP, 256, 128), lambda i: (i, 0, 0)),
            pl.BlockSpec((GROUP, 128, 128), lambda i: (i, 0, 0)),
            rest,
            rest,
        ),
    )(where, alpha, ensemble, c, smat, loc)


def last_kernel(start, first_ref, second_ref, edge_ref, hmat_ref, loc_ref, unused_ref, out_ref, held, sems):
    hmat = hmat_ref[...]
    loc = loc_ref[...]
    copies = []
    for g in range(first_ref.shape[0] // GROUP):
        for k in range(g * GROUP, (g + 1) * GROUP):
            halo = jnp.concatenate([first_ref[k], second_ref[k]], axis=0)
            full = edge_ref[start + k] + drop(smooth(hmat, halo), loc)
            held[k, 0] = full[:64]
            held[k, 1] = full[64:]
        here, there = pl.ds(g * GROUP, GROUP), pl.ds(start + g * GROUP, GROUP)
        for side in range(2):
            copies.append(
                pltpu.make_async_copy(held.at[here, side], out_ref.at[there, 3 * side], sems.at[g, side])
            )
            copies[-1].start()
    for copy in copies:
        copy.wait()


def last_part(start, first, second, edge, hmat, loc, out):
    count = first.shape[0]
    return call(
        functools.partial(last_kernel, start),
        sds(*out.shape),
        ins=[VMEM] * 5 + [ANY],
        outs=ANY,
        scratch=[pltpu.VMEM((count, 2, 64, 128), F32), pltpu.SemaphoreType.DMA((count // GROUP, 2))],
        aliases={5: 0},
    )(first, second, edge, hmat, loc, out)


def stencil(gap):
    gap = jnp.abs(gap)
    return jnp.where(gap == 0, 6.0, jnp.where(gap == 1, 4.0, jnp.where(gap == 2, 1.0, 0.0)))


def matrices(tile, tiles, first_high):
    def across(i, j):
        gap = stencil(i - j)
        return jnp.where((i == j) & ((i == 0) | (i == 31)), 5.0, gap)

    i = lax.broadcasted_iota(jnp.int32, (256, 256), 0)
    j = lax.broadcasted_iota(jnp.int32, (256, 256), 1)
    ri, rj = i // 32, j // 32
    ends = ((ri == 0) & (tile == 0)) | ((ri == 7) & (tile == tiles - 1))
    down = jnp.where((ri == rj) & ends, 5.0, stencil(ri - rj))
    smat = (down * across(i % 32, j % 32) * (1.0 / 256.0)).astype(BF16)
    i = lax.broadcasted_iota(jnp.int32, (128, 128), 0)
    j = lax.broadcasted_iota(jnp.int32, (128, 128), 1)
    ri = i // 32
    ri = jnp.where(ri < 2, ri, ri + 4)
    above = (j < 64) == first_high
    rj = jnp.where(above, 8, -2) + (j // 32) % 2
    there = (above & (tile < tiles - 1)) | (jnp.logical_not(above) & (tile > 0))
    hmat = jnp.where(there, stencil(ri - rj), 0.0) * across(i % 32, j % 32) * (1.0 / 256.0)
    return smat, hmat.astype(BF16)


def swap_first(x):
    return lax.ppermute(x, ("mem", "tile"), FIRST)


def swap_second(x):
    return lax.ppermute(x, ("mem", "tile"), SECOND)


def swap_near(x):
    return lax.ppermute(x, ("mem", "tile"), NEAR)


def swap_core(x):
    return lax.ppermute(x, "mem", [(m, m ^ 1) for m in range(MEMS)])


def swap_chip(x):
    return lax.ppermute(x, "mem", [(m, m ^ 2) for m in range(MEMS)])


def on_device(alpha, ensemble, loc_vert, obs_col, obs_lev, obs_count, innovation, obs_weight):
    members = alpha.shape[0]
    tile = lax.axis_index("tile")
    tiles = lax.axis_size("tile")
    even = tile % 2 == 0
    core = lax.axis_index("mem") % 2
    first_low = side_of_first()
    where = jnp.stack(
        [
            jnp.where(even, 7 * 32, 0),
            jnp.where(even, 0, 7 * 32),
            jnp.where(even, 8, -1),
            jnp.where(even, -1, 8),
            ((tile > 0) & (tile < tiles - 1)).astype(jnp.int32),
            tile % 2,
            tile,
            first_low,
            7 * 32 * (1 - (tile + core) % 2),
            7 * 32 * ((tile + core) % 2),
            core,
        ]
    ).astype(jnp.int32)
    flat = alpha.reshape(members, 256, 128)
    flat_ens = ensemble.reshape(members, V, 256, 128)

    quarters = alpha.reshape(members, 4, 64, 128)
    send_first, send_second, token = send_part(quarters)
    first, second = swap_first(send_first), swap_second(send_second)
    inner, own_edge, x, smat, hmat = own_part(where, flat, flat_ens, loc_vert, token)
    send_first, send_second, own_obs = rest_part(
        obs_count, obs_col, obs_lev, innovation, obs_weight, quarters, hmat
    )
    first_rest, second_rest = swap_first(send_first), swap_second(send_second)
    head = head_part(first, second, own_edge, x, hmat, loc_vert)
    inc, keep, give = edge_part(where, first_rest, second_rest, own_edge, x, hmat, loc_vert, inner, head)
    got = swap_core(give)
    edges = keep + got[: V * 32]
    near = swap_near(edges)
    wown, wnear, lev, innov, weight, hot = weights(where, own_obs, give, got, edges)
    mine = mine_part(where, inc, wown, wnear, lev)
    vals = values(where, mine, near, wown, wnear, lev)
    vals = vals + swap_core(vals)
    vals = vals, swap_chip(vals)
    c, back_first, back_second = adjoint(where, vals, innov, weight, hot, wown, wnear, x)
    halo_first, halo_second = swap_first(back_first), swap_second(back_second)
    out, edge, back_first, back_second = back_part(where, flat, flat_ens, c, smat, loc_vert)
    rest_first, rest_second = swap_first(back_first), swap_second(back_second)
    out = last_part(0, halo_first, halo_second, edge, hmat, loc_vert, out.reshape(members, 4, 64, 128))
    out = last_part(HEAD_BACK, rest_first, rest_second, edge, hmat, loc_vert, out)
    return out.reshape(members, 8, 32, 128)


def solution(mesh):
    in_specs = (
        P("mem", "tile", None, None),
        P("mem", None, "tile", None, None),
        P(),
        P("tile", None),
        P("tile", None),
        P("tile"),
        P("tile", None),
        P("tile", None),
    )
    out_specs = P("mem", "tile", None, None)
    return jax.shard_map(
        on_device, mesh=mesh, in_specs=in_specs, out_specs=out_specs, check_vma=False
    )
```

```python
import functools

import jax
import jax.numpy as jnp
from jax import lax
from jax.experimental import pallas as pl
from jax.experimental.pallas import tpu as pltpu
from jax.sharding import PartitionSpec as P

V = 3
F32 = jnp.float32
BF16 = jnp.bfloat16
SLOTS = 768
GROUP = 4
HEAD = 16
HEAD_BACK = 12
OBS = 80
HALF = OBS // 2

TILES = 64
MEMS = 4


def partners(odd, spare):
    pairs = []
    for m in range(MEMS):
        for t in range(TILES):
            beside = ((t - 1) ^ 1) + 1 if odd(m) else t ^ 1
            there = (m, beside) if 0 <= beside < TILES else (m ^ spare, t)
            pairs.append((TILES * m + t, TILES * there[0] + there[1]))
    return pairs


FIRST = partners(lambda m: True, 1)
SECOND = partners(lambda m: False, 1)
NEAR = partners(lambda m: m % 2 == 1, 2)


def nn(a, b):
    return lax.dot_general(a, b, (((1,), (0,)), ((), ())), preferred_element_type=F32)


def nt(a, b):
    return lax.dot_general(a, b, (((1,), (1,)), ((), ())), preferred_element_type=F32)


def tn(a, b):
    return lax.dot_general(a, b, (((0,), (0,)), ((), ())), preferred_element_type=F32)


def halves(x):
    high = x.astype(BF16)
    low = (x - high.astype(F32)).astype(BF16)
    return high, low


def lift(smoothed, loc):
    high, low = halves(smoothed)
    return nt(high, loc) + nt(low, loc)


def call(kernel, out, grid=None, ins=None, outs=None, scratch=(), aliases=None, cost=1000, vmem=16):
    kw = {}
    if grid is not None:
        kw["grid"] = grid
    return pl.pallas_call(
        kernel,
        out_shape=out,
        in_specs=ins,
        out_specs=outs if outs is not None else jax.tree.map(lambda o: VMEM, out),
        scratch_shapes=scratch,
        input_output_aliases=aliases or {},
        compiler_params=pltpu.CompilerParams(vmem_limit_bytes=vmem * 1024 * 1024),
        cost_estimate=pl.CostEstimate(flops=cost, bytes_accessed=cost, transcendentals=0),
        **kw,
    )


def sds(*shape, dtype=F32):
    return jax.ShapeDtypeStruct(shape, dtype)


ANY = pl.BlockSpec(memory_space=pl.ANY)
SMEM = pl.BlockSpec(memory_space=pltpu.SMEM)
VMEM = pl.BlockSpec(memory_space=pltpu.VMEM)
HBM = pl.BlockSpec(memory_space=pltpu.HBM)


def smooth(matrix, field):
    both = jnp.concatenate(halves(field), axis=1)
    out = nn(matrix, both)
    return out[:, :128] + out[:, 128:]


def side_of_first():
    return lax.rem(lax.axis_index("tile") + 1, 2)


def sort_observations(count, col_ref, lev_ref, innov_ref, weight_ref, out_ref):
    slots = col_ref.shape[1]
    live = lax.broadcasted_iota(jnp.int32, (1, slots), 1) < count
    rows = []
    for field in (
        col_ref[...].astype(F32),
        lev_ref[...].astype(F32),
        innov_ref[...],
        jnp.where(live, weight_ref[...], 0.0),
    ):
        field = jnp.concatenate([field, jnp.zeros((1, V * SLOTS - slots), F32)], axis=1)
        rows += [field[:, 384 * a : 384 * a + 384] for a in range(6)]
    rest = jnp.concatenate(rows, axis=0)
    i = lax.broadcasted_iota(jnp.int32, (384, 384), 0)
    j = lax.broadcasted_iota(jnp.int32, (384, 384), 1)
    order = (i == 3 * (j % 128) + j // 128).astype(F32).astype(BF16)
    total = jnp.zeros((24, 384), F32)
    for piece in range(3):
        part = rest.astype(BF16)
        rest = rest - part.astype(F32)
        total = total + nn(part, order)
    out_ref[72:] = jnp.zeros((OBS - 72, 128), F32)
    for f in range(4):
        for a in range(6):
            for v in range(V):
                row = 6 * (V * f + v) + a
                out_ref[row : row + 1] = total[6 * f + a : 6 * f + a + 1, 128 * v : 128 * v + 128]


def send_kernel(quarters_ref, first_ref, second_ref, token_ref, edges, sems):
    members = pl.ds(0, HEAD)
    copies = [pltpu.make_async_copy(quarters_ref.at[members, 3 * n], edges.at[n], sems.at[n]) for n in range(2)]
    for copy in copies:
        copy.start()
    token_ref[...] = jnp.zeros_like(token_ref)
    for copy in copies:
        copy.wait()
    low = side_of_first()
    for k in range(HEAD):
        first_ref[64 * k : 64 * k + 64] = edges[1 - low, k].astype(F32)
        second_ref[64 * k : 64 * k + 64] = edges[low, k].astype(F32)


def send_part(quarters):
    return call(
        send_kernel,
        (sds(64 * HEAD, 128), sds(64 * HEAD, 128), sds(8, 128)),
        ins=[HBM],
        outs=(VMEM,) * 3,
        scratch=[pltpu.VMEM((2, HEAD, 64, 128), BF16), pltpu.SemaphoreType.DMA((2,))],
        vmem=56,
    )(quarters)


def rest_kernel(count_ref, col_ref, lev_ref, innov_ref, weight_ref, quarters_ref, after_ref, first_ref, second_ref, obs_ref, edges, sems):
    count = edges.shape[1]
    members = pl.ds(HEAD, count)
    copies = [pltpu.make_async_copy(quarters_ref.at[members, 3 * n], edges.at[n], sems.at[n]) for n in range(2)]
    for copy in copies:
        copy.start()
    sort_observations(count_ref[0], col_ref, lev_ref, innov_ref, weight_ref, obs_ref)
    core = lax.rem(lax.axis_index("mem"), 2)
    half = obs_ref[pl.ds(pl.multiple_of(HALF * core, 8), HALF)]
    first_ref[64 * count :] = half
    second_ref[64 * count :] = half
    for copy in copies:
        copy.wait()
    low = side_of_first()
    for k in range(count):
        first_ref[64 * k : 64 * k + 64] = edges[1 - low, k].astype(F32)
        second_ref[64 * k : 64 * k + 64] = edges[low, k].astype(F32)


def rest_part(count, col, lev, innov, weight, quarters, after):
    members = quarters.shape[0] - HEAD
    return call(
        rest_kernel,
        (sds(64 * members + HALF, 128), sds(64 * members + HALF, 128), sds(OBS, 128)),
        ins=[SMEM] + [VMEM] * 4 + [ANY, VMEM],
        outs=(VMEM,) * 3,
        scratch=[pltpu.VMEM((2, members, 64, 128), BF16), pltpu.SemaphoreType.DMA((2,))],
    )(count, col, lev, innov, weight, quarters, after)


def own_kernel(where_ref, alpha_ref, ens_ref, loc_ref, after_ref, inner_ref, edge_ref, x_ref, smat_ref, hmat_ref):
    @pl.when(pl.program_id(0) == 0)
    def _():
        inner_ref[...] = jnp.zeros_like(inner_ref)
        smat, hmat = matrices(where_ref[6], TILES, where_ref[7] == 0)
        smat_ref[...] = smat
        hmat_ref[...] = hmat

    smat = smat_ref[...]
    loc = loc_ref[...]
    total = [inner_ref[v] for v in range(V)]
    for k in range(GROUP):
        full = lift(nn(smat, alpha_ref[k]), loc)
        edge_ref[k, :64] = full[:64]
        edge_ref[k, 64:] = full[192:]
        lifted = full[64:192].astype(BF16).astype(F32)
        for v in range(V):
            total[v] = total[v] + ens_ref[k, v, 64:192].astype(F32) * lifted
            x_ref[k, v, :64] = ens_ref[k, v, :64]
            x_ref[k, v, 64:] = ens_ref[k, v, 192:]
    for v in range(V):
        inner_ref[v] = total[v]


def own_part(where, alpha, ensemble, loc, after):
    members = alpha.shape[0]
    whole = lambda *shape: pl.BlockSpec(shape, lambda i: (0,) * len(shape))
    return call(
        own_kernel,
        (
            sds(V, 128, 128),
            sds(members, 128, 128),
            sds(members, V, 128, 128, dtype=BF16),
            sds(256, 256, dtype=BF16),
            sds(128, 128, dtype=BF16),
        ),
        grid=(members // GROUP,),
        ins=[
            SMEM,
            pl.BlockSpec((GROUP, 256, 128), lambda i: (i, 0, 0)),
            pl.BlockSpec((GROUP, V, 256, 128), lambda i: (i, 0, 0, 0)),
            whole(128, 128),
            whole(8, 128),
        ],
        outs=(
            whole(V, 128, 128),
            pl.BlockSpec((GROUP, 128, 128), lambda i: (i, 0, 0)),
            pl.BlockSpec((GROUP, V, 128, 128), lambda i: (i, 0, 0, 0)),
            whole(256, 256),
            whole(128, 128),
        ),
    )(where, alpha, ensemble, loc, after)


def edge_terms(first_ref, second_ref, own_ref, x_ref, hmat_ref, loc_ref, start, count, total):
    hmat = hmat_ref[...]
    loc = loc_ref[...]
    for k in range(count):
        rows = slice(64 * k, 64 * k + 64)
        halo = jnp.concatenate([first_ref[rows].astype(BF16), second_ref[rows].astype(BF16)], axis=0)
        lifted = (own_ref[start + k] + lift(nn(hmat, halo), loc)).astype(BF16).astype(F32)
        for v in range(V):
            total[v] = total[v] + x_ref[start + k, v].astype(F32) * lifted
    return total


def head_kernel(first_ref, second_ref, own_ref, x_ref, hmat_ref, loc_ref, total_ref):
    zeros = [jnp.zeros((128, 128), F32) for v in range(V)]
    total = edge_terms(first_ref, second_ref, own_ref, x_ref, hmat_ref, loc_ref, 0, HEAD, zeros)
    for v in range(V):
        total_ref[v] = total[v]


def head_part(first, second, own, x, hmat, loc):
    return call(head_kernel, sds(V, 128, 128), ins=[VMEM] * 6, outs=VMEM)(first, second, own, x, hmat, loc)


def edge_kernel(where_ref, first_ref, second_ref, own_ref, x_ref, hmat_ref, loc_ref, inner_ref, head_ref, inc_ref, keep_ref, give_ref):
    total = [head_ref[v] for v in range(V)]
    total = edge_terms(first_ref, second_ref, own_ref, x_ref, hmat_ref, loc_ref, HEAD, own_ref.shape[0] - HEAD, total)
    for v in range(V):
        inc_ref[v, :64] = total[v][:64]
        inc_ref[v, 64:192] = inner_ref[v]
        inc_ref[v, 192:] = total[v][64:]
        keep_ref[32 * v : 32 * v + 32] = inc_ref[v, pl.ds(pl.multiple_of(where_ref[8], 32), 32)]
        give_ref[32 * v : 32 * v + 32] = inc_ref[v, pl.ds(pl.multiple_of(where_ref[9], 32), 32)]
    end = first_ref.shape[0] - HALF
    give_ref[32 * V : 32 * V + HALF] = first_ref[end:]
    give_ref[32 * V + HALF :] = second_ref[end:]


def edge_part(where, first, second, own, x, hmat, loc, inner, head):
    return call(
        edge_kernel,
        (sds(V, 256, 128), sds(V * 32, 128), sds(V * 32 + OBS, 128)),
        ins=[SMEM] + [VMEM] * 8,
        outs=(VMEM,) * 3,
    )(where, first, second, own, x, hmat, loc, inner, head)


def tent(distance):
    return jnp.maximum(1.0 - jnp.abs(distance), 0.0)


def weights_kernel(where_ref, own_ref, here_ref, there_ref, after_ref, wown_ref, wnear_ref, lev_ref, innov_ref, weight_ref, hot_ref, o_ref, e_ref):
    core = where_ref[10]
    for half, ref in ((core, here_ref), (1 - core, there_ref)):
        rows = pl.ds(pl.multiple_of(HALF * half, 8), HALF)
        o_ref[rows] = ref[32 * V : 32 * V + HALF]
        e_ref[rows] = ref[32 * V + HALF :]
    level = lax.broadcasted_iota(jnp.int32, (128, SLOTS), 0).astype(F32)
    even_row = where_ref[2].astype(F32)
    odd_row = where_ref[3].astype(F32)
    odd_there = where_ref[4].astype(F32)
    cell = lax.broadcasted_iota(jnp.int32, (32, SLOTS), 0).astype(F32)

    def line(ref, field, v):
        at = 6 * (V * field + v)
        return jnp.concatenate([ref[at + a : at + a + 1] for a in range(6)], axis=1)

    def columns(code):
        row = jnp.floor(code * (1.0 / 64.0))
        column = code - 64.0 * row
        return row, tent(cell - (column * 0.5 - 0.25))

    for v in range(V):
        row, across = columns(line(own_ref, 0, v))
        middle = row * 0.5 - 0.25
        for r in range(8):
            wown_ref[v, 32 * r : 32 * r + 32] = (tent(r - middle) * across).astype(BF16)
        wown_ref[v, 256:288] = (tent(even_row - middle) * across).astype(BF16)
        wown_ref[v, 288:320] = (tent(odd_row - middle) * odd_there * across).astype(BF16)
        for n, ref in enumerate((e_ref, o_ref)):
            row, across = columns(line(ref, 0, v))
            wnear_ref[n, v, :32] = (0.25 * across).astype(BF16)
            wnear_ref[n, v, 32:] = (0.75 * across).astype(BF16)
    is_odd = where_ref[5]
    for n, ref in enumerate((own_ref, e_ref, o_ref)):
        for v in range(V):
            row = slice(3 * n + v, 3 * n + v + 1)
            lev = line(ref, 1, v)
            lev_ref[row] = lev
            hot_ref[3 * n + v] = jnp.where(level == lev, 1.0, 0.0).astype(BF16)
            innov_ref[row] = line(ref, 2, v)
            weight = line(ref, 3, v)
            if n > 0:
                code = line(ref, 0, v)
                first = is_odd == (0 if n == 1 else 1)
                at_edge = jnp.where(first, code, 1023.0 - code) < 64.0
                there = at_edge & ((n == 1) | (where_ref[4] == 1))
                weight = jnp.where(there, weight, 0.0)
            weight_ref[row] = weight


def weights(where, own, here, there, after):
    return call(
        weights_kernel,
        (
            sds(V, 320, SLOTS, dtype=BF16),
            sds(2, V, 64, SLOTS, dtype=BF16),
            sds(9, SLOTS),
            sds(9, SLOTS),
            sds(9, SLOTS),
            sds(9, 128, SLOTS, dtype=BF16),
        ),
        ins=[SMEM] + [VMEM] * 4,
        scratch=[pltpu.VMEM((OBS, 128), F32), pltpu.VMEM((OBS, 128), F32)],
    )(where, own, here, there, after)


def picker(lev_ref):
    level = lax.broadcasted_iota(jnp.int32, (128, SLOTS), 0).astype(F32)

    def pick(cells, weight, row):
        both = jnp.concatenate(halves(cells), axis=0)
        at_all = tn(both, jnp.concatenate([weight, weight], axis=0))
        hot = level == lev_ref[pl.ds(row, 1), :]
        return jnp.sum(jnp.where(hot, at_all, 0.0), axis=0, keepdims=True)

    return pick


def mine_kernel(where_ref, inc_ref, wown_ref, wnear_ref, lev_ref, out_ref):
    pick = picker(lev_ref)
    for v in range(V):
        out_ref[v : v + 1] = pick(inc_ref[v], wown_ref[v, :256], v)
        for n in range(2):
            cells = inc_ref[v, pl.ds(pl.multiple_of(where_ref[n], 32), 32)]
            row = 3 * n + 3 + v
            out_ref[row : row + 1] = pick(cells, wnear_ref[n, v, :32], row)


def mine_part(where, inc, wown, wnear, lev):
    return call(
        mine_kernel,
        sds(9, SLOTS),
        ins=[SMEM] + [VMEM] * 4,
        outs=VMEM,
    )(where, inc, wown, wnear, lev)


def values_kernel(where_ref, mine_ref, near_ref, wown_ref, wnear_ref, lev_ref, out_ref):
    pick = picker(lev_ref)
    core = where_ref[10]

    def put(row, line):
        for a in range(6):
            out_ref[pl.ds(6 * row + a, 1)] = line[:, 128 * a : 128 * a + 128]

    for v in range(V):
        for n in range(2):
            row = 3 * n + 3 + v
            put(row, mine_ref[row : row + 1])
    for v in range(V):
        halo = pl.ds(pl.multiple_of(256 + 32 * core, 32), 32)
        put(v, mine_ref[v : v + 1] + pick(near_ref[32 * v : 32 * v + 32], wown_ref[v, halo], v))
        row = 3 * core + 3 + v
        put(row, mine_ref[pl.ds(row, 1)] + pick(near_ref[32 * v : 32 * v + 32], wnear_ref[core, v, 32:], row))


def values(where, mine, near, wown, wnear, lev):
    return call(
        values_kernel,
        sds(9 * SLOTS // 128, 128),
        ins=[SMEM] + [VMEM] * 5,
        outs=VMEM,
    )(where, mine, near, wown, wnear, lev)


def adjoint_kernel(where_ref, v0, v1, innov_ref, weight_ref, hot_ref, wown_ref, wnear_ref, x_ref, c_ref, first_ref, second_ref):
    value = v0[...] + v1[...]

    def weighted(row):
        line = jnp.concatenate([value[6 * row + a : 6 * row + a + 1] for a in range(6)], axis=1)
        return weight_ref[row : row + 1] * (line - innov_ref[row : row + 1])

    def place(weight, row):
        hot = hot_ref[row]
        both = jnp.concatenate([hot * half for half in halves(weighted(row))], axis=0)
        out = nt(weight, both)
        return out[:, :128] + out[:, 128:]

    def place_near(weight, row):
        both = jnp.concatenate(halves(weight.astype(F32) * weighted(row)), axis=0)
        out = nt(both, hot_ref[row])
        return out[:32] + out[32:]

    adj = []
    for v in range(V):
        c_ref[v] = place(wown_ref[v, :256], v)
        for n in range(2):
            rows = pl.ds(pl.multiple_of(where_ref[n], 32), 32)
            c_ref[v, rows] = c_ref[v, rows] + place_near(wnear_ref[n, v, :32], 3 * n + 3 + v)
        adj.append(jnp.concatenate([c_ref[v, :64], c_ref[v, 192:]], axis=0))
    first_low = where_ref[7] == 1
    for k in range(first_ref.shape[0]):
        total = x_ref[k, 0].astype(F32) * adj[0]
        for v in range(1, V):
            total = total + x_ref[k, v].astype(F32) * adj[v]
        low, high = total[:64], total[64:]
        first_ref[k] = jnp.where(first_low, low, high)
        second_ref[k] = jnp.where(first_low, high, low)


def adjoint(where, vals, innov, weight, hot, wown, wnear, x):
    members = HEAD_BACK
    return call(
        adjoint_kernel,
        (sds(V, 256, 128), sds(members, 64, 128), sds(members, 64, 128)),
        ins=[SMEM] + [VMEM] * 8,
        outs=(VMEM,) * 3,
    )(where, *vals, innov, weight, hot, wown, wnear, x)


def drop(smoothed, loc):
    high, low = halves(smoothed)
    return nn(high, loc) + nn(low, loc)


def back_kernel(where_ref, alpha_ref, ens_ref, c_ref, smat_ref, loc_ref, out_ref, edge_ref, first_ref, second_ref):
    low = where_ref[7] == 1
    smat = smat_ref[...]
    loc = loc_ref[...]
    for k in range(GROUP):
        back = ens_ref[k, 0].astype(F32) * c_ref[0]
        for v in range(1, V):
            back = back + ens_ref[k, v].astype(F32) * c_ref[v]
        first_ref[k] = jnp.where(low, back[:64], back[192:])
        second_ref[k] = jnp.where(low, back[192:], back[:64])
        full = alpha_ref[k].astype(F32) + drop(smooth(smat, back), loc)
        out_ref[k] = full
        edge_ref[k, :64] = full[:64]
        edge_ref[k, 64:] = full[192:]


def back_part(where, alpha, ensemble, c, smat, loc):
    members = alpha.shape[0]
    rest = pl.BlockSpec((GROUP, 64, 128), lambda i: (jnp.maximum(i - HEAD_BACK // GROUP, 0), 0, 0))
    return call(
        back_kernel,
        (
            sds(members, 256, 128),
            sds(members, 128, 128),
            sds(members - HEAD_BACK, 64, 128),
            sds(members - HEAD_BACK, 64, 128),
        ),
        grid=(members // GROUP,),
        ins=[
            SMEM,
            pl.BlockSpec((GROUP, 256, 128), lambda i: (i, 0, 0)),
            pl.BlockSpec((GROUP, V, 256, 128), lambda i: (i, 0, 0, 0)),
            pl.BlockSpec((V, 256, 128), lambda i: (0, 0, 0)),
            pl.BlockSpec((256, 256), lambda i: (0, 0)),
            pl.BlockSpec((128, 128), lambda i: (0, 0)),
        ],
        outs=(
            pl.BlockSpec((GROUP, 256, 128), lambda i: (i, 0, 0)),
            pl.BlockSpec((GROUP, 128, 128), lambda i: (i, 0, 0)),
            rest,
            rest,
        ),
    )(where, alpha, ensemble, c, smat, loc)


def last_kernel(start, first_ref, second_ref, edge_ref, hmat_ref, loc_ref, unused_ref, out_ref, held, sems):
    hmat = hmat_ref[...]
    loc = loc_ref[...]
    copies = []
    for g in range(first_ref.shape[0] // GROUP):
        for k in range(g * GROUP, (g + 1) * GROUP):
            halo = jnp.concatenate([first_ref[k], second_ref[k]], axis=0)
            full = edge_ref[start + k] + drop(smooth(hmat, halo), loc)
            held[k, 0] = full[:64]
            held[k, 1] = full[64:]
        here, there = pl.ds(g * GROUP, GROUP), pl.ds(start + g * GROUP, GROUP)
        for side in range(2):
            copies.append(
                pltpu.make_async_copy(held.at[here, side], out_ref.at[there, 3 * side], sems.at[g, side])
            )
            copies[-1].start()
    for copy in copies:
        copy.wait()


def last_part(start, first, second, edge, hmat, loc, out):
    count = first.shape[0]
    return call(
        functools.partial(last_kernel, start),
        sds(*out.shape),
        ins=[VMEM] * 5 + [ANY],
        outs=ANY,
        scratch=[pltpu.VMEM((count, 2, 64, 128), F32), pltpu.SemaphoreType.DMA((count // GROUP, 2))],
        aliases={5: 0},
    )(first, second, edge, hmat, loc, out)


def stencil(gap):
    gap = jnp.abs(gap)
    return jnp.where(gap == 0, 6.0, jnp.where(gap == 1, 4.0, jnp.where(gap == 2, 1.0, 0.0)))


def matrices(tile, tiles, first_high):
    def across(i, j):
        gap = stencil(i - j)
        return jnp.where((i == j) & ((i == 0) | (i == 31)), 5.0, gap)

    i = lax.broadcasted_iota(jnp.int32, (256, 256), 0)
    j = lax.broadcasted_iota(jnp.int32, (256, 256), 1)
    ri, rj = i // 32, j // 32
    ends = ((ri == 0) & (tile == 0)) | ((ri == 7) & (tile == tiles - 1))
    down = jnp.where((ri == rj) & ends, 5.0, stencil(ri - rj))
    smat = (down * across(i % 32, j % 32) * (1.0 / 256.0)).astype(BF16)
    i = lax.broadcasted_iota(jnp.int32, (128, 128), 0)
    j = lax.broadcasted_iota(jnp.int32, (128, 128), 1)
    ri = i // 32
    ri = jnp.where(ri < 2, ri, ri + 4)
    above = (j < 64) == first_high
    rj = jnp.where(above, 8, -2) + (j // 32) % 2
    there = (above & (tile < tiles - 1)) | (jnp.logical_not(above) & (tile > 0))
    hmat = jnp.where(there, stencil(ri - rj), 0.0) * across(i % 32, j % 32) * (1.0 / 256.0)
    return smat, hmat.astype(BF16)


def swap_first(x):
    return lax.ppermute(x, ("mem", "tile"), FIRST)


def swap_second(x):
    return lax.ppermute(x, ("mem", "tile"), SECOND)


def swap_near(x):
    return lax.ppermute(x, ("mem", "tile"), NEAR)


def swap_core(x):
    return lax.ppermute(x, "mem", [(m, m ^ 1) for m in range(MEMS)])


def swap_chip(x):
    return lax.ppermute(x, "mem", [(m, m ^ 2) for m in range(MEMS)])


def on_device(alpha, ensemble, loc_vert, obs_col, obs_lev, obs_count, innovation, obs_weight):
    members = alpha.shape[0]
    tile = lax.axis_index("tile")
    tiles = lax.axis_size("tile")
    even = tile % 2 == 0
    core = lax.axis_index("mem") % 2
    first_low = side_of_first()
    where = jnp.stack(
        [
            jnp.where(even, 7 * 32, 0),
            jnp.where(even, 0, 7 * 32),
            jnp.where(even, 8, -1),
            jnp.where(even, -1, 8),
            ((tile > 0) & (tile < tiles - 1)).astype(jnp.int32),
            tile % 2,
            tile,
            first_low,
            7 * 32 * (1 - (tile + core) % 2),
            7 * 32 * ((tile + core) % 2),
            core,
        ]
    ).astype(jnp.int32)
    flat = alpha.reshape(members, 256, 128)
    flat_ens = ensemble.reshape(members, V, 256, 128)

    quarters = alpha.reshape(members, 4, 64, 128)
    send_first, send_second, token = send_part(quarters)
    first, second = swap_first(send_first), swap_second(send_second)
    inner, own_edge, x, smat, hmat = own_part(where, flat, flat_ens, loc_vert, token)
    send_first, send_second, own_obs = rest_part(
        obs_count, obs_col, obs_lev, innovation, obs_weight, quarters, hmat
    )
    first_rest, second_rest = swap_first(send_first), swap_second(send_second)
    head = head_part(first, second, own_edge, x, hmat, loc_vert)
    inc, keep, give = edge_part(where, first_rest, second_rest, own_edge, x, hmat, loc_vert, inner, head)
    got = swap_core(give)
    edges = keep + got[: V * 32]
    near = swap_near(edges)
    wown, wnear, lev, innov, weight, hot = weights(where, own_obs, give, got, edges)
    mine = mine_part(where, inc, wown, wnear, lev)
    vals = values(where, mine, near, wown, wnear, lev)
    vals = vals + swap_core(vals)
    vals = vals, swap_chip(vals)
    c, back_first, back_second = adjoint(where, vals, innov, weight, hot, wown, wnear, x)
    halo_first, halo_second = swap_first(back_first), swap_second(back_second)
    out, edge, back_first, back_second = back_part(where, flat, flat_ens, c, smat, loc_vert)
    rest_first, rest_second = swap_first(back_first), swap_second(back_second)
    out = last_part(0, halo_first, halo_second, edge, hmat, loc_vert, out.reshape(members, 4, 64, 128))
    out = last_part(HEAD_BACK, rest_first, rest_second, edge, hmat, loc_vert, out)
    return out.reshape(members, 8, 32, 128)


def solution(mesh):
    in_specs = (
        P("mem", "tile", None, None),
        P("mem", None, "tile", None, None),
        P(),
        P("tile", None),
        P("tile", None),
        P("tile"),
        P("tile", None),
        P("tile", None),
    )
    out_specs = P("mem", "tile", None, None)
    return jax.shard_map(
        on_device, mesh=mesh, in_specs=in_specs, out_specs=out_specs, check_vma=False
    )
```

```python
import functools

import jax
import jax.numpy as jnp
from jax import lax
from jax.experimental import pallas as pl
from jax.experimental.pallas import tpu as pltpu
from jax.sharding import PartitionSpec as P

V = 3
F32 = jnp.float32
BF16 = jnp.bfloat16
SLOTS = 768
GROUP = 4
HEAD = 16
HEAD_BACK = 16
OBS = 80
HALF = OBS // 2

TILES = 64
MEMS = 4


def partners(odd, spare):
    pairs = []
    for m in range(MEMS):
        for t in range(TILES):
            beside = ((t - 1) ^ 1) + 1 if odd(m) else t ^ 1
            there = (m, beside) if 0 <= beside < TILES else (m ^ spare, t)
            pairs.append((TILES * m + t, TILES * there[0] + there[1]))
    return pairs


FIRST = partners(lambda m: True, 1)
SECOND = partners(lambda m: False, 1)
NEAR = partners(lambda m: m % 2 == 1, 2)


def nn(a, b):
    return lax.dot_general(a, b, (((1,), (0,)), ((), ())), preferred_element_type=F32)


def nt(a, b):
    return lax.dot_general(a, b, (((1,), (1,)), ((), ())), preferred_element_type=F32)


def tn(a, b):
    return lax.dot_general(a, b, (((0,), (0,)), ((), ())), preferred_element_type=F32)


def halves(x):
    high = x.astype(BF16)
    low = (x - high.astype(F32)).astype(BF16)
    return high, low


def lift(smoothed, loc):
    high, low = halves(smoothed)
    return nt(high, loc) + nt(low, loc)


def call(kernel, out, grid=None, ins=None, outs=None, scratch=(), aliases=None, cost=1000, vmem=16):
    kw = {}
    if grid is not None:
        kw["grid"] = grid
    return pl.pallas_call(
        kernel,
        out_shape=out,
        in_specs=ins,
        out_specs=outs if outs is not None else jax.tree.map(lambda o: VMEM, out),
        scratch_shapes=scratch,
        input_output_aliases=aliases or {},
        compiler_params=pltpu.CompilerParams(vmem_limit_bytes=vmem * 1024 * 1024),
        cost_estimate=pl.CostEstimate(flops=cost, bytes_accessed=cost, transcendentals=0),
        **kw,
    )


def sds(*shape, dtype=F32):
    return jax.ShapeDtypeStruct(shape, dtype)


ANY = pl.BlockSpec(memory_space=pl.ANY)
SMEM = pl.BlockSpec(memory_space=pltpu.SMEM)
VMEM = pl.BlockSpec(memory_space=pltpu.VMEM)
HBM = pl.BlockSpec(memory_space=pltpu.HBM)


def smooth(matrix, field):
    both = jnp.concatenate(halves(field), axis=1)
    out = nn(matrix, both)
    return out[:, :128] + out[:, 128:]


def side_of_first():
    return lax.rem(lax.axis_index("tile") + 1, 2)


def sort_observations(count, col_ref, lev_ref, innov_ref, weight_ref, out_ref):
    slots = col_ref.shape[1]
    live = lax.broadcasted_iota(jnp.int32, (1, slots), 1) < count
    rows = []
    for field in (
        col_ref[...].astype(F32),
        lev_ref[...].astype(F32),
        innov_ref[...],
        jnp.where(live, weight_ref[...], 0.0),
    ):
        field = jnp.concatenate([field, jnp.zeros((1, V * SLOTS - slots), F32)], axis=1)
        rows += [field[:, 384 * a : 384 * a + 384] for a in range(6)]
    rest = jnp.concatenate(rows, axis=0)
    i = lax.broadcasted_iota(jnp.int32, (384, 384), 0)
    j = lax.broadcasted_iota(jnp.int32, (384, 384), 1)
    order = (i == 3 * (j % 128) + j // 128).astype(F32).astype(BF16)
    total = jnp.zeros((24, 384), F32)
    for piece in range(3):
        part = rest.astype(BF16)
        rest = rest - part.astype(F32)
        total = total + nn(part, order)
    out_ref[72:] = jnp.zeros((OBS - 72, 128), F32)
    for f in range(4):
        for a in range(6):
            for v in range(V):
                row = 6 * (V * f + v) + a
                out_ref[row : row + 1] = total[6 * f + a : 6 * f + a + 1, 128 * v : 128 * v + 128]


def send_kernel(quarters_ref, first_ref, second_ref, token_ref, edges, sems):
    members = pl.ds(0, HEAD)
    copies = [pltpu.make_async_copy(quarters_ref.at[members, 3 * n], edges.at[n], sems.at[n]) for n in range(2)]
    for copy in copies:
        copy.start()
    token_ref[...] = jnp.zeros_like(token_ref)
    for copy in copies:
        copy.wait()
    low = side_of_first()
    for k in range(HEAD):
        first_ref[64 * k : 64 * k + 64] = edges[1 - low, k].astype(F32)
        second_ref[64 * k : 64 * k + 64] = edges[low, k].astype(F32)


def send_part(quarters):
    return call(
        send_kernel,
        (sds(64 * HEAD, 128), sds(64 * HEAD, 128), sds(8, 128)),
        ins=[HBM],
        outs=(VMEM,) * 3,
        scratch=[pltpu.VMEM((2, HEAD, 64, 128), BF16), pltpu.SemaphoreType.DMA((2,))],
        vmem=56,
    )(quarters)


def rest_kernel(count_ref, col_ref, lev_ref, innov_ref, weight_ref, quarters_ref, after_ref, first_ref, second_ref, obs_ref, edges, sems):
    count = edges.shape[1]
    members = pl.ds(HEAD, count)
    copies = [pltpu.make_async_copy(quarters_ref.at[members, 3 * n], edges.at[n], sems.at[n]) for n in range(2)]
    for copy in copies:
        copy.start()
    sort_observations(count_ref[0], col_ref, lev_ref, innov_ref, weight_ref, obs_ref)
    core = lax.rem(lax.axis_index("mem"), 2)
    half = obs_ref[pl.ds(pl.multiple_of(HALF * core, 8), HALF)]
    first_ref[64 * count :] = half
    second_ref[64 * count :] = half
    for copy in copies:
        copy.wait()
    low = side_of_first()
    for k in range(count):
        first_ref[64 * k : 64 * k + 64] = edges[1 - low, k].astype(F32)
        second_ref[64 * k : 64 * k + 64] = edges[low, k].astype(F32)


def rest_part(count, col, lev, innov, weight, quarters, after):
    members = quarters.shape[0] - HEAD
    return call(
        rest_kernel,
        (sds(64 * members + HALF, 128), sds(64 * members + HALF, 128), sds(OBS, 128)),
        ins=[SMEM] + [VMEM] * 4 + [ANY, VMEM],
        outs=(VMEM,) * 3,
        scratch=[pltpu.VMEM((2, members, 64, 128), BF16), pltpu.SemaphoreType.DMA((2,))],
    )(count, col, lev, innov, weight, quarters, after)


def own_kernel(where_ref, alpha_ref, ens_ref, loc_ref, after_ref, inner_ref, edge_ref, x_ref, smat_ref, hmat_ref):
    @pl.when(pl.program_id(0) == 0)
    def _():
        inner_ref[...] = jnp.zeros_like(inner_ref)
        smat, hmat = matrices(where_ref[6], TILES, where_ref[7] == 0)
        smat_ref[...] = smat
        hmat_ref[...] = hmat

    smat = smat_ref[...]
    loc = loc_ref[...]
    total = [inner_ref[v] for v in range(V)]
    for k in range(GROUP):
        full = lift(nn(smat, alpha_ref[k]), loc)
        edge_ref[k, :64] = full[:64]
        edge_ref[k, 64:] = full[192:]
        lifted = full[64:192].astype(BF16).astype(F32)
        for v in range(V):
            total[v] = total[v] + ens_ref[k, v, 64:192].astype(F32) * lifted
            x_ref[k, v, :64] = ens_ref[k, v, :64]
            x_ref[k, v, 64:] = ens_ref[k, v, 192:]
    for v in range(V):
        inner_ref[v] = total[v]


def own_part(where, alpha, ensemble, loc, after):
    members = alpha.shape[0]
    whole = lambda *shape: pl.BlockSpec(shape, lambda i: (0,) * len(shape))
    return call(
        own_kernel,
        (
            sds(V, 128, 128),
            sds(members, 128, 128),
            sds(members, V, 128, 128, dtype=BF16),
            sds(256, 256, dtype=BF16),
            sds(128, 128, dtype=BF16),
        ),
        grid=(members // GROUP,),
        ins=[
            SMEM,
            pl.BlockSpec((GROUP, 256, 128), lambda i: (i, 0, 0)),
            pl.BlockSpec((GROUP, V, 256, 128), lambda i: (i, 0, 0, 0)),
            whole(128, 128),
            whole(8, 128),
        ],
        outs=(
            whole(V, 128, 128),
            pl.BlockSpec((GROUP, 128, 128), lambda i: (i, 0, 0)),
            pl.BlockSpec((GROUP, V, 128, 128), lambda i: (i, 0, 0, 0)),
            whole(256, 256),
            whole(128, 128),
        ),
    )(where, alpha, ensemble, loc, after)


def edge_terms(first_ref, second_ref, own_ref, x_ref, hmat_ref, loc_ref, start, count, total):
    hmat = hmat_ref[...]
    loc = loc_ref[...]
    for k in range(count):
        rows = slice(64 * k, 64 * k + 64)
        halo = jnp.concatenate([first_ref[rows].astype(BF16), second_ref[rows].astype(BF16)], axis=0)
        lifted = (own_ref[start + k] + lift(nn(hmat, halo), loc)).astype(BF16).astype(F32)
        for v in range(V):
            total[v] = total[v] + x_ref[start + k, v].astype(F32) * lifted
    return total


def head_kernel(first_ref, second_ref, own_ref, x_ref, hmat_ref, loc_ref, total_ref):
    zeros = [jnp.zeros((128, 128), F32) for v in range(V)]
    total = edge_terms(first_ref, second_ref, own_ref, x_ref, hmat_ref, loc_ref, 0, HEAD, zeros)
    for v in range(V):
        total_ref[v] = total[v]


def head_part(first, second, own, x, hmat, loc):
    return call(head_kernel, sds(V, 128, 128), ins=[VMEM] * 6, outs=VMEM)(first, second, own, x, hmat, loc)


def edge_kernel(where_ref, first_ref, second_ref, own_ref, x_ref, hmat_ref, loc_ref, inner_ref, head_ref, inc_ref, keep_ref, give_ref):
    total = [head_ref[v] for v in range(V)]
    total = edge_terms(first_ref, second_ref, own_ref, x_ref, hmat_ref, loc_ref, HEAD, own_ref.shape[0] - HEAD, total)
    for v in range(V):
        inc_ref[v, :64] = total[v][:64]
        inc_ref[v, 64:192] = inner_ref[v]
        inc_ref[v, 192:] = total[v][64:]
        keep_ref[32 * v : 32 * v + 32] = inc_ref[v, pl.ds(pl.multiple_of(where_ref[8], 32), 32)]
        give_ref[32 * v : 32 * v + 32] = inc_ref[v, pl.ds(pl.multiple_of(where_ref[9], 32), 32)]
    end = first_ref.shape[0] - HALF
    give_ref[32 * V : 32 * V + HALF] = first_ref[end:]
    give_ref[32 * V + HALF :] = second_ref[end:]


def edge_part(where, first, second, own, x, hmat, loc, inner, head):
    return call(
        edge_kernel,
        (sds(V, 256, 128), sds(V * 32, 128), sds(V * 32 + OBS, 128)),
        ins=[SMEM] + [VMEM] * 8,
        outs=(VMEM,) * 3,
    )(where, first, second, own, x, hmat, loc, inner, head)


def tent(distance):
    return jnp.maximum(1.0 - jnp.abs(distance), 0.0)


def weights_kernel(where_ref, own_ref, here_ref, there_ref, after_ref, wown_ref, wnear_ref, lev_ref, innov_ref, weight_ref, hot_ref, o_ref, e_ref):
    core = where_ref[10]
    for half, ref in ((core, here_ref), (1 - core, there_ref)):
        rows = pl.ds(pl.multiple_of(HALF * half, 8), HALF)
        o_ref[rows] = ref[32 * V : 32 * V + HALF]
        e_ref[rows] = ref[32 * V + HALF :]
    level = lax.broadcasted_iota(jnp.int32, (128, SLOTS), 0).astype(F32)
    even_row = where_ref[2].astype(F32)
    odd_row = where_ref[3].astype(F32)
    odd_there = where_ref[4].astype(F32)
    cell = lax.broadcasted_iota(jnp.int32, (32, SLOTS), 0).astype(F32)

    def line(ref, field, v):
        at = 6 * (V * field + v)
        return jnp.concatenate([ref[at + a : at + a + 1] for a in range(6)], axis=1)

    def columns(code):
        row = jnp.floor(code * (1.0 / 64.0))
        column = code - 64.0 * row
        return row, tent(cell - (column * 0.5 - 0.25))

    for v in range(V):
        row, across = columns(line(own_ref, 0, v))
        middle = row * 0.5 - 0.25
        for r in range(8):
            wown_ref[v, 32 * r : 32 * r + 32] = (tent(r - middle) * across).astype(BF16)
        wown_ref[v, 256:288] = (tent(even_row - middle) * across).astype(BF16)
        wown_ref[v, 288:320] = (tent(odd_row - middle) * odd_there * across).astype(BF16)
        for n, ref in enumerate((e_ref, o_ref)):
            row, across = columns(line(ref, 0, v))
            wnear_ref[n, v, :32] = (0.25 * across).astype(BF16)
            wnear_ref[n, v, 32:] = (0.75 * across).astype(BF16)
    is_odd = where_ref[5]
    for n, ref in enumerate((own_ref, e_ref, o_ref)):
        for v in range(V):
            row = slice(3 * n + v, 3 * n + v + 1)
            lev = line(ref, 1, v)
            lev_ref[row] = lev
            hot_ref[3 * n + v] = jnp.where(level == lev, 1.0, 0.0).astype(BF16)
            innov_ref[row] = line(ref, 2, v)
            weight = line(ref, 3, v)
            if n > 0:
                code = line(ref, 0, v)
                first = is_odd == (0 if n == 1 else 1)
                at_edge = jnp.where(first, code, 1023.0 - code) < 64.0
                there = at_edge & ((n == 1) | (where_ref[4] == 1))
                weight = jnp.where(there, weight, 0.0)
            weight_ref[row] = weight


def weights(where, own, here, there, after):
    return call(
        weights_kernel,
        (
            sds(V, 320, SLOTS, dtype=BF16),
            sds(2, V, 64, SLOTS, dtype=BF16),
            sds(9, SLOTS),
            sds(9, SLOTS),
            sds(9, SLOTS),
            sds(9, 128, SLOTS, dtype=BF16),
        ),
        ins=[SMEM] + [VMEM] * 4,
        scratch=[pltpu.VMEM((OBS, 128), F32), pltpu.VMEM((OBS, 128), F32)],
    )(where, own, here, there, after)


def picker(lev_ref):
    level = lax.broadcasted_iota(jnp.int32, (128, SLOTS), 0).astype(F32)

    def pick(cells, weight, row):
        both = jnp.concatenate(halves(cells), axis=0)
        at_all = tn(both, jnp.concatenate([weight, weight], axis=0))
        hot = level == lev_ref[pl.ds(row, 1), :]
        return jnp.sum(jnp.where(hot, at_all, 0.0), axis=0, keepdims=True)

    return pick


def mine_kernel(where_ref, inc_ref, wown_ref, wnear_ref, lev_ref, out_ref):
    pick = picker(lev_ref)
    for v in range(V):
        out_ref[v : v + 1] = pick(inc_ref[v], wown_ref[v, :256], v)
        for n in range(2):
            cells = inc_ref[v, pl.ds(pl.multiple_of(where_ref[n], 32), 32)]
            row = 3 * n + 3 + v
            out_ref[row : row + 1] = pick(cells, wnear_ref[n, v, :32], row)


def mine_part(where, inc, wown, wnear, lev):
    return call(
        mine_kernel,
        sds(9, SLOTS),
        ins=[SMEM] + [VMEM] * 4,
        outs=VMEM,
    )(where, inc, wown, wnear, lev)


def values_kernel(where_ref, mine_ref, near_ref, wown_ref, wnear_ref, hot_ref, out_ref):
    core = where_ref[10]

    def pick(cells, weight, row):
        both = jnp.concatenate(halves(cells), axis=0)
        at_level = nn(both, hot_ref[row])
        at_level = at_level[:32] + at_level[32:]
        return jnp.sum(weight.astype(F32) * at_level, axis=0, keepdims=True)

    def put(row, line):
        for a in range(6):
            out_ref[pl.ds(6 * row + a, 1)] = line[:, 128 * a : 128 * a + 128]

    for v in range(V):
        for n in range(2):
            row = 3 * n + 3 + v
            put(row, mine_ref[row : row + 1])
    for v in range(V):
        halo = pl.ds(pl.multiple_of(256 + 32 * core, 32), 32)
        put(v, mine_ref[v : v + 1] + pick(near_ref[32 * v : 32 * v + 32], wown_ref[v, halo], v))
        row = 3 * core + 3 + v
        put(row, mine_ref[pl.ds(row, 1)] + pick(near_ref[32 * v : 32 * v + 32], wnear_ref[core, v, 32:], row))


def values(where, mine, near, wown, wnear, hot):
    return call(
        values_kernel,
        sds(9 * SLOTS // 128, 128),
        ins=[SMEM] + [VMEM] * 5,
        outs=VMEM,
    )(where, mine, near, wown, wnear, hot)


def adjoint_kernel(where_ref, v0, v1, innov_ref, weight_ref, hot_ref, wown_ref, wnear_ref, x_ref, c_ref, first_ref, second_ref):
    value = v0[...] + v1[...]

    def weighted(row):
        line = jnp.concatenate([value[6 * row + a : 6 * row + a + 1] for a in range(6)], axis=1)
        return weight_ref[row : row + 1] * (line - innov_ref[row : row + 1])

    def place(weight, row):
        hot = hot_ref[row]
        both = jnp.concatenate([hot * half for half in halves(weighted(row))], axis=0)
        out = nt(weight, both)
        return out[:, :128] + out[:, 128:]

    def place_near(weight, row):
        both = jnp.concatenate(halves(weight.astype(F32) * weighted(row)), axis=0)
        out = nt(both, hot_ref[row])
        return out[:32] + out[32:]

    adj = []
    for v in range(V):
        c_ref[v] = place(wown_ref[v, :256], v)
        for n in range(2):
            rows = pl.ds(pl.multiple_of(where_ref[n], 32), 32)
            c_ref[v, rows] = c_ref[v, rows] + place_near(wnear_ref[n, v, :32], 3 * n + 3 + v)
        adj.append(jnp.concatenate([c_ref[v, :64], c_ref[v, 192:]], axis=0))
    first_low = where_ref[7] == 1
    for k in range(first_ref.shape[0]):
        total = x_ref[k, 0].astype(F32) * adj[0]
        for v in range(1, V):
            total = total + x_ref[k, v].astype(F32) * adj[v]
        low, high = total[:64], total[64:]
        first_ref[k] = jnp.where(first_low, low, high)
        second_ref[k] = jnp.where(first_low, high, low)


def adjoint(where, vals, innov, weight, hot, wown, wnear, x):
    members = HEAD_BACK
    return call(
        adjoint_kernel,
        (sds(V, 256, 128), sds(members, 64, 128), sds(members, 64, 128)),
        ins=[SMEM] + [VMEM] * 8,
        outs=(VMEM,) * 3,
    )(where, *vals, innov, weight, hot, wown, wnear, x)


def drop(smoothed, loc):
    high, low = halves(smoothed)
    return nn(high, loc) + nn(low, loc)


def back_kernel(where_ref, alpha_ref, ens_ref, c_ref, smat_ref, loc_ref, out_ref, edge_ref, first_ref, second_ref):
    low = where_ref[7] == 1
    smat = smat_ref[...]
    loc = loc_ref[...]
    for k in range(GROUP):
        back = ens_ref[k, 0].astype(F32) * c_ref[0]
        for v in range(1, V):
            back = back + ens_ref[k, v].astype(F32) * c_ref[v]
        first_ref[k] = jnp.where(low, back[:64], back[192:])
        second_ref[k] = jnp.where(low, back[192:], back[:64])
        full = alpha_ref[k].astype(F32) + drop(smooth(smat, back), loc)
        out_ref[k] = full
        edge_ref[k, :64] = full[:64]
        edge_ref[k, 64:] = full[192:]


def back_part(where, alpha, ensemble, c, smat, loc):
    members = alpha.shape[0]
    rest = pl.BlockSpec((GROUP, 64, 128), lambda i: (jnp.maximum(i - HEAD_BACK // GROUP, 0), 0, 0))
    return call(
        back_kernel,
        (
            sds(members, 256, 128),
            sds(members, 128, 128),
            sds(members - HEAD_BACK, 64, 128),
            sds(members - HEAD_BACK, 64, 128),
        ),
        grid=(members // GROUP,),
        ins=[
            SMEM,
            pl.BlockSpec((GROUP, 256, 128), lambda i: (i, 0, 0)),
            pl.BlockSpec((GROUP, V, 256, 128), lambda i: (i, 0, 0, 0)),
            pl.BlockSpec((V, 256, 128), lambda i: (0, 0, 0)),
            pl.BlockSpec((256, 256), lambda i: (0, 0)),
            pl.BlockSpec((128, 128), lambda i: (0, 0)),
        ],
        outs=(
            pl.BlockSpec((GROUP, 256, 128), lambda i: (i, 0, 0)),
            pl.BlockSpec((GROUP, 128, 128), lambda i: (i, 0, 0)),
            rest,
            rest,
        ),
    )(where, alpha, ensemble, c, smat, loc)


def last_kernel(start, first_ref, second_ref, edge_ref, hmat_ref, loc_ref, unused_ref, out_ref, held, sems):
    hmat = hmat_ref[...]
    loc = loc_ref[...]
    copies = []
    for g in range(first_ref.shape[0] // GROUP):
        for k in range(g * GROUP, (g + 1) * GROUP):
            halo = jnp.concatenate([first_ref[k], second_ref[k]], axis=0)
            full = edge_ref[start + k] + drop(smooth(hmat, halo), loc)
            held[k, 0] = full[:64]
            held[k, 1] = full[64:]
        here, there = pl.ds(g * GROUP, GROUP), pl.ds(start + g * GROUP, GROUP)
        for side in range(2):
            copies.append(
                pltpu.make_async_copy(held.at[here, side], out_ref.at[there, 3 * side], sems.at[g, side])
            )
            copies[-1].start()
    for copy in copies:
        copy.wait()


def last_part(start, first, second, edge, hmat, loc, out):
    count = first.shape[0]
    return call(
        functools.partial(last_kernel, start),
        sds(*out.shape),
        ins=[VMEM] * 5 + [ANY],
        outs=ANY,
        scratch=[pltpu.VMEM((count, 2, 64, 128), F32), pltpu.SemaphoreType.DMA((count // GROUP, 2))],
        aliases={5: 0},
    )(first, second, edge, hmat, loc, out)


def stencil(gap):
    gap = jnp.abs(gap)
    return jnp.where(gap == 0, 6.0, jnp.where(gap == 1, 4.0, jnp.where(gap == 2, 1.0, 0.0)))


def matrices(tile, tiles, first_high):
    def across(i, j):
        gap = stencil(i - j)
        return jnp.where((i == j) & ((i == 0) | (i == 31)), 5.0, gap)

    i = lax.broadcasted_iota(jnp.int32, (256, 256), 0)
    j = lax.broadcasted_iota(jnp.int32, (256, 256), 1)
    ri, rj = i // 32, j // 32
    ends = ((ri == 0) & (tile == 0)) | ((ri == 7) & (tile == tiles - 1))
    down = jnp.where((ri == rj) & ends, 5.0, stencil(ri - rj))
    smat = (down * across(i % 32, j % 32) * (1.0 / 256.0)).astype(BF16)
    i = lax.broadcasted_iota(jnp.int32, (128, 128), 0)
    j = lax.broadcasted_iota(jnp.int32, (128, 128), 1)
    ri = i // 32
    ri = jnp.where(ri < 2, ri, ri + 4)
    above = (j < 64) == first_high
    rj = jnp.where(above, 8, -2) + (j // 32) % 2
    there = (above & (tile < tiles - 1)) | (jnp.logical_not(above) & (tile > 0))
    hmat = jnp.where(there, stencil(ri - rj), 0.0) * across(i % 32, j % 32) * (1.0 / 256.0)
    return smat, hmat.astype(BF16)


def swap_first(x):
    return lax.ppermute(x, ("mem", "tile"), FIRST)


def swap_second(x):
    return lax.ppermute(x, ("mem", "tile"), SECOND)


def swap_near(x):
    return lax.ppermute(x, ("mem", "tile"), NEAR)


def swap_core(x):
    return lax.ppermute(x, "mem", [(m, m ^ 1) for m in range(MEMS)])


def swap_chip(x):
    return lax.ppermute(x, "mem", [(m, m ^ 2) for m in range(MEMS)])


def on_device(alpha, ensemble, loc_vert, obs_col, obs_lev, obs_count, innovation, obs_weight):
    members = alpha.shape[0]
    tile = lax.axis_index("tile")
    tiles = lax.axis_size("tile")
    even = tile % 2 == 0
    core = lax.axis_index("mem") % 2
    first_low = side_of_first()
    where = jnp.stack(
        [
            jnp.where(even, 7 * 32, 0),
            jnp.where(even, 0, 7 * 32),
            jnp.where(even, 8, -1),
            jnp.where(even, -1, 8),
            ((tile > 0) & (tile < tiles - 1)).astype(jnp.int32),
            tile % 2,
            tile,
            first_low,
            7 * 32 * (1 - (tile + core) % 2),
            7 * 32 * ((tile + core) % 2),
            core,
        ]
    ).astype(jnp.int32)
    flat = alpha.reshape(members, 256, 128)
    flat_ens = ensemble.reshape(members, V, 256, 128)

    quarters = alpha.reshape(members, 4, 64, 128)
    send_first, send_second, token = send_part(quarters)
    first, second = swap_first(send_first), swap_second(send_second)
    inner, own_edge, x, smat, hmat = own_part(where, flat, flat_ens, loc_vert, token)
    send_first, send_second, own_obs = rest_part(
        obs_count, obs_col, obs_lev, innovation, obs_weight, quarters, hmat
    )
    first_rest, second_rest = swap_first(send_first), swap_second(send_second)
    head = head_part(first, second, own_edge, x, hmat, loc_vert)
    inc, keep, give = edge_part(where, first_rest, second_rest, own_edge, x, hmat, loc_vert, inner, head)
    got = swap_core(give)
    edges = keep + got[: V * 32]
    near = swap_near(edges)
    wown, wnear, lev, innov, weight, hot = weights(where, own_obs, give, got, edges)
    mine = mine_part(where, inc, wown, wnear, lev)
    vals = values(where, mine, near, wown, wnear, hot)
    vals = vals + swap_core(vals)
    vals = vals, swap_chip(vals)
    c, back_first, back_second = adjoint(where, vals, innov, weight, hot, wown, wnear, x)
    halo_first, halo_second = swap_first(back_first), swap_second(back_second)
    out, edge, back_first, back_second = back_part(where, flat, flat_ens, c, smat, loc_vert)
    rest_first, rest_second = swap_first(back_first), swap_second(back_second)
    out = last_part(0, halo_first, halo_second, edge, hmat, loc_vert, out.reshape(members, 4, 64, 128))
    out = last_part(HEAD_BACK, rest_first, rest_second, edge, hmat, loc_vert, out)
    return out.reshape(members, 8, 32, 128)


def solution(mesh):
    in_specs = (
        P("mem", "tile", None, None),
        P("mem", None, "tile", None, None),
        P(),
        P("tile", None),
        P("tile", None),
        P("tile"),
        P("tile", None),
        P("tile", None),
    )
    out_specs = P("mem", "tile", None, None)
    return jax.shard_map(
        on_device, mesh=mesh, in_specs=in_specs, out_specs=out_specs, check_vma=False
    )
```

```python
import functools

import jax
import jax.numpy as jnp
from jax import lax
from jax.experimental import pallas as pl
from jax.experimental.pallas import tpu as pltpu
from jax.sharding import PartitionSpec as P

V = 3
F32 = jnp.float32
BF16 = jnp.bfloat16
SLOTS = 768
GROUP = 4
HEAD = 16
HEAD_BACK = 12
OBS = 80
HALF = OBS // 2

TILES = 64
MEMS = 4


def partners(odd, spare):
    pairs = []
    for m in range(MEMS):
        for t in range(TILES):
            beside = ((t - 1) ^ 1) + 1 if odd(m) else t ^ 1
            there = (m, beside) if 0 <= beside < TILES else (m ^ spare, t)
            pairs.append((TILES * m + t, TILES * there[0] + there[1]))
    return pairs


FIRST = partners(lambda m: True, 1)
SECOND = partners(lambda m: False, 1)
NEAR = partners(lambda m: m % 2 == 1, 2)


def nn(a, b):
    return lax.dot_general(a, b, (((1,), (0,)), ((), ())), preferred_element_type=F32)


def nt(a, b):
    return lax.dot_general(a, b, (((1,), (1,)), ((), ())), preferred_element_type=F32)


def tn(a, b):
    return lax.dot_general(a, b, (((0,), (0,)), ((), ())), preferred_element_type=F32)


def halves(x):
    high = x.astype(BF16)
    low = (x - high.astype(F32)).astype(BF16)
    return high, low


def lift(smoothed, loc):
    high, low = halves(smoothed)
    return nt(high, loc) + nt(low, loc)


def call(kernel, out, grid=None, ins=None, outs=None, scratch=(), aliases=None, cost=1000, vmem=16):
    kw = {}
    if grid is not None:
        kw["grid"] = grid
    return pl.pallas_call(
        kernel,
        out_shape=out,
        in_specs=ins,
        out_specs=outs if outs is not None else jax.tree.map(lambda o: VMEM, out),
        scratch_shapes=scratch,
        input_output_aliases=aliases or {},
        compiler_params=pltpu.CompilerParams(vmem_limit_bytes=vmem * 1024 * 1024),
        cost_estimate=pl.CostEstimate(flops=cost, bytes_accessed=cost, transcendentals=0),
        **kw,
    )


def sds(*shape, dtype=F32):
    return jax.ShapeDtypeStruct(shape, dtype)


ANY = pl.BlockSpec(memory_space=pl.ANY)
SMEM = pl.BlockSpec(memory_space=pltpu.SMEM)
VMEM = pl.BlockSpec(memory_space=pltpu.VMEM)
HBM = pl.BlockSpec(memory_space=pltpu.HBM)


def smooth(matrix, field):
    both = jnp.concatenate(halves(field), axis=1)
    out = nn(matrix, both)
    return out[:, :128] + out[:, 128:]


def side_of_first():
    return lax.rem(lax.axis_index("tile") + 1, 2)


def sort_observations(count, col_ref, lev_ref, innov_ref, weight_ref, out_ref):
    slots = col_ref.shape[1]
    live = lax.broadcasted_iota(jnp.int32, (1, slots), 1) < count
    rows = []
    for field in (
        col_ref[...].astype(F32),
        lev_ref[...].astype(F32),
        innov_ref[...],
        jnp.where(live, weight_ref[...], 0.0),
    ):
        field = jnp.concatenate([field, jnp.zeros((1, V * SLOTS - slots), F32)], axis=1)
        rows += [field[:, 384 * a : 384 * a + 384] for a in range(6)]
    rest = jnp.concatenate(rows, axis=0)
    i = lax.broadcasted_iota(jnp.int32, (384, 384), 0)
    j = lax.broadcasted_iota(jnp.int32, (384, 384), 1)
    order = (i == 3 * (j % 128) + j // 128).astype(F32).astype(BF16)
    total = jnp.zeros((24, 384), F32)
    for piece in range(3):
        part = rest.astype(BF16)
        rest = rest - part.astype(F32)
        total = total + nn(part, order)
    out_ref[72:] = jnp.zeros((OBS - 72, 128), F32)
    for f in range(4):
        for a in range(6):
            for v in range(V):
                row = 6 * (V * f + v) + a
                out_ref[row : row + 1] = total[6 * f + a : 6 * f + a + 1, 128 * v : 128 * v + 128]


def send_kernel(quarters_ref, first_ref, second_ref, token_ref, edges, sems):
    members = pl.ds(0, HEAD)
    copies = [pltpu.make_async_copy(quarters_ref.at[members, 3 * n], edges.at[n], sems.at[n]) for n in range(2)]
    for copy in copies:
        copy.start()
    token_ref[...] = jnp.zeros_like(token_ref)
    for copy in copies:
        copy.wait()
    low = side_of_first()
    for k in range(HEAD):
        first_ref[64 * k : 64 * k + 64] = edges[1 - low, k].astype(F32)
        second_ref[64 * k : 64 * k + 64] = edges[low, k].astype(F32)


def send_part(quarters):
    return call(
        send_kernel,
        (sds(64 * HEAD, 128), sds(64 * HEAD, 128), sds(8, 128)),
        ins=[HBM],
        outs=(VMEM,) * 3,
        scratch=[pltpu.VMEM((2, HEAD, 64, 128), BF16), pltpu.SemaphoreType.DMA((2,))],
        vmem=56,
    )(quarters)


def rest_kernel(count_ref, col_ref, lev_ref, innov_ref, weight_ref, quarters_ref, after_ref, first_ref, second_ref, obs_ref, edges, sems):
    count = edges.shape[1]
    members = pl.ds(HEAD, count)
    copies = [pltpu.make_async_copy(quarters_ref.at[members, 3 * n], edges.at[n], sems.at[n]) for n in range(2)]
    for copy in copies:
        copy.start()
    sort_observations(count_ref[0], col_ref, lev_ref, innov_ref, weight_ref, obs_ref)
    core = lax.rem(lax.axis_index("mem"), 2)
    half = obs_ref[pl.ds(pl.multiple_of(HALF * core, 8), HALF)]
    first_ref[64 * count :] = half
    second_ref[64 * count :] = half
    for copy in copies:
        copy.wait()
    low = side_of_first()
    for k in range(count):
        first_ref[64 * k : 64 * k + 64] = edges[1 - low, k].astype(F32)
        second_ref[64 * k : 64 * k + 64] = edges[low, k].astype(F32)


def rest_part(count, col, lev, innov, weight, quarters, after):
    members = quarters.shape[0] - HEAD
    return call(
        rest_kernel,
        (sds(64 * members + HALF, 128), sds(64 * members + HALF, 128), sds(OBS, 128)),
        ins=[SMEM] + [VMEM] * 4 + [ANY, VMEM],
        outs=(VMEM,) * 3,
        scratch=[pltpu.VMEM((2, members, 64, 128), BF16), pltpu.SemaphoreType.DMA((2,))],
    )(count, col, lev, innov, weight, quarters, after)


def own_kernel(where_ref, alpha_ref, ens_ref, loc_ref, after_ref, inner_ref, edge_ref, x_ref, smat_ref, hmat_ref):
    @pl.when(pl.program_id(0) == 0)
    def _():
        inner_ref[...] = jnp.zeros_like(inner_ref)
        smat, hmat = matrices(where_ref[6], TILES, where_ref[7] == 0)
        smat_ref[...] = smat
        hmat_ref[...] = hmat

    smat = smat_ref[...]
    loc = loc_ref[...]
    total = [inner_ref[v] for v in range(V)]
    for k in range(GROUP):
        full = lift(nn(smat, alpha_ref[k]), loc)
        edge_ref[k, :64] = full[:64]
        edge_ref[k, 64:] = full[192:]
        lifted = full[64:192].astype(BF16).astype(F32)
        for v in range(V):
            total[v] = total[v] + ens_ref[k, v, 64:192].astype(F32) * lifted
            x_ref[k, v, :64] = ens_ref[k, v, :64]
            x_ref[k, v, 64:] = ens_ref[k, v, 192:]
    for v in range(V):
        inner_ref[v] = total[v]


def own_part(where, alpha, ensemble, loc, after):
    members = alpha.shape[0]
    whole = lambda *shape: pl.BlockSpec(shape, lambda i: (0,) * len(shape))
    return call(
        own_kernel,
        (
            sds(V, 128, 128),
            sds(members, 128, 128),
            sds(members, V, 128, 128, dtype=BF16),
            sds(256, 256, dtype=BF16),
            sds(128, 128, dtype=BF16),
        ),
        grid=(members // GROUP,),
        ins=[
            SMEM,
            pl.BlockSpec((GROUP, 256, 128), lambda i: (i, 0, 0)),
            pl.BlockSpec((GROUP, V, 256, 128), lambda i: (i, 0, 0, 0)),
            whole(128, 128),
            whole(8, 128),
        ],
        outs=(
            whole(V, 128, 128),
            pl.BlockSpec((GROUP, 128, 128), lambda i: (i, 0, 0)),
            pl.BlockSpec((GROUP, V, 128, 128), lambda i: (i, 0, 0, 0)),
            whole(256, 256),
            whole(128, 128),
        ),
    )(where, alpha, ensemble, loc, after)


def edge_terms(first_ref, second_ref, own_ref, x_ref, hmat_ref, loc_ref, start, count, total):
    hmat = hmat_ref[...]
    loc = loc_ref[...]
    for k in range(count):
        rows = slice(64 * k, 64 * k + 64)
        halo = jnp.concatenate([first_ref[rows].astype(BF16), second_ref[rows].astype(BF16)], axis=0)
        lifted = (own_ref[start + k] + lift(nn(hmat, halo), loc)).astype(BF16).astype(F32)
        for v in range(V):
            total[v] = total[v] + x_ref[start + k, v].astype(F32) * lifted
    return total


def head_kernel(first_ref, second_ref, own_ref, x_ref, hmat_ref, loc_ref, total_ref):
    zeros = [jnp.zeros((128, 128), F32) for v in range(V)]
    total = edge_terms(first_ref, second_ref, own_ref, x_ref, hmat_ref, loc_ref, 0, HEAD, zeros)
    for v in range(V):
        total_ref[v] = total[v]


def head_part(first, second, own, x, hmat, loc):
    return call(head_kernel, sds(V, 128, 128), ins=[VMEM] * 6, outs=VMEM)(first, second, own, x, hmat, loc)


def edge_kernel(where_ref, first_ref, second_ref, own_ref, x_ref, hmat_ref, loc_ref, inner_ref, head_ref, inc_ref, keep_ref, give_ref):
    total = [head_ref[v] for v in range(V)]
    total = edge_terms(first_ref, second_ref, own_ref, x_ref, hmat_ref, loc_ref, HEAD, own_ref.shape[0] - HEAD, total)
    for v in range(V):
        inc_ref[v, :64] = total[v][:64]
        inc_ref[v, 64:192] = inner_ref[v]
        inc_ref[v, 192:] = total[v][64:]
        keep_ref[32 * v : 32 * v + 32] = inc_ref[v, pl.ds(pl.multiple_of(where_ref[8], 32), 32)]
        give_ref[32 * v : 32 * v + 32] = inc_ref[v, pl.ds(pl.multiple_of(where_ref[9], 32), 32)]
    end = first_ref.shape[0] - HALF
    give_ref[32 * V : 32 * V + HALF] = first_ref[end:]
    give_ref[32 * V + HALF :] = second_ref[end:]


def edge_part(where, first, second, own, x, hmat, loc, inner, head):
    return call(
        edge_kernel,
        (sds(V, 256, 128), sds(V * 32, 128), sds(V * 32 + OBS, 128)),
        ins=[SMEM] + [VMEM] * 8,
        outs=(VMEM,) * 3,
    )(where, first, second, own, x, hmat, loc, inner, head)


def tent(distance):
    return jnp.maximum(1.0 - jnp.abs(distance), 0.0)


def weights_kernel(where_ref, own_ref, here_ref, there_ref, after_ref, wown_ref, wnear_ref, lev_ref, innov_ref, weight_ref, hot_ref, o_ref, e_ref):
    core = where_ref[10]
    for half, ref in ((core, here_ref), (1 - core, there_ref)):
        rows = pl.ds(pl.multiple_of(HALF * half, 8), HALF)
        o_ref[rows] = ref[32 * V : 32 * V + HALF]
        e_ref[rows] = ref[32 * V + HALF :]
    level = lax.broadcasted_iota(jnp.int32, (128, SLOTS), 0).astype(F32)
    even_row = where_ref[2].astype(F32)
    odd_row = where_ref[3].astype(F32)
    odd_there = where_ref[4].astype(F32)
    cell = lax.broadcasted_iota(jnp.int32, (32, SLOTS), 0).astype(F32)

    def line(ref, field, v):
        at = 6 * (V * field + v)
        return jnp.concatenate([ref[at + a : at + a + 1] for a in range(6)], axis=1)

    def columns(code):
        row = jnp.floor(code * (1.0 / 64.0))
        column = code - 64.0 * row
        return row, tent(cell - (column * 0.5 - 0.25))

    for v in range(V):
        row, across = columns(line(own_ref, 0, v))
        middle = row * 0.5 - 0.25
        for r in range(8):
            wown_ref[v, 32 * r : 32 * r + 32] = (tent(r - middle) * across).astype(BF16)
        wown_ref[v, 256:288] = (tent(even_row - middle) * across).astype(BF16)
        wown_ref[v, 288:320] = (tent(odd_row - middle) * odd_there * across).astype(BF16)
        for n, ref in enumerate((e_ref, o_ref)):
            row, across = columns(line(ref, 0, v))
            wnear_ref[n, v, :32] = (0.25 * across).astype(BF16)
            wnear_ref[n, v, 32:] = (0.75 * across).astype(BF16)
    is_odd = where_ref[5]
    for n, ref in enumerate((own_ref, e_ref, o_ref)):
        for v in range(V):
            row = slice(3 * n + v, 3 * n + v + 1)
            lev = line(ref, 1, v)
            lev_ref[row] = lev
            hot_ref[3 * n + v] = jnp.where(level == lev, 1.0, 0.0).astype(BF16)
            innov_ref[row] = line(ref, 2, v)
            weight = line(ref, 3, v)
            if n > 0:
                code = line(ref, 0, v)
                first = is_odd == (0 if n == 1 else 1)
                at_edge = jnp.where(first, code, 1023.0 - code) < 64.0
                there = at_edge & ((n == 1) | (where_ref[4] == 1))
                weight = jnp.where(there, weight, 0.0)
            weight_ref[row] = weight


def weights(where, own, here, there, after):
    return call(
        weights_kernel,
        (
            sds(V, 320, SLOTS, dtype=BF16),
            sds(2, V, 64, SLOTS, dtype=BF16),
            sds(9, SLOTS),
            sds(9, SLOTS),
            sds(9, SLOTS),
            sds(9, 128, SLOTS, dtype=BF16),
        ),
        ins=[SMEM] + [VMEM] * 4,
        scratch=[pltpu.VMEM((OBS, 128), F32), pltpu.VMEM((OBS, 128), F32)],
    )(where, own, here, there, after)


def picker(lev_ref):
    level = lax.broadcasted_iota(jnp.int32, (128, SLOTS), 0).astype(F32)

    def pick(cells, weight, row):
        both = jnp.concatenate(halves(cells), axis=0)
        at_all = tn(both, jnp.concatenate([weight, weight], axis=0))
        hot = level == lev_ref[pl.ds(row, 1), :]
        return jnp.sum(jnp.where(hot, at_all, 0.0), axis=0, keepdims=True)

    return pick


def mine_kernel(where_ref, inc_ref, wown_ref, wnear_ref, lev_ref, out_ref):
    pick = picker(lev_ref)
    for v in range(V):
        out_ref[v : v + 1] = pick(inc_ref[v], wown_ref[v, :256], v)
        for n in range(2):
            cells = inc_ref[v, pl.ds(pl.multiple_of(where_ref[n], 32), 32)]
            row = 3 * n + 3 + v
            out_ref[row : row + 1] = pick(cells, wnear_ref[n, v, :32], row)


def mine_part(where, inc, wown, wnear, lev):
    return call(
        mine_kernel,
        sds(9, SLOTS),
        ins=[SMEM] + [VMEM] * 4,
        outs=VMEM,
    )(where, inc, wown, wnear, lev)


def values_kernel(where_ref, mine_ref, near_ref, wown_ref, wnear_ref, hot_ref, out_ref):
    core = where_ref[10]

    def pick(cells, weight, row):
        both = jnp.concatenate(halves(cells), axis=0)
        at_level = nn(both, hot_ref[row])
        at_level = at_level[:32] + at_level[32:]
        return jnp.sum(weight.astype(F32) * at_level, axis=0, keepdims=True)

    def put(row, line):
        for a in range(6):
            out_ref[pl.ds(6 * row + a, 1)] = line[:, 128 * a : 128 * a + 128]

    for v in range(V):
        for n in range(2):
            row = 3 * n + 3 + v
            put(row, mine_ref[row : row + 1])
    for v in range(V):
        halo = pl.ds(pl.multiple_of(256 + 32 * core, 32), 32)
        put(v, mine_ref[v : v + 1] + pick(near_ref[32 * v : 32 * v + 32], wown_ref[v, halo], v))
        row = 3 * core + 3 + v
        put(row, mine_ref[pl.ds(row, 1)] + pick(near_ref[32 * v : 32 * v + 32], wnear_ref[core, v, 32:], row))


def values(where, mine, near, wown, wnear, hot):
    return call(
        values_kernel,
        sds(9 * SLOTS // 128, 128),
        ins=[SMEM] + [VMEM] * 5,
        outs=VMEM,
    )(where, mine, near, wown, wnear, hot)


def adjoint_kernel(where_ref, v0, v1, innov_ref, weight_ref, hot_ref, wown_ref, wnear_ref, x_ref, c_ref, first_ref, second_ref):
    value = v0[...] + v1[...]

    def weighted(row):
        line = jnp.concatenate([value[6 * row + a : 6 * row + a + 1] for a in range(6)], axis=1)
        return weight_ref[row : row + 1] * (line - innov_ref[row : row + 1])

    def place(weight, row):
        hot = hot_ref[row]
        both = jnp.concatenate([hot * half for half in halves(weighted(row))], axis=0)
        out = nt(weight, both)
        return out[:, :128] + out[:, 128:]

    def place_near(weight, row):
        both = jnp.concatenate(halves(weight.astype(F32) * weighted(row)), axis=0)
        out = nt(both, hot_ref[row])
        return out[:32] + out[32:]

    adj = []
    for v in range(V):
        c_ref[v] = place(wown_ref[v, :256], v)
        for n in range(2):
            rows = pl.ds(pl.multiple_of(where_ref[n], 32), 32)
            c_ref[v, rows] = c_ref[v, rows] + place_near(wnear_ref[n, v, :32], 3 * n + 3 + v)
        adj.append(jnp.concatenate([c_ref[v, :64], c_ref[v, 192:]], axis=0))
    first_low = where_ref[7] == 1
    for k in range(first_ref.shape[0]):
        total = x_ref[k, 0].astype(F32) * adj[0]
        for v in range(1, V):
            total = total + x_ref[k, v].astype(F32) * adj[v]
        low, high = total[:64], total[64:]
        first_ref[k] = jnp.where(first_low, low, high)
        second_ref[k] = jnp.where(first_low, high, low)


def adjoint(where, vals, innov, weight, hot, wown, wnear, x):
    members = HEAD_BACK
    return call(
        adjoint_kernel,
        (sds(V, 256, 128), sds(members, 64, 128), sds(members, 64, 128)),
        ins=[SMEM] + [VMEM] * 8,
        outs=(VMEM,) * 3,
    )(where, *vals, innov, weight, hot, wown, wnear, x)


def drop(smoothed, loc):
    high, low = halves(smoothed)
    return nn(high, loc) + nn(low, loc)


def back_kernel(where_ref, alpha_ref, ens_ref, c_ref, smat_ref, loc_ref, out_ref, edge_ref, first_ref, second_ref):
    low = where_ref[7] == 1
    smat = smat_ref[...]
    loc = loc_ref[...]
    for k in range(GROUP):
        back = ens_ref[k, 0].astype(F32) * c_ref[0]
        for v in range(1, V):
            back = back + ens_ref[k, v].astype(F32) * c_ref[v]
        first_ref[k] = jnp.where(low, back[:64], back[192:])
        second_ref[k] = jnp.where(low, back[192:], back[:64])
        full = alpha_ref[k].astype(F32) + drop(smooth(smat, back), loc)
        out_ref[k] = full
        edge_ref[k, :64] = full[:64]
        edge_ref[k, 64:] = full[192:]


def back_part(where, alpha, ensemble, c, smat, loc):
    members = alpha.shape[0]
    rest = pl.BlockSpec((GROUP, 64, 128), lambda i: (jnp.maximum(i - HEAD_BACK // GROUP, 0), 0, 0))
    return call(
        back_kernel,
        (
            sds(members, 256, 128),
            sds(members, 128, 128),
            sds(members - HEAD_BACK, 64, 128),
            sds(members - HEAD_BACK, 64, 128),
        ),
        grid=(members // GROUP,),
        ins=[
            SMEM,
            pl.BlockSpec((GROUP, 256, 128), lambda i: (i, 0, 0)),
            pl.BlockSpec((GROUP, V, 256, 128), lambda i: (i, 0, 0, 0)),
            pl.BlockSpec((V, 256, 128), lambda i: (0, 0, 0)),
            pl.BlockSpec((256, 256), lambda i: (0, 0)),
            pl.BlockSpec((128, 128), lambda i: (0, 0)),
        ],
        outs=(
            pl.BlockSpec((GROUP, 256, 128), lambda i: (i, 0, 0)),
            pl.BlockSpec((GROUP, 128, 128), lambda i: (i, 0, 0)),
            rest,
            rest,
        ),
    )(where, alpha, ensemble, c, smat, loc)


def last_kernel(start, first_ref, second_ref, edge_ref, hmat_ref, loc_ref, unused_ref, out_ref, held, sems):
    hmat = hmat_ref[...]
    loc = loc_ref[...]
    copies = []
    for g in range(first_ref.shape[0] // GROUP):
        for k in range(g * GROUP, (g + 1) * GROUP):
            halo = jnp.concatenate([first_ref[k], second_ref[k]], axis=0)
            full = edge_ref[start + k] + drop(smooth(hmat, halo), loc)
            held[k, 0] = full[:64]
            held[k, 1] = full[64:]
        here, there = pl.ds(g * GROUP, GROUP), pl.ds(start + g * GROUP, GROUP)
        for side in range(2):
            copies.append(
                pltpu.make_async_copy(held.at[here, side], out_ref.at[there, 3 * side], sems.at[g, side])
            )
            copies[-1].start()
    for copy in copies:
        copy.wait()


def last_part(start, first, second, edge, hmat, loc, out):
    count = first.shape[0]
    return call(
        functools.partial(last_kernel, start),
        sds(*out.shape),
        ins=[VMEM] * 5 + [ANY],
        outs=ANY,
        scratch=[pltpu.VMEM((count, 2, 64, 128), F32), pltpu.SemaphoreType.DMA((count // GROUP, 2))],
        aliases={5: 0},
    )(first, second, edge, hmat, loc, out)


def stencil(gap):
    gap = jnp.abs(gap)
    return jnp.where(gap == 0, 6.0, jnp.where(gap == 1, 4.0, jnp.where(gap == 2, 1.0, 0.0)))


def matrices(tile, tiles, first_high):
    def across(i, j):
        gap = stencil(i - j)
        return jnp.where((i == j) & ((i == 0) | (i == 31)), 5.0, gap)

    i = lax.broadcasted_iota(jnp.int32, (256, 256), 0)
    j = lax.broadcasted_iota(jnp.int32, (256, 256), 1)
    ri, rj = i // 32, j // 32
    ends = ((ri == 0) & (tile == 0)) | ((ri == 7) & (tile == tiles - 1))
    down = jnp.where((ri == rj) & ends, 5.0, stencil(ri - rj))
    smat = (down * across(i % 32, j % 32) * (1.0 / 256.0)).astype(BF16)
    i = lax.broadcasted_iota(jnp.int32, (128, 128), 0)
    j = lax.broadcasted_iota(jnp.int32, (128, 128), 1)
    ri = i // 32
    ri = jnp.where(ri < 2, ri, ri + 4)
    above = (j < 64) == first_high
    rj = jnp.where(above, 8, -2) + (j // 32) % 2
    there = (above & (tile < tiles - 1)) | (jnp.logical_not(above) & (tile > 0))
    hmat = jnp.where(there, stencil(ri - rj), 0.0) * across(i % 32, j % 32) * (1.0 / 256.0)
    return smat, hmat.astype(BF16)


def swap_first(x):
    return lax.ppermute(x, ("mem", "tile"), FIRST)


def swap_second(x):
    return lax.ppermute(x, ("mem", "tile"), SECOND)


def swap_near(x):
    return lax.ppermute(x, ("mem", "tile"), NEAR)


def swap_core(x):
    return lax.ppermute(x, "mem", [(m, m ^ 1) for m in range(MEMS)])


def swap_chip(x):
    return lax.ppermute(x, "mem", [(m, m ^ 2) for m in range(MEMS)])


def on_device(alpha, ensemble, loc_vert, obs_col, obs_lev, obs_count, innovation, obs_weight):
    members = alpha.shape[0]
    tile = lax.axis_index("tile")
    tiles = lax.axis_size("tile")
    even = tile % 2 == 0
    core = lax.axis_index("mem") % 2
    first_low = side_of_first()
    where = jnp.stack(
        [
            jnp.where(even, 7 * 32, 0),
            jnp.where(even, 0, 7 * 32),
            jnp.where(even, 8, -1),
            jnp.where(even, -1, 8),
            ((tile > 0) & (tile < tiles - 1)).astype(jnp.int32),
            tile % 2,
            tile,
            first_low,
            7 * 32 * (1 - (tile + core) % 2),
            7 * 32 * ((tile + core) % 2),
            core,
        ]
    ).astype(jnp.int32)
    flat = alpha.reshape(members, 256, 128)
    flat_ens = ensemble.reshape(members, V, 256, 128)

    quarters = alpha.reshape(members, 4, 64, 128)
    send_first, send_second, token = send_part(quarters)
    first, second = swap_first(send_first), swap_second(send_second)
    inner, own_edge, x, smat, hmat = own_part(where, flat, flat_ens, loc_vert, token)
    send_first, send_second, own_obs = rest_part(
        obs_count, obs_col, obs_lev, innovation, obs_weight, quarters, hmat
    )
    first_rest, second_rest = swap_first(send_first), swap_second(send_second)
    head = head_part(first, second, own_edge, x, hmat, loc_vert)
    inc, keep, give = edge_part(where, first_rest, second_rest, own_edge, x, hmat, loc_vert, inner, head)
    got = swap_core(give)
    edges = keep + got[: V * 32]
    near = swap_near(edges)
    wown, wnear, lev, innov, weight, hot = weights(where, own_obs, give, got, edges)
    mine = mine_part(where, inc, wown, wnear, lev)
    vals = values(where, mine, near, wown, wnear, hot)
    vals = vals + swap_core(vals)
    vals = vals, swap_chip(vals)
    c, back_first, back_second = adjoint(where, vals, innov, weight, hot, wown, wnear, x)
    halo_first, halo_second = swap_first(back_first), swap_second(back_second)
    out, edge, back_first, back_second = back_part(where, flat, flat_ens, c, smat, loc_vert)
    rest_first, rest_second = swap_first(back_first), swap_second(back_second)
    out = last_part(0, halo_first, halo_second, edge, hmat, loc_vert, out.reshape(members, 4, 64, 128))
    out = last_part(HEAD_BACK, rest_first, rest_second, edge, hmat, loc_vert, out)
    return out.reshape(members, 8, 32, 128)


def solution(mesh):
    in_specs = (
        P("mem", "tile", None, None),
        P("mem", None, "tile", None, None),
        P(),
        P("tile", None),
        P("tile", None),
        P("tile"),
        P("tile", None),
        P("tile", None),
    )
    out_specs = P("mem", "tile", None, None)
    return jax.shard_map(
        on_device, mesh=mesh, in_specs=in_specs, out_specs=out_specs, check_vma=False
    )
```

```python
import functools

import jax
import jax.numpy as jnp
from jax import lax
from jax.experimental import pallas as pl
from jax.experimental.pallas import tpu as pltpu
from jax.sharding import PartitionSpec as P

V = 3
F32 = jnp.float32
BF16 = jnp.bfloat16
SLOTS = 768
GROUP = 4
HEAD = 16
HEAD_BACK = 12
OBS = 80
HALF = OBS // 2

TILES = 64
MEMS = 4


def partners(odd, spare):
    pairs = []
    for m in range(MEMS):
        for t in range(TILES):
            beside = ((t - 1) ^ 1) + 1 if odd(m) else t ^ 1
            there = (m, beside) if 0 <= beside < TILES else (m ^ spare, t)
            pairs.append((TILES * m + t, TILES * there[0] + there[1]))
    return pairs


FIRST = partners(lambda m: False, 1)
SECOND = partners(lambda m: True, 1)
NEAR = partners(lambda m: m % 2 == 1, 2)


def nn(a, b):
    return lax.dot_general(a, b, (((1,), (0,)), ((), ())), preferred_element_type=F32)


def nt(a, b):
    return lax.dot_general(a, b, (((1,), (1,)), ((), ())), preferred_element_type=F32)


def tn(a, b):
    return lax.dot_general(a, b, (((0,), (0,)), ((), ())), preferred_element_type=F32)


def halves(x):
    high = x.astype(BF16)
    low = (x - high.astype(F32)).astype(BF16)
    return high, low


def lift(smoothed, loc):
    high, low = halves(smoothed)
    return nt(high, loc) + nt(low, loc)


def call(kernel, out, grid=None, ins=None, outs=None, scratch=(), aliases=None, cost=1000, vmem=16):
    kw = {}
    if grid is not None:
        kw["grid"] = grid
    return pl.pallas_call(
        kernel,
        out_shape=out,
        in_specs=ins,
        out_specs=outs if outs is not None else jax.tree.map(lambda o: VMEM, out),
        scratch_shapes=scratch,
        input_output_aliases=aliases or {},
        compiler_params=pltpu.CompilerParams(vmem_limit_bytes=vmem * 1024 * 1024),
        cost_estimate=pl.CostEstimate(flops=cost, bytes_accessed=cost, transcendentals=0),
        **kw,
    )


def sds(*shape, dtype=F32):
    return jax.ShapeDtypeStruct(shape, dtype)


ANY = pl.BlockSpec(memory_space=pl.ANY)
SMEM = pl.BlockSpec(memory_space=pltpu.SMEM)
VMEM = pl.BlockSpec(memory_space=pltpu.VMEM)
HBM = pl.BlockSpec(memory_space=pltpu.HBM)


def smooth(matrix, field):
    both = jnp.concatenate(halves(field), axis=1)
    out = nn(matrix, both)
    return out[:, :128] + out[:, 128:]


def side_of_first():
    return lax.rem(lax.axis_index("tile"), 2)


def sort_observations(count, col_ref, lev_ref, innov_ref, weight_ref, out_ref):
    slots = col_ref.shape[1]
    live = lax.broadcasted_iota(jnp.int32, (1, slots), 1) < count
    rows = []
    for field in (
        col_ref[...].astype(F32),
        lev_ref[...].astype(F32),
        innov_ref[...],
        jnp.where(live, weight_ref[...], 0.0),
    ):
        field = jnp.concatenate([field, jnp.zeros((1, V * SLOTS - slots), F32)], axis=1)
        rows += [field[:, 384 * a : 384 * a + 384] for a in range(6)]
    rest = jnp.concatenate(rows, axis=0)
    i = lax.broadcasted_iota(jnp.int32, (384, 384), 0)
    j = lax.broadcasted_iota(jnp.int32, (384, 384), 1)
    order = (i == 3 * (j % 128) + j // 128).astype(F32).astype(BF16)
    total = jnp.zeros((24, 384), F32)
    for piece in range(3):
        part = rest.astype(BF16)
        rest = rest - part.astype(F32)
        total = total + nn(part, order)
    out_ref[72:] = jnp.zeros((OBS - 72, 128), F32)
    for f in range(4):
        for a in range(6):
            for v in range(V):
                row = 6 * (V * f + v) + a
                out_ref[row : row + 1] = total[6 * f + a : 6 * f + a + 1, 128 * v : 128 * v + 128]


def send_kernel(quarters_ref, first_ref, second_ref, token_ref, edges, sems):
    members = pl.ds(0, HEAD)
    copies = [pltpu.make_async_copy(quarters_ref.at[members, 3 * n], edges.at[n], sems.at[n]) for n in range(2)]
    for copy in copies:
        copy.start()
    token_ref[...] = jnp.zeros_like(token_ref)
    for copy in copies:
        copy.wait()
    low = side_of_first()
    for k in range(HEAD):
        first_ref[64 * k : 64 * k + 64] = edges[1 - low, k].astype(F32)
        second_ref[64 * k : 64 * k + 64] = edges[low, k].astype(F32)


def send_part(quarters):
    return call(
        send_kernel,
        (sds(64 * HEAD, 128), sds(64 * HEAD, 128), sds(8, 128)),
        ins=[HBM],
        outs=(VMEM,) * 3,
        scratch=[pltpu.VMEM((2, HEAD, 64, 128), BF16), pltpu.SemaphoreType.DMA((2,))],
        vmem=56,
    )(quarters)


def rest_kernel(count_ref, col_ref, lev_ref, innov_ref, weight_ref, quarters_ref, after_ref, first_ref, second_ref, obs_ref, edges, sems):
    count = edges.shape[1]
    members = pl.ds(HEAD, count)
    copies = [pltpu.make_async_copy(quarters_ref.at[members, 3 * n], edges.at[n], sems.at[n]) for n in range(2)]
    for copy in copies:
        copy.start()
    sort_observations(count_ref[0], col_ref, lev_ref, innov_ref, weight_ref, obs_ref)
    core = lax.rem(lax.axis_index("mem"), 2)
    half = obs_ref[pl.ds(pl.multiple_of(HALF * core, 8), HALF)]
    first_ref[64 * count :] = half
    second_ref[64 * count :] = half
    for copy in copies:
        copy.wait()
    low = side_of_first()
    for k in range(count):
        first_ref[64 * k : 64 * k + 64] = edges[1 - low, k].astype(F32)
        second_ref[64 * k : 64 * k + 64] = edges[low, k].astype(F32)


def rest_part(count, col, lev, innov, weight, quarters, after):
    members = quarters.shape[0] - HEAD
    return call(
        rest_kernel,
        (sds(64 * members + HALF, 128), sds(64 * members + HALF, 128), sds(OBS, 128)),
        ins=[SMEM] + [VMEM] * 4 + [ANY, VMEM],
        outs=(VMEM,) * 3,
        scratch=[pltpu.VMEM((2, members, 64, 128), BF16), pltpu.SemaphoreType.DMA((2,))],
    )(count, col, lev, innov, weight, quarters, after)


def own_kernel(where_ref, alpha_ref, ens_ref, loc_ref, after_ref, inner_ref, edge_ref, x_ref, smat_ref, hmat_ref):
    @pl.when(pl.program_id(0) == 0)
    def _():
        inner_ref[...] = jnp.zeros_like(inner_ref)
        smat, hmat = matrices(where_ref[6], TILES, where_ref[7] == 0)
        smat_ref[...] = smat
        hmat_ref[...] = hmat

    smat = smat_ref[...]
    loc = loc_ref[...]
    total = [inner_ref[v] for v in range(V)]
    for k in range(GROUP):
        full = lift(nn(smat, alpha_ref[k]), loc)
        edge_ref[k, :64] = full[:64]
        edge_ref[k, 64:] = full[192:]
        lifted = full[64:192].astype(BF16).astype(F32)
        for v in range(V):
            total[v] = total[v] + ens_ref[k, v, 64:192].astype(F32) * lifted
            x_ref[k, v, :64] = ens_ref[k, v, :64]
            x_ref[k, v, 64:] = ens_ref[k, v, 192:]
    for v in range(V):
        inner_ref[v] = total[v]


def own_part(where, alpha, ensemble, loc, after):
    members = alpha.shape[0]
    whole = lambda *shape: pl.BlockSpec(shape, lambda i: (0,) * len(shape))
    return call(
        own_kernel,
        (
            sds(V, 128, 128),
            sds(members, 128, 128),
            sds(members, V, 128, 128, dtype=BF16),
            sds(256, 256, dtype=BF16),
            sds(128, 128, dtype=BF16),
        ),
        grid=(members // GROUP,),
        ins=[
            SMEM,
            pl.BlockSpec((GROUP, 256, 128), lambda i: (i, 0, 0)),
            pl.BlockSpec((GROUP, V, 256, 128), lambda i: (i, 0, 0, 0)),
            whole(128, 128),
            whole(8, 128),
        ],
        outs=(
            whole(V, 128, 128),
            pl.BlockSpec((GROUP, 128, 128), lambda i: (i, 0, 0)),
            pl.BlockSpec((GROUP, V, 128, 128), lambda i: (i, 0, 0, 0)),
            whole(256, 256),
            whole(128, 128),
        ),
    )(where, alpha, ensemble, loc, after)


def edge_terms(first_ref, second_ref, own_ref, x_ref, hmat_ref, loc_ref, start, count, total):
    hmat = hmat_ref[...]
    loc = loc_ref[...]
    for k in range(count):
        rows = slice(64 * k, 64 * k + 64)
        halo = jnp.concatenate([first_ref[rows].astype(BF16), second_ref[rows].astype(BF16)], axis=0)
        lifted = (own_ref[start + k] + lift(nn(hmat, halo), loc)).astype(BF16).astype(F32)
        for v in range(V):
            total[v] = total[v] + x_ref[start + k, v].astype(F32) * lifted
    return total


def head_kernel(first_ref, second_ref, own_ref, x_ref, hmat_ref, loc_ref, total_ref):
    zeros = [jnp.zeros((128, 128), F32) for v in range(V)]
    total = edge_terms(first_ref, second_ref, own_ref, x_ref, hmat_ref, loc_ref, 0, HEAD, zeros)
    for v in range(V):
        total_ref[v] = total[v]


def head_part(first, second, own, x, hmat, loc):
    return call(head_kernel, sds(V, 128, 128), ins=[VMEM] * 6, outs=VMEM)(first, second, own, x, hmat, loc)


def edge_kernel(where_ref, first_ref, second_ref, own_ref, x_ref, hmat_ref, loc_ref, inner_ref, head_ref, inc_ref, keep_ref, give_ref):
    total = [head_ref[v] for v in range(V)]
    total = edge_terms(first_ref, second_ref, own_ref, x_ref, hmat_ref, loc_ref, HEAD, own_ref.shape[0] - HEAD, total)
    for v in range(V):
        inc_ref[v, :64] = total[v][:64]
        inc_ref[v, 64:192] = inner_ref[v]
        inc_ref[v, 192:] = total[v][64:]
        keep_ref[32 * v : 32 * v + 32] = inc_ref[v, pl.ds(pl.multiple_of(where_ref[8], 32), 32)]
        give_ref[32 * v : 32 * v + 32] = inc_ref[v, pl.ds(pl.multiple_of(where_ref[9], 32), 32)]
    end = first_ref.shape[0] - HALF
    give_ref[32 * V : 32 * V + HALF] = second_ref[end:]
    give_ref[32 * V + HALF :] = first_ref[end:]


def edge_part(where, first, second, own, x, hmat, loc, inner, head):
    return call(
        edge_kernel,
        (sds(V, 256, 128), sds(V * 32, 128), sds(V * 32 + OBS, 128)),
        ins=[SMEM] + [VMEM] * 8,
        outs=(VMEM,) * 3,
    )(where, first, second, own, x, hmat, loc, inner, head)


def tent(distance):
    return jnp.maximum(1.0 - jnp.abs(distance), 0.0)


def weights_kernel(where_ref, own_ref, here_ref, there_ref, after_ref, wown_ref, wnear_ref, lev_ref, innov_ref, weight_ref, hot_ref, o_ref, e_ref):
    core = where_ref[10]
    for half, ref in ((core, here_ref), (1 - core, there_ref)):
        rows = pl.ds(pl.multiple_of(HALF * half, 8), HALF)
        o_ref[rows] = ref[32 * V : 32 * V + HALF]
        e_ref[rows] = ref[32 * V + HALF :]
    level = lax.broadcasted_iota(jnp.int32, (128, SLOTS), 0).astype(F32)
    even_row = where_ref[2].astype(F32)
    odd_row = where_ref[3].astype(F32)
    odd_there = where_ref[4].astype(F32)
    cell = lax.broadcasted_iota(jnp.int32, (32, SLOTS), 0).astype(F32)

    def line(ref, field, v):
        at = 6 * (V * field + v)
        return jnp.concatenate([ref[at + a : at + a + 1] for a in range(6)], axis=1)

    def columns(code):
        row = jnp.floor(code * (1.0 / 64.0))
        column = code - 64.0 * row
        return row, tent(cell - (column * 0.5 - 0.25))

    for v in range(V):
        row, across = columns(line(own_ref, 0, v))
        middle = row * 0.5 - 0.25
        for r in range(8):
            wown_ref[v, 32 * r : 32 * r + 32] = (tent(r - middle) * across).astype(BF16)
        wown_ref[v, 256:288] = (tent(even_row - middle) * across).astype(BF16)
        wown_ref[v, 288:320] = (tent(odd_row - middle) * odd_there * across).astype(BF16)
        for n, ref in enumerate((e_ref, o_ref)):
            row, across = columns(line(ref, 0, v))
            wnear_ref[n, v, :32] = (0.25 * across).astype(BF16)
            wnear_ref[n, v, 32:] = (0.75 * across).astype(BF16)
    is_odd = where_ref[5]
    for n, ref in enumerate((own_ref, e_ref, o_ref)):
        for v in range(V):
            row = slice(3 * n + v, 3 * n + v + 1)
            lev = line(ref, 1, v)
            lev_ref[row] = lev
            hot_ref[3 * n + v] = jnp.where(level == lev, 1.0, 0.0).astype(BF16)
            innov_ref[row] = line(ref, 2, v)
            weight = line(ref, 3, v)
            if n > 0:
                code = line(ref, 0, v)
                first = is_odd == (0 if n == 1 else 1)
                at_edge = jnp.where(first, code, 1023.0 - code) < 64.0
                there = at_edge & ((n == 1) | (where_ref[4] == 1))
                weight = jnp.where(there, weight, 0.0)
            weight_ref[row] = weight


def weights(where, own, here, there, after):
    return call(
        weights_kernel,
        (
            sds(V, 320, SLOTS, dtype=BF16),
            sds(2, V, 64, SLOTS, dtype=BF16),
            sds(9, SLOTS),
            sds(9, SLOTS),
            sds(9, SLOTS),
            sds(9, 128, SLOTS, dtype=BF16),
        ),
        ins=[SMEM] + [VMEM] * 4,
        scratch=[pltpu.VMEM((OBS, 128), F32), pltpu.VMEM((OBS, 128), F32)],
    )(where, own, here, there, after)


def picker(lev_ref):
    level = lax.broadcasted_iota(jnp.int32, (128, SLOTS), 0).astype(F32)

    def pick(cells, weight, row):
        both = jnp.concatenate(halves(cells), axis=0)
        at_all = tn(both, jnp.concatenate([weight, weight], axis=0))
        hot = level == lev_ref[pl.ds(row, 1), :]
        return jnp.sum(jnp.where(hot, at_all, 0.0), axis=0, keepdims=True)

    return pick


def mine_kernel(where_ref, inc_ref, wown_ref, wnear_ref, lev_ref, out_ref):
    pick = picker(lev_ref)
    for v in range(V):
        out_ref[v : v + 1] = pick(inc_ref[v], wown_ref[v, :256], v)
        for n in range(2):
            cells = inc_ref[v, pl.ds(pl.multiple_of(where_ref[n], 32), 32)]
            row = 3 * n + 3 + v
            out_ref[row : row + 1] = pick(cells, wnear_ref[n, v, :32], row)


def mine_part(where, inc, wown, wnear, lev):
    return call(
        mine_kernel,
        sds(9, SLOTS),
        ins=[SMEM] + [VMEM] * 4,
        outs=VMEM,
    )(where, inc, wown, wnear, lev)


def values_kernel(where_ref, mine_ref, near_ref, wown_ref, wnear_ref, hot_ref, out_ref):
    core = where_ref[10]

    def pick(cells, weight, row):
        both = jnp.concatenate(halves(cells), axis=0)
        at_level = nn(both, hot_ref[row])
        at_level = at_level[:32] + at_level[32:]
        return jnp.sum(weight.astype(F32) * at_level, axis=0, keepdims=True)

    def put(row, line):
        for a in range(6):
            out_ref[pl.ds(6 * row + a, 1)] = line[:, 128 * a : 128 * a + 128]

    for v in range(V):
        for n in range(2):
            row = 3 * n + 3 + v
            put(row, mine_ref[row : row + 1])
    for v in range(V):
        halo = pl.ds(pl.multiple_of(256 + 32 * core, 32), 32)
        put(v, mine_ref[v : v + 1] + pick(near_ref[32 * v : 32 * v + 32], wown_ref[v, halo], v))
        row = 3 * core + 3 + v
        put(row, mine_ref[pl.ds(row, 1)] + pick(near_ref[32 * v : 32 * v + 32], wnear_ref[core, v, 32:], row))


def values(where, mine, near, wown, wnear, hot):
    return call(
        values_kernel,
        sds(9 * SLOTS // 128, 128),
        ins=[SMEM] + [VMEM] * 5,
        outs=VMEM,
    )(where, mine, near, wown, wnear, hot)


def adjoint_kernel(where_ref, v0, v1, innov_ref, weight_ref, hot_ref, wown_ref, wnear_ref, x_ref, c_ref, first_ref, second_ref):
    value = v0[...] + v1[...]

    def weighted(row):
        line = jnp.concatenate([value[6 * row + a : 6 * row + a + 1] for a in range(6)], axis=1)
        return weight_ref[row : row + 1] * (line - innov_ref[row : row + 1])

    def place(weight, row):
        hot = hot_ref[row]
        both = jnp.concatenate([hot * half for half in halves(weighted(row))], axis=0)
        out = nt(weight, both)
        return out[:, :128] + out[:, 128:]

    def place_near(weight, row):
        both = jnp.concatenate(halves(weight.astype(F32) * weighted(row)), axis=0)
        out = nt(both, hot_ref[row])
        return out[:32] + out[32:]

    adj = []
    for v in range(V):
        c_ref[v] = place(wown_ref[v, :256], v)
        for n in range(2):
            rows = pl.ds(pl.multiple_of(where_ref[n], 32), 32)
            c_ref[v, rows] = c_ref[v, rows] + place_near(wnear_ref[n, v, :32], 3 * n + 3 + v)
        adj.append(jnp.concatenate([c_ref[v, :64], c_ref[v, 192:]], axis=0))
    first_low = where_ref[7] == 1
    for k in range(first_ref.shape[0]):
        total = x_ref[k, 0].astype(F32) * adj[0]
        for v in range(1, V):
            total = total + x_ref[k, v].astype(F32) * adj[v]
        low, high = total[:64], total[64:]
        first_ref[k] = jnp.where(first_low, low, high)
        second_ref[k] = jnp.where(first_low, high, low)


def adjoint(where, vals, innov, weight, hot, wown, wnear, x):
    members = HEAD_BACK
    return call(
        adjoint_kernel,
        (sds(V, 256, 128), sds(members, 64, 128), sds(members, 64, 128)),
        ins=[SMEM] + [VMEM] * 8,
        outs=(VMEM,) * 3,
    )(where, *vals, innov, weight, hot, wown, wnear, x)


def drop(smoothed, loc):
    high, low = halves(smoothed)
    return nn(high, loc) + nn(low, loc)


def back_kernel(where_ref, alpha_ref, ens_ref, c_ref, smat_ref, loc_ref, out_ref, edge_ref, first_ref, second_ref):
    low = where_ref[7] == 1
    smat = smat_ref[...]
    loc = loc_ref[...]
    for k in range(GROUP):
        back = ens_ref[k, 0].astype(F32) * c_ref[0]
        for v in range(1, V):
            back = back + ens_ref[k, v].astype(F32) * c_ref[v]
        first_ref[k] = jnp.where(low, back[:64], back[192:])
        second_ref[k] = jnp.where(low, back[192:], back[:64])
        full = alpha_ref[k].astype(F32) + drop(smooth(smat, back), loc)
        out_ref[k] = full
        edge_ref[k, :64] = full[:64]
        edge_ref[k, 64:] = full[192:]


def back_part(where, alpha, ensemble, c, smat, loc):
    members = alpha.shape[0]
    rest = pl.BlockSpec((GROUP, 64, 128), lambda i: (jnp.maximum(i - HEAD_BACK // GROUP, 0), 0, 0))
    return call(
        back_kernel,
        (
            sds(members, 256, 128),
            sds(members, 128, 128),
            sds(members - HEAD_BACK, 64, 128),
            sds(members - HEAD_BACK, 64, 128),
        ),
        grid=(members // GROUP,),
        ins=[
            SMEM,
            pl.BlockSpec((GROUP, 256, 128), lambda i: (i, 0, 0)),
            pl.BlockSpec((GROUP, V, 256, 128), lambda i: (i, 0, 0, 0)),
            pl.BlockSpec((V, 256, 128), lambda i: (0, 0, 0)),
            pl.BlockSpec((256, 256), lambda i: (0, 0)),
            pl.BlockSpec((128, 128), lambda i: (0, 0)),
        ],
        outs=(
            pl.BlockSpec((GROUP, 256, 128), lambda i: (i, 0, 0)),
            pl.BlockSpec((GROUP, 128, 128), lambda i: (i, 0, 0)),
            rest,
            rest,
        ),
    )(where, alpha, ensemble, c, smat, loc)


def last_kernel(start, first_ref, second_ref, edge_ref, hmat_ref, loc_ref, unused_ref, out_ref, held, sems):
    hmat = hmat_ref[...]
    loc = loc_ref[...]
    copies = []
    for g in range(first_ref.shape[0] // GROUP):
        for k in range(g * GROUP, (g + 1) * GROUP):
            halo = jnp.concatenate([first_ref[k], second_ref[k]], axis=0)
            full = edge_ref[start + k] + drop(smooth(hmat, halo), loc)
            held[k, 0] = full[:64]
            held[k, 1] = full[64:]
        here, there = pl.ds(g * GROUP, GROUP), pl.ds(start + g * GROUP, GROUP)
        for side in range(2):
            copies.append(
                pltpu.make_async_copy(held.at[here, side], out_ref.at[there, 3 * side], sems.at[g, side])
            )
            copies[-1].start()
    for copy in copies:
        copy.wait()


def last_part(start, first, second, edge, hmat, loc, out):
    count = first.shape[0]
    return call(
        functools.partial(last_kernel, start),
        sds(*out.shape),
        ins=[VMEM] * 5 + [ANY],
        outs=ANY,
        scratch=[pltpu.VMEM((count, 2, 64, 128), F32), pltpu.SemaphoreType.DMA((count // GROUP, 2))],
        aliases={5: 0},
    )(first, second, edge, hmat, loc, out)


def stencil(gap):
    gap = jnp.abs(gap)
    return jnp.where(gap == 0, 6.0, jnp.where(gap == 1, 4.0, jnp.where(gap == 2, 1.0, 0.0)))


def matrices(tile, tiles, first_high):
    def across(i, j):
        gap = stencil(i - j)
        return jnp.where((i == j) & ((i == 0) | (i == 31)), 5.0, gap)

    i = lax.broadcasted_iota(jnp.int32, (256, 256), 0)
    j = lax.broadcasted_iota(jnp.int32, (256, 256), 1)
    ri, rj = i // 32, j // 32
    ends = ((ri == 0) & (tile == 0)) | ((ri == 7) & (tile == tiles - 1))
    down = jnp.where((ri == rj) & ends, 5.0, stencil(ri - rj))
    smat = (down * across(i % 32, j % 32) * (1.0 / 256.0)).astype(BF16)
    i = lax.broadcasted_iota(jnp.int32, (128, 128), 0)
    j = lax.broadcasted_iota(jnp.int32, (128, 128), 1)
    ri = i // 32
    ri = jnp.where(ri < 2, ri, ri + 4)
    above = (j < 64) == first_high
    rj = jnp.where(above, 8, -2) + (j // 32) % 2
    there = (above & (tile < tiles - 1)) | (jnp.logical_not(above) & (tile > 0))
    hmat = jnp.where(there, stencil(ri - rj), 0.0) * across(i % 32, j % 32) * (1.0 / 256.0)
    return smat, hmat.astype(BF16)


def swap_first(x):
    return lax.ppermute(x, ("mem", "tile"), FIRST)


def swap_second(x):
    return lax.ppermute(x, ("mem", "tile"), SECOND)


def swap_near(x):
    return lax.ppermute(x, ("mem", "tile"), NEAR)


def swap_core(x):
    return lax.ppermute(x, "mem", [(m, m ^ 1) for m in range(MEMS)])


def swap_chip(x):
    return lax.ppermute(x, "mem", [(m, m ^ 2) for m in range(MEMS)])


def on_device(alpha, ensemble, loc_vert, obs_col, obs_lev, obs_count, innovation, obs_weight):
    members = alpha.shape[0]
    tile = lax.axis_index("tile")
    tiles = lax.axis_size("tile")
    even = tile % 2 == 0
    core = lax.axis_index("mem") % 2
    first_low = side_of_first()
    where = jnp.stack(
        [
            jnp.where(even, 7 * 32, 0),
            jnp.where(even, 0, 7 * 32),
            jnp.where(even, 8, -1),
            jnp.where(even, -1, 8),
            ((tile > 0) & (tile < tiles - 1)).astype(jnp.int32),
            tile % 2,
            tile,
            first_low,
            7 * 32 * (1 - (tile + core) % 2),
            7 * 32 * ((tile + core) % 2),
            core,
        ]
    ).astype(jnp.int32)
    flat = alpha.reshape(members, 256, 128)
    flat_ens = ensemble.reshape(members, V, 256, 128)

    quarters = alpha.reshape(members, 4, 64, 128)
    send_first, send_second, token = send_part(quarters)
    first, second = swap_first(send_first), swap_second(send_second)
    inner, own_edge, x, smat, hmat = own_part(where, flat, flat_ens, loc_vert, token)
    send_first, send_second, own_obs = rest_part(
        obs_count, obs_col, obs_lev, innovation, obs_weight, quarters, hmat
    )
    first_rest, second_rest = swap_first(send_first), swap_second(send_second)
    head = head_part(first, second, own_edge, x, hmat, loc_vert)
    inc, keep, give = edge_part(where, first_rest, second_rest, own_edge, x, hmat, loc_vert, inner, head)
    got = swap_core(give)
    edges = keep + got[: V * 32]
    near = swap_near(edges)
    wown, wnear, lev, innov, weight, hot = weights(where, own_obs, give, got, edges)
    mine = mine_part(where, inc, wown, wnear, lev)
    vals = values(where, mine, near, wown, wnear, hot)
    vals = vals + swap_core(vals)
    vals = vals, swap_chip(vals)
    c, back_first, back_second = adjoint(where, vals, innov, weight, hot, wown, wnear, x)
    halo_first, halo_second = swap_first(back_first), swap_second(back_second)
    out, edge, back_first, back_second = back_part(where, flat, flat_ens, c, smat, loc_vert)
    rest_first, rest_second = swap_first(back_first), swap_second(back_second)
    out = last_part(0, halo_first, halo_second, edge, hmat, loc_vert, out.reshape(members, 4, 64, 128))
    out = last_part(HEAD_BACK, rest_first, rest_second, edge, hmat, loc_vert, out)
    return out.reshape(members, 8, 32, 128)


def solution(mesh):
    in_specs = (
        P("mem", "tile", None, None),
        P("mem", None, "tile", None, None),
        P(),
        P("tile", None),
        P("tile", None),
        P("tile"),
        P("tile", None),
        P("tile", None),
    )
    out_specs = P("mem", "tile", None, None)
    return jax.shard_map(
        on_device, mesh=mesh, in_specs=in_specs, out_specs=out_specs, check_vma=False
    )
```
